32 devices in a mesh: dp: 32 (over z, y, x, core).
Axes of the slice: x: 2, y: 2, z: 4, core: 2. Of those that a mesh axis runs over, the one named last changes fastest.
Arguments:
- tokens: bfloat16 [16384, 1024], P('dp'), may hold values from -6 to 6
- segment_ids: int32 [16384], P('dp'), may hold values from 0 to 511, never falling along the last dimension, each value on 1 to 512 neighbouring positions
- cotangent: bfloat16 [16384, 1024], P('dp'), may hold values from -6 to 6
- norm1_gain: float32 [1024], P('dp'), may hold values from 0.5 to 1.5
- mixer_in: float32 [1024, 6144], P('dp'), may hold values from -0.1875 to 0.1875
- decay_in: float32 [1024, 16], P('dp'), may hold values from -0.375 to 0.375
- conv_weight: float32 [4, 4096], P(None, 'dp'), may hold values from -3 to 3
- decay_log: float32 [8], replicated, may hold values from -1 to 2.5
- decay_bias: float32 [8], replicated, may hold values from -7 to -2
- head_gain: float32 [256], replicated, may hold values from 0.25 to 1.75
- mixer_out: float32 [2048, 1024], P(None, 'dp'), may hold values from -0.25 to 0.25
- norm2_gain: float32 [1024], P('dp'), may hold values from 0.5 to 1.5
- ffn_in: float32 [1024, 5632], P('dp'), may hold values from -0.1875 to 0.1875
- ffn_out: float32 [2816, 1024], P(None, 'dp'), may hold values from -0.21875 to 0.21875
Outputs:
- output: bfloat16 [16384, 1024], P('dp')
- input_grad: float32 [16384, 1024], P('dp')
- norm1_grad: float32 [1024], P('dp')
- mixer_in_grad: float32 [1024, 6144], P('dp')
- decay_in_grad: float32 [1024, 16], P('dp')
- conv_grad: float32 [4, 4096], P(None, 'dp')
- decay_log_grad: float32 [8], replicated
- decay_bias_grad: float32 [8], replicated
- head_gain_grad: float32 [256], replicated
- mixer_out_grad: float32 [2048, 1024], P(None, 'dp')
- norm2_grad: float32 [1024], P('dp')
- ffn_in_grad: float32 [1024, 5632], P('dp')
- ffn_out_grad: float32 [2816, 1024], P(None, 'dp')
The draws below stay inside these ranges and needn't reach their ends.
Inputs may be any that keep to these rules, and one draw needn't show every extreme that they name: `segment_ids`: segment numbers never fall along the tokens; each of the 512 documents holds 1 to 512 tokens, one of them exactly 512.
All inputs are finite; a program needn't handle non-finite values.
Results may differ from the reference program's by a relative error of at most 0.009.
The reference program's roundings to bfloat16 on the way count: a program that leaves them out, or rounds other values in their place, can miss the bound.
Values may be sent and summed in bfloat16 or wider, within the bound.
A program may use at most 384 MiB of HBM per device.

```python
import math
import jax
import jax.numpy as jnp
import numpy as np
from jax import lax

D = 1024
HEADS = 8
DK = 128
DV = 256
FF = 2816
CONV = 4
GROUP = 64
SEQ = 256
TOKENS = 16384
DOCS = 512


def block_levels(key, shape, shards, smallest, largest):
    factor_of = 1.0
    for axis_at, blocks in shards:
        draws = jax.random.uniform(jax.random.fold_in(jax.random.fold_in(key, 6), axis_at), (blocks,), jnp.float32, smallest / len(shards), largest / len(shards))
        factor_of = factor_of * jnp.repeat(jnp.exp(draws), shape[axis_at] // blocks).reshape((-1,) + (1,) * (len(shape) - 1 - axis_at))
    return factor_of


def split_up(number_of, total, reach, slope):
    weights = [(1 << 20) // math.isqrt(grade ** slope) + 1 for grade in range(2, number_of + 1)]
    surplus, given = total - reach - (number_of - 1), [1] * (number_of - 1)
    while surplus > 0:
        free = [i for i in range(number_of - 1) if given[i] < reach]
        whole, budget = sum([weights[i] for i in free]), surplus
        for i in free:
            addition = min(reach - given[i], max(1, budget * weights[i] // whole), surplus)
            given[i] = given[i] + addition
            surplus = surplus - addition
    return np.array([reach] + given)


def uneven_parts(own_key, count, total, bound, slope):
    if count == 2:
        one = jax.random.randint(own_key, (), max(1, total - bound), min(bound, total - 1) + 1)
        return jnp.stack([one, total - one])
    tallies = jnp.asarray(split_up(count, total, bound, slope), jnp.int32)
    couples = (count - 1) // 2
    source_of, receiver = tallies[1:1 + 2 * couples:2], tallies[2:2 + 2 * couples:2]
    room = jnp.minimum(source_of - 1, bound - receiver)
    moved = jax.random.randint(jax.random.fold_in(own_key, 1), (couples,), 0, 1 << 20) % (room + 1)
    tallies = tallies.at[1:1 + 2 * couples:2].set(source_of - moved).at[2:2 + 2 * couples:2].set(receiver + moved)
    return tallies[jax.random.permutation(jax.random.fold_in(own_key, 2), count)]


def scatter_about(key, shape, deviation, most, cuts=(), kind=jnp.bfloat16):
    drawn = jax.random.normal(key, shape, jnp.float32) * deviation
    if len(cuts) > 0:
        drawn = block_levels(key, shape, cuts, -0.22, 0.18) * drawn
    return jnp.clip(drawn, min=-most, max=most).astype(kind)


def setup_inputs(seed: int = 0) -> dict:
    keys = jax.random.split(jax.random.key(seed), 15)
    return {
        "tokens": scatter_about(keys[0], (TOKENS, D), 1.0, 6.0, ((0, 32),)),
        "segment_ids": jnp.searchsorted(jnp.cumsum(uneven_parts(keys[1], DOCS, TOKENS, 2 * SEQ, 2)), jnp.arange(TOKENS), side="right").astype(jnp.int32),
        "cotangent": scatter_about(keys[2], (TOKENS, D), 1.0, 6.0, ((0, 32),)),
        "norm1_gain": jnp.clip(1.0 + 0.1 * jax.random.normal(keys[3], (D,), jnp.float32), 0.5, 1.5),
        "mixer_in": scatter_about(keys[4], (D, 2 * HEADS * DK + 2 * HEADS * DV), D ** -0.5, 0.1875, ((0, 32),), jnp.float32),
        "decay_in": scatter_about(keys[5], (D, 2 * HEADS), (D // 4) ** -0.5, 0.375, ((0, 32),), jnp.float32),
        "conv_weight": scatter_about(keys[6], (CONV, 2 * HEADS * DK + HEADS * DV), CONV ** -0.5, 3.0, ((1, 32),), jnp.float32),
        "decay_log": jnp.clip(jax.random.uniform(keys[7], (HEADS,), jnp.float32, -1.0, 2.5), -1.0, 2.5),
        "decay_bias": jnp.clip(jax.random.uniform(keys[8], (HEADS,), jnp.float32, -7.0, -2.0), -7.0, -2.0),
        "head_gain": jnp.clip(1.0 + 0.15 * jax.random.normal(keys[9], (DV,), jnp.float32), 0.25, 1.75),
        "mixer_out": scatter_about(keys[10], (HEADS * DV, D), (HEADS * DV // 4) ** -0.5, 0.25, ((1, 32),), jnp.float32),
        "norm2_gain": jnp.clip(1.0 + 0.1 * jax.random.normal(keys[11], (D,), jnp.float32), 0.5, 1.5),
        "ffn_in": scatter_about(keys[12], (D, 2 * FF), D ** -0.5, 0.1875, ((0, 32),), jnp.float32),
        "ffn_out": scatter_about(keys[13], (FF, D), (FF // 4) ** -0.5, 0.21875, ((1, 32),), jnp.float32),
    }


MATMUL_EXACTNESS = lax.Precision.HIGHEST
epsilon = 1e-06
head_epsilon = 0.001

@jax.custom_vjp
def low(v):
    return lax.optimization_barrier(v.astype(jnp.bfloat16)).astype(jnp.float32)

@jax.custom_vjp
def low_back(v):
    return v

def low_keep(v):
    return (low(v), None)

def low_pass(kept, grad):
    return (grad,)

def back_keep(v):
    return (v, None)

def back_low(kept, grad):
    return (low(grad),)
low.defvjp(low_keep, low_pass)
low_back.defvjp(back_keep, back_low)

def rms_scale(values, gain_vec):
    return values * lax.rsqrt(lax.optimization_barrier(jnp.mean(values * values, axis=-1, keepdims=True)) + epsilon) * gain_vec

def product(left, right):
    return jnp.dot(left, right, precision=MATMUL_EXACTNESS, preferred_element_type=jnp.float32)

def swiglu(gate_up):
    split_at = gate_up.shape[-1] // 2
    return jax.nn.silu(gate_up[:, :split_at]) * gate_up[:, split_at:]

def short_conv(values, weight, segment):
    summed = values * weight[0]
    for offset in range(1, weight.shape[0]):
        shifted = jnp.pad(values[:-offset], ((offset, 0), (0, 0)))
        earlier = jnp.pad(segment[:-offset], (offset, 0), constant_values=-1)
        same_doc = (earlier == segment).astype(jnp.float32)[:, None]
        summed = summed + shifted * same_doc * weight[offset]
    return summed

def group_inverse(coupling):
    order_size = coupling.shape[-1]
    identity = jnp.eye(order_size, dtype=coupling.dtype)
    powers = -coupling
    result = identity + powers
    for section_index in range(order_size.bit_length() - 2):
        powers = jnp.matmul(powers, powers, precision=MATMUL_EXACTNESS)
        result = jnp.matmul(result, identity + powers, precision=MATMUL_EXACTNESS)
    return result

def delta_core(queries, key_vecs, values, log_decay, write_rate, segment):
    length, heads, key_size = queries.shape
    value_size = values.shape[-1]
    blocks = length // GROUP

    def by_block(array):
        shaped = array.reshape((blocks, GROUP) + array.shape[1:])
        return jnp.moveaxis(shaped, 2, 1)
    query_b = by_block(queries)
    keys_b = by_block(key_vecs)
    values_b = by_block(values)
    decay_b = by_block(log_decay)
    rate_b = by_block(write_rate)
    seg_b = segment.reshape(blocks, GROUP)
    previous = jnp.concatenate([jnp.full((1,), -1, jnp.int32), seg_b[:-1, -1].astype(jnp.int32)])
    carried = (seg_b == previous[:, None]).astype(jnp.float32)
    position = jnp.arange(GROUP)
    lower_tri = position[:, None] >= position[None, :]
    strict = position[:, None] > position[None, :]
    same_doc = ((seg_b[:, :, None] == seg_b[:, None, :]) & lower_tri)[:, None]
    cumulative = jnp.cumsum(decay_b, axis=-1)
    spread = cumulative[..., :, None] - cumulative[..., None, :]
    pair_decay = jnp.where(same_doc, jnp.exp(jnp.where(same_doc, spread, 0.0)), 0.0)
    start_decay = jnp.exp(cumulative) * carried[:, None, :]
    key_dots = jnp.einsum('nhik,nhjk->nhij', keys_b, keys_b, precision=MATMUL_EXACTNESS)
    coupling = jnp.where(strict, pair_decay * key_dots, 0.0) * rate_b[..., :, None]
    inverse = group_inverse(coupling)
    base_values = jnp.einsum('nhij,nhjv->nhiv', inverse, rate_b[..., None] * values_b, precision=MATMUL_EXACTNESS)
    base_keys = jnp.einsum('nhij,nhjk->nhik', inverse, (rate_b * start_decay)[..., None] * keys_b, precision=MATMUL_EXACTNESS)
    scores = pair_decay * jnp.einsum('nhik,nhjk->nhij', query_b, keys_b, precision=MATMUL_EXACTNESS)
    start_query = start_decay[..., None] * query_b
    end_keys = pair_decay[..., -1, :, None] * keys_b
    end_decay = start_decay[..., -1]

    def advance(running_state, pieces):
        value_basis, key_basis, score, leading_query, final_keys, final_decay = pieces
        state_update = value_basis - jnp.einsum('bil,blw->biw', key_basis, running_state, precision=MATMUL_EXACTNESS)
        output = jnp.einsum('bil,blw->biw', leading_query, running_state, precision=MATMUL_EXACTNESS)
        output = output + jnp.einsum('hij,hjv->hiv', score, state_update, precision=MATMUL_EXACTNESS)
        running_state = final_decay[:, None, None] * running_state + jnp.einsum('uxp,uxo->upo', final_keys, state_update, precision=MATMUL_EXACTNESS)
        return (running_state, output)
    initial = jnp.zeros((heads, key_size, value_size), jnp.float32)
    _, outputs = lax.scan(advance, initial, (base_values, base_keys, scores, start_query, end_keys, end_decay))
    return jnp.moveaxis(outputs, 1, 2).reshape(length, heads, value_size)

def mixer_piece(segment, projected, gate_logits, conv_taps, decay_log, decay_bias, head_gain):
    length = projected.shape[0]
    conv_width = conv_taps.shape[1]
    key_width = HEADS * DK
    activated = jax.nn.silu(short_conv(projected[:, :conv_width], conv_taps, segment))
    queries = activated[:, :key_width].reshape(length, HEADS, DK)
    key_vecs = activated[:, key_width:2 * key_width].reshape(length, HEADS, DK)
    values = activated[:, 2 * key_width:].reshape(length, HEADS, DV)
    queries = queries * lax.rsqrt(lax.optimization_barrier(jnp.sum(queries * queries, axis=-1, keepdims=True)) + epsilon) * DK ** (-0.5)
    key_vecs = key_vecs * lax.rsqrt(lax.optimization_barrier(jnp.sum(key_vecs * key_vecs, axis=-1, keepdims=True)) + epsilon)
    log_decay = -jnp.exp(decay_log) * jax.nn.softplus(gate_logits[:, :HEADS] + decay_bias)
    write_rate = jax.nn.sigmoid(gate_logits[:, HEADS:])
    core = delta_core(queries, key_vecs, values, log_decay, write_rate, segment)
    normed = core * lax.rsqrt(lax.optimization_barrier(jnp.mean(core * core, axis=-1, keepdims=True)) + head_epsilon) * head_gain
    gated = normed * jax.nn.silu(projected[:, conv_width:].reshape(length, HEADS, DV))
    return gated.reshape(length, HEADS * DV)

def layer(inputs, segment, params):
    norm_first, weight_in, weight_decay, conv_taps, decay_log, decay_bias, head_gain, weight_out, norm_second, weight_ffin, weight_ffout = params
    normed_in = low(rms_scale(inputs, norm_first))
    projected = low_back(product(normed_in, weight_in))
    gate_logits = low_back(product(normed_in, weight_decay))
    mixed = low(mixer_piece(segment, projected, gate_logits, conv_taps, decay_log, decay_bias, head_gain))
    middle = inputs + low_back(product(mixed, weight_out))
    normed_mid = low(rms_scale(middle, norm_second))
    gate_up = low_back(product(normed_mid, weight_ffin))
    hidden = low(swiglu(gate_up))
    return middle + low_back(product(hidden, weight_ffout))

def reference(tokens, segment_ids, cotangent, norm1_gain, mixer_in, decay_in, conv_weight, decay_log, decay_bias, head_gain, mixer_out, norm2_gain, ffn_in, ffn_out):
    masters = (norm1_gain, mixer_in, decay_in, conv_weight, decay_log, decay_bias, head_gain, mixer_out, norm2_gain, ffn_in, ffn_out)
    inputs = tokens.astype(jnp.float32)
    sequences = segment_ids.reshape(-1, SEQ)
    checked = jax.checkpoint(layer)

    def whole(params, values):
        rounded = (low(params[0]), low(params[1]), low(params[2]), low(params[3]), params[4], params[5], params[6], low(params[7]), low(params[8]), low(params[9]), low(params[10]))

        def scan_step(carry, pair):
            return (carry, checked(pair[0], pair[1], rounded))
        _, result = lax.scan(scan_step, jnp.zeros((), jnp.float32), (values.reshape(-1, SEQ, D), sequences))
        return result.reshape(-1, D)
    output, pullback = jax.vjp(whole, masters, inputs)
    grads, input_grad = pullback(cotangent.astype(jnp.float32))
    return (output.astype(jnp.bfloat16), input_grad, grads[0], grads[1], grads[2], grads[3], grads[4], grads[5], grads[6], grads[7], grads[8], grads[9], grads[10])
```

```python
from functools import partial

import jax
import jax.numpy as jnp
from jax import lax
from jax.experimental import pallas as pl
from jax.experimental.pallas import tpu as pltpu
from jax.sharding import PartitionSpec as P

HEADS = 8
DK = 128
DV = 256
SEQ = 256
HEAD_COLS = 2 * DK + 2 * DV
CONV_COLS = 2 * DK + DV
TILE = 256
SMALL = 128
F32 = jnp.float32
BF16 = jnp.bfloat16
MESH = pl.DeviceIdType.MESH
MIB = 1 << 20
epsilon = 1e-06
head_epsilon = 0.001

NN = ((1,), (0,))
NT = ((1,), (1,))
TN = ((0,), (0,))


def dot1(left, right, dims):
    return lax.dot_general(
        left.astype(BF16), right.astype(BF16), (dims, ((), ())), preferred_element_type=F32
    )


def split(value):
    high = value.astype(BF16)
    return high, (value - high.astype(F32)).astype(BF16)


def dot3(left, right, dims):
    lh, ll = split(left)
    rh, rl = split(right)
    return dot1(lh, rh, dims) + (dot1(lh, rl, dims) + dot1(ll, rh, dims))


def sigmoid(value):
    return 1.0 / (1.0 + jnp.exp(-value))


def grid_of(size):
    rows = lax.broadcasted_iota(jnp.int32, (size, size), 0)
    cols = lax.broadcasted_iota(jnp.int32, (size, size), 1)
    return rows, cols


def unit_inverses(couplings):
    size = couplings[0].shape[0]
    rows, cols = grid_of(size)
    apart = rows ^ cols
    eye = jnp.where(apart == 0, 1.0, 0.0)
    lows = [a.astype(BF16) for a in couplings]
    inverses = [eye - jnp.where(apart < 2, a, 0.0) for a in couplings]
    block = 2
    while block < size:
        here = jnp.where((apart >= block) & (apart < 2 * block), 1.0, 0.0).astype(BF16)
        firsts = [dot1(low * here, inv, NN) for low, inv in zip(lows, inverses)]
        inverses = [inv - dot1(inv, first, NN) for inv, first in zip(inverses, firsts)]
        block *= 2
    return inverses


def pick_lane(columns, lane):
    at = lax.broadcasted_iota(jnp.int32, columns.shape, 1)
    return jnp.sum(jnp.where(at == lane, columns, 0.0), axis=1, keepdims=True)


def conv_of(values, taps, keep):
    total = values * taps[0:1]
    for back in (1, 2, 3):
        total = total + pltpu.roll(values, back, 0) * keep[back - 1] * taps[back : back + 1]
    return total


def decays(seg_col, seg_row, cum_col, cum_row):
    rows, cols = grid_of(SEQ)
    linked = (seg_col == seg_row) & (rows >= cols)
    return jnp.where(linked, jnp.exp(jnp.where(linked, cum_col - cum_row, 0.0)), 0.0)


def strict(value):
    rows, cols = grid_of(SEQ)
    return jnp.where(rows > cols, value, 0.0)


def head_inputs(projected, taps, cols, head):
    keep = [pick_lane(cols, 16 + i) for i in range(3)]
    conv = conv_of(projected[:, :CONV_COLS], taps, keep)
    gate = sigmoid(conv)
    act = conv * gate
    q_act, k_act, value = act[:, :DK], act[:, DK : 2 * DK], act[:, 2 * DK :]
    q_scale = lax.rsqrt(jnp.sum(q_act * q_act, axis=1, keepdims=True) + epsilon)
    k_scale = lax.rsqrt(jnp.sum(k_act * k_act, axis=1, keepdims=True) + epsilon)
    cum = pick_lane(cols, head)
    rate = pick_lane(cols, 8 + head)
    seg = pick_lane(cols, 19)
    return keep, conv, gate, act, q_act * q_scale, k_act * k_scale, value, q_scale, k_scale, cum, rate, seg


def mixer_fwd_body(xn_ref, w_ref, taps_ref, cols_ref, rows_ref, gain_ref, proj_ref, mixed_ref, inv_ref, upd_ref, core_ref):
    head = pl.program_id(0)
    tokens = xn_ref.shape[0]
    projected = jnp.dot(xn_ref[...], w_ref[...], preferred_element_type=F32)
    proj_ref[...] = projected
    _, _, _, _, q, k, value, _, _, cum, rate, seg = head_inputs(
        projected, taps_ref[...], cols_ref[...], head
    )
    q = q * DK**-0.5
    cum_row = rows_ref[pl.ds(head, 1), :]
    seg_row = rows_ref[8:9, :]
    parts = [slice(s, s + SEQ) for s in range(0, tokens, SEQ)]
    scores, couplings = [], []
    for part in parts:
        pair = decays(seg[part], seg_row[:, part], cum[part], cum_row[:, part])
        key_dots = dot3(k[part], k[part], NT)
        scores.append(pair * dot3(q[part], k[part], NT))
        couplings.append(strict(pair * key_dots) * rate[part])
    inverses = unit_inverses(couplings)
    for i, part in enumerate(parts):
        update = dot3(inverses[i], rate[part] * value[part], NN)
        core = dot3(scores[i], update, NN)
        inv_ref[0, part, :] = inverses[i].astype(BF16)
        upd_ref[0, part, :] = update
        core_ref[0, part, :] = core
        scale = lax.rsqrt(jnp.mean(core * core, axis=1, keepdims=True) + head_epsilon)
        out_gate = projected[part, CONV_COLS:]
        mixed_ref[part, :] = (core * scale * gain_ref[...] * (out_gate * sigmoid(out_gate))).astype(BF16)


def mixer_fwd(xn, w, taps, cols, rows, gain):
    tokens, width = xn.shape
    const = lambda h: (0, 0)
    by_head = lambda h: (0, h)
    save = pl.BlockSpec((1, tokens, SEQ), lambda h: (h, 0, 0))
    return pl.pallas_call(
        mixer_fwd_body,
        grid=(HEADS,),
        in_specs=[
            pl.BlockSpec((tokens, width), const),
            pl.BlockSpec((width, HEAD_COLS), by_head),
            pl.BlockSpec((4, CONV_COLS), by_head),
            pl.BlockSpec(cols.shape, const),
            pl.BlockSpec(rows.shape, const),
            pl.BlockSpec((1, DV), const),
        ],
        out_specs=[
            pl.BlockSpec((tokens, HEAD_COLS), by_head),
            pl.BlockSpec((tokens, DV), by_head),
            save,
            save,
            save,
        ],
        out_shape=[
            jax.ShapeDtypeStruct((tokens, HEADS * HEAD_COLS), F32),
            jax.ShapeDtypeStruct((tokens, HEADS * DV), BF16),
            jax.ShapeDtypeStruct((HEADS, tokens, SEQ), BF16),
            jax.ShapeDtypeStruct((HEADS, tokens, DV), F32),
            jax.ShapeDtypeStruct((HEADS, tokens, DV), F32),
        ],
        compiler_params=pltpu.CompilerParams(vmem_limit_bytes=56 * MIB),
        name="mixer_fwd",
    )(xn, w, taps, cols, rows, gain)


def mixer_bwd_body(
    gb_ref, gbt_ref, xnt_ref, wo_ref, w_ref, proj_ref, mixed_ref, inv_ref, upd_ref, core_ref,
    taps_ref, cols_ref, rows_ref, gain_ref,
    dw_ref, dwo_ref, gxn_ref, dcols_ref, drows_ref, dtaps_ref, dgain_ref, dproj_ref,
):
    head = pl.program_id(0)
    tokens = gb_ref.shape[0]

    @pl.when(head == 0)
    def _():
        gxn_ref[...] = jnp.zeros_like(gxn_ref)
        dcols_ref[...] = jnp.zeros_like(dcols_ref)
        drows_ref[...] = jnp.zeros_like(drows_ref)
        dgain_ref[...] = jnp.zeros_like(dgain_ref)

    grad_mixed = jnp.dot(gb_ref[...], wo_ref[...], preferred_element_type=F32)
    dwo_ref[...] = jnp.dot(gbt_ref[...], mixed_ref[...], preferred_element_type=F32).astype(BF16)

    projected = proj_ref[...]
    taps = taps_ref[...]
    keep, conv, gate, act, qn, k, value, q_scale, k_scale, cum, rate, seg = head_inputs(
        projected, taps, cols_ref[...], head
    )
    q = qn * DK**-0.5
    cum_row = rows_ref[pl.ds(head, 1), :]
    seg_row = rows_ref[8:9, :]
    gain = gain_ref[...]
    lanes = lax.broadcasted_iota(jnp.int32, (SEQ, 128), 1)
    d_act, d_gain = [], jnp.zeros((1, DV), F32)
    for start in range(0, tokens, SEQ):
        part = slice(start, start + SEQ)
        core, update, inverse = core_ref[0, part, :], upd_ref[0, part, :], inv_ref[0, part, :]
        grad = grad_mixed[part]
        scale = lax.rsqrt(jnp.mean(core * core, axis=1, keepdims=True) + head_epsilon)
        normed = core * scale
        out_gate = projected[part, CONV_COLS:]
        out_sig = sigmoid(out_gate)
        swish = out_gate * out_sig
        dproj_ref[part, CONV_COLS:] = (grad * normed * gain * (out_sig + swish * (1.0 - out_sig))).astype(BF16)
        d_normed = grad * swish
        d_gain = d_gain + jnp.sum(d_normed * normed, axis=0, keepdims=True)
        d_scaled = d_normed * gain
        d_core = scale * (d_scaled - normed * jnp.mean(d_scaled * normed, axis=1, keepdims=True))

        qs, ks, vs, rs = q[part], k[part], value[part], rate[part]
        pair = decays(seg[part], seg_row[:, part], cum[part], cum_row[:, part])
        key_dots = dot3(ks, ks, NT)
        query_dots = dot3(qs, ks, NT)
        d_scores = dot3(d_core, update, NT)
        d_update = dot1(pair * query_dots, d_core, TN)
        solved = dot1(inverse, d_update, TN)
        d_coupling = strict(-dot1(solved, update, NT)) * pair
        d_query_dots = pair * d_scores
        d_key_dots = d_coupling * rs
        weighed = d_coupling * key_dots
        d_spread = d_query_dots * query_dots + weighed * rs
        d_q = dot1(d_query_dots, ks, NN) * DK**-0.5
        d_k = dot1(d_query_dots, qs, TN) + dot1(d_key_dots, ks, NN) + dot1(d_key_dots, ks, TN)
        d_rate = jnp.sum(solved * vs, axis=1, keepdims=True) + jnp.sum(weighed, axis=1, keepdims=True)
        row_sum = jnp.sum(d_spread, axis=1, keepdims=True)
        dcols_ref[part, :] += jnp.where(lanes == head, d_rate, 0.0) + jnp.where(lanes == 8 + head, row_sum, 0.0)
        drows_ref[pl.ds(head, 1), part] = jnp.sum(d_spread, axis=0, keepdims=True)
        d_q_act = q_scale[part] * (d_q - qn[part] * jnp.sum(d_q * qn[part], axis=1, keepdims=True))
        d_k_act = k_scale[part] * (d_k - ks * jnp.sum(d_k * ks, axis=1, keepdims=True))
        d_act.append(jnp.concatenate([d_q_act, d_k_act, rs * solved], axis=1))
    dgain_ref[...] += d_gain
    d_conv = jnp.concatenate(d_act, axis=0) * (gate + act * (1.0 - gate))
    source = projected[:, :CONV_COLS]
    d_source = d_conv * taps[0:1]
    d_taps = [jnp.sum(d_conv * source, axis=0, keepdims=True)]
    for back in (1, 2, 3):
        kept = d_conv * keep[back - 1]
        d_source = d_source + pltpu.roll(kept, tokens - back, 0) * taps[back : back + 1]
        d_taps.append(jnp.sum(kept * pltpu.roll(source, back, 0), axis=0, keepdims=True))
    dtaps_ref[...] = jnp.concatenate(d_taps, axis=0)
    dproj_ref[:, :CONV_COLS] = d_source.astype(BF16)
    d_proj = dproj_ref[...]
    dw_ref[...] = jnp.dot(xnt_ref[...], d_proj, preferred_element_type=F32).astype(BF16)
    gxn_ref[...] += lax.dot_general(d_proj, w_ref[...], (NT, ((), ())), preferred_element_type=F32)


def mixer_bwd(gb, gbt, xnt, wo, w, proj, mixed, inv, upd, core, taps, cols, rows, gain):
    tokens, width = gb.shape
    const = lambda h: (0, 0)
    by_head = lambda h: (0, h)
    save = pl.BlockSpec((1, tokens, SEQ), lambda h: (h, 0, 0))
    return pl.pallas_call(
        mixer_bwd_body,
        grid=(HEADS,),
        in_specs=[
            pl.BlockSpec((tokens, width), const),
            pl.BlockSpec((width, tokens), const),
            pl.BlockSpec((width, tokens), const),
            pl.BlockSpec((width, DV), by_head),
            pl.BlockSpec((width, HEAD_COLS), by_head),
            pl.BlockSpec((tokens, HEAD_COLS), by_head),
            pl.BlockSpec((tokens, DV), by_head),
            save,
            save,
            save,
            pl.BlockSpec((4, CONV_COLS), by_head),
            pl.BlockSpec(cols.shape, const),
            pl.BlockSpec(rows.shape, const),
            pl.BlockSpec((1, DV), const),
        ],
        out_specs=[
            pl.BlockSpec((width, HEAD_COLS), by_head),
            pl.BlockSpec((width, DV), by_head),
            pl.BlockSpec((tokens, width), const),
            pl.BlockSpec((tokens, 128), const),
            pl.BlockSpec((HEADS, tokens), const),
            pl.BlockSpec((4, CONV_COLS), by_head),
            pl.BlockSpec((1, DV), const),
        ],
        out_shape=[
            jax.ShapeDtypeStruct((width, HEADS * HEAD_COLS), BF16),
            jax.ShapeDtypeStruct((width, HEADS * DV), BF16),
            jax.ShapeDtypeStruct((tokens, width), F32),
            jax.ShapeDtypeStruct((tokens, 128), F32),
            jax.ShapeDtypeStruct((HEADS, tokens), F32),
            jax.ShapeDtypeStruct((4, HEADS * CONV_COLS), F32),
            jax.ShapeDtypeStruct((1, DV), F32),
        ],
        scratch_shapes=[pltpu.VMEM((tokens, HEAD_COLS), BF16)],
        compiler_params=pltpu.CompilerParams(vmem_limit_bytes=60 * MIB),
        name="mixer_bwd",
    )(gb, gbt, xnt, wo, w, proj, mixed, inv, upd, core, taps, cols, rows, gain)


def ffn_body(nm_ref, nmt_ref, cot_ref, cott_ref, w_ref, dw_ref, out_ref, gnm_ref):
    @pl.when(pl.program_id(0) == 0)
    def _():
        out_ref[...] = jnp.zeros_like(out_ref)
        gnm_ref[...] = jnp.zeros_like(gnm_ref)

    w = w_ref[...]
    gate_up = jnp.dot(nm_ref[...], w[:, : 2 * TILE], preferred_element_type=F32)
    gate, up = gate_up[:, :TILE], gate_up[:, TILE:]
    sig = sigmoid(gate)
    swish = gate * sig
    hidden = (swish * up).astype(BF16)
    grad_hidden = jnp.dot(cot_ref[...], w[:, 2 * TILE :], preferred_element_type=F32)
    grad_gate = grad_hidden * up * (sig + swish * (1.0 - sig))
    grad_up = grad_hidden * swish
    grad_low = jnp.concatenate([grad_gate, grad_up], axis=1).astype(BF16)
    out_ref[...] += lax.dot_general(hidden, w[:, 2 * TILE :], (NT, ((), ())), preferred_element_type=F32)
    gnm_ref[...] += lax.dot_general(grad_low, w[:, : 2 * TILE], (NT, ((), ())), preferred_element_type=F32)
    dw_ref[:, : 2 * TILE] = jnp.dot(nmt_ref[...], grad_low, preferred_element_type=F32).astype(BF16)
    dw_ref[:, 2 * TILE :] = jnp.dot(cott_ref[...], hidden, preferred_element_type=F32).astype(BF16)


def ffn(nm, nmt, cot, cott, w):
    tokens, width = nm.shape
    tiles = w.shape[1] // (3 * TILE)
    const = lambda t: (0, 0)
    by_tile = lambda t: (0, t)
    return pl.pallas_call(
        ffn_body,
        grid=(tiles,),
        in_specs=[
            pl.BlockSpec((tokens, width), const),
            pl.BlockSpec((width, tokens), const),
            pl.BlockSpec((tokens, width), const),
            pl.BlockSpec((width, tokens), const),
            pl.BlockSpec((width, 3 * TILE), by_tile),
        ],
        out_specs=[
            pl.BlockSpec((width, 3 * TILE), by_tile),
            pl.BlockSpec((tokens, width), const),
            pl.BlockSpec((tokens, width), const),
        ],
        out_shape=[
            jax.ShapeDtypeStruct((width, tiles * 3 * TILE), BF16),
            jax.ShapeDtypeStruct((tokens, width), F32),
            jax.ShapeDtypeStruct((tokens, width), F32),
        ],
        compiler_params=pltpu.CompilerParams(vmem_limit_bytes=48 * MIB),
        name="ffn",
    )(nm, nmt, cot, cott, w)


def flip(number, bit):
    return number + bit - 2 * bit * ((number // bit) % 2)


def z_partner(me, planes, k):
    other = me
    bit = 1
    while bit < planes:
        if k & bit:
            other = flip(other, 8 * bit)
        bit *= 2
    return other


def z_of(plane, planes, k):
    bit = 1
    while bit < planes:
        if k & bit:
            plane = flip(plane, bit)
        bit *= 2
    return plane


def enter(planes):
    me = lax.axis_index("dp")
    barrier = pltpu.get_barrier_semaphore()
    partners = [flip(me, 1), flip(me, 2), flip(me, 4)]
    partners += [z_partner(me, planes, k) for k in range(1, planes)]
    for other in partners:
        pl.semaphore_signal(barrier, inc=1, device_id=(other,), device_id_type=MESH)
    pl.semaphore_wait(barrier, len(partners))
    return me


class Gather:
    def __init__(self, me, planes, shards, fulls, chunks, local_sem, send_sem, recv_sem):
        self.me, self.planes, self.shards, self.fulls, self.chunks = me, planes, shards, fulls, chunks
        self.local_sem, self.send_sem, self.recv_sem = local_sem, send_sem, recv_sem
        self.plane, self.place = me // 8, me % 8
        self.copies = {}

    def slot(self, k, place):
        array, start, size, _ = self.chunks[k]
        return self.fulls[array].at[:, place, :, pl.ds(start, size)]

    def send(self, k, number, source, target, other):
        copy = pltpu.make_async_remote_copy(
            src_ref=source,
            dst_ref=target,
            send_sem=self.send_sem.at[k, number],
            recv_sem=self.recv_sem.at[k, number],
            device_id=(other,),
            device_id_type=MESH,
        )
        copy.start()
        self.copies[k, number] = copy

    def forward(self, k, number, place, other):
        self.send(k, number, self.slot(k, place), self.slot(k, place), other)

    def planes_step(self, k):
        array, start, size, _ = self.chunks[k]
        own = self.shards[array].at[:, pl.ds(start, size)]
        home = self.fulls[array].at[self.plane, self.place, :, pl.ds(start, size)]
        local = pltpu.make_async_copy(own, home, self.local_sem.at[k])
        local.start()
        self.copies[k, "local"] = local
        for d in range(1, self.planes):
            self.send(k, 6 + d, own, home, z_partner(self.me, self.planes, d))

    def square_step(self, k):
        self.copies[k, "local"].wait()
        for d in range(1, self.planes):
            self.copies[k, 6 + d].wait_recv()
        self.forward(k, 0, self.place, flip(self.me, 2))
        self.forward(k, 1, self.place, flip(self.me, 4))
        self.forward(k, 3, self.place, flip(self.me, 1))

    def diagonal_step(self, k):
        by_y = self.chunks[k][3]
        for number, bit in ((1, 4), (0, 2)) if by_y else ((0, 2), (1, 4)):
            self.copies[k, number].wait_recv()
            place = flip(self.place, bit)
            if number == int(by_y):
                self.forward(k, 2, place, flip(self.me, 6 - bit))
            self.forward(k, 4 + number, place, flip(self.me, 1))

    def core_step(self, k):
        self.copies[k, 2].wait_recv()
        self.forward(k, 6, flip(flip(self.place, 2), 4), flip(self.me, 1))

    def finish(self, k):
        for number in (3, 4, 5, 6):
            self.copies[k, number].wait_recv()
        for number in range(6 + self.planes):
            self.copies[k, number].wait_send()


def gather_body(planes, chunks, count, *refs):
    shards, fulls = refs[:count], refs[count : 2 * count]
    me = enter(planes)
    work = Gather(me, planes, shards, fulls, chunks, *refs[2 * count :])
    total = len(chunks)
    for k in range(-2, total + 2):
        for ahead, step in ((2, work.planes_step), (0, work.square_step), (-1, work.diagonal_step), (-2, work.core_step)):
            if 0 <= k + ahead < total:
                step(k + ahead)
    for k in range(total):
        work.finish(k)


def gather_all(devices, shards, chunks):
    rows = shards[0].shape[0]
    planes = devices // 8
    hbm = pl.BlockSpec(memory_space=pl.ANY)
    fulls = pl.pallas_call(
        partial(gather_body, planes, chunks, len(shards)),
        in_specs=[hbm] * len(shards),
        out_specs=[hbm] * len(shards),
        out_shape=[jax.ShapeDtypeStruct((planes, 8, rows, s.shape[1]), s.dtype) for s in shards],
        scratch_shapes=[
            pltpu.SemaphoreType.DMA((len(chunks),)),
            pltpu.SemaphoreType.DMA((len(chunks), 6 + planes)),
            pltpu.SemaphoreType.DMA((len(chunks), 6 + planes)),
        ],
        compiler_params=pltpu.CompilerParams(collective_id=0, has_side_effects=True),
        name="gather_weights",
    )(*shards)
    return [f.reshape(devices * rows, f.shape[-1]) for f in fulls]


class Scatter:
    def __init__(self, me, planes, grads, out_ref, chunks, from_core, keep, from_x, from_y, from_xy, from_z,
                 local_sem, send_sem, recv_sem):
        self.me, self.planes, self.grads, self.out_ref, self.chunks = me, planes, grads, out_ref, chunks
        self.from_core, self.keep = from_core, keep
        self.from_x, self.from_y, self.from_xy, self.from_z = from_x, from_y, from_xy, from_z
        self.local_sem, self.send_sem, self.recv_sem = local_sem, send_sem, recv_sem
        self.plane, self.core = me // 8, me % 2
        self.here = (me // 2) % 4
        self.copies = {}

    def send(self, k, number, source, target, other):
        copy = pltpu.make_async_remote_copy(
            src_ref=source,
            dst_ref=target,
            send_sem=self.send_sem.at[k, number],
            recv_sem=self.recv_sem.at[k, number],
            device_id=(other,),
            device_id_type=MESH,
        )
        copy.start()
        self.copies[k, number] = copy

    def span(self, k):
        return pl.ds(self.chunks[k][4], self.chunks[k][2])

    def core_step(self, k):
        array, start, size, _, _ = self.chunks[k]
        source = self.grads[array].at[:, :, 1 - self.core, :, pl.ds(start, size)]
        self.send(k, 0, source, self.from_core.at[:, :, :, self.span(k)], flip(self.me, 1))
        mine = self.grads[array].at[:, :, self.core, :, pl.ds(start, size)]
        local = pltpu.make_async_copy(mine, self.keep.at[k % 2, :, :, :, pl.ds(0, size)], self.local_sem.at[k])
        local.start()
        self.copies[k, "local"] = local

    def add(self, k, place, others):
        span = self.span(k)

        def one(plane, carry):
            total = self.from_core[plane, place, :, span].astype(F32)
            for read in others:
                total = total + read(plane).astype(F32)
            self.from_core[plane, place, :, span] = total.astype(BF16)
            return carry

        lax.fori_loop(0, self.planes, one, 0)

    def chip_step(self, k):
        size, by_y = self.chunks[k][2], self.chunks[k][3]
        span = self.span(k)
        self.copies[k, 0].wait_recv()
        self.copies[k, "local"].wait()
        across_x, across_y = flip(self.here, 1), flip(self.here, 2)
        both = flip(across_x, 2)
        order = (both, across_y, across_x) if by_y else (both, across_x, across_y)
        for place in order + (self.here,):
            self.add(k, place, [lambda plane, place=place: self.keep[k % 2, plane, place, :, pl.ds(0, size)]])
            if place is both:
                source = self.from_core.at[:, both, :, span]
                self.send(k, 1, source, self.from_xy.at[:, :, span], flip(self.me, 4 if by_y else 2))
            elif place is order[1]:
                if by_y:
                    self.send_y(k)
                else:
                    self.send_x(k)

    def send_x(self, k):
        span = self.span(k)
        self.send(k, 2, self.from_core.at[:, flip(self.here, 1), :, span], self.from_x.at[:, :, span], flip(self.me, 2))

    def send_y(self, k):
        span = self.span(k)
        self.send(k, 3, self.from_core.at[:, flip(self.here, 2), :, span], self.from_y.at[:, :, span], flip(self.me, 4))

    def diagonal_step(self, k):
        by_y = self.chunks[k][3]
        span = self.span(k)
        self.copies[k, 1].wait_recv()
        place = flip(self.here, 1 if by_y else 2)
        self.add(k, place, [lambda plane: self.from_xy[plane, :, span]])
        if by_y:
            self.send_x(k)
        else:
            self.send_y(k)

    def square_step(self, k):
        span = self.span(k)
        self.copies[k, 2].wait_recv()
        self.copies[k, 3].wait_recv()
        self.add(k, self.here, [lambda plane: self.from_x[plane, :, span], lambda plane: self.from_y[plane, :, span]])
        for d in range(1, self.planes):
            source = self.from_core.at[z_of(self.plane, self.planes, d), self.here, :, span]
            self.send(k, 3 + d, source, self.from_z.at[d - 1, :, span], z_partner(self.me, self.planes, d))

    def planes_step(self, k):
        span = self.span(k)
        total = self.from_core[self.plane, self.here, :, span].astype(F32)
        for d in range(1, self.planes):
            self.copies[k, 3 + d].wait_recv()
            total = total + self.from_z[d - 1, :, span].astype(F32)
        self.out_ref[:, span] = total

    def finish(self, k):
        for number in range(3 + self.planes):
            self.copies[k, number].wait_send()


class Total:
    def __init__(self, me, planes, value_ref, out_ref, got, stage, send_sem, recv_sem):
        self.me, self.planes, self.value_ref, self.out_ref = me, planes, value_ref, out_ref
        self.got, self.stage, self.send_sem, self.recv_sem = got, stage, send_sem, recv_sem
        self.copies = {}

    def send(self, number, source, target, other):
        copy = pltpu.make_async_remote_copy(
            src_ref=source, dst_ref=target, send_sem=self.send_sem.at[number], recv_sem=self.recv_sem.at[number],
            device_id=(other,), device_id_type=MESH,
        )
        copy.start()
        self.copies[number] = copy

    def step(self, number):
        planes, plane = self.planes, self.me // 8
        if number == 0:
            self.stage[0] = self.value_ref[...]
        elif number <= 3:
            self.copies[number - 1].wait_recv()
            self.stage[number] = self.stage[number - 1] + self.got[number - 1]
        if number < 3:
            self.send(number, self.stage.at[number], self.got.at[number], flip(self.me, 1 << number))
        elif number == 3:
            for d in range(1, planes):
                self.send(2 + d, self.stage.at[3], self.got.at[3 + plane], z_partner(self.me, planes, d))
            self.got[3 + plane] = self.stage[3]
        else:
            for d in range(1, planes):
                self.copies[2 + d].wait_recv()
            total = self.got[3]
            for other in range(1, planes):
                total = total + self.got[3 + other]
            self.out_ref[...] = total
            for number in range(2 + planes):
                self.copies[number].wait_send()


def scatter_body(planes, chunks, count, *refs):
    grads, value_ref, out_ref, total_ref = refs[:count], refs[count], refs[count + 1], refs[count + 2]
    me = enter(planes)
    work = Scatter(me, planes, grads, out_ref, chunks, *refs[count + 3 : count + 12])
    small = Total(me, planes, value_ref, total_ref, *refs[count + 12 :])
    total = len(chunks)
    for k in range(-1, total + 3):
        stages = (
            (-3, work.planes_step),
            (-2, work.square_step),
            (-1, work.diagonal_step),
            (0, work.chip_step),
            (1, work.core_step),
        )
        for ahead, step in stages:
            if 0 <= k + ahead < total:
                step(k + ahead)
        if 0 <= k < 5:
            small.step(k)
    for k in range(total):
        work.finish(k)


def scatter_all(devices, grads, value, chunks):
    rows = grads[0].shape[0] // devices
    planes = devices // 8
    width = sum(c[2] for c in chunks)
    widest = max(c[2] for c in chunks)
    hbm = pl.BlockSpec(memory_space=pl.ANY)
    whole = pl.BlockSpec(memory_space=pltpu.VMEM)
    kinds = 3 + planes
    return pl.pallas_call(
        partial(scatter_body, planes, chunks, len(grads)),
        in_specs=[hbm] * len(grads) + [whole],
        out_specs=[whole, whole],
        out_shape=[jax.ShapeDtypeStruct((rows, width), F32), jax.ShapeDtypeStruct(value.shape, F32)],
        scratch_shapes=[
            pltpu.VMEM((planes, 4, rows, width), BF16),
            pltpu.VMEM((2, planes, 4, rows, widest), BF16),
            pltpu.VMEM((planes, rows, width), BF16),
            pltpu.VMEM((planes, rows, width), BF16),
            pltpu.VMEM((planes, rows, width), BF16),
            pltpu.VMEM((planes - 1, rows, width), BF16),
            pltpu.SemaphoreType.DMA((len(chunks),)),
            pltpu.SemaphoreType.DMA((len(chunks), kinds)),
            pltpu.SemaphoreType.DMA((len(chunks), kinds)),
            pltpu.VMEM((3 + planes,) + value.shape, F32),
            pltpu.VMEM((4,) + value.shape, F32),
            pltpu.SemaphoreType.DMA((2 + planes,)),
            pltpu.SemaphoreType.DMA((2 + planes,)),
        ],
        compiler_params=pltpu.CompilerParams(
            collective_id=1, has_side_effects=True, vmem_limit_bytes=60 * MIB
        ),
        name="scatter_grads",
    )(*[g.reshape(planes, 4, 2, rows, g.shape[1]) for g in grads], value)


def cut(chunk_sizes, widths):
    chunks, at = [], 0
    for array, sizes in enumerate(chunk_sizes):
        start = 0
        for size in sizes:
            chunks.append((array, start, size, len(chunks) % 2 == 1, at))
            start, at = start + size, at + size
        assert start == widths[array]
    return chunks


def rms_scale(values):
    return lax.rsqrt(jnp.mean(values * values, axis=-1, keepdims=True) + epsilon)


def rms_back(grad, values, scale, gain):
    normed = values * scale
    d_normed = grad * gain
    d_values = scale * (d_normed - normed * jnp.mean(d_normed * normed, axis=-1, keepdims=True))
    return d_values, jnp.sum(grad * normed, axis=0)


def by_head(parts):
    shaped = [p.reshape(p.shape[0], HEADS, -1) for p in parts]
    return jnp.concatenate(shaped, axis=2).reshape(parts[0].shape[0], -1)


def from_head(values, sizes):
    shaped = values.reshape(values.shape[0], HEADS, -1)
    ends = [sum(sizes[: i + 1]) for i in range(len(sizes))]
    cuts = [shaped[:, :, e - s : e].reshape(values.shape[0], -1) for s, e in zip(sizes, ends)]
    return jnp.concatenate(cuts, axis=1)


def split_heads(values):
    key = HEADS * DK
    val = HEADS * DV
    edges = [0, key, 2 * key, 2 * key + val, 2 * key + 2 * val]
    return [values[:, a:b] for a, b in zip(edges[:-1], edges[1:]) if b <= values.shape[1]]


def on_device(
    devices, tokens, segment_ids, cotangent, norm1_gain, mixer_in, decay_in, conv_weight, decay_log, decay_bias,
    head_gain, mixer_out, norm2_gain, ffn_in, ffn_out,
):
    rows, width = decay_in.shape[0], tokens.shape[1]
    count = tokens.shape[0]
    hidden = ffn_out.shape[0]
    tiles = hidden // TILE
    direct = rows % 16 == 0 and devices % 8 == 0

    low = lambda v: v.astype(BF16)
    shard_mixer = by_head(split_heads(low(mixer_in)))
    conv_cols = conv_weight.shape[1]
    shard_small = jnp.concatenate(
        [low(decay_in), low(norm1_gain)[:, None], low(norm2_gain)[:, None], low(conv_weight).reshape(rows, -1)], axis=1
    )
    shard_small = jnp.pad(shard_small, ((0, 0), (0, SMALL - shard_small.shape[1])))
    shard_out = low(mixer_out).T
    ffn_low = low(ffn_in)
    pieces = [ffn_low[:, :hidden], ffn_low[:, hidden:], low(ffn_out).T]
    shard_ffn = jnp.concatenate([p.reshape(rows, tiles, TILE) for p in pieces], axis=2).reshape(rows, -1)
    shards = [shard_small, shard_mixer, shard_out, shard_ffn]

    x = tokens.astype(F32)
    scale1 = rms_scale(x)
    if direct:
        sizes = [[SMALL], [768, 1536, 1536, 2304], [2048], [1536] * 5 + [768]]
        full_small, full_mixer, full_out, full_ffn = gather_all(
            devices, shards, [c[:4] for c in cut(sizes, [s.shape[1] for s in shards])]
        )
    else:
        full_small, full_mixer, full_out, full_ffn = [
            lax.all_gather(s, "dp", axis=0, tiled=True) for s in shards
        ]

    decay_full = full_small[:, :16]
    gain1 = full_small[:, 16].astype(F32)
    gain2 = full_small[:, 17].astype(F32)
    taps = full_small[:, 18 : 18 + 16].reshape(devices, 4, conv_cols)
    taps = jnp.moveaxis(taps, 0, 1).reshape(4, -1).astype(F32)
    taps = by_head(split_heads(taps))

    normed_in = low(x * scale1 * gain1)
    logits = jnp.dot(normed_in, decay_full, preferred_element_type=F32)
    shifted = logits[:, :HEADS] + decay_bias
    log_decay = -jnp.exp(decay_log) * jax.nn.softplus(shifted)
    rate = jax.nn.sigmoid(logits[:, HEADS:])
    sequences = count // SEQ
    lower = jnp.tril(jnp.ones((SEQ, SEQ), F32))
    cumulative = jnp.einsum(
        "ij,sjh->sih", lower, log_decay.reshape(sequences, SEQ, HEADS), precision=lax.Precision.HIGHEST
    ).reshape(count, HEADS)
    position = jnp.arange(count) % SEQ
    keeps = []
    for back in (1, 2, 3):
        earlier = jnp.pad(segment_ids[:-back], (back, 0), constant_values=-1)
        keeps.append(((earlier == segment_ids) & (position >= back)).astype(F32)[:, None])
    segment = segment_ids.astype(F32)
    cols = jnp.concatenate([cumulative, rate] + keeps + [segment[:, None]], axis=1)
    cols = jnp.pad(cols, ((0, 0), (0, 128 - cols.shape[1])))
    seq_rows = jnp.concatenate([cumulative.T, segment[None], jnp.zeros((7, count), F32)], axis=0)
    gain_row = head_gain[None]

    proj, mixed, inverse, update, core = mixer_fwd(normed_in, full_mixer, taps, cols, seq_rows, gain_row)

    middle = x + lax.dot_general(mixed, full_out, (NT, ((), ())), preferred_element_type=F32)
    scale2 = rms_scale(middle)
    normed_mid = low(middle * scale2 * gain2)
    dw_ffn, ffn_sum, grad_nm = ffn(normed_mid, normed_mid.T, cotangent, cotangent.T, full_ffn)
    output = low(middle + ffn_sum)

    d_middle, d_gain2 = rms_back(grad_nm, middle, scale2, gain2)
    grad_middle = d_middle + cotangent.astype(F32)
    branch = low(grad_middle)
    dw_mixer, dw_out, grad_xn, d_cols, d_rows, d_taps, d_gain = mixer_bwd(
        branch, branch.T, normed_in.T, full_out, full_mixer, proj, mixed, inverse, update, core,
        taps, cols, seq_rows, gain_row,
    )

    d_cum = d_cols[:, 8:16] - d_rows.T
    d_decay = jnp.einsum(
        "ji,sjh->sih", lower, d_cum.reshape(sequences, SEQ, HEADS), precision=lax.Precision.HIGHEST
    ).reshape(count, HEADS)
    d_shifted = -d_decay * jnp.exp(decay_log) * jax.nn.sigmoid(shifted)
    d_rate = d_cols[:, :8] * rate * (1.0 - rate)
    d_logits = low(jnp.concatenate([d_shifted, d_rate], axis=1))
    grad_xn = grad_xn + lax.dot_general(d_logits, decay_full, (NT, ((), ())), preferred_element_type=F32)
    d_x, d_gain1 = rms_back(grad_xn, x, scale1, gain1)
    input_grad = d_x + grad_middle

    d_decay_in = lax.dot_general(normed_in, d_logits, (TN, ((), ())), preferred_element_type=F32)
    d_taps = from_head(d_taps, [DK, DK, DV])
    d_taps = jnp.moveaxis(d_taps.reshape(4, devices, conv_cols), 1, 0).reshape(width, -1)
    dw_small = jnp.concatenate([d_decay_in, d_gain1[:, None], d_gain2[:, None], d_taps], axis=1)
    dw_small = low(jnp.pad(dw_small, ((0, 0), (0, SMALL - dw_small.shape[1]))))
    shared = jnp.concatenate([jnp.sum(d_decay * log_decay, axis=0), jnp.sum(d_shifted, axis=0), d_gain[0]])

    if direct:
        grads = [dw_ffn, dw_out, dw_mixer, dw_small]
        sizes = [[1536] * 5 + [768], [2048], [1536] * 4, [SMALL]]
        block = jnp.pad(shared, (0, 1024 - shared.shape[0])).reshape(8, 128)
        own, total = scatter_all(devices, grads, block, cut(sizes, [g.shape[1] for g in grads]))
        shared = total.reshape(-1)
        edges = [0]
        for g in grads:
            edges.append(edges[-1] + g.shape[1])
        own_ffn, own_out, own_mixer, own_small = [own[:, a:b] for a, b in zip(edges[:-1], edges[1:])]
    else:
        own_ffn, own_out, own_mixer, own_small = [
            lax.psum_scatter(g.astype(F32), "dp", scatter_dimension=0, tiled=True)
            for g in (dw_ffn, dw_out, dw_mixer, dw_small)
        ]
        shared = lax.psum(shared, "dp")

    own_tiles = own_ffn.reshape(rows, tiles, 3, TILE)
    ffn_in_grad = jnp.concatenate([own_tiles[:, :, i].reshape(rows, hidden) for i in (0, 1)], axis=1)
    ffn_out_grad = own_tiles[:, :, 2].reshape(rows, hidden).T
    return (
        output,
        input_grad,
        own_small[:, 16],
        from_head(own_mixer, [DK, DK, DV, DV]),
        own_small[:, :16],
        own_small[:, 18 : 18 + 16].reshape(4, conv_cols),
        shared[:HEADS],
        shared[HEADS : 2 * HEADS],
        shared[2 * HEADS : 2 * HEADS + DV],
        own_out.T,
        own_small[:, 17],
        ffn_in_grad,
        ffn_out_grad,
    )


def solution(mesh):
    in_specs = (
        P("dp", None), P("dp"), P("dp", None), P("dp"), P("dp", None), P("dp", None), P(None, "dp"), P(), P(), P(),
        P(None, "dp"), P("dp"), P("dp", None), P(None, "dp"),
    )
    out_specs = (
        P("dp", None), P("dp", None), P("dp"), P("dp", None), P("dp", None), P(None, "dp"), P(), P(), P(),
        P(None, "dp"), P("dp"), P("dp", None), P(None, "dp"),
    )
    return jax.shard_map(
        partial(on_device, mesh.shape["dp"]), mesh=mesh, in_specs=in_specs, out_specs=out_specs, check_vma=False
    )
```

```python
from functools import partial

import jax
import jax.numpy as jnp
from jax import lax
from jax.experimental import pallas as pl
from jax.experimental.pallas import tpu as pltpu
from jax.sharding import PartitionSpec as P

HEADS = 8
DK = 128
DV = 256
SEQ = 256
HEAD_COLS = 2 * DK + 2 * DV
CONV_COLS = 2 * DK + DV
TILE = 256
SMALL = 128
F32 = jnp.float32
BF16 = jnp.bfloat16
MESH = pl.DeviceIdType.MESH
MIB = 1 << 20
epsilon = 1e-06
head_epsilon = 0.001

NN = ((1,), (0,))
NT = ((1,), (1,))
TN = ((0,), (0,))


def dot1(left, right, dims):
    return lax.dot_general(
        left.astype(BF16), right.astype(BF16), (dims, ((), ())), preferred_element_type=F32
    )


def split(value):
    high = value.astype(BF16)
    return high, (value - high.astype(F32)).astype(BF16)


def dot3(left, right, dims):
    lh, ll = split(left)
    rh, rl = split(right)
    return dot1(lh, rh, dims) + (dot1(lh, rl, dims) + dot1(ll, rh, dims))


def sigmoid(value):
    return 1.0 / (1.0 + jnp.exp(-value))


def grid_of(size):
    rows = lax.broadcasted_iota(jnp.int32, (size, size), 0)
    cols = lax.broadcasted_iota(jnp.int32, (size, size), 1)
    return rows, cols


def unit_inverses(couplings):
    size = couplings[0].shape[0]
    rows, cols = grid_of(size)
    apart = rows ^ cols
    eye = jnp.where(apart == 0, 1.0, 0.0)
    lows = [a.astype(BF16) for a in couplings]
    inverses = [eye - jnp.where(apart < 2, a, 0.0) for a in couplings]
    block = 2
    while block < size:
        here = jnp.where((apart >= block) & (apart < 2 * block), 1.0, 0.0).astype(BF16)
        firsts = [dot1(low * here, inv, NN) for low, inv in zip(lows, inverses)]
        inverses = [inv - dot1(inv, first, NN) for inv, first in zip(inverses, firsts)]
        block *= 2
    return inverses


def pick_lane(columns, lane):
    at = lax.broadcasted_iota(jnp.int32, columns.shape, 1)
    return jnp.sum(jnp.where(at == lane, columns, 0.0), axis=1, keepdims=True)


def conv_of(values, taps, keep):
    total = values * taps[0:1]
    for back in (1, 2, 3):
        total = total + pltpu.roll(values, back, 0) * keep[back - 1] * taps[back : back + 1]
    return total


def decays(seg_col, seg_row, cum_col, cum_row):
    rows, cols = grid_of(SEQ)
    linked = (seg_col == seg_row) & (rows >= cols)
    return jnp.where(linked, jnp.exp(jnp.where(linked, cum_col - cum_row, 0.0)), 0.0)


def strict(value):
    rows, cols = grid_of(SEQ)
    return jnp.where(rows > cols, value, 0.0)


def head_inputs(projected, taps, cols, head):
    keep = [pick_lane(cols, 16 + i) for i in range(3)]
    conv = conv_of(projected[:, :CONV_COLS], taps, keep)
    gate = sigmoid(conv)
    act = conv * gate
    q_act, k_act, value = act[:, :DK], act[:, DK : 2 * DK], act[:, 2 * DK :]
    q_scale = lax.rsqrt(jnp.sum(q_act * q_act, axis=1, keepdims=True) + epsilon)
    k_scale = lax.rsqrt(jnp.sum(k_act * k_act, axis=1, keepdims=True) + epsilon)
    cum = pick_lane(cols, head)
    rate = pick_lane(cols, 8 + head)
    seg = pick_lane(cols, 19)
    return keep, conv, gate, act, q_act * q_scale, k_act * k_scale, value, q_scale, k_scale, cum, rate, seg


def flip(number, bit):
    return number + bit - 2 * bit * ((number // bit) % 2)


def flips(number, planes, k, unit):
    bit = 1
    while bit < planes:
        if k & bit:
            number = flip(number, unit * bit)
        bit *= 2
    return number


def enter(planes):
    me = lax.axis_index("dp")
    barrier = pltpu.get_barrier_semaphore()
    partners = [flip(me, 1), flip(me, 2), flip(me, 4)]
    partners += [flips(me, planes, k, 8) for k in range(1, planes)]
    for other in partners:
        pl.semaphore_signal(barrier, inc=1, device_id=(other,), device_id_type=MESH)
    pl.semaphore_wait(barrier, len(partners))
    return me


def columns(k, width):
    start = k * width
    return pl.ds(start if isinstance(start, int) else pl.multiple_of(start, 128), width)


def remote(source, target, send_sem, recv_sem, other):
    return pltpu.make_async_remote_copy(
        src_ref=source, dst_ref=target, send_sem=send_sem, recv_sem=recv_sem,
        device_id=(other,), device_id_type=MESH,
    )


class Gather:
    def __init__(self, me, planes, kinds, local_sem, send_sem, recv_sem):
        self.me, self.planes, self.kinds = me, planes, kinds
        self.local_sem, self.send_sem, self.recv_sem = local_sem, send_sem, recv_sem
        self.plane, self.place = me // 8, me % 8

    def local(self, kind, k):
        shard, full, width, base = self.kinds[kind]
        cols = columns(k, width)
        return pltpu.make_async_copy(
            shard.at[:, cols], full.at[self.plane, self.place, :, cols], self.local_sem.at[base + k]
        )

    def copy(self, kind, k, number, by_y=False):
        shard, full, width, base = self.kinds[kind]
        cols = columns(k, width)
        me, place = self.me, self.place
        sems = self.send_sem.at[base + k, number], self.recv_sem.at[base + k, number]
        if number > 6:
            home = full.at[self.plane, place, :, cols]
            return remote(shard.at[:, cols], home, *sems, flips(me, self.planes, number - 6, 8))
        across_x, across_y = flip(place, 2), flip(place, 4)
        which, other = (
            (place, flip(me, 2)),
            (place, flip(me, 4)),
            (across_y, flip(me, 2)) if by_y else (across_x, flip(me, 4)),
            (place, flip(me, 1)),
            (across_x, flip(me, 1)),
            (across_y, flip(me, 1)),
            (flip(across_x, 4), flip(me, 1)),
        )[number]
        piece = full.at[:, which, :, cols]
        return remote(piece, piece, *sems, other)

    def planes_step(self, kind, k):
        self.local(kind, k).start()
        for d in range(1, self.planes):
            self.copy(kind, k, 6 + d).start()

    def square_step(self, kind, k):
        self.local(kind, k).wait()
        for d in range(1, self.planes):
            self.copy(kind, k, 6 + d).wait_recv()
        for number in (0, 1, 3):
            self.copy(kind, k, number).start()

    def diagonal_step(self, kind, k):
        def go(by_y):
            for number in (1, 0) if by_y else (0, 1):
                self.copy(kind, k, number).wait_recv()
                if number == int(by_y):
                    self.copy(kind, k, 2, by_y).start()
                self.copy(kind, k, 4 + number).start()

        if isinstance(k, int):
            go(k % 2 == 1)
        else:
            pl.when(k % 2 == 0)(lambda: go(False))
            pl.when(k % 2 == 1)(lambda: go(True))

    def core_step(self, kind, k):
        self.copy(kind, k, 2).wait_recv()
        self.copy(kind, k, 6).start()
        for number in (3, 4, 5, 6):
            self.copy(kind, k, number).wait_recv()

    def finish(self, kind, k):
        for number in range(6 + self.planes):
            self.copy(kind, k, number).wait_send()


class Scatter:
    depths = {"core": 4, "keep": 2, "sums": 6, "x": 6, "y": 6, "xy": 4, "z": 4}

    def __init__(self, me, planes, kinds, store, core, keep, sums, x, y, xy, z, local_sem, send_sem, recv_sem):
        self.me, self.planes, self.kinds, self.store = me, planes, kinds, store
        self.from_core, self.keep, self.sums = core, keep, sums
        self.from_x, self.from_y, self.from_xy, self.from_z = x, y, xy, z
        self.local_sem, self.send_sem, self.recv_sem = local_sem, send_sem, recv_sem
        self.plane, self.core, self.here = me // 8, me % 2, (me // 2) % 4

    def piece(self, r, place, width):
        return self.sums.at[r % self.depths["sums"], :, place, :, pl.ds(0, width)]

    def copy(self, kind, r, k, number, by_y=False):
        width, source, _ = self.kinds[kind]
        cols = pl.ds(0, width)
        sems = self.send_sem.at[r, number], self.recv_sem.at[r, number]
        me, here = self.me, self.here
        if number == 0:
            target = self.from_core.at[r % self.depths["core"], :, :, :, cols]
            return remote(source(k, 1 - self.core), target, *sems, flip(me, 1))
        if number == 1:
            target = self.from_xy.at[r % self.depths["xy"], :, :, cols]
            return remote(self.piece(r, flip(flip(here, 1), 2), width), target, *sems, flip(me, 4 if by_y else 2))
        if number == 2:
            target = self.from_x.at[r % self.depths["x"], :, :, cols]
            return remote(self.piece(r, flip(here, 1), width), target, *sems, flip(me, 2))
        if number == 3:
            target = self.from_y.at[r % self.depths["y"], :, :, cols]
            return remote(self.piece(r, flip(here, 2), width), target, *sems, flip(me, 4))
        d = number - 3
        own = self.sums.at[r % self.depths["sums"], flips(self.plane, self.planes, d, 1), here, :, cols]
        target = self.from_z.at[r % self.depths["z"], d - 1, :, cols]
        return remote(own, target, *sems, flips(me, self.planes, d, 8))

    def load(self, kind, r, k):
        width, source, in_place = self.kinds[kind]
        return pltpu.make_async_copy(
            source(k, self.core), self.keep.at[r % 2, :, :, :, pl.ds(0, width)], self.local_sem.at[r]
        )

    def core_step(self, kind, r, k):
        self.copy(kind, r, k, 0).start()

    def load_step(self, kind, r, k):
        if self.kinds[kind][2] is None:
            self.load(kind, r, k).start()

    def add(self, kind, r, place, first, others):
        cols = pl.ds(0, self.kinds[kind][0])

        def one(plane, carry):
            total = first(plane, cols).astype(F32)
            for read in others:
                total = total + read(plane, cols).astype(F32)
            self.sums[r % self.depths["sums"], plane, place, :, cols] = total.astype(BF16)
            return carry

        lax.fori_loop(0, self.planes, one, 0)

    def held(self, r, place):
        return lambda plane, cols: self.sums[r % self.depths["sums"], plane, place, :, cols]

    def chip_step(self, kind, r, k):
        width, _, in_place = self.kinds[kind]
        self.copy(kind, r, k, 0).wait_recv()
        if in_place is None:
            self.load(kind, r, k).wait()
            mine = lambda place: (lambda plane, cols: self.keep[r % 2, plane, place, :, cols])
        else:
            mine = lambda place: (lambda plane, cols: in_place(k, plane, place, self.core))
        got = lambda place: (lambda plane, cols: self.from_core[r % self.depths["core"], plane, place, :, cols])
        across_x, across_y = flip(self.here, 1), flip(self.here, 2)
        both = flip(across_x, 2)

        def go(by_y):
            self.add(kind, r, both, got(both), [mine(both)])
            self.copy(kind, r, k, 1, by_y).start()
            if by_y:
                self.add(kind, r, across_y, got(across_y), [mine(across_y)])
                self.copy(kind, r, k, 3).start()
                self.add(kind, r, across_x, got(across_x), [mine(across_x)])
            else:
                self.add(kind, r, across_x, got(across_x), [mine(across_x)])
                self.copy(kind, r, k, 2).start()
                self.add(kind, r, across_y, got(across_y), [mine(across_y)])

        pl.when(r % 2 == 0)(lambda: go(False))
        pl.when(r % 2 == 1)(lambda: go(True))
        self.add(kind, r, self.here, got(self.here), [mine(self.here)])
        self.copy(kind, r, k, 0).wait_send()

    def diagonal_step(self, kind, r, k):
        self.copy(kind, r, k, 1).wait_recv()

        def go(by_y):
            place = flip(self.here, 1 if by_y else 2)
            passed = lambda plane, cols: self.from_xy[r % self.depths["xy"], plane, :, cols]
            self.add(kind, r, place, self.held(r, place), [passed])
            self.copy(kind, r, k, 2 if by_y else 3).start()

        pl.when(r % 2 == 0)(lambda: go(False))
        pl.when(r % 2 == 1)(lambda: go(True))

    def square_step(self, kind, r, k):
        self.copy(kind, r, k, 2).wait_recv()
        self.copy(kind, r, k, 3).wait_recv()
        from_x = lambda plane, cols: self.from_x[r % self.depths["x"], plane, :, cols]
        from_y = lambda plane, cols: self.from_y[r % self.depths["y"], plane, :, cols]
        self.add(kind, r, self.here, self.held(r, self.here), [from_x, from_y])
        for d in range(1, self.planes):
            self.copy(kind, r, k, 3 + d).start()

    def planes_step(self, kind, r, k):
        cols = pl.ds(0, self.kinds[kind][0])
        total = self.held(r, self.here)(self.plane, cols).astype(F32)
        for d in range(1, self.planes):
            self.copy(kind, r, k, 3 + d).wait_recv()
            total = total + self.from_z[r % self.depths["z"], d - 1, :, cols].astype(F32)
        self.store(kind, k, total)
        for number in range(1, 3 + self.planes):
            self.copy(kind, r, k, number).wait_send()


class Total:
    def __init__(self, me, planes, value_ref, out_ref, got, stage, send_sem, recv_sem):
        self.me, self.planes, self.value_ref, self.out_ref = me, planes, value_ref, out_ref
        self.got, self.stage, self.send_sem, self.recv_sem = got, stage, send_sem, recv_sem

    def copy(self, number):
        sems = self.send_sem.at[number], self.recv_sem.at[number]
        if number < 3:
            return remote(self.stage.at[number], self.got.at[number], *sems, flip(self.me, 1 << number))
        other = flips(self.me, self.planes, number - 2, 8)
        return remote(self.stage.at[3], self.got.at[3 + self.me // 8], *sems, other)

    def step(self, number):
        planes = self.planes
        if number == 0:
            self.stage[0] = self.value_ref[...]
        elif number <= 3:
            self.copy(number - 1).wait_recv()
            self.stage[number] = self.stage[number - 1] + self.got[number - 1]
        if number < 3:
            self.copy(number).start()
        elif number == 3:
            for d in range(1, planes):
                self.copy(2 + d).start()
            self.got[3 + self.me // 8] = self.stage[3]
        else:
            for d in range(1, planes):
                self.copy(2 + d).wait_recv()
            total = self.got[3]
            for other in range(1, planes):
                total = total + self.got[3 + other]
            self.out_ref[...] = total
            for number in range(2 + planes):
                self.copy(number).wait_send()


def triangle_sum(values, dims):
    rows, cols = grid_of(SEQ)
    ones = jnp.where(rows >= cols, 1.0, 0.0).astype(BF16)
    first, rest = values.astype(BF16), values - values.astype(BF16).astype(F32)
    second, third = split(rest)
    return dot1(ones, first, dims) + (dot1(ones, second, dims) + dot1(ones, third, dims))


def log1p(value):
    series = value * (1.0 - value * (0.5 - value * (1.0 / 3.0 - value * (0.25 - value * 0.2))))
    return jnp.where(value < 0.01, series, jnp.log(1.0 + value))


def softplus(value):
    return jnp.maximum(value, 0.0) + log1p(jnp.exp(-jnp.abs(value)))


def merge(block):
    return block.reshape(-1, block.shape[-1])


def head_taps(small_ref, head):
    wide = 2 * head
    places = [(0, head), (1, head)] + [(2 + head // 4, wide % 8 + i) for i in (0, 1)]
    blocks = [small_ref[z, p, 0:16, SMALL : 2 * SMALL][0:4].astype(F32) for z, p in places]
    return jnp.concatenate(blocks, axis=1)


def row_blocks(count, body, size=128):
    def one(i, carry):
        body(pl.ds(pl.multiple_of(i * size, size), size))
        return carry

    lax.fori_loop(0, count // size, one, 0)


def lane_index(shape):
    return lax.broadcasted_iota(jnp.int32, shape, 1)


def forward_body(
    planes, tiles,
    shard_small, shard_heads, shard_tiles, x_ref, cot_ref, aux_ref, seg_ref, consts_ref, gain_ref,
    full_small, full_heads, full_tiles, small_ref, xnt_ref, cols_ref, rows_ref, logs_ref, factor_ref,
    proj_ref, mixed_ref, inv_ref, upd_ref, core_ref, dw_ref,
    output_ref, grad_mid_ref, branch_ref, brancht_ref, d_gain2_ref,
    w_buf, xn, cott, middle, nm, nmt, out_sum, nm_sum, gains, scale2_ref, copy_sem, local_sem, send_sem, recv_sem,
):
    step = pl.program_id(0)
    tokens = x_ref.shape[0]
    chunks = HEADS + tiles
    me = lax.axis_index("dp")
    kinds = {
        "small": (shard_small, full_small, 2 * SMALL, chunks),
        "head": (shard_heads, full_heads, HEAD_COLS + DV, 0),
        "tile": (shard_tiles, full_tiles, 3 * TILE, HEADS),
    }
    work = Gather(me, planes, kinds, local_sem, send_sem, recv_sem)

    def at(chunk, act):
        pl.when((chunk >= 0) & (chunk < HEADS))(lambda: act("head", chunk))
        pl.when((chunk >= HEADS) & (chunk < chunks))(lambda: act("tile", chunk - HEADS))

    @pl.when(step == 0)
    def _():
        enter(planes)
        work.planes_step("small", 0)
        for k in (0, 1, 2):
            work.planes_step("head", k)

        def prepare(rows):
            middle[rows, :] = x_ref[rows, :].astype(F32)
            cott[:, rows] = cot_ref[rows, :].astype(F32).T.astype(BF16)

        row_blocks(tokens, prepare)
        out_sum[...] = jnp.zeros_like(out_sum)
        nm_sum[...] = jnp.zeros_like(nm_sum)
        d_gain2_ref[...] = jnp.zeros_like(d_gain2_ref)
        work.square_step("small", 0)
        work.square_step("head", 0)
        work.diagonal_step("small", 0)
        work.square_step("head", 1)
        work.core_step("small", 0)
        work.diagonal_step("head", 0)
        copy = pltpu.make_async_copy(full_small, small_ref, copy_sem)
        copy.start()
        copy.wait()
        small = merge(small_ref[:, :, :, 0:SMALL])
        turned = small.astype(F32).T
        gains[0:1, :] = turned[16:17, :]
        gains[1:2, :] = turned[17:18, :]

        def norm(rows):
            x = middle[rows, :]
            scale = lax.rsqrt(jnp.mean(x * x, axis=1, keepdims=True) + epsilon)
            normed = x * scale * gains[0:1, :]
            xn[rows, :] = normed.astype(BF16)
            xnt_ref[:, rows] = normed.T.astype(BF16)

        row_blocks(tokens, norm)
        logits = jnp.dot(xn[...], small, preferred_element_type=F32)
        lanes = lane_index(logits.shape)
        decay_scale, bias = consts_ref[0:1, :], consts_ref[1:2, :]
        shifted = logits + bias
        rate = sigmoid(logits)
        log_decay = decay_scale * softplus(shifted)
        logs_ref[...] = log_decay
        factor_ref[...] = jnp.where(
            lanes < 8, decay_scale * sigmoid(shifted), jnp.where(lanes < 16, rate * (1.0 - rate), 0.0)
        )
        for start in range(0, tokens, SEQ):
            part = slice(start, start + SEQ)
            cum = triangle_sum(log_decay[part], NN)
            cols_ref[part, :] = jnp.where(
                lanes[part] < 8, cum, jnp.where(lanes[part] < 16, rate[part], aux_ref[part, :])
            )
            rows_ref[0:8, part] = cum.T[0:8]
        rows_ref[8:16, :] = seg_ref[...]
        work.finish("small", 0)

    at(step + 3, work.planes_step)
    at(step + 2, work.square_step)
    at(step + 1, work.diagonal_step)
    at(step, work.core_step)
    at(step - 1, work.finish)

    @pl.when(step < HEADS)
    def _():
        copy = pltpu.make_async_copy(full_heads.at[:, :, :, columns(step, HEAD_COLS + DV)], w_buf, copy_sem)
        copy.start()
        copy.wait()
        w = merge(w_buf[...])
        projected = jnp.dot(xn[...], w[:, :HEAD_COLS], preferred_element_type=F32)
        proj_ref[...] = projected
        _, _, _, _, q, k, value, _, _, cum, rate, seg = head_inputs(
            projected, head_taps(small_ref, step), cols_ref[...], step
        )
        q = q * DK**-0.5
        cum_row = rows_ref[pl.ds(step, 1), :]
        seg_row = rows_ref[8:9, :]
        parts = [slice(s, s + SEQ) for s in range(0, tokens, SEQ)]
        scores, couplings = [], []
        for part in parts:
            pair = decays(seg[part], seg_row[:, part], cum[part], cum_row[:, part])
            key_dots = dot3(k[part], k[part], NT)
            scores.append(pair * dot3(q[part], k[part], NT))
            couplings.append(strict(pair * key_dots) * rate[part])
        inverses = unit_inverses(couplings)
        for i, part in enumerate(parts):
            update = dot3(inverses[i], rate[part] * value[part], NN)
            core = dot3(scores[i], update, NN)
            inv_ref[0, part, :] = inverses[i].astype(BF16)
            upd_ref[0, part, :] = update
            core_ref[0, part, :] = core
            scale = lax.rsqrt(jnp.mean(core * core, axis=1, keepdims=True) + head_epsilon)
            out_gate = projected[part, CONV_COLS:]
            mixed_ref[part, :] = (core * scale * gain_ref[...] * (out_gate * sigmoid(out_gate))).astype(BF16)
        middle[...] += lax.dot_general(mixed_ref[...], w[:, HEAD_COLS:], (NT, ((), ())), preferred_element_type=F32)

    @pl.when(step == HEADS)
    def _():
        def norm(rows):
            mid = middle[rows, :]
            scale = lax.rsqrt(jnp.mean(mid * mid, axis=1, keepdims=True) + epsilon)
            normed = mid * scale * gains[1:2, :]
            nm[rows, :] = normed.astype(BF16)
            nmt[:, rows] = normed.T.astype(BF16)

        row_blocks(tokens, norm)

    @pl.when(step >= HEADS)
    def _():
        place = w_buf.at[:, :, :, pl.ds(0, 3 * TILE)]
        copy = pltpu.make_async_copy(full_tiles.at[:, :, :, columns(step - HEADS, 3 * TILE)], place, copy_sem)
        copy.start()
        copy.wait()
        w = merge(w_buf[:, :, :, 0 : 3 * TILE])
        gate_up = jnp.dot(nm[...], w[:, : 2 * TILE], preferred_element_type=F32)
        gate, up = gate_up[:, :TILE], gate_up[:, TILE:]
        sig = sigmoid(gate)
        swish = gate * sig
        hidden = (swish * up).astype(BF16)
        grad_hidden = jnp.dot(cot_ref[...], w[:, 2 * TILE :], preferred_element_type=F32)
        grad_gate = grad_hidden * up * (sig + swish * (1.0 - sig))
        grad_up = grad_hidden * swish
        grad_low = jnp.concatenate([grad_gate, grad_up], axis=1).astype(BF16)
        out_sum[...] += lax.dot_general(hidden, w[:, 2 * TILE :], (NT, ((), ())), preferred_element_type=F32)
        nm_sum[...] += lax.dot_general(grad_low, w[:, : 2 * TILE], (NT, ((), ())), preferred_element_type=F32)
        dw_ref[:, : 2 * TILE] = jnp.dot(nmt[...], grad_low, preferred_element_type=F32).astype(BF16)
        dw_ref[:, 2 * TILE :] = jnp.dot(cott[...], hidden, preferred_element_type=F32).astype(BF16)

    @pl.when(step == chunks - 1)
    def _():
        def back(rows):
            mid = middle[rows, :]
            output_ref[rows, :] = (mid + out_sum[rows, :]).astype(BF16)
            scale = lax.rsqrt(jnp.mean(mid * mid, axis=1, keepdims=True) + epsilon)
            normed = mid * scale
            grad = nm_sum[rows, :]
            d_gain2_ref[0:1, :] += jnp.sum(grad * normed, axis=0, keepdims=True)
            d_normed = grad * gains[1:2, :]
            d_mid = scale * (d_normed - normed * jnp.mean(d_normed * normed, axis=1, keepdims=True))
            d_mid = d_mid + cot_ref[rows, :].astype(F32)
            grad_mid_ref[rows, :] = d_mid
            branch_ref[rows, :] = d_mid.astype(BF16)
            brancht_ref[:, rows] = d_mid.T.astype(BF16)

        row_blocks(tokens, back)
        work.finish("tile", tiles - 1)


def once(shape):
    return pl.BlockSpec(shape, lambda i: (0,) * len(shape), pipeline_mode=pl.Buffered(1))


def forward(planes, shards, x, cot, aux, seg_rows, consts, gain):
    rows, tokens, width = shards[0].shape[0], *x.shape
    tiles = shards[2].shape[1] // (3 * TILE)
    chunks = HEADS + tiles
    hbm = pl.BlockSpec(memory_space=pl.ANY)
    head = lambda i: jnp.minimum(i, HEADS - 1)
    tile = lambda i: jnp.maximum(i - HEADS, 0)
    save = pl.BlockSpec((1, tokens, SEQ), lambda i: (head(i), 0, 0))
    shape = jax.ShapeDtypeStruct
    whole = [((planes, 8, rows, s.shape[1]), BF16) for s in shards]
    outs = [
        (hbm, *whole[0]),
        (hbm, *whole[1]),
        (hbm, *whole[2]),
        (once(whole[0][0]), *whole[0]),
        (once((width, tokens)), (width, tokens), BF16),
        (once((tokens, 128)), (tokens, 128), F32),
        (once((16, tokens)), (16, tokens), F32),
        (once((tokens, 128)), (tokens, 128), F32),
        (once((tokens, 128)), (tokens, 128), F32),
        (pl.BlockSpec((tokens, HEAD_COLS), lambda i: (0, head(i))), (tokens, HEADS * HEAD_COLS), F32),
        (pl.BlockSpec((tokens, DV), lambda i: (0, head(i))), (tokens, HEADS * DV), BF16),
        (save, (HEADS, tokens, SEQ), BF16),
        (save, (HEADS, tokens, DV), F32),
        (save, (HEADS, tokens, DV), F32),
        (pl.BlockSpec((width, 3 * TILE), lambda i: (0, tile(i))), (width, tiles * 3 * TILE), BF16),
        (once((tokens, width)), (tokens, width), BF16),
        (once((tokens, width)), (tokens, width), F32),
        (once((tokens, width)), (tokens, width), BF16),
        (once((width, tokens)), (width, tokens), BF16),
        (once((8, width)), (8, width), F32),
    ]
    return pl.pallas_call(
        partial(forward_body, planes, tiles),
        grid=(chunks,),
        in_specs=[hbm, hbm, hbm] + [once(a.shape) for a in (x, cot, aux, seg_rows, consts, gain)],
        out_specs=[o[0] for o in outs],
        out_shape=[shape(o[1], o[2]) for o in outs],
        scratch_shapes=[
            pltpu.VMEM((planes, 8, rows, HEAD_COLS + DV), BF16),
            pltpu.VMEM((tokens, width), BF16),
            pltpu.VMEM((width, tokens), BF16),
            pltpu.VMEM((tokens, width), F32),
            pltpu.VMEM((tokens, width), BF16),
            pltpu.VMEM((width, tokens), BF16),
            pltpu.VMEM((tokens, width), F32),
            pltpu.VMEM((tokens, width), F32),
            pltpu.VMEM((8, width), F32),
            pltpu.VMEM((tokens, 128), F32),
            pltpu.SemaphoreType.DMA,
            pltpu.SemaphoreType.DMA((chunks + 1,)),
            pltpu.SemaphoreType.DMA((chunks + 1, 6 + planes)),
            pltpu.SemaphoreType.DMA((chunks + 1, 6 + planes)),
        ],
        compiler_params=pltpu.CompilerParams(
            collective_id=0, has_side_effects=True, vmem_limit_bytes=60 * MIB
        ),
        name="forward",
    )(*shards, x, cot, aux, seg_rows, consts, gain)


LAG = 2


def head_step(j):
    return jnp.minimum(j // 2, HEADS - 1)


def backward_body(
    planes, tiles, total_chunks,
    dwf_ref, gb_ref, gbt_ref, xnt_ref, w_ref, proj_ref, mixed_ref, inv_ref, upd_ref, core_ref,
    small_ref, cols_ref, rows_ref, logs_ref, factor_ref, gain_ref, x_ref, grad_mid_ref, d_gain2_ref,
    input_grad_ref, own_mixer, own_out, own_ffn, own_down, own_small, shared_ref,
    dw, d_small, gxn, dcols, drows, dgain, dproj, value_ref,
    from_core, keep, sums, from_x, from_y, from_xy, from_z, got, stage,
    local_sem, send_sem, recv_sem, total_send, total_recv,
):
    step = pl.program_id(0)
    tokens = gb_ref.shape[0]
    rows = own_small.shape[0]
    hidden = tiles * TILE
    me = lax.axis_index("dp")

    def tile_source(k, core):
        return dwf_ref.at[:, :, core, :, columns(k, 3 * TILE)]

    kinds = {
        "tile": (3 * TILE, tile_source, None),
        "head": (
            HEAD_COLS + DV,
            lambda k, core: dw.at[k % 2, :, :, core],
            lambda k, plane, place, core: dw[k % 2, plane, place, core],
        ),
        "small": (
            2 * SMALL,
            lambda k, core: d_small.at[:, :, core],
            lambda k, plane, place, core: d_small[plane, place, core],
        ),
    }

    def store(kind, k, total):
        def put(ref, start, source, width):
            ref[:, pl.ds(pl.multiple_of(start, 128), width)] = total[:, source : source + width]

        if kind == "small":
            own_small[...] = total
        elif kind == "head":
            put(own_mixer, k * DK, 0, DK)
            put(own_mixer, HEADS * DK + k * DK, DK, DK)
            put(own_mixer, 2 * HEADS * DK + k * DV, 2 * DK, DV)
            put(own_mixer, 2 * HEADS * DK + HEADS * DV + k * DV, 2 * DK + DV, DV)
            put(own_out, k * DV, HEAD_COLS, DV)
        else:
            put(own_ffn, k * TILE, 0, TILE)
            put(own_ffn, hidden + k * TILE, TILE, TILE)
            put(own_down, k * TILE, 2 * TILE, TILE)

    work = Scatter(
        me, planes, kinds, store, from_core, keep, sums, from_x, from_y, from_xy, from_z, local_sem, send_sem, recv_sem
    )
    small_sum = Total(me, planes, value_ref, shared_ref, got, stage, total_send, total_recv)

    last = total_chunks - 1

    def at(r, act):
        is_head = (r >= 3) & (r < last) & (r % 2 == 1)
        is_tile = (r >= 0) & (r < last) & ((r < 3) | (r % 2 == 0))
        pl.when(is_tile)(lambda: act("tile", r, r // 2 + (r + last - 2) // (last - 1)))
        pl.when(is_head)(lambda: act("head", r, (r - 3) // 2))
        pl.when(r == last)(lambda: act("small", r, 0))

    @pl.when(step == 0)
    def _():
        enter(planes)
        for r in (0, 1):
            work.core_step("tile", r, r)
        work.load_step("tile", 0, 0)
        gxn[...] = jnp.zeros_like(gxn)
        dcols[...] = jnp.zeros_like(dcols)
        drows[...] = jnp.zeros_like(drows)
        dgain[...] = jnp.zeros_like(dgain)
        d_small[...] = jnp.zeros_like(d_small)

    at(step - 3 * LAG, work.planes_step)
    at(step - 2 * LAG, work.square_step)
    at(step - LAG, work.diagonal_step)
    at(step, work.chip_step)
    at(step + 2, work.core_step)
    at(step + 1, work.load_step)

    @pl.when((step < 2 * HEADS) & (step % 2 == 0))
    def _():
        head = step // 2
        w = merge(w_ref[...])
        grad_mixed = jnp.dot(gb_ref[...], w[:, HEAD_COLS:], preferred_element_type=F32)
        d_out = jnp.dot(gbt_ref[...], mixed_ref[...], preferred_element_type=F32).astype(BF16)
        dw[head % 2, :, :, :, :, pl.ds(HEAD_COLS, DV)] = d_out.reshape(dw.shape[1:5] + (DV,))

        projected = proj_ref[...]
        taps = head_taps(small_ref, head)
        keeps, conv, gate, act, qn, k, value, q_scale, k_scale, cum, rate, seg = head_inputs(
            projected, taps, cols_ref[...], head
        )
        q = qn * DK**-0.5
        cum_row = rows_ref[pl.ds(head, 1), :]
        seg_row = rows_ref[8:9, :]
        gain = gain_ref[...]
        lanes = lane_index((SEQ, 128))
        d_act, d_gain = [], jnp.zeros((1, DV), F32)
        for start in range(0, tokens, SEQ):
            part = slice(start, start + SEQ)
            core, update, inverse = core_ref[0, part, :], upd_ref[0, part, :], inv_ref[0, part, :]
            grad = grad_mixed[part]
            scale = lax.rsqrt(jnp.mean(core * core, axis=1, keepdims=True) + head_epsilon)
            normed = core * scale
            out_gate = projected[part, CONV_COLS:]
            out_sig = sigmoid(out_gate)
            swish = out_gate * out_sig
            dproj[part, CONV_COLS:] = (grad * normed * gain * (out_sig + swish * (1.0 - out_sig))).astype(BF16)
            d_normed = grad * swish
            d_gain = d_gain + jnp.sum(d_normed * normed, axis=0, keepdims=True)
            d_scaled = d_normed * gain
            d_core = scale * (d_scaled - normed * jnp.mean(d_scaled * normed, axis=1, keepdims=True))

            qs, ks, vs, rs = q[part], k[part], value[part], rate[part]
            pair = decays(seg[part], seg_row[:, part], cum[part], cum_row[:, part])
            key_dots = dot3(ks, ks, NT)
            query_dots = dot3(qs, ks, NT)
            d_scores = dot3(d_core, update, NT)
            d_update = dot1(pair * query_dots, d_core, TN)
            solved = dot1(inverse, d_update, TN)
            d_coupling = strict(-dot1(solved, update, NT)) * pair
            d_query_dots = pair * d_scores
            d_key_dots = d_coupling * rs
            weighed = d_coupling * key_dots
            d_spread = d_query_dots * query_dots + weighed * rs
            d_q = dot1(d_query_dots, ks, NN) * DK**-0.5
            d_k = dot1(d_query_dots, qs, TN) + dot1(d_key_dots, ks, NN) + dot1(d_key_dots, ks, TN)
            d_rate = jnp.sum(solved * vs, axis=1, keepdims=True) + jnp.sum(weighed, axis=1, keepdims=True)
            row_sum = jnp.sum(d_spread, axis=1, keepdims=True)
            dcols[part, :] += jnp.where(lanes == head, row_sum, 0.0) + jnp.where(lanes == 8 + head, d_rate, 0.0)
            drows[pl.ds(head, 1), part] = jnp.sum(d_spread, axis=0, keepdims=True)
            d_q_act = q_scale[part] * (d_q - qn[part] * jnp.sum(d_q * qn[part], axis=1, keepdims=True))
            d_k_act = k_scale[part] * (d_k - ks * jnp.sum(d_k * ks, axis=1, keepdims=True))
            d_act.append(jnp.concatenate([d_q_act, d_k_act, rs * solved], axis=1))
        dgain[0:1, :] += d_gain
        d_conv = jnp.concatenate(d_act, axis=0) * (gate + act * (1.0 - gate))
        source = projected[:, :CONV_COLS]
        d_source = d_conv * taps[0:1]
        d_taps = [jnp.sum(d_conv * source, axis=0, keepdims=True)]
        for back in (1, 2, 3):
            kept = d_conv * keeps[back - 1]
            d_source = d_source + pltpu.roll(kept, tokens - back, 0) * taps[back : back + 1]
            d_taps.append(jnp.sum(kept * pltpu.roll(source, back, 0), axis=0, keepdims=True))
        d_taps = jnp.concatenate(d_taps + [jnp.zeros((rows - 4, CONV_COLS), F32)], axis=0).astype(BF16)
        wide = 2 * head
        places = [(0, head), (1, head)] + [(2 + head // 4, wide % 8 + i) for i in (0, 1)]
        for i, (z, p) in enumerate(places):
            d_small[z, p // 2, p % 2, :, SMALL:] = d_taps[:, i * SMALL : (i + 1) * SMALL]
        dproj[:, :CONV_COLS] = d_source.astype(BF16)
        d_proj = dproj[...]
        d_in = jnp.dot(xnt_ref[...], d_proj, preferred_element_type=F32).astype(BF16)
        dw[head % 2, :, :, :, :, pl.ds(0, HEAD_COLS)] = d_in.reshape(dw.shape[1:5] + (HEAD_COLS,))
        gxn[...] += lax.dot_general(d_proj, w[:, :HEAD_COLS], (NT, ((), ())), preferred_element_type=F32)

    @pl.when(step == 2 * HEADS - 1)
    def _():
        small = merge(small_ref[:, :, :, 0:SMALL])
        turned = small.astype(F32).T
        gain1 = turned[16:17, :]
        lanes = lane_index((SEQ, 128))
        padded = jnp.concatenate([drows[...], jnp.zeros((120, tokens), F32)], axis=0).T
        d_logs = jnp.zeros((1, 128), F32)
        d_bias = jnp.zeros((1, 128), F32)
        d_logits = []
        for start in range(0, tokens, SEQ):
            part = slice(start, start + SEQ)
            d_cum = jnp.where(lanes < 8, dcols[part, :], 0.0) - padded[part]
            d_decay = triangle_sum(d_cum, TN)
            d_logit = jnp.where(lanes < 8, d_decay, dcols[part, :]) * factor_ref[part, :]
            d_logs = d_logs + jnp.sum(jnp.where(lanes < 8, d_decay * logs_ref[part, :], 0.0), axis=0, keepdims=True)
            d_bias = d_bias + jnp.sum(jnp.where(lanes < 8, d_logit, 0.0), axis=0, keepdims=True)
            d_logits.append(d_logit.astype(BF16))
        d_logits = jnp.concatenate(d_logits, axis=0)
        value_ref[...] = jnp.concatenate(
            [d_logs, d_bias, dgain[0:1, :128], dgain[0:1, 128:], jnp.zeros((4, 128), F32)], axis=0
        )
        gxn[...] += lax.dot_general(d_logits, small, (NT, ((), ())), preferred_element_type=F32)
        drows[...] = jnp.zeros_like(drows)
        d_gain1 = [jnp.zeros((1, gxn.shape[1]), F32)]

        def back(at_rows, total):
            x = x_ref[at_rows, :].astype(F32)
            scale = lax.rsqrt(jnp.mean(x * x, axis=1, keepdims=True) + epsilon)
            normed = x * scale
            grad = gxn[at_rows, :]
            d_normed = grad * gain1
            d_x = scale * (d_normed - normed * jnp.mean(d_normed * normed, axis=1, keepdims=True))
            input_grad_ref[at_rows, :] = d_x + grad_mid_ref[at_rows, :]
            return total + jnp.sum(grad * normed, axis=0, keepdims=True)

        total = lax.fori_loop(
            0, tokens // 128, lambda i, t: back(pl.ds(pl.multiple_of(i * 128, 128), 128), t), d_gain1[0]
        )
        line = lax.broadcasted_iota(jnp.int32, (128, total.shape[1]), 0)
        gains = jnp.where(line == 16, total, jnp.where(line == 17, d_gain2_ref[0:1, :], 0.0))
        own = jnp.dot(xnt_ref[...], d_logits, preferred_element_type=F32) + gains.T
        d_small[:, :, :, :, 0:SMALL] = own.astype(BF16).reshape(d_small.shape[:4] + (SMALL,))

    for number in range(5):
        pl.when(step == 2 * HEADS + number)(lambda number=number: small_sum.step(number))


def backward(planes, dwf, gb, gbt, xnt, w, proj, mixed, inv, upd, core, small, cols, seq_rows, logs, factor, gain, x,
             grad_mid, d_gain2):
    tokens, width = gb.shape
    rows = small.shape[2]
    tiles = dwf.shape[1] // (3 * TILE)
    chunks = tiles + HEADS + 1
    hbm = pl.BlockSpec(memory_space=pl.ANY)
    head = head_step
    save = pl.BlockSpec((1, tokens, SEQ), lambda i: (head(i), 0, 0))
    shape = jax.ShapeDtypeStruct
    widest = HEAD_COLS + DV
    depth = Scatter.depths
    kinds = 3 + planes
    outs = [
        ((tokens, width), F32),
        ((rows, HEADS * HEAD_COLS), F32),
        ((rows, HEADS * DV), F32),
        ((rows, 2 * tiles * TILE), F32),
        ((rows, tiles * TILE), F32),
        ((rows, 2 * SMALL), F32),
        ((8, 128), F32),
    ]
    return pl.pallas_call(
        partial(backward_body, planes, tiles, chunks),
        grid=(chunks + 3 * LAG,),
        in_specs=[
            hbm,
            once((tokens, width)),
            once((width, tokens)),
            once((width, tokens)),
            pl.BlockSpec((planes, 8, rows, widest), lambda i: (0, 0, 0, head(i))),
            pl.BlockSpec((tokens, HEAD_COLS), lambda i: (0, head(i))),
            pl.BlockSpec((tokens, DV), lambda i: (0, head(i))),
            save,
            save,
            save,
        ]
        + [once(a.shape) for a in (small, cols, seq_rows, logs, factor, gain, x, grad_mid, d_gain2)],
        out_specs=[once(o[0]) for o in outs],
        out_shape=[shape(*o) for o in outs],
        scratch_shapes=[
            pltpu.VMEM((2, planes, 4, 2, rows, widest), BF16),
            pltpu.VMEM((planes, 4, 2, rows, 2 * SMALL), BF16),
            pltpu.VMEM((tokens, width), F32),
            pltpu.VMEM((tokens, 128), F32),
            pltpu.VMEM((HEADS, tokens), F32),
            pltpu.VMEM((8, DV), F32),
            pltpu.VMEM((tokens, HEAD_COLS), BF16),
            pltpu.VMEM((8, 128), F32),
            pltpu.VMEM((depth["core"], planes, 4, rows, widest), BF16),
            pltpu.VMEM((depth["keep"], planes, 4, rows, 3 * TILE), BF16),
            pltpu.VMEM((depth["sums"], planes, 4, rows, widest), BF16),
            pltpu.VMEM((depth["x"], planes, rows, widest), BF16),
            pltpu.VMEM((depth["y"], planes, rows, widest), BF16),
            pltpu.VMEM((depth["xy"], planes, rows, widest), BF16),
            pltpu.VMEM((depth["z"], planes - 1, rows, widest), BF16),
            pltpu.VMEM((3 + planes, 8, 128), F32),
            pltpu.VMEM((4, 8, 128), F32),
            pltpu.SemaphoreType.DMA((chunks,)),
            pltpu.SemaphoreType.DMA((chunks, kinds)),
            pltpu.SemaphoreType.DMA((chunks, kinds)),
            pltpu.SemaphoreType.DMA((2 + planes,)),
            pltpu.SemaphoreType.DMA((2 + planes,)),
        ],
        compiler_params=pltpu.CompilerParams(
            collective_id=1, has_side_effects=True, vmem_limit_bytes=63 * MIB
        ),
        name="backward",
    )(
        dwf.reshape(planes, 4, 2, rows, dwf.shape[1]), gb, gbt, xnt, w, proj, mixed, inv, upd, core, small, cols,
        seq_rows, logs, factor, gain, x, grad_mid, d_gain2,
    )


def mixer_fwd_body(xn_ref, w_ref, taps_ref, cols_ref, rows_ref, gain_ref, proj_ref, mixed_ref, inv_ref, upd_ref, core_ref):
    head = pl.program_id(0)
    tokens = xn_ref.shape[0]
    projected = jnp.dot(xn_ref[...], w_ref[...], preferred_element_type=F32)
    proj_ref[...] = projected
    _, _, _, _, q, k, value, _, _, cum, rate, seg = head_inputs(
        projected, taps_ref[...], cols_ref[...], head
    )
    q = q * DK**-0.5
    cum_row = rows_ref[pl.ds(head, 1), :]
    seg_row = rows_ref[8:9, :]
    parts = [slice(s, s + SEQ) for s in range(0, tokens, SEQ)]
    scores, couplings = [], []
    for part in parts:
        pair = decays(seg[part], seg_row[:, part], cum[part], cum_row[:, part])
        key_dots = dot3(k[part], k[part], NT)
        scores.append(pair * dot3(q[part], k[part], NT))
        couplings.append(strict(pair * key_dots) * rate[part])
    inverses = unit_inverses(couplings)
    for i, part in enumerate(parts):
        update = dot3(inverses[i], rate[part] * value[part], NN)
        core = dot3(scores[i], update, NN)
        inv_ref[0, part, :] = inverses[i].astype(BF16)
        upd_ref[0, part, :] = update
        core_ref[0, part, :] = core
        scale = lax.rsqrt(jnp.mean(core * core, axis=1, keepdims=True) + head_epsilon)
        out_gate = projected[part, CONV_COLS:]
        mixed_ref[part, :] = (core * scale * gain_ref[...] * (out_gate * sigmoid(out_gate))).astype(BF16)


def mixer_fwd(xn, w, taps, cols, rows, gain):
    tokens, width = xn.shape
    const = lambda h: (0, 0)
    by_head = lambda h: (0, h)
    save = pl.BlockSpec((1, tokens, SEQ), lambda h: (h, 0, 0))
    return pl.pallas_call(
        mixer_fwd_body,
        grid=(HEADS,),
        in_specs=[
            pl.BlockSpec((tokens, width), const),
            pl.BlockSpec((width, HEAD_COLS), by_head),
            pl.BlockSpec((4, CONV_COLS), by_head),
            pl.BlockSpec(cols.shape, const),
            pl.BlockSpec(rows.shape, const),
            pl.BlockSpec((1, DV), const),
        ],
        out_specs=[
            pl.BlockSpec((tokens, HEAD_COLS), by_head),
            pl.BlockSpec((tokens, DV), by_head),
            save,
            save,
            save,
        ],
        out_shape=[
            jax.ShapeDtypeStruct((tokens, HEADS * HEAD_COLS), F32),
            jax.ShapeDtypeStruct((tokens, HEADS * DV), BF16),
            jax.ShapeDtypeStruct((HEADS, tokens, SEQ), BF16),
            jax.ShapeDtypeStruct((HEADS, tokens, DV), F32),
            jax.ShapeDtypeStruct((HEADS, tokens, DV), F32),
        ],
        compiler_params=pltpu.CompilerParams(vmem_limit_bytes=56 * MIB),
        name="mixer_fwd",
    )(xn, w, taps, cols, rows, gain)


def mixer_bwd_body(
    gb_ref, gbt_ref, xnt_ref, wo_ref, w_ref, proj_ref, mixed_ref, inv_ref, upd_ref, core_ref,
    taps_ref, cols_ref, rows_ref, gain_ref,
    dw_ref, dwo_ref, gxn_ref, dcols_ref, drows_ref, dtaps_ref, dgain_ref, dproj_ref,
):
    head = pl.program_id(0)
    tokens = gb_ref.shape[0]

    @pl.when(head == 0)
    def _():
        gxn_ref[...] = jnp.zeros_like(gxn_ref)
        dcols_ref[...] = jnp.zeros_like(dcols_ref)
        drows_ref[...] = jnp.zeros_like(drows_ref)
        dgain_ref[...] = jnp.zeros_like(dgain_ref)

    grad_mixed = jnp.dot(gb_ref[...], wo_ref[...], preferred_element_type=F32)
    dwo_ref[...] = jnp.dot(gbt_ref[...], mixed_ref[...], preferred_element_type=F32).astype(BF16)

    projected = proj_ref[...]
    taps = taps_ref[...]
    keep, conv, gate, act, qn, k, value, q_scale, k_scale, cum, rate, seg = head_inputs(
        projected, taps, cols_ref[...], head
    )
    q = qn * DK**-0.5
    cum_row = rows_ref[pl.ds(head, 1), :]
    seg_row = rows_ref[8:9, :]
    gain = gain_ref[...]
    lanes = lax.broadcasted_iota(jnp.int32, (SEQ, 128), 1)
    d_act, d_gain = [], jnp.zeros((1, DV), F32)
    for start in range(0, tokens, SEQ):
        part = slice(start, start + SEQ)
        core, update, inverse = core_ref[0, part, :], upd_ref[0, part, :], inv_ref[0, part, :]
        grad = grad_mixed[part]
        scale = lax.rsqrt(jnp.mean(core * core, axis=1, keepdims=True) + head_epsilon)
        normed = core * scale
        out_gate = projected[part, CONV_COLS:]
        out_sig = sigmoid(out_gate)
        swish = out_gate * out_sig
        dproj_ref[part, CONV_COLS:] = (grad * normed * gain * (out_sig + swish * (1.0 - out_sig))).astype(BF16)
        d_normed = grad * swish
        d_gain = d_gain + jnp.sum(d_normed * normed, axis=0, keepdims=True)
        d_scaled = d_normed * gain
        d_core = scale * (d_scaled - normed * jnp.mean(d_scaled * normed, axis=1, keepdims=True))

        qs, ks, vs, rs = q[part], k[part], value[part], rate[part]
        pair = decays(seg[part], seg_row[:, part], cum[part], cum_row[:, part])
        key_dots = dot3(ks, ks, NT)
        query_dots = dot3(qs, ks, NT)
        d_scores = dot3(d_core, update, NT)
        d_update = dot1(pair * query_dots, d_core, TN)
        solved = dot1(inverse, d_update, TN)
        d_coupling = strict(-dot1(solved, update, NT)) * pair
        d_query_dots = pair * d_scores
        d_key_dots = d_coupling * rs
        weighed = d_coupling * key_dots
        d_spread = d_query_dots * query_dots + weighed * rs
        d_q = dot1(d_query_dots, ks, NN) * DK**-0.5
        d_k = dot1(d_query_dots, qs, TN) + dot1(d_key_dots, ks, NN) + dot1(d_key_dots, ks, TN)
        d_rate = jnp.sum(solved * vs, axis=1, keepdims=True) + jnp.sum(weighed, axis=1, keepdims=True)
        row_sum = jnp.sum(d_spread, axis=1, keepdims=True)
        dcols_ref[part, :] += jnp.where(lanes == head, d_rate, 0.0) + jnp.where(lanes == 8 + head, row_sum, 0.0)
        drows_ref[pl.ds(head, 1), part] = jnp.sum(d_spread, axis=0, keepdims=True)
        d_q_act = q_scale[part] * (d_q - qn[part] * jnp.sum(d_q * qn[part], axis=1, keepdims=True))
        d_k_act = k_scale[part] * (d_k - ks * jnp.sum(d_k * ks, axis=1, keepdims=True))
        d_act.append(jnp.concatenate([d_q_act, d_k_act, rs * solved], axis=1))
    dgain_ref[...] += d_gain
    d_conv = jnp.concatenate(d_act, axis=0) * (gate + act * (1.0 - gate))
    source = projected[:, :CONV_COLS]
    d_source = d_conv * taps[0:1]
    d_taps = [jnp.sum(d_conv * source, axis=0, keepdims=True)]
    for back in (1, 2, 3):
        kept = d_conv * keep[back - 1]
        d_source = d_source + pltpu.roll(kept, tokens - back, 0) * taps[back : back + 1]
        d_taps.append(jnp.sum(kept * pltpu.roll(source, back, 0), axis=0, keepdims=True))
    dtaps_ref[...] = jnp.concatenate(d_taps, axis=0)
    dproj_ref[:, :CONV_COLS] = d_source.astype(BF16)
    d_proj = dproj_ref[...]
    dw_ref[...] = jnp.dot(xnt_ref[...], d_proj, preferred_element_type=F32).astype(BF16)
    gxn_ref[...] += lax.dot_general(d_proj, w_ref[...], (NT, ((), ())), preferred_element_type=F32)


def mixer_bwd(gb, gbt, xnt, wo, w, proj, mixed, inv, upd, core, taps, cols, rows, gain):
    tokens, width = gb.shape
    const = lambda h: (0, 0)
    by_head = lambda h: (0, h)
    save = pl.BlockSpec((1, tokens, SEQ), lambda h: (h, 0, 0))
    return pl.pallas_call(
        mixer_bwd_body,
        grid=(HEADS,),
        in_specs=[
            pl.BlockSpec((tokens, width), const),
            pl.BlockSpec((width, tokens), const),
            pl.BlockSpec((width, tokens), const),
            pl.BlockSpec((width, DV), by_head),
            pl.BlockSpec((width, HEAD_COLS), by_head),
            pl.BlockSpec((tokens, HEAD_COLS), by_head),
            pl.BlockSpec((tokens, DV), by_head),
            save,
            save,
            save,
            pl.BlockSpec((4, CONV_COLS), by_head),
            pl.BlockSpec(cols.shape, const),
            pl.BlockSpec(rows.shape, const),
            pl.BlockSpec((1, DV), const),
        ],
        out_specs=[
            pl.BlockSpec((width, HEAD_COLS), by_head),
            pl.BlockSpec((width, DV), by_head),
            pl.BlockSpec((tokens, width), const),
            pl.BlockSpec((tokens, 128), const),
            pl.BlockSpec((HEADS, tokens), const),
            pl.BlockSpec((4, CONV_COLS), by_head),
            pl.BlockSpec((1, DV), const),
        ],
        out_shape=[
            jax.ShapeDtypeStruct((width, HEADS * HEAD_COLS), BF16),
            jax.ShapeDtypeStruct((width, HEADS * DV), BF16),
            jax.ShapeDtypeStruct((tokens, width), F32),
            jax.ShapeDtypeStruct((tokens, 128), F32),
            jax.ShapeDtypeStruct((HEADS, tokens), F32),
            jax.ShapeDtypeStruct((4, HEADS * CONV_COLS), F32),
            jax.ShapeDtypeStruct((1, DV), F32),
        ],
        scratch_shapes=[pltpu.VMEM((tokens, HEAD_COLS), BF16)],
        compiler_params=pltpu.CompilerParams(vmem_limit_bytes=60 * MIB),
        name="mixer_bwd",
    )(gb, gbt, xnt, wo, w, proj, mixed, inv, upd, core, taps, cols, rows, gain)


def ffn_body(nm_ref, nmt_ref, cot_ref, cott_ref, w_ref, dw_ref, out_ref, gnm_ref):
    @pl.when(pl.program_id(0) == 0)
    def _():
        out_ref[...] = jnp.zeros_like(out_ref)
        gnm_ref[...] = jnp.zeros_like(gnm_ref)

    w = w_ref[...]
    gate_up = jnp.dot(nm_ref[...], w[:, : 2 * TILE], preferred_element_type=F32)
    gate, up = gate_up[:, :TILE], gate_up[:, TILE:]
    sig = sigmoid(gate)
    swish = gate * sig
    hidden = (swish * up).astype(BF16)
    grad_hidden = jnp.dot(cot_ref[...], w[:, 2 * TILE :], preferred_element_type=F32)
    grad_gate = grad_hidden * up * (sig + swish * (1.0 - sig))
    grad_up = grad_hidden * swish
    grad_low = jnp.concatenate([grad_gate, grad_up], axis=1).astype(BF16)
    out_ref[...] += lax.dot_general(hidden, w[:, 2 * TILE :], (NT, ((), ())), preferred_element_type=F32)
    gnm_ref[...] += lax.dot_general(grad_low, w[:, : 2 * TILE], (NT, ((), ())), preferred_element_type=F32)
    dw_ref[:, : 2 * TILE] = jnp.dot(nmt_ref[...], grad_low, preferred_element_type=F32).astype(BF16)
    dw_ref[:, 2 * TILE :] = jnp.dot(cott_ref[...], hidden, preferred_element_type=F32).astype(BF16)


def ffn(nm, nmt, cot, cott, w):
    tokens, width = nm.shape
    tiles = w.shape[1] // (3 * TILE)
    const = lambda t: (0, 0)
    by_tile = lambda t: (0, t)
    return pl.pallas_call(
        ffn_body,
        grid=(tiles,),
        in_specs=[
            pl.BlockSpec((tokens, width), const),
            pl.BlockSpec((width, tokens), const),
            pl.BlockSpec((tokens, width), const),
            pl.BlockSpec((width, tokens), const),
            pl.BlockSpec((width, 3 * TILE), by_tile),
        ],
        out_specs=[
            pl.BlockSpec((width, 3 * TILE), by_tile),
            pl.BlockSpec((tokens, width), const),
            pl.BlockSpec((tokens, width), const),
        ],
        out_shape=[
            jax.ShapeDtypeStruct((width, tiles * 3 * TILE), BF16),
            jax.ShapeDtypeStruct((tokens, width), F32),
            jax.ShapeDtypeStruct((tokens, width), F32),
        ],
        compiler_params=pltpu.CompilerParams(vmem_limit_bytes=48 * MIB),
        name="ffn",
    )(nm, nmt, cot, cott, w)


def rms_scale(values):
    return lax.rsqrt(jnp.mean(values * values, axis=-1, keepdims=True) + epsilon)


def rms_back(grad, values, scale, gain):
    normed = values * scale
    d_normed = grad * gain
    d_values = scale * (d_normed - normed * jnp.mean(d_normed * normed, axis=-1, keepdims=True))
    return d_values, jnp.sum(grad * normed, axis=0)


def by_head(parts):
    shaped = [p.reshape(p.shape[0], HEADS, -1) for p in parts]
    return jnp.concatenate(shaped, axis=2).reshape(parts[0].shape[0], -1)


def from_head(values, sizes):
    shaped = values.reshape(values.shape[0], HEADS, -1)
    ends = [sum(sizes[: i + 1]) for i in range(len(sizes))]
    cuts = [shaped[:, :, e - s : e].reshape(values.shape[0], -1) for s, e in zip(sizes, ends)]
    return jnp.concatenate(cuts, axis=1)


def split_heads(values):
    key = HEADS * DK
    val = HEADS * DV
    edges = [0, key, 2 * key, 2 * key + val, 2 * key + 2 * val]
    return [values[:, a:b] for a, b in zip(edges[:-1], edges[1:]) if b <= values.shape[1]]


def plain_block(
    devices, tokens, segment_ids, cotangent, norm1_gain, mixer_in, decay_in, conv_weight, decay_log, decay_bias,
    head_gain, mixer_out, norm2_gain, ffn_in, ffn_out,
):
    rows, width = decay_in.shape[0], tokens.shape[1]
    count = tokens.shape[0]
    hidden = ffn_out.shape[0]
    tiles = hidden // TILE

    low = lambda v: v.astype(BF16)
    shard_mixer = by_head(split_heads(low(mixer_in)))
    conv_cols = conv_weight.shape[1]
    shard_small = jnp.concatenate(
        [low(decay_in), low(norm1_gain)[:, None], low(norm2_gain)[:, None], low(conv_weight).reshape(rows, -1)], axis=1
    )
    shard_small = jnp.pad(shard_small, ((0, 0), (0, SMALL - shard_small.shape[1])))
    shard_out = low(mixer_out).T
    ffn_low = low(ffn_in)
    pieces = [ffn_low[:, :hidden], ffn_low[:, hidden:], low(ffn_out).T]
    shard_ffn = jnp.concatenate([p.reshape(rows, tiles, TILE) for p in pieces], axis=2).reshape(rows, -1)
    shards = [shard_small, shard_mixer, shard_out, shard_ffn]

    x = tokens.astype(F32)
    scale1 = rms_scale(x)
    full_small, full_mixer, full_out, full_ffn = [lax.all_gather(s, "dp", axis=0, tiled=True) for s in shards]

    decay_full = full_small[:, :16]
    gain1 = full_small[:, 16].astype(F32)
    gain2 = full_small[:, 17].astype(F32)
    taps = full_small[:, 18 : 18 + 16].reshape(devices, 4, conv_cols)
    taps = jnp.moveaxis(taps, 0, 1).reshape(4, -1).astype(F32)
    taps = by_head(split_heads(taps))

    normed_in = low(x * scale1 * gain1)
    logits = jnp.dot(normed_in, decay_full, preferred_element_type=F32)
    shifted = logits[:, :HEADS] + decay_bias
    log_decay = -jnp.exp(decay_log) * jax.nn.softplus(shifted)
    rate = jax.nn.sigmoid(logits[:, HEADS:])
    sequences = count // SEQ
    lower = jnp.tril(jnp.ones((SEQ, SEQ), F32))
    cumulative = jnp.einsum(
        "ij,sjh->sih", lower, log_decay.reshape(sequences, SEQ, HEADS), precision=lax.Precision.HIGHEST
    ).reshape(count, HEADS)
    position = jnp.arange(count) % SEQ
    keeps = []
    for back in (1, 2, 3):
        earlier = jnp.pad(segment_ids[:-back], (back, 0), constant_values=-1)
        keeps.append(((earlier == segment_ids) & (position >= back)).astype(F32)[:, None])
    segment = segment_ids.astype(F32)
    cols = jnp.concatenate([cumulative, rate] + keeps + [segment[:, None]], axis=1)
    cols = jnp.pad(cols, ((0, 0), (0, 128 - cols.shape[1])))
    seq_rows = jnp.concatenate([cumulative.T, segment[None], jnp.zeros((7, count), F32)], axis=0)
    gain_row = head_gain[None]

    proj, mixed, inverse, update, core = mixer_fwd(normed_in, full_mixer, taps, cols, seq_rows, gain_row)

    middle = x + lax.dot_general(mixed, full_out, (NT, ((), ())), preferred_element_type=F32)
    scale2 = rms_scale(middle)
    normed_mid = low(middle * scale2 * gain2)
    dw_ffn, ffn_sum, grad_nm = ffn(normed_mid, normed_mid.T, cotangent, cotangent.T, full_ffn)
    output = low(middle + ffn_sum)

    d_middle, d_gain2 = rms_back(grad_nm, middle, scale2, gain2)
    grad_middle = d_middle + cotangent.astype(F32)
    branch = low(grad_middle)
    dw_mixer, dw_out, grad_xn, d_cols, d_rows, d_taps, d_gain = mixer_bwd(
        branch, branch.T, normed_in.T, full_out, full_mixer, proj, mixed, inverse, update, core,
        taps, cols, seq_rows, gain_row,
    )

    d_cum = d_cols[:, 8:16] - d_rows.T
    d_decay = jnp.einsum(
        "ji,sjh->sih", lower, d_cum.reshape(sequences, SEQ, HEADS), precision=lax.Precision.HIGHEST
    ).reshape(count, HEADS)
    d_shifted = -d_decay * jnp.exp(decay_log) * jax.nn.sigmoid(shifted)
    d_rate = d_cols[:, :8] * rate * (1.0 - rate)
    d_logits = low(jnp.concatenate([d_shifted, d_rate], axis=1))
    grad_xn = grad_xn + lax.dot_general(d_logits, decay_full, (NT, ((), ())), preferred_element_type=F32)
    d_x, d_gain1 = rms_back(grad_xn, x, scale1, gain1)
    input_grad = d_x + grad_middle

    d_decay_in = lax.dot_general(normed_in, d_logits, (TN, ((), ())), preferred_element_type=F32)
    d_taps = from_head(d_taps, [DK, DK, DV])
    d_taps = jnp.moveaxis(d_taps.reshape(4, devices, conv_cols), 1, 0).reshape(width, -1)
    dw_small = jnp.concatenate([d_decay_in, d_gain1[:, None], d_gain2[:, None], d_taps], axis=1)
    dw_small = low(jnp.pad(dw_small, ((0, 0), (0, SMALL - dw_small.shape[1]))))
    shared = jnp.concatenate([jnp.sum(d_decay * log_decay, axis=0), jnp.sum(d_shifted, axis=0), d_gain[0]])

    own_ffn, own_out, own_mixer, own_small = [
        lax.psum_scatter(g.astype(F32), "dp", scatter_dimension=0, tiled=True)
        for g in (dw_ffn, dw_out, dw_mixer, dw_small)
    ]
    shared = lax.psum(shared, "dp")

    own_tiles = own_ffn.reshape(rows, tiles, 3, TILE)
    ffn_in_grad = jnp.concatenate([own_tiles[:, :, i].reshape(rows, hidden) for i in (0, 1)], axis=1)
    ffn_out_grad = own_tiles[:, :, 2].reshape(rows, hidden).T
    return (
        output,
        input_grad,
        own_small[:, 16],
        from_head(own_mixer, [DK, DK, DV, DV]),
        own_small[:, :16],
        own_small[:, 18 : 18 + 16].reshape(4, conv_cols),
        shared[:HEADS],
        shared[HEADS : 2 * HEADS],
        shared[2 * HEADS : 2 * HEADS + DV],
        own_out.T,
        own_small[:, 17],
        ffn_in_grad,
        ffn_out_grad,
    )


def direct_block(
    devices, tokens, segment_ids, cotangent, norm1_gain, mixer_in, decay_in, conv_weight, decay_log, decay_bias,
    head_gain, mixer_out, norm2_gain, ffn_in, ffn_out,
):
    rows = decay_in.shape[0]
    count = tokens.shape[0]
    hidden = ffn_out.shape[0]
    tiles = hidden // TILE
    planes = devices // 8
    low = lambda v: v.astype(BF16)
    pad = lambda v, lanes: jnp.pad(v, ((0, 0), (0, lanes - v.shape[1])))

    first = pad(jnp.concatenate([low(decay_in), low(norm1_gain)[:, None], low(norm2_gain)[:, None]], axis=1), SMALL)
    second = jnp.pad(low(conv_weight), ((0, rows - 4), (0, 0)))
    shard_small = jnp.concatenate([first, second], axis=1)
    shard_heads = by_head(split_heads(low(mixer_in)) + [low(mixer_out).T])
    ffn_low = low(ffn_in)
    pieces = [ffn_low[:, :hidden], ffn_low[:, hidden:], low(ffn_out).T]
    shard_tiles = jnp.concatenate([p.reshape(rows, tiles, TILE) for p in pieces], axis=2).reshape(rows, -1)

    position = jnp.arange(count) % SEQ
    keeps = [jnp.zeros((count, 16), F32)]
    for back in (1, 2, 3):
        earlier = jnp.pad(segment_ids[:-back], (back, 0), constant_values=-1)
        keeps.append(((earlier == segment_ids) & (position >= back)).astype(F32)[:, None])
    segment = segment_ids.astype(F32)
    aux = pad(jnp.concatenate(keeps + [segment[:, None]], axis=1), 128)
    seg_rows = jnp.broadcast_to(segment[None], (8, count))
    lines = jnp.stack([-jnp.exp(decay_log), decay_bias])
    consts = jnp.pad(lines, ((0, 6), (0, 128 - HEADS)))
    gain = head_gain[None]

    (
        _, full_heads, _, small, xnt, cols, seq_rows, logs, factor, proj, mixed, inverse, update, core, dwf,
        output, grad_mid, branch, brancht, d_gain2,
    ) = forward(planes, [shard_small, shard_heads, shard_tiles], tokens, cotangent, aux, seg_rows, consts, gain)
    input_grad, own_mixer, own_out, own_ffn, own_down, own_small, shared = backward(
        planes, dwf, branch, brancht, xnt, full_heads, proj, mixed, inverse, update, core, small, cols, seq_rows, logs,
        factor, gain, tokens, grad_mid, d_gain2,
    )
    return (
        output,
        input_grad,
        own_small[:, 16],
        own_mixer,
        own_small[:, :16],
        own_small[:4, SMALL:],
        shared[0, :HEADS],
        shared[1, :HEADS],
        shared[2:4].reshape(-1),
        own_out.T,
        own_small[:, 17],
        own_ffn,
        own_down.T,
    )


def on_device(devices, *arguments):
    rows, conv_cols = arguments[4].shape[0], arguments[6].shape[1]
    direct = rows % 16 == 0 and devices == 32 and conv_cols == 128
    return (direct_block if direct else plain_block)(devices, *arguments)


def solution(mesh):
    in_specs = (
        P("dp", None), P("dp"), P("dp", None), P("dp"), P("dp", None), P("dp", None), P(None, "dp"), P(), P(), P(),
        P(None, "dp"), P("dp"), P("dp", None), P(None, "dp"),
    )
    out_specs = (
        P("dp", None), P("dp", None), P("dp"), P("dp", None), P("dp", None), P(None, "dp"), P(), P(), P(),
        P(None, "dp"), P("dp"), P("dp", None), P(None, "dp"),
    )
    return jax.shard_map(
        partial(on_device, mesh.shape["dp"]), mesh=mesh, in_specs=in_specs, out_specs=out_specs, check_vma=False
    )
```

```python
from functools import partial

import jax
import jax.numpy as jnp
from jax import lax
from jax.experimental import pallas as pl
from jax.experimental.pallas import tpu as pltpu
from jax.sharding import PartitionSpec as P

HEADS = 8
DK = 128
DV = 256
SEQ = 256
HEAD_COLS = 2 * DK + 2 * DV
CONV_COLS = 2 * DK + DV
TILE = 256
SMALL = 128
F32 = jnp.float32
BF16 = jnp.bfloat16
MESH = pl.DeviceIdType.MESH
MIB = 1 << 20
epsilon = 1e-06
head_epsilon = 0.001

NN = ((1,), (0,))
NT = ((1,), (1,))
TN = ((0,), (0,))


def dot1(left, right, dims):
    return lax.dot_general(
        left.astype(BF16), right.astype(BF16), (dims, ((), ())), preferred_element_type=F32
    )


def split(value):
    high = value.astype(BF16)
    return high, (value - high.astype(F32)).astype(BF16)


def dot3(left, right, dims):
    lh, ll = split(left)
    rh, rl = split(right)
    return dot1(lh, rh, dims) + (dot1(lh, rl, dims) + dot1(ll, rh, dims))


def sigmoid(value):
    return 1.0 / (1.0 + jnp.exp(-value))


def grid_of(size):
    rows = lax.broadcasted_iota(jnp.int32, (size, size), 0)
    cols = lax.broadcasted_iota(jnp.int32, (size, size), 1)
    return rows, cols


def unit_inverses(couplings):
    size = couplings[0].shape[0]
    rows, cols = grid_of(size)
    apart = rows ^ cols
    eye = jnp.where(apart == 0, 1.0, 0.0)
    lows = [a.astype(BF16) for a in couplings]
    inverses = [eye - jnp.where(apart < 2, a, 0.0) for a in couplings]
    block = 2
    while block < size:
        here = jnp.where((apart >= block) & (apart < 2 * block), 1.0, 0.0).astype(BF16)
        firsts = [dot1(low * here, inv, NN) for low, inv in zip(lows, inverses)]
        inverses = [inv - dot1(inv, first, NN) for inv, first in zip(inverses, firsts)]
        block *= 2
    return inverses


def pick_lane(columns, lane):
    at = lax.broadcasted_iota(jnp.int32, columns.shape, 1)
    return jnp.sum(jnp.where(at == lane, columns, 0.0), axis=1, keepdims=True)


def conv_of(values, taps, keep):
    total = values * taps[0:1]
    for back in (1, 2, 3):
        total = total + pltpu.roll(values, back, 0) * keep[back - 1] * taps[back : back + 1]
    return total


def decays(seg_col, seg_row, cum_col, cum_row):
    rows, cols = grid_of(SEQ)
    linked = (seg_col == seg_row) & (rows >= cols)
    return jnp.where(linked, jnp.exp(jnp.where(linked, cum_col - cum_row, 0.0)), 0.0)


def strict(value):
    rows, cols = grid_of(SEQ)
    return jnp.where(rows > cols, value, 0.0)


def head_inputs(projected, taps, cols, head):
    keep = [pick_lane(cols, 16 + i) for i in range(3)]
    conv = conv_of(projected[:, :CONV_COLS], taps, keep)
    gate = sigmoid(conv)
    act = conv * gate
    q_act, k_act, value = act[:, :DK], act[:, DK : 2 * DK], act[:, 2 * DK :]
    q_scale = lax.rsqrt(jnp.sum(q_act * q_act, axis=1, keepdims=True) + epsilon)
    k_scale = lax.rsqrt(jnp.sum(k_act * k_act, axis=1, keepdims=True) + epsilon)
    cum = pick_lane(cols, head)
    rate = pick_lane(cols, 8 + head)
    seg = pick_lane(cols, 19)
    return keep, conv, gate, act, q_act * q_scale, k_act * k_scale, value, q_scale, k_scale, cum, rate, seg


def flip(number, bit):
    return number + bit - 2 * bit * ((number // bit) % 2)


def enter():
    me = lax.axis_index("dp")
    barrier = pltpu.get_barrier_semaphore()
    partners = [flip(me, bit) for bit in (1, 2, 4, 8, 16)]
    for other in partners:
        pl.semaphore_signal(barrier, inc=1, device_id=(other,), device_id_type=MESH)
    pl.semaphore_wait(barrier, len(partners))
    return me


def span(k, width, start, size):
    first = k * width + start
    return pl.ds(first if isinstance(first, int) else pl.multiple_of(first, 128), size)


def remote(source, target, send_sem, recv_sem, other):
    return pltpu.make_async_remote_copy(
        src_ref=source, dst_ref=target, send_sem=send_sem, recv_sem=recv_sem,
        device_id=(other,), device_id_type=MESH,
    )


(
    G_NEAR, G_FAR, G_RELAY, G_X, G_Y, G_CORNER_Y, G_CORNER_X, G_CORE_OWN,
    G_CORE_OTHER, G_TWO_X, G_TWO_Y, G_TWO_CORNER, G_TWO_NEAR, G_TWO_FAR, G_TWO_RELAY, G_TWO_CORE,
) = range(16)
(
    S_CORE, S_XY_X, S_XY_Y, S_X_EARLY, S_X_LATE, S_Y_EARLY, S_Y_LATE, S_RELAY,
    S_NEAR, S_FAR, S_TWO_RELAY, S_TWO_NEAR, S_TWO_FAR, S_TWO_XY, S_TWO_X, S_TWO_Y,
) = range(16)
B_CORE, B_KEEP, B_SUMS, B_XY, B_X, B_Y, B_Z, B_TWO_Z, B_TWO = range(9)
HEAD, FFN_TILE, SMALLS = range(3)


SHAPES = {
    HEAD: (HEAD_COLS + DV, HEAD_COLS, HEAD_COLS // 2),
    FFN_TILE: (3 * TILE, 5 * TILE // 2, 3 * TILE // 2),
    SMALLS: (2 * SMALL, 2 * SMALL, SMALL),
}


class Gather:
    copies = 16

    def __init__(self, me, kinds, local_sem, send_sem, recv_sem):
        self.me, self.kinds = me, kinds
        self.local_sem, self.send_sem, self.recv_sem = local_sem, send_sem, recv_sem
        self.z, self.y, self.x, self.core = me // 8, (me // 4) % 2, (me // 2) % 2, me % 2

    def local(self, kind, k):
        shard, full, base = self.kinds[kind]
        width = SHAPES[kind][0]
        cols = span(k, width, 0, width)
        return pltpu.make_async_copy(
            shard.at[:, cols], full.at[self.z, self.y, self.x, self.core, :, cols], self.local_sem.at[base + k]
        )

    def copy(self, kind, k, name):
        shard, full, base = self.kinds[kind]
        width, part, half = SHAPES[kind]
        one = span(k, width, 0, part)
        two = span(k, width, part, width - part)
        z, y, x, core = self.z, self.y, self.x, self.core
        near, far = flip(z, 1), flip(z, 2)
        here = lambda cols: (shard.at[:, cols], full.at[z, y, x, core, :, cols])
        same = lambda ref: (ref, ref)
        by_y = kind == FFN_TILE
        (source, target), bit = {
            G_NEAR: lambda: (here(one), 8),
            G_FAR: lambda: (here(one), 16),
            G_RELAY: lambda: (same(full.at[far, y, x, core, :, one]), 8),
            G_X: lambda: (same(full.at[:, y, x, core, :, one]), 2),
            G_Y: lambda: (same(full.at[:, y, x, core, :, one]), 4),
            G_CORNER_Y: lambda: (same(full.at[:, y, 1 - x, core, :, span(k, width, 0, half)]), 4),
            G_CORNER_X: lambda: (same(full.at[:, 1 - y, x, core, :, span(k, width, half, part - half)]), 2),
            G_CORE_OWN: lambda: (same(full.at[:, y, :, core, :, one]), 1),
            G_CORE_OTHER: lambda: (same(full.at[:, 1 - y, :, core, :, one]), 1),
            G_TWO_X: lambda: (here(two), 2),
            G_TWO_Y: lambda: (here(two), 4),
            G_TWO_CORNER: lambda: (
                (same(full.at[z, 1 - y, x, core, :, two]), 2)
                if by_y
                else (same(full.at[z, y, 1 - x, core, :, two]), 4)
            ),
            G_TWO_NEAR: lambda: (same(full.at[z, :, :, core, :, two]), 8),
            G_TWO_FAR: lambda: (same(full.at[z, :, :, core, :, two]), 16),
            G_TWO_RELAY: lambda: (same(full.at[far, :, :, core, :, two]), 8),
            G_TWO_CORE: lambda: (same(full.at[:, :, :, core, :, two]), 1),
        }[name]()
        sems = self.send_sem.at[base + k, name], self.recv_sem.at[base + k, name]
        return remote(source, target, *sems, flip(self.me, bit))

    def send(self, kind, k, *names):
        for name in names:
            self.copy(kind, k, name).start()

    def wait(self, kind, k, *names):
        for name in names:
            self.copy(kind, k, name).wait_recv()

    def two(self, kind):
        return SHAPES[kind][0] > SHAPES[kind][1]

    def start(self, kind, k):
        self.local(kind, k).start()
        self.send(kind, k, G_FAR, G_NEAR)
        if self.two(kind):
            self.send(kind, k, G_TWO_X, G_TWO_Y)

    def relay(self, kind, k):
        self.wait(kind, k, G_FAR)
        self.send(kind, k, G_RELAY)
        if self.two(kind):
            self.wait(kind, k, *((G_TWO_Y,) if kind == FFN_TILE else (G_TWO_X,)))
            self.send(kind, k, G_TWO_CORNER)

    def square(self, kind, k):
        self.local(kind, k).wait()
        self.wait(kind, k, G_NEAR, G_RELAY)
        self.send(kind, k, G_X, G_Y)
        if self.two(kind):
            self.wait(kind, k, *((G_TWO_X,) if kind == FFN_TILE else (G_TWO_Y,)), G_TWO_CORNER)
            self.send(kind, k, G_TWO_FAR, G_TWO_NEAR)

    def corner(self, kind, k):
        self.wait(kind, k, G_X)
        self.send(kind, k, G_CORNER_Y, G_CORE_OWN)
        self.wait(kind, k, G_Y)
        self.send(kind, k, G_CORNER_X)
        if self.two(kind):
            self.wait(kind, k, G_TWO_FAR)
            self.send(kind, k, G_TWO_RELAY)

    def across(self, kind, k):
        self.wait(kind, k, G_CORNER_Y, G_CORNER_X)
        self.send(kind, k, G_CORE_OTHER)
        if self.two(kind):
            self.wait(kind, k, G_TWO_NEAR, G_TWO_RELAY)
            self.send(kind, k, G_TWO_CORE)

    def complete(self, kind, k):
        self.wait(kind, k, G_CORE_OWN, G_CORE_OTHER)
        if self.two(kind):
            self.wait(kind, k, G_TWO_CORE)

    def finish(self, kind, k):
        names = [G_NEAR, G_FAR, G_RELAY, G_X, G_Y, G_CORNER_Y, G_CORNER_X, G_CORE_OWN, G_CORE_OTHER]
        if self.two(kind):
            names += [G_TWO_X, G_TWO_Y, G_TWO_CORNER, G_TWO_NEAR, G_TWO_FAR, G_TWO_RELAY, G_TWO_CORE]
        for name in names:
            self.copy(kind, k, name).wait_send()


class Scatter:
    copies = 16
    depths = {B_CORE: 4, B_KEEP: 2, B_SUMS: 6, B_XY: 4, B_X: 8, B_Y: 8, B_Z: 4, B_TWO_Z: 8, B_TWO: 4}

    def __init__(self, me, kinds, store, core, keep, sums, xy, x, y, z, two_z, two, local_sem, send_sem, recv_sem):
        self.me, self.kinds, self.store = me, kinds, store
        self.from_core, self.keep, self.sums = core, keep, sums
        self.from_xy, self.from_x, self.from_y, self.from_z = xy, x, y, z
        self.two_z, self.from_two = two_z, two
        self.local_sem, self.send_sem, self.recv_sem = local_sem, send_sem, recv_sem
        self.z, self.core = me // 8, me % 2
        self.here = (me // 2) % 4
        self.across_x, self.across_y = flip(self.here, 1), flip(self.here, 2)
        self.both = 3 - self.here
        self.near, self.far = flip(self.z, 1), flip(self.z, 2)
        self.opposite = 3 - self.z

    def slot(self, name, r):
        return r % self.depths[name]

    def copy(self, kind, r, k, name):
        source = self.kinds[kind][0]
        width, part, half = SHAPES[kind]
        whole, one, two = pl.ds(0, width), pl.ds(0, part), pl.ds(part, width - part)
        first, second = pl.ds(0, half), pl.ds(half, part - half)
        rest = pl.ds(0, width - part)
        sums = self.sums.at[self.slot(B_SUMS, r)]
        here, across_x, across_y, both, z = self.here, self.across_x, self.across_y, self.both, self.z
        by_y = kind == FFN_TILE
        place = lambda where, cols: sums.at[:, where, :, cols]
        origin, target, bit = {
            S_CORE: lambda: (
                source(k, 1 - self.core), self.from_core.at[self.slot(B_CORE, r), :, :, :, whole], 1
            ),
            S_XY_X: lambda: (place(both, first), self.from_xy.at[self.slot(B_XY, r), :, :, first], 2),
            S_XY_Y: lambda: (place(both, second), self.from_xy.at[self.slot(B_XY, r), :, :, second], 4),
            S_X_EARLY: lambda: (place(across_x, first), self.from_x.at[self.slot(B_X, r), :, :, first], 2),
            S_X_LATE: lambda: (place(across_x, second), self.from_x.at[self.slot(B_X, r), :, :, second], 2),
            S_Y_EARLY: lambda: (place(across_y, second), self.from_y.at[self.slot(B_Y, r), :, :, second], 4),
            S_Y_LATE: lambda: (place(across_y, first), self.from_y.at[self.slot(B_Y, r), :, :, first], 4),
            S_RELAY: lambda: (sums.at[self.opposite, here, :, one], self.from_z.at[self.slot(B_Z, r), 0, :, one], 8),
            S_NEAR: lambda: (sums.at[self.near, here, :, one], self.from_z.at[self.slot(B_Z, r), 1, :, one], 8),
            S_FAR: lambda: (sums.at[self.far, here, :, one], self.from_z.at[self.slot(B_Z, r), 2, :, one], 16),
            S_TWO_RELAY: lambda: (
                sums.at[self.opposite, :, :, two], self.two_z.at[self.slot(B_TWO_Z, r), 0, :, :, rest], 8
            ),
            S_TWO_NEAR: lambda: (
                sums.at[self.near, :, :, two], self.two_z.at[self.slot(B_TWO_Z, r), 1, :, :, rest], 8
            ),
            S_TWO_FAR: lambda: (
                sums.at[self.far, :, :, two], self.two_z.at[self.slot(B_TWO_Z, r), 2, :, :, rest], 16
            ),
            S_TWO_XY: lambda: (
                sums.at[z, both, :, two], self.from_two.at[self.slot(B_TWO, r), 0, :, rest], 4 if by_y else 2
            ),
            S_TWO_X: lambda: (sums.at[z, across_x, :, two], self.from_two.at[self.slot(B_TWO, r), 1, :, rest], 2),
            S_TWO_Y: lambda: (sums.at[z, across_y, :, two], self.from_two.at[self.slot(B_TWO, r), 2, :, rest], 4),
        }[name]()
        sems = self.send_sem.at[r, name], self.recv_sem.at[r, name]
        return remote(origin, target, *sems, flip(self.me, bit))

    def send(self, kind, r, k, *names):
        for name in names:
            self.copy(kind, r, k, name).start()

    def wait(self, kind, r, k, *names):
        for name in names:
            self.copy(kind, r, k, name).wait_recv()

    def two(self, kind):
        return SHAPES[kind][0] > SHAPES[kind][1]

    def load(self, kind, r, k):
        source = self.kinds[kind][0]
        return pltpu.make_async_copy(
            source(k, self.core), self.keep.at[r % 2, :, :, :, pl.ds(0, SHAPES[kind][0])], self.local_sem.at[r]
        )

    def core_step(self, kind, r, k):
        self.send(kind, r, k, S_CORE)

    def load_step(self, kind, r, k):
        if self.kinds[kind][1] is None:
            self.load(kind, r, k).start()

    def add_planes(self, r, place, cols, first, others):
        def one(plane, carry):
            total = first(plane).astype(F32)
            for read in others:
                total = total + read(plane).astype(F32)
            self.sums[self.slot(B_SUMS, r), plane, place, :, cols] = total.astype(BF16)
            return carry

        lax.fori_loop(0, 4, one, 0)

    def add_places(self, r, plane, cols, others):
        slot = self.slot(B_SUMS, r)
        for place in range(4):
            total = self.sums[slot, plane, place, :, cols].astype(F32)
            for read in others:
                total = total + read(place).astype(F32)
            self.sums[slot, plane, place, :, cols] = total.astype(BF16)

    def held(self, r, place, cols):
        return lambda plane: self.sums[self.slot(B_SUMS, r), plane, place, :, cols]

    def chip_step(self, kind, r, k):
        in_place = self.kinds[kind][1]
        width, part, half = SHAPES[kind]
        whole = pl.ds(0, width)
        self.wait(kind, r, k, S_CORE)
        if in_place is None:
            self.load(kind, r, k).wait()
            mine = lambda place: (lambda plane: self.keep[r % 2, plane, place, :, whole])
        else:
            mine = lambda place: (lambda plane: in_place(k, plane, place, self.core))
        got = lambda place: (lambda plane: self.from_core[self.slot(B_CORE, r), plane, place, :, whole])
        for place, names in (
            (self.both, (S_XY_X, S_XY_Y)),
            (self.across_x, (S_X_EARLY,)),
            (self.across_y, (S_Y_EARLY,)),
            (self.here, (S_TWO_RELAY, S_TWO_NEAR) if self.two(kind) else ()),
        ):
            self.add_planes(r, place, whole, got(place), [mine(place)])
            self.send(kind, r, k, *names)
        self.copy(kind, r, k, S_CORE).wait_send()

    def corner_step(self, kind, r, k):
        width, part, half = SHAPES[kind]
        first, second = pl.ds(0, half), pl.ds(half, part - half)
        passed = lambda cols: (lambda plane: self.from_xy[self.slot(B_XY, r), plane, :, cols])
        self.wait(kind, r, k, S_XY_X)
        self.add_planes(r, self.across_y, first, self.held(r, self.across_y, first), [passed(first)])
        self.send(kind, r, k, S_Y_LATE)
        self.wait(kind, r, k, S_XY_Y)
        self.add_planes(r, self.across_x, second, self.held(r, self.across_x, second), [passed(second)])
        self.send(kind, r, k, S_X_LATE)
        if self.two(kind):
            two, rest = pl.ds(part, width - part), pl.ds(0, width - part)
            self.wait(kind, r, k, S_TWO_RELAY)
            self.add_places(r, self.far, two, [lambda place: self.two_z[self.slot(B_TWO_Z, r), 0, place, :, rest]])
            self.send(kind, r, k, S_TWO_FAR)

    def square_step(self, kind, r, k):
        width, part, half = SHAPES[kind]
        one = pl.ds(0, part)
        self.wait(kind, r, k, S_X_EARLY, S_X_LATE, S_Y_EARLY, S_Y_LATE)
        from_x = lambda plane: self.from_x[self.slot(B_X, r), plane, :, one]
        from_y = lambda plane: self.from_y[self.slot(B_Y, r), plane, :, one]
        self.add_planes(r, self.here, one, self.held(r, self.here, one), [from_x, from_y])
        self.send(kind, r, k, S_RELAY, S_NEAR)
        if self.two(kind):
            two, rest = pl.ds(part, width - part), pl.ds(0, width - part)
            self.wait(kind, r, k, S_TWO_NEAR, S_TWO_FAR)
            self.add_places(
                r, self.z, two,
                [lambda place, i=i: self.two_z[self.slot(B_TWO_Z, r), i, place, :, rest] for i in (1, 2)],
            )
            self.send(kind, r, k, S_TWO_XY, S_TWO_X if kind != FFN_TILE else S_TWO_Y)

    def relay_step(self, kind, r, k):
        width, part, half = SHAPES[kind]
        slot, one = self.slot(B_SUMS, r), pl.ds(0, part)
        self.wait(kind, r, k, S_RELAY)
        total = self.sums[slot, self.far, self.here, :, one].astype(F32)
        total = total + self.from_z[self.slot(B_Z, r), 0, :, one].astype(F32)
        self.sums[slot, self.far, self.here, :, one] = total.astype(BF16)
        self.send(kind, r, k, S_FAR)
        if self.two(kind):
            two, rest = pl.ds(part, width - part), pl.ds(0, width - part)
            place = self.across_x if kind == FFN_TILE else self.across_y
            self.wait(kind, r, k, S_TWO_XY)
            total = self.sums[slot, self.z, place, :, two].astype(F32)
            total = total + self.from_two[self.slot(B_TWO, r), 0, :, rest].astype(F32)
            self.sums[slot, self.z, place, :, two] = total.astype(BF16)
            self.send(kind, r, k, S_TWO_X if kind == FFN_TILE else S_TWO_Y)

    def last_step(self, kind, r, k):
        width, part, half = SHAPES[kind]
        slot, one = self.slot(B_SUMS, r), pl.ds(0, part)
        self.wait(kind, r, k, S_NEAR, S_FAR)
        total = self.sums[slot, self.z, self.here, :, one].astype(F32)
        for i in (1, 2):
            total = total + self.from_z[self.slot(B_Z, r), i, :, one].astype(F32)
        names = [S_XY_X, S_XY_Y, S_X_EARLY, S_X_LATE, S_Y_EARLY, S_Y_LATE, S_RELAY, S_NEAR, S_FAR]
        if self.two(kind):
            two, rest = pl.ds(part, width - part), pl.ds(0, width - part)
            self.wait(kind, r, k, S_TWO_X, S_TWO_Y)
            more = self.sums[slot, self.z, self.here, :, two].astype(F32)
            for i in (1, 2):
                more = more + self.from_two[self.slot(B_TWO, r), i, :, rest].astype(F32)
            total = jnp.concatenate([total, more], axis=1)
            names += [S_TWO_RELAY, S_TWO_NEAR, S_TWO_FAR, S_TWO_XY, S_TWO_X, S_TWO_Y]
        self.store(kind, k, total)
        for name in names:
            self.copy(kind, r, k, name).wait_send()


class Total:
    bits = (1, 2, 4, 8, 16)

    def __init__(self, me, value_ref, out_ref, got, stage, send_sem, recv_sem):
        self.me, self.value_ref, self.out_ref = me, value_ref, out_ref
        self.got, self.stage, self.send_sem, self.recv_sem = got, stage, send_sem, recv_sem

    def copy(self, number):
        sems = self.send_sem.at[number], self.recv_sem.at[number]
        return remote(self.stage.at[number], self.got.at[number], *sems, flip(self.me, self.bits[number]))

    def step(self, number):
        last = len(self.bits)
        value = self.value_ref[...]
        if number > 0:
            self.copy(number - 1).wait_recv()
            value = self.stage[number - 1] + self.got[number - 1]
        if number < last:
            self.stage[number] = value
            self.copy(number).start()
        else:
            self.out_ref[...] = value
            for number in range(last):
                self.copy(number).wait_send()


def triangle_sum(values, dims):
    rows, cols = grid_of(SEQ)
    ones = jnp.where(rows >= cols, 1.0, 0.0).astype(BF16)
    first, rest = values.astype(BF16), values - values.astype(BF16).astype(F32)
    second, third = split(rest)
    return dot1(ones, first, dims) + (dot1(ones, second, dims) + dot1(ones, third, dims))


def log1p(value):
    series = value * (1.0 - value * (0.5 - value * (1.0 / 3.0 - value * (0.25 - value * 0.2))))
    return jnp.where(value < 0.01, series, jnp.log(1.0 + value))


def softplus(value):
    return jnp.maximum(value, 0.0) + log1p(jnp.exp(-jnp.abs(value)))


def merge(block):
    return block.reshape(-1, block.shape[-1])


def head_taps(small_ref, head):
    wide = 2 * head
    places = [(0, head), (1, head)] + [(2 + head // 4, wide % 8 + i) for i in (0, 1)]
    blocks = [
        small_ref[z, p // 4, (p // 2) % 2, p % 2, 0:16, SMALL : 2 * SMALL][0:4].astype(F32) for z, p in places
    ]
    return jnp.concatenate(blocks, axis=1)


def row_blocks(count, body, size=128):
    def one(i, carry):
        body(pl.ds(pl.multiple_of(i * size, size), size))
        return carry

    lax.fori_loop(0, count // size, one, 0)


def lane_index(shape):
    return lax.broadcasted_iota(jnp.int32, shape, 1)


def forward_body(
    planes, tiles,
    shard_small, shard_heads, shard_tiles, x_ref, cot_ref, aux_ref, seg_ref, consts_ref, gain_ref,
    full_small, full_heads, full_tiles, small_ref, xnt_ref, cols_ref, rows_ref, logs_ref, factor_ref,
    proj_ref, mixed_ref, inv_ref, upd_ref, core_ref, dw_ref,
    output_ref, middle, nm_sum,
    w_buf, xn, cott, nm, nmt, out_sum, gains, copy_sem, w_sem, local_sem, send_sem, recv_sem,
):
    step = pl.program_id(0)
    tokens = x_ref.shape[0]
    chunks = HEADS + tiles
    me = lax.axis_index("dp")
    kinds = {
        SMALLS: (shard_small, full_small, chunks),
        HEAD: (shard_heads, full_heads, 0),
        FFN_TILE: (shard_tiles, full_tiles, HEADS),
    }
    work = Gather(me, kinds, local_sem, send_sem, recv_sem)

    def at(chunk, act):
        pl.when((chunk >= 0) & (chunk < HEADS))(lambda: act(HEAD, chunk))
        pl.when((chunk >= HEADS) & (chunk < chunks))(lambda: act(FFN_TILE, chunk - HEADS))

    def weights(kind, k, slot):
        full, width = kinds[kind][1], SHAPES[kind][0]
        place = w_buf.at[slot, :, :, :, :, :, pl.ds(0, width)]
        return pltpu.make_async_copy(full.at[:, :, :, :, :, span(k, width, 0, width)], place, w_sem.at[slot])

    ahead = ((6, work.start), (5, work.relay), (4, work.square), (2, work.corner), (1, work.across))

    def early(step):
        for lead, act in ahead:
            if step + lead >= 0:
                act(HEAD, step + lead)

    def midway():
        for lead, act in ahead[:3]:
            at(step + lead, act)
        at(step + 1, work.complete)
        at(step + 1, lambda kind, k: weights(kind, k, (step + 1) % 2).start())

    @pl.when(step == 0)
    def _():
        enter()
        work.start(SMALLS, 0)
        early(-6)

        def prepare(rows):
            middle[rows, :] = x_ref[rows, :].astype(F32)
            cott[:, rows] = cot_ref[rows, :].astype(F32).T.astype(BF16)

        row_blocks(tokens, prepare)
        work.relay(SMALLS, 0)
        early(-5)
        work.square(SMALLS, 0)
        early(-4)
        work.corner(SMALLS, 0)
        early(-3)
        work.across(SMALLS, 0)
        out_sum[...] = jnp.zeros_like(out_sum)
        nm_sum[...] = jnp.zeros_like(nm_sum)
        work.complete(SMALLS, 0)
        early(-2)
        copy = pltpu.make_async_copy(full_small, small_ref, copy_sem)
        copy.start()
        copy.wait()
        small = merge(small_ref[..., 0:SMALL])
        turned = small.astype(F32).T
        gains[0:1, :] = turned[16:17, :]
        gains[1:2, :] = turned[17:18, :]

        def norm(rows):
            x = middle[rows, :]
            scale = lax.rsqrt(jnp.mean(x * x, axis=1, keepdims=True) + epsilon)
            normed = x * scale * gains[0:1, :]
            xn[rows, :] = normed.astype(BF16)
            xnt_ref[:, rows] = normed.T.astype(BF16)

        row_blocks(tokens, norm)
        logits = jnp.dot(xn[...], small, preferred_element_type=F32)
        lanes = lane_index(logits.shape)
        decay_scale, bias = consts_ref[0:1, :], consts_ref[1:2, :]
        shifted = logits + bias
        rate = sigmoid(logits)
        log_decay = decay_scale * softplus(shifted)
        logs_ref[...] = log_decay
        factor_ref[...] = jnp.where(
            lanes < 8, decay_scale * sigmoid(shifted), jnp.where(lanes < 16, rate * (1.0 - rate), 0.0)
        )
        for start in range(0, tokens, SEQ):
            part = slice(start, start + SEQ)
            cum = triangle_sum(log_decay[part], NN)
            cols_ref[part, :] = jnp.where(
                lanes[part] < 8, cum, jnp.where(lanes[part] < 16, rate[part], aux_ref[part, :])
            )
            rows_ref[0:8, part] = cum.T[0:8]
        rows_ref[8:16, :] = seg_ref[...]
        early(-1)
        work.finish(SMALLS, 0)
        work.complete(HEAD, 0)
        weights(HEAD, 0, 0).start()

    for lead, act in ahead[3:]:
        at(step + lead, act)
    at(step, lambda kind, k: weights(kind, k, step % 2).wait())
    at(step - 1, work.finish)

    @pl.when(step < HEADS)
    def _():
        w = merge(w_buf[step % 2])
        projected = jnp.dot(xn[...], w[:, :HEAD_COLS], preferred_element_type=F32)
        proj_ref[...] = projected
        midway()
        _, _, _, _, q, k, value, _, _, cum, rate, seg = head_inputs(
            projected, head_taps(small_ref, step), cols_ref[...], step
        )
        q = q * DK**-0.5
        cum_row = rows_ref[pl.ds(step, 1), :]
        seg_row = rows_ref[8:9, :]
        parts = [slice(s, s + SEQ) for s in range(0, tokens, SEQ)]
        scores, couplings = [], []
        for part in parts:
            pair = decays(seg[part], seg_row[:, part], cum[part], cum_row[:, part])
            key_dots = dot3(k[part], k[part], NT)
            scores.append(pair * dot3(q[part], k[part], NT))
            couplings.append(strict(pair * key_dots) * rate[part])
        inverses = unit_inverses(couplings)
        for i, part in enumerate(parts):
            update = dot3(inverses[i], rate[part] * value[part], NN)
            core = dot3(scores[i], update, NN)
            inv_ref[0, part, :] = inverses[i].astype(BF16)
            upd_ref[0, part, :] = update
            core_ref[0, part, :] = core
            scale = lax.rsqrt(jnp.mean(core * core, axis=1, keepdims=True) + head_epsilon)
            out_gate = projected[part, CONV_COLS:]
            mixed_ref[part, :] = (core * scale * gain_ref[...] * (out_gate * sigmoid(out_gate))).astype(BF16)
        middle[...] += lax.dot_general(mixed_ref[...], w[:, HEAD_COLS:], (NT, ((), ())), preferred_element_type=F32)

    @pl.when(step == HEADS)
    def _():
        def norm(rows):
            mid = middle[rows, :]
            scale = lax.rsqrt(jnp.mean(mid * mid, axis=1, keepdims=True) + epsilon)
            normed = mid * scale * gains[1:2, :]
            nm[rows, :] = normed.astype(BF16)
            nmt[:, rows] = normed.T.astype(BF16)

        row_blocks(tokens, norm)

    @pl.when(step >= HEADS)
    def _():
        w = merge(w_buf[step % 2, :, :, :, :, :, 0 : 3 * TILE])
        gate_up = jnp.dot(nm[...], w[:, : 2 * TILE], preferred_element_type=F32)
        gate, up = gate_up[:, :TILE], gate_up[:, TILE:]
        sig = sigmoid(gate)
        swish = gate * sig
        hidden = (swish * up).astype(BF16)
        midway()
        grad_hidden = jnp.dot(cot_ref[...], w[:, 2 * TILE :], preferred_element_type=F32)
        grad_gate = grad_hidden * up * (sig + swish * (1.0 - sig))
        grad_up = grad_hidden * swish
        grad_low = jnp.concatenate([grad_gate, grad_up], axis=1).astype(BF16)
        out_sum[...] += lax.dot_general(hidden, w[:, 2 * TILE :], (NT, ((), ())), preferred_element_type=F32)
        nm_sum[...] += lax.dot_general(grad_low, w[:, : 2 * TILE], (NT, ((), ())), preferred_element_type=F32)
        dw_ref[:, : 2 * TILE] = jnp.dot(nmt[...], grad_low, preferred_element_type=F32).astype(BF16)
        dw_ref[:, 2 * TILE :] = jnp.dot(cott[...], hidden, preferred_element_type=F32).astype(BF16)

    @pl.when(step == chunks - 1)
    def _():
        def add(rows):
            output_ref[rows, :] = (middle[rows, :] + out_sum[rows, :]).astype(BF16)

        row_blocks(tokens, add)
        work.finish(FFN_TILE, tiles - 1)


def once(shape):
    return pl.BlockSpec(shape, lambda i: (0,) * len(shape), pipeline_mode=pl.Buffered(1))


def forward(planes, shards, x, cot, aux, seg_rows, consts, gain):
    rows, tokens, width = shards[0].shape[0], *x.shape
    tiles = shards[2].shape[1] // (3 * TILE)
    chunks = HEADS + tiles
    hbm = pl.BlockSpec(memory_space=pl.ANY)
    head = lambda i: jnp.minimum(i, HEADS - 1)
    tile = lambda i: jnp.maximum(i - HEADS, 0)
    save = pl.BlockSpec((1, tokens, SEQ), lambda i: (head(i), 0, 0))
    shape = jax.ShapeDtypeStruct
    whole = [((planes, 2, 2, 2, rows, s.shape[1]), BF16) for s in shards]
    outs = [
        (hbm, *whole[0]),
        (hbm, *whole[1]),
        (hbm, *whole[2]),
        (once(whole[0][0]), *whole[0]),
        (once((width, tokens)), (width, tokens), BF16),
        (once((tokens, 128)), (tokens, 128), F32),
        (once((16, tokens)), (16, tokens), F32),
        (once((tokens, 128)), (tokens, 128), F32),
        (once((tokens, 128)), (tokens, 128), F32),
        (pl.BlockSpec((tokens, HEAD_COLS), lambda i: (0, head(i))), (tokens, HEADS * HEAD_COLS), F32),
        (pl.BlockSpec((tokens, DV), lambda i: (0, head(i))), (tokens, HEADS * DV), BF16),
        (save, (HEADS, tokens, SEQ), BF16),
        (save, (HEADS, tokens, DV), F32),
        (save, (HEADS, tokens, DV), F32),
        (pl.BlockSpec((width, 3 * TILE), lambda i: (0, tile(i))), (width, tiles * 3 * TILE), BF16),
        (once((tokens, width)), (tokens, width), BF16),
        (once((tokens, width)), (tokens, width), F32),
        (once((tokens, width)), (tokens, width), F32),
    ]
    return pl.pallas_call(
        partial(forward_body, planes, tiles),
        grid=(chunks,),
        in_specs=[hbm, hbm, hbm] + [once(a.shape) for a in (x, cot, aux, seg_rows, consts, gain)],
        out_specs=[o[0] for o in outs],
        out_shape=[shape(o[1], o[2]) for o in outs],
        scratch_shapes=[
            pltpu.VMEM((2, planes, 2, 2, 2, rows, HEAD_COLS + DV), BF16),
            pltpu.VMEM((tokens, width), BF16),
            pltpu.VMEM((width, tokens), BF16),
            pltpu.VMEM((tokens, width), BF16),
            pltpu.VMEM((width, tokens), BF16),
            pltpu.VMEM((tokens, width), F32),
            pltpu.VMEM((8, width), F32),
            pltpu.SemaphoreType.DMA,
            pltpu.SemaphoreType.DMA((2,)),
            pltpu.SemaphoreType.DMA((chunks + 1,)),
            pltpu.SemaphoreType.DMA((chunks + 1, Gather.copies)),
            pltpu.SemaphoreType.DMA((chunks + 1, Gather.copies)),
        ],
        compiler_params=pltpu.CompilerParams(
            collective_id=0, has_side_effects=True, vmem_limit_bytes=60 * MIB
        ),
        name="forward",
    )(*shards, x, cot, aux, seg_rows, consts, gain)


FIRST = 4


def row_sums(count, body, width, size=128):
    def one(i, total):
        return body(pl.ds(pl.multiple_of(i * size, size), size), total)

    return lax.fori_loop(0, count // size, one, jnp.zeros((1, width), F32))


def head_step(j):
    return jnp.minimum(j // 2, HEADS - 1)


def backward_body(
    planes, tiles, total_chunks,
    dwf_ref, middle_ref, nm_sum_ref, cot_ref, xnt_ref, w_ref, proj_ref, mixed_ref, inv_ref, upd_ref, core_ref,
    small_ref, cols_ref, rows_ref, logs_ref, factor_ref, gain_ref, x_ref,
    input_grad_ref, own_mixer, own_out, own_ffn, own_down, own_small, shared_ref,
    gb_ref, gbt_ref, grad_mid_ref, gains, dw, d_small, gxn, dcols, drows, dgain, dproj, value_ref,
    *scratch,
):
    *buffers, got, stage, local_sem, send_sem, recv_sem, total_send, total_recv = scratch
    step = pl.program_id(0)
    tokens = middle_ref.shape[0]
    rows = own_small.shape[0]
    hidden = tiles * TILE
    me = lax.axis_index("dp")

    def tile_source(k, core):
        return dwf_ref.at[:, :, core, :, span(k, 3 * TILE, 0, 3 * TILE)]

    kinds = {
        FFN_TILE: (tile_source, None),
        HEAD: (
            lambda k, core: dw.at[k % 2, :, :, core],
            lambda k, plane, place, core: dw[k % 2, plane, place, core],
        ),
        SMALLS: (
            lambda k, core: d_small.at[:, :, core],
            lambda k, plane, place, core: d_small[plane, place, core],
        ),
    }

    def store(kind, k, total):
        def put(ref, start, source, width):
            ref[:, pl.ds(pl.multiple_of(start, 128), width)] = total[:, source : source + width]

        if kind == SMALLS:
            own_small[...] = total
        elif kind == HEAD:
            put(own_mixer, k * DK, 0, DK)
            put(own_mixer, HEADS * DK + k * DK, DK, DK)
            put(own_mixer, 2 * HEADS * DK + k * DV, 2 * DK, DV)
            put(own_mixer, 2 * HEADS * DK + HEADS * DV + k * DV, 2 * DK + DV, DV)
            put(own_out, k * DV, HEAD_COLS, DV)
        else:
            put(own_ffn, k * TILE, 0, TILE)
            put(own_ffn, hidden + k * TILE, TILE, TILE)
            put(own_down, k * TILE, 2 * TILE, TILE)

    work = Scatter(me, kinds, store, *buffers, local_sem, send_sem, recv_sem)
    small_sum = Total(me, value_ref, shared_ref, got, stage, total_send, total_recv)

    last = total_chunks - 1

    def at(r, act):
        is_head = (r >= FIRST) & (r < last) & ((r - FIRST) % 2 == 0)
        is_early = (r >= 0) & (r < FIRST)
        is_tile = (r > FIRST) & (r < last) & ((r - FIRST) % 2 == 1)
        pl.when(is_early)(lambda: act(FFN_TILE, r, r))
        pl.when(is_tile)(lambda: act(FFN_TILE, r, (r + FIRST - 1) // 2))
        pl.when(is_head)(lambda: act(HEAD, r, (r - FIRST) // 2))
        pl.when(r == last)(lambda: act(SMALLS, r, 0))

    @pl.when(step == 0)
    def _():
        enter()
        work.core_step(FFN_TILE, 0, 0)
        work.core_step(FFN_TILE, 1, 1)
        work.load_step(FFN_TILE, 0, 0)
        gxn[...] = jnp.zeros_like(gxn)
        dcols[...] = jnp.zeros_like(dcols)
        drows[...] = jnp.zeros_like(drows)
        dgain[...] = jnp.zeros_like(dgain)
        d_small[...] = jnp.zeros_like(d_small)
        for r in (0, 1):
            work.chip_step(FFN_TILE, r, r)
            work.core_step(FFN_TILE, r + 2, r + 2)
            work.load_step(FFN_TILE, r + 1, r + 1)

    at(step - 4, work.last_step)
    at(step - 3, work.relay_step)
    at(step - 2, work.square_step)
    at(step, work.corner_step)
    at(step + 2, work.chip_step)
    at(step + 3, work.load_step)

    @pl.when(step == 0)
    def _():
        turned = merge(small_ref[..., 0:SMALL]).astype(F32).T
        gains[0:1, :] = turned[16:17, :]
        gains[1:2, :] = turned[17:18, :]

        def back(rows, total):
            mid = middle_ref[rows, :]
            scale = lax.rsqrt(jnp.mean(mid * mid, axis=1, keepdims=True) + epsilon)
            normed = mid * scale
            grad = nm_sum_ref[rows, :]
            d_normed = grad * gains[1:2, :]
            d_mid = scale * (d_normed - normed * jnp.mean(d_normed * normed, axis=1, keepdims=True))
            d_mid = d_mid + cot_ref[rows, :].astype(F32)
            grad_mid_ref[rows, :] = d_mid
            gb_ref[rows, :] = d_mid.astype(BF16)
            gbt_ref[:, rows] = d_mid.T.astype(BF16)
            return total + jnp.sum(grad * normed, axis=0, keepdims=True)

        gains[2:3, :] = row_sums(tokens, back, gains.shape[1])

    @pl.when((step < 2 * HEADS) & (step % 2 == 0))
    def _():
        head = step // 2
        w = merge(w_ref[...])
        grad_mixed = jnp.dot(gb_ref[...], w[:, HEAD_COLS:], preferred_element_type=F32)
        d_out = jnp.dot(gbt_ref[...], mixed_ref[...], preferred_element_type=F32).astype(BF16)
        dw[head % 2, :, :, :, :, pl.ds(HEAD_COLS, DV)] = d_out.reshape(dw.shape[1:5] + (DV,))

        projected = proj_ref[...]
        taps = head_taps(small_ref, head)
        keeps, conv, gate, act, qn, k, value, q_scale, k_scale, cum, rate, seg = head_inputs(
            projected, taps, cols_ref[...], head
        )
        q = qn * DK**-0.5
        cum_row = rows_ref[pl.ds(head, 1), :]
        seg_row = rows_ref[8:9, :]
        gain = gain_ref[...]
        lanes = lane_index((SEQ, 128))
        d_act, d_gain = [], jnp.zeros((1, DV), F32)
        for start in range(0, tokens, SEQ):
            part = slice(start, start + SEQ)
            core, update, inverse = core_ref[0, part, :], upd_ref[0, part, :], inv_ref[0, part, :]
            grad = grad_mixed[part]
            scale = lax.rsqrt(jnp.mean(core * core, axis=1, keepdims=True) + head_epsilon)
            normed = core * scale
            out_gate = projected[part, CONV_COLS:]
            out_sig = sigmoid(out_gate)
            swish = out_gate * out_sig
            dproj[part, CONV_COLS:] = (grad * normed * gain * (out_sig + swish * (1.0 - out_sig))).astype(BF16)
            d_normed = grad * swish
            d_gain = d_gain + jnp.sum(d_normed * normed, axis=0, keepdims=True)
            d_scaled = d_normed * gain
            d_core = scale * (d_scaled - normed * jnp.mean(d_scaled * normed, axis=1, keepdims=True))

            qs, ks, vs, rs = q[part], k[part], value[part], rate[part]
            pair = decays(seg[part], seg_row[:, part], cum[part], cum_row[:, part])
            key_dots = dot3(ks, ks, NT)
            query_dots = dot3(qs, ks, NT)
            d_scores = dot3(d_core, update, NT)
            d_update = dot1(pair * query_dots, d_core, TN)
            solved = dot1(inverse, d_update, TN)
            d_coupling = strict(-dot1(solved, update, NT)) * pair
            d_query_dots = pair * d_scores
            d_key_dots = d_coupling * rs
            weighed = d_coupling * key_dots
            d_spread = d_query_dots * query_dots + weighed * rs
            d_q = dot1(d_query_dots, ks, NN) * DK**-0.5
            d_k = dot1(d_query_dots, qs, TN) + dot1(d_key_dots, ks, NN) + dot1(d_key_dots, ks, TN)
            d_rate = jnp.sum(solved * vs, axis=1, keepdims=True) + jnp.sum(weighed, axis=1, keepdims=True)
            row_sum = jnp.sum(d_spread, axis=1, keepdims=True)
            dcols[part, :] += jnp.where(lanes == head, row_sum, 0.0) + jnp.where(lanes == 8 + head, d_rate, 0.0)
            drows[pl.ds(head, 1), part] = jnp.sum(d_spread, axis=0, keepdims=True)
            d_q_act = q_scale[part] * (d_q - qn[part] * jnp.sum(d_q * qn[part], axis=1, keepdims=True))
            d_k_act = k_scale[part] * (d_k - ks * jnp.sum(d_k * ks, axis=1, keepdims=True))
            d_act.append(jnp.concatenate([d_q_act, d_k_act, rs * solved], axis=1))
        dgain[0:1, :] += d_gain
        d_conv = jnp.concatenate(d_act, axis=0) * (gate + act * (1.0 - gate))
        source = projected[:, :CONV_COLS]
        d_source = d_conv * taps[0:1]
        d_taps = [jnp.sum(d_conv * source, axis=0, keepdims=True)]
        for back in (1, 2, 3):
            kept = d_conv * keeps[back - 1]
            d_source = d_source + pltpu.roll(kept, tokens - back, 0) * taps[back : back + 1]
            d_taps.append(jnp.sum(kept * pltpu.roll(source, back, 0), axis=0, keepdims=True))
        d_taps = jnp.concatenate(d_taps + [jnp.zeros((rows - 4, CONV_COLS), F32)], axis=0).astype(BF16)
        wide = 2 * head
        places = [(0, head), (1, head)] + [(2 + head // 4, wide % 8 + i) for i in (0, 1)]
        for i, (z, p) in enumerate(places):
            d_small[z, p // 2, p % 2, :, SMALL:] = d_taps[:, i * SMALL : (i + 1) * SMALL]
        dproj[:, :CONV_COLS] = d_source.astype(BF16)
        d_proj = dproj[...]
        d_in = jnp.dot(xnt_ref[...], d_proj, preferred_element_type=F32).astype(BF16)
        dw[head % 2, :, :, :, :, pl.ds(0, HEAD_COLS)] = d_in.reshape(dw.shape[1:5] + (HEAD_COLS,))
        gxn[...] += lax.dot_general(d_proj, w[:, :HEAD_COLS], (NT, ((), ())), preferred_element_type=F32)

    @pl.when(step == 2 * HEADS - 1)
    def _():
        small = merge(small_ref[..., 0:SMALL])
        lanes = lane_index((SEQ, 128))
        padded = jnp.concatenate([drows[...], jnp.zeros((120, tokens), F32)], axis=0).T
        d_logs = jnp.zeros((1, 128), F32)
        d_bias = jnp.zeros((1, 128), F32)
        d_logits = []
        for start in range(0, tokens, SEQ):
            part = slice(start, start + SEQ)
            d_cum = jnp.where(lanes < 8, dcols[part, :], 0.0) - padded[part]
            d_decay = triangle_sum(d_cum, TN)
            d_logit = jnp.where(lanes < 8, d_decay, dcols[part, :]) * factor_ref[part, :]
            d_logs = d_logs + jnp.sum(jnp.where(lanes < 8, d_decay * logs_ref[part, :], 0.0), axis=0, keepdims=True)
            d_bias = d_bias + jnp.sum(jnp.where(lanes < 8, d_logit, 0.0), axis=0, keepdims=True)
            d_logits.append(d_logit.astype(BF16))
        d_logits = jnp.concatenate(d_logits, axis=0)
        value_ref[...] = jnp.concatenate(
            [d_logs, d_bias, dgain[0:1, :128], dgain[0:1, 128:], jnp.zeros((4, 128), F32)], axis=0
        )
        gxn[...] += lax.dot_general(d_logits, small, (NT, ((), ())), preferred_element_type=F32)

        def back(at_rows, total):
            x = x_ref[at_rows, :].astype(F32)
            scale = lax.rsqrt(jnp.mean(x * x, axis=1, keepdims=True) + epsilon)
            normed = x * scale
            grad = gxn[at_rows, :]
            d_normed = grad * gains[0:1, :]
            d_x = scale * (d_normed - normed * jnp.mean(d_normed * normed, axis=1, keepdims=True))
            input_grad_ref[at_rows, :] = d_x + grad_mid_ref[at_rows, :]
            return total + jnp.sum(grad * normed, axis=0, keepdims=True)

        total = row_sums(tokens, back, gxn.shape[1])
        line = lax.broadcasted_iota(jnp.int32, (128, total.shape[1]), 0)
        lines = jnp.where(line == 16, total, jnp.where(line == 17, gains[2:3, :], 0.0))
        own = jnp.dot(xnt_ref[...], d_logits, preferred_element_type=F32) + lines.T
        d_small[:, :, :, :, 0:SMALL] = own.astype(BF16).reshape(d_small.shape[:4] + (SMALL,))

    at(step + 4, work.core_step)
    for number in range(len(Total.bits) + 1):
        pl.when(step == 2 * HEADS + number)(lambda number=number: small_sum.step(number))


def backward(planes, dwf, middle, nm_sum, cot, xnt, w, proj, mixed, inv, upd, core, small, cols, seq_rows, logs, factor,
             gain, x):
    tokens, width = middle.shape
    rows = small.shape[4]
    tiles = dwf.shape[1] // (3 * TILE)
    chunks = FIRST + 2 * HEADS
    assert tiles == FIRST + HEADS - 1
    hbm = pl.BlockSpec(memory_space=pl.ANY)
    head = head_step
    save = pl.BlockSpec((1, tokens, SEQ), lambda i: (head(i), 0, 0))
    shape = jax.ShapeDtypeStruct
    widest = HEAD_COLS + DV
    depth = Scatter.depths
    outs = [
        ((tokens, width), F32),
        ((rows, HEADS * HEAD_COLS), F32),
        ((rows, HEADS * DV), F32),
        ((rows, 2 * tiles * TILE), F32),
        ((rows, tiles * TILE), F32),
        ((rows, 2 * SMALL), F32),
        ((8, 128), F32),
    ]
    return pl.pallas_call(
        partial(backward_body, planes, tiles, chunks),
        grid=(chunks + 4,),
        in_specs=[
            hbm,
            once((tokens, width)),
            once((tokens, width)),
            once((tokens, width)),
            once((width, tokens)),
            pl.BlockSpec((planes, 2, 2, 2, rows, widest), lambda i: (0, 0, 0, 0, 0, head(i))),
            pl.BlockSpec((tokens, HEAD_COLS), lambda i: (0, head(i))),
            pl.BlockSpec((tokens, DV), lambda i: (0, head(i))),
            save,
            save,
            save,
        ]
        + [once(a.shape) for a in (small, cols, seq_rows, logs, factor, gain, x)],
        out_specs=[once(o[0]) for o in outs],
        out_shape=[shape(*o) for o in outs],
        scratch_shapes=[
            pltpu.VMEM((tokens, width), BF16),
            pltpu.VMEM((width, tokens), BF16),
            pltpu.VMEM((tokens, width), F32),
            pltpu.VMEM((8, width), F32),
            pltpu.VMEM((2, planes, 4, 2, rows, widest), BF16),
            pltpu.VMEM((planes, 4, 2, rows, 2 * SMALL), BF16),
            pltpu.VMEM((tokens, width), F32),
            pltpu.VMEM((tokens, 128), F32),
            pltpu.VMEM((HEADS, tokens), F32),
            pltpu.VMEM((8, DV), F32),
            pltpu.VMEM((tokens, HEAD_COLS), BF16),
            pltpu.VMEM((8, 128), F32),
            pltpu.VMEM((depth[B_CORE], planes, 4, rows, widest), BF16),
            pltpu.VMEM((depth[B_KEEP], planes, 4, rows, 3 * TILE), BF16),
            pltpu.VMEM((depth[B_SUMS], planes, 4, rows, widest), BF16),
            pltpu.VMEM((depth[B_XY], planes, rows, HEAD_COLS), BF16),
            pltpu.VMEM((depth[B_X], planes, rows, HEAD_COLS), BF16),
            pltpu.VMEM((depth[B_Y], planes, rows, HEAD_COLS), BF16),
            pltpu.VMEM((depth[B_Z], 3, rows, HEAD_COLS), BF16),
            pltpu.VMEM((depth[B_TWO_Z], 3, 4, rows, DV), BF16),
            pltpu.VMEM((depth[B_TWO], 3, rows, DV), BF16),
            pltpu.VMEM((len(Total.bits), 8, 128), F32),
            pltpu.VMEM((len(Total.bits), 8, 128), F32),
            pltpu.SemaphoreType.DMA((chunks,)),
            pltpu.SemaphoreType.DMA((chunks, Scatter.copies)),
            pltpu.SemaphoreType.DMA((chunks, Scatter.copies)),
            pltpu.SemaphoreType.DMA((len(Total.bits),)),
            pltpu.SemaphoreType.DMA((len(Total.bits),)),
        ],
        compiler_params=pltpu.CompilerParams(
            collective_id=1, has_side_effects=True, vmem_limit_bytes=63 * MIB
        ),
        name="backward",
    )(
        dwf.reshape(planes, 4, 2, rows, dwf.shape[1]), middle, nm_sum, cot, xnt, w, proj, mixed, inv, upd, core, small,
        cols, seq_rows, logs, factor, gain, x,
    )


def mixer_fwd_body(xn_ref, w_ref, taps_ref, cols_ref, rows_ref, gain_ref, proj_ref, mixed_ref, inv_ref, upd_ref, core_ref):
    head = pl.program_id(0)
    tokens = xn_ref.shape[0]
    projected = jnp.dot(xn_ref[...], w_ref[...], preferred_element_type=F32)
    proj_ref[...] = projected
    _, _, _, _, q, k, value, _, _, cum, rate, seg = head_inputs(
        projected, taps_ref[...], cols_ref[...], head
    )
    q = q * DK**-0.5
    cum_row = rows_ref[pl.ds(head, 1), :]
    seg_row = rows_ref[8:9, :]
    parts = [slice(s, s + SEQ) for s in range(0, tokens, SEQ)]
    scores, couplings = [], []
    for part in parts:
        pair = decays(seg[part], seg_row[:, part], cum[part], cum_row[:, part])
        key_dots = dot3(k[part], k[part], NT)
        scores.append(pair * dot3(q[part], k[part], NT))
        couplings.append(strict(pair * key_dots) * rate[part])
    inverses = unit_inverses(couplings)
    for i, part in enumerate(parts):
        update = dot3(inverses[i], rate[part] * value[part], NN)
        core = dot3(scores[i], update, NN)
        inv_ref[0, part, :] = inverses[i].astype(BF16)
        upd_ref[0, part, :] = update
        core_ref[0, part, :] = core
        scale = lax.rsqrt(jnp.mean(core * core, axis=1, keepdims=True) + head_epsilon)
        out_gate = projected[part, CONV_COLS:]
        mixed_ref[part, :] = (core * scale * gain_ref[...] * (out_gate * sigmoid(out_gate))).astype(BF16)


def mixer_fwd(xn, w, taps, cols, rows, gain):
    tokens, width = xn.shape
    const = lambda h: (0, 0)
    by_head = lambda h: (0, h)
    save = pl.BlockSpec((1, tokens, SEQ), lambda h: (h, 0, 0))
    return pl.pallas_call(
        mixer_fwd_body,
        grid=(HEADS,),
        in_specs=[
            pl.BlockSpec((tokens, width), const),
            pl.BlockSpec((width, HEAD_COLS), by_head),
            pl.BlockSpec((4, CONV_COLS), by_head),
            pl.BlockSpec(cols.shape, const),
            pl.BlockSpec(rows.shape, const),
            pl.BlockSpec((1, DV), const),
        ],
        out_specs=[
            pl.BlockSpec((tokens, HEAD_COLS), by_head),
            pl.BlockSpec((tokens, DV), by_head),
            save,
            save,
            save,
        ],
        out_shape=[
            jax.ShapeDtypeStruct((tokens, HEADS * HEAD_COLS), F32),
            jax.ShapeDtypeStruct((tokens, HEADS * DV), BF16),
            jax.ShapeDtypeStruct((HEADS, tokens, SEQ), BF16),
            jax.ShapeDtypeStruct((HEADS, tokens, DV), F32),
            jax.ShapeDtypeStruct((HEADS, tokens, DV), F32),
        ],
        compiler_params=pltpu.CompilerParams(vmem_limit_bytes=56 * MIB),
        name="mixer_fwd",
    )(xn, w, taps, cols, rows, gain)


def mixer_bwd_body(
    gb_ref, gbt_ref, xnt_ref, wo_ref, w_ref, proj_ref, mixed_ref, inv_ref, upd_ref, core_ref,
    taps_ref, cols_ref, rows_ref, gain_ref,
    dw_ref, dwo_ref, gxn_ref, dcols_ref, drows_ref, dtaps_ref, dgain_ref, dproj_ref,
):
    head = pl.program_id(0)
    tokens = gb_ref.shape[0]

    @pl.when(head == 0)
    def _():
        gxn_ref[...] = jnp.zeros_like(gxn_ref)
        dcols_ref[...] = jnp.zeros_like(dcols_ref)
        drows_ref[...] = jnp.zeros_like(drows_ref)
        dgain_ref[...] = jnp.zeros_like(dgain_ref)

    grad_mixed = jnp.dot(gb_ref[...], wo_ref[...], preferred_element_type=F32)
    dwo_ref[...] = jnp.dot(gbt_ref[...], mixed_ref[...], preferred_element_type=F32).astype(BF16)

    projected = proj_ref[...]
    taps = taps_ref[...]
    keep, conv, gate, act, qn, k, value, q_scale, k_scale, cum, rate, seg = head_inputs(
        projected, taps, cols_ref[...], head
    )
    q = qn * DK**-0.5
    cum_row = rows_ref[pl.ds(head, 1), :]
    seg_row = rows_ref[8:9, :]
    gain = gain_ref[...]
    lanes = lax.broadcasted_iota(jnp.int32, (SEQ, 128), 1)
    d_act, d_gain = [], jnp.zeros((1, DV), F32)
    for start in range(0, tokens, SEQ):
        part = slice(start, start + SEQ)
        core, update, inverse = core_ref[0, part, :], upd_ref[0, part, :], inv_ref[0, part, :]
        grad = grad_mixed[part]
        scale = lax.rsqrt(jnp.mean(core * core, axis=1, keepdims=True) + head_epsilon)
        normed = core * scale
        out_gate = projected[part, CONV_COLS:]
        out_sig = sigmoid(out_gate)
        swish = out_gate * out_sig
        dproj_ref[part, CONV_COLS:] = (grad * normed * gain * (out_sig + swish * (1.0 - out_sig))).astype(BF16)
        d_normed = grad * swish
        d_gain = d_gain + jnp.sum(d_normed * normed, axis=0, keepdims=True)
        d_scaled = d_normed * gain
        d_core = scale * (d_scaled - normed * jnp.mean(d_scaled * normed, axis=1, keepdims=True))

        qs, ks, vs, rs = q[part], k[part], value[part], rate[part]
        pair = decays(seg[part], seg_row[:, part], cum[part], cum_row[:, part])
        key_dots = dot3(ks, ks, NT)
        query_dots = dot3(qs, ks, NT)
        d_scores = dot3(d_core, update, NT)
        d_update = dot1(pair * query_dots, d_core, TN)
        solved = dot1(inverse, d_update, TN)
        d_coupling = strict(-dot1(solved, update, NT)) * pair
        d_query_dots = pair * d_scores
        d_key_dots = d_coupling * rs
        weighed = d_coupling * key_dots
        d_spread = d_query_dots * query_dots + weighed * rs
        d_q = dot1(d_query_dots, ks, NN) * DK**-0.5
        d_k = dot1(d_query_dots, qs, TN) + dot1(d_key_dots, ks, NN) + dot1(d_key_dots, ks, TN)
        d_rate = jnp.sum(solved * vs, axis=1, keepdims=True) + jnp.sum(weighed, axis=1, keepdims=True)
        row_sum = jnp.sum(d_spread, axis=1, keepdims=True)
        dcols_ref[part, :] += jnp.where(lanes == head, d_rate, 0.0) + jnp.where(lanes == 8 + head, row_sum, 0.0)
        drows_ref[pl.ds(head, 1), part] = jnp.sum(d_spread, axis=0, keepdims=True)
        d_q_act = q_scale[part] * (d_q - qn[part] * jnp.sum(d_q * qn[part], axis=1, keepdims=True))
        d_k_act = k_scale[part] * (d_k - ks * jnp.sum(d_k * ks, axis=1, keepdims=True))
        d_act.append(jnp.concatenate([d_q_act, d_k_act, rs * solved], axis=1))
    dgain_ref[...] += d_gain
    d_conv = jnp.concatenate(d_act, axis=0) * (gate + act * (1.0 - gate))
    source = projected[:, :CONV_COLS]
    d_source = d_conv * taps[0:1]
    d_taps = [jnp.sum(d_conv * source, axis=0, keepdims=True)]
    for back in (1, 2, 3):
        kept = d_conv * keep[back - 1]
        d_source = d_source + pltpu.roll(kept, tokens - back, 0) * taps[back : back + 1]
        d_taps.append(jnp.sum(kept * pltpu.roll(source, back, 0), axis=0, keepdims=True))
    dtaps_ref[...] = jnp.concatenate(d_taps, axis=0)
    dproj_ref[:, :CONV_COLS] = d_source.astype(BF16)
    d_proj = dproj_ref[...]
    dw_ref[...] = jnp.dot(xnt_ref[...], d_proj, preferred_element_type=F32).astype(BF16)
    gxn_ref[...] += lax.dot_general(d_proj, w_ref[...], (NT, ((), ())), preferred_element_type=F32)


def mixer_bwd(gb, gbt, xnt, wo, w, proj, mixed, inv, upd, core, taps, cols, rows, gain):
    tokens, width = gb.shape
    const = lambda h: (0, 0)
    by_head = lambda h: (0, h)
    save = pl.BlockSpec((1, tokens, SEQ), lambda h: (h, 0, 0))
    return pl.pallas_call(
        mixer_bwd_body,
        grid=(HEADS,),
        in_specs=[
            pl.BlockSpec((tokens, width), const),
            pl.BlockSpec((width, tokens), const),
            pl.BlockSpec((width, tokens), const),
            pl.BlockSpec((width, DV), by_head),
            pl.BlockSpec((width, HEAD_COLS), by_head),
            pl.BlockSpec((tokens, HEAD_COLS), by_head),
            pl.BlockSpec((tokens, DV), by_head),
            save,
            save,
            save,
            pl.BlockSpec((4, CONV_COLS), by_head),
            pl.BlockSpec(cols.shape, const),
            pl.BlockSpec(rows.shape, const),
            pl.BlockSpec((1, DV), const),
        ],
        out_specs=[
            pl.BlockSpec((width, HEAD_COLS), by_head),
            pl.BlockSpec((width, DV), by_head),
            pl.BlockSpec((tokens, width), const),
            pl.BlockSpec((tokens, 128), const),
            pl.BlockSpec((HEADS, tokens), const),
            pl.BlockSpec((4, CONV_COLS), by_head),
            pl.BlockSpec((1, DV), const),
        ],
        out_shape=[
            jax.ShapeDtypeStruct((width, HEADS * HEAD_COLS), BF16),
            jax.ShapeDtypeStruct((width, HEADS * DV), BF16),
            jax.ShapeDtypeStruct((tokens, width), F32),
            jax.ShapeDtypeStruct((tokens, 128), F32),
            jax.ShapeDtypeStruct((HEADS, tokens), F32),
            jax.ShapeDtypeStruct((4, HEADS * CONV_COLS), F32),
            jax.ShapeDtypeStruct((1, DV), F32),
        ],
        scratch_shapes=[pltpu.VMEM((tokens, HEAD_COLS), BF16)],
        compiler_params=pltpu.CompilerParams(vmem_limit_bytes=60 * MIB),
        name="mixer_bwd",
    )(gb, gbt, xnt, wo, w, proj, mixed, inv, upd, core, taps, cols, rows, gain)


def ffn_body(nm_ref, nmt_ref, cot_ref, cott_ref, w_ref, dw_ref, out_ref, gnm_ref):
    @pl.when(pl.program_id(0) == 0)
    def _():
        out_ref[...] = jnp.zeros_like(out_ref)
        gnm_ref[...] = jnp.zeros_like(gnm_ref)

    w = w_ref[...]
    gate_up = jnp.dot(nm_ref[...], w[:, : 2 * TILE], preferred_element_type=F32)
    gate, up = gate_up[:, :TILE], gate_up[:, TILE:]
    sig = sigmoid(gate)
    swish = gate * sig
    hidden = (swish * up).astype(BF16)
    grad_hidden = jnp.dot(cot_ref[...], w[:, 2 * TILE :], preferred_element_type=F32)
    grad_gate = grad_hidden * up * (sig + swish * (1.0 - sig))
    grad_up = grad_hidden * swish
    grad_low = jnp.concatenate([grad_gate, grad_up], axis=1).astype(BF16)
    out_ref[...] += lax.dot_general(hidden, w[:, 2 * TILE :], (NT, ((), ())), preferred_element_type=F32)
    gnm_ref[...] += lax.dot_general(grad_low, w[:, : 2 * TILE], (NT, ((), ())), preferred_element_type=F32)
    dw_ref[:, : 2 * TILE] = jnp.dot(nmt_ref[...], grad_low, preferred_element_type=F32).astype(BF16)
    dw_ref[:, 2 * TILE :] = jnp.dot(cott_ref[...], hidden, preferred_element_type=F32).astype(BF16)


def ffn(nm, nmt, cot, cott, w):
    tokens, width = nm.shape
    tiles = w.shape[1] // (3 * TILE)
    const = lambda t: (0, 0)
    by_tile = lambda t: (0, t)
    return pl.pallas_call(
        ffn_body,
        grid=(tiles,),
        in_specs=[
            pl.BlockSpec((tokens, width), const),
            pl.BlockSpec((width, tokens), const),
            pl.BlockSpec((tokens, width), const),
            pl.BlockSpec((width, tokens), const),
            pl.BlockSpec((width, 3 * TILE), by_tile),
        ],
        out_specs=[
            pl.BlockSpec((width, 3 * TILE), by_tile),
            pl.BlockSpec((tokens, width), const),
            pl.BlockSpec((tokens, width), const),
        ],
        out_shape=[
            jax.ShapeDtypeStruct((width, tiles * 3 * TILE), BF16),
            jax.ShapeDtypeStruct((tokens, width), F32),
            jax.ShapeDtypeStruct((tokens, width), F32),
        ],
        compiler_params=pltpu.CompilerParams(vmem_limit_bytes=48 * MIB),
        name="ffn",
    )(nm, nmt, cot, cott, w)


def rms_scale(values):
    return lax.rsqrt(jnp.mean(values * values, axis=-1, keepdims=True) + epsilon)


def rms_back(grad, values, scale, gain):
    normed = values * scale
    d_normed = grad * gain
    d_values = scale * (d_normed - normed * jnp.mean(d_normed * normed, axis=-1, keepdims=True))
    return d_values, jnp.sum(grad * normed, axis=0)


def by_head(parts):
    shaped = [p.reshape(p.shape[0], HEADS, -1) for p in parts]
    return jnp.concatenate(shaped, axis=2).reshape(parts[0].shape[0], -1)


def from_head(values, sizes):
    shaped = values.reshape(values.shape[0], HEADS, -1)
    ends = [sum(sizes[: i + 1]) for i in range(len(sizes))]
    cuts = [shaped[:, :, e - s : e].reshape(values.shape[0], -1) for s, e in zip(sizes, ends)]
    return jnp.concatenate(cuts, axis=1)


def split_heads(values):
    key = HEADS * DK
    val = HEADS * DV
    edges = [0, key, 2 * key, 2 * key + val, 2 * key + 2 * val]
    return [values[:, a:b] for a, b in zip(edges[:-1], edges[1:]) if b <= values.shape[1]]


def plain_block(
    devices, tokens, segment_ids, cotangent, norm1_gain, mixer_in, decay_in, conv_weight, decay_log, decay_bias,
    head_gain, mixer_out, norm2_gain, ffn_in, ffn_out,
):
    rows, width = decay_in.shape[0], tokens.shape[1]
    count = tokens.shape[0]
    hidden = ffn_out.shape[0]
    tiles = hidden // TILE

    low = lambda v: v.astype(BF16)
    shard_mixer = by_head(split_heads(low(mixer_in)))
    conv_cols = conv_weight.shape[1]
    shard_small = jnp.concatenate(
        [low(decay_in), low(norm1_gain)[:, None], low(norm2_gain)[:, None], low(conv_weight).reshape(rows, -1)], axis=1
    )
    shard_small = jnp.pad(shard_small, ((0, 0), (0, SMALL - shard_small.shape[1])))
    shard_out = low(mixer_out).T
    ffn_low = low(ffn_in)
    pieces = [ffn_low[:, :hidden], ffn_low[:, hidden:], low(ffn_out).T]
    shard_ffn = jnp.concatenate([p.reshape(rows, tiles, TILE) for p in pieces], axis=2).reshape(rows, -1)
    shards = [shard_small, shard_mixer, shard_out, shard_ffn]

    x = tokens.astype(F32)
    scale1 = rms_scale(x)
    full_small, full_mixer, full_out, full_ffn = [lax.all_gather(s, "dp", axis=0, tiled=True) for s in shards]

    decay_full = full_small[:, :16]
    gain1 = full_small[:, 16].astype(F32)
    gain2 = full_small[:, 17].astype(F32)
    taps = full_small[:, 18 : 18 + 16].reshape(devices, 4, conv_cols)
    taps = jnp.moveaxis(taps, 0, 1).reshape(4, -1).astype(F32)
    taps = by_head(split_heads(taps))

    normed_in = low(x * scale1 * gain1)
    logits = jnp.dot(normed_in, decay_full, preferred_element_type=F32)
    shifted = logits[:, :HEADS] + decay_bias
    log_decay = -jnp.exp(decay_log) * jax.nn.softplus(shifted)
    rate = jax.nn.sigmoid(logits[:, HEADS:])
    sequences = count // SEQ
    lower = jnp.tril(jnp.ones((SEQ, SEQ), F32))
    cumulative = jnp.einsum(
        "ij,sjh->sih", lower, log_decay.reshape(sequences, SEQ, HEADS), precision=lax.Precision.HIGHEST
    ).reshape(count, HEADS)
    position = jnp.arange(count) % SEQ
    keeps = []
    for back in (1, 2, 3):
        earlier = jnp.pad(segment_ids[:-back], (back, 0), constant_values=-1)
        keeps.append(((earlier == segment_ids) & (position >= back)).astype(F32)[:, None])
    segment = segment_ids.astype(F32)
    cols = jnp.concatenate([cumulative, rate] + keeps + [segment[:, None]], axis=1)
    cols = jnp.pad(cols, ((0, 0), (0, 128 - cols.shape[1])))
    seq_rows = jnp.concatenate([cumulative.T, segment[None], jnp.zeros((7, count), F32)], axis=0)
    gain_row = head_gain[None]

    proj, mixed, inverse, update, core = mixer_fwd(normed_in, full_mixer, taps, cols, seq_rows, gain_row)

    middle = x + lax.dot_general(mixed, full_out, (NT, ((), ())), preferred_element_type=F32)
    scale2 = rms_scale(middle)
    normed_mid = low(middle * scale2 * gain2)
    dw_ffn, ffn_sum, grad_nm = ffn(normed_mid, normed_mid.T, cotangent, cotangent.T, full_ffn)
    output = low(middle + ffn_sum)

    d_middle, d_gain2 = rms_back(grad_nm, middle, scale2, gain2)
    grad_middle = d_middle + cotangent.astype(F32)
    branch = low(grad_middle)
    dw_mixer, dw_out, grad_xn, d_cols, d_rows, d_taps, d_gain = mixer_bwd(
        branch, branch.T, normed_in.T, full_out, full_mixer, proj, mixed, inverse, update, core,
        taps, cols, seq_rows, gain_row,
    )

    d_cum = d_cols[:, 8:16] - d_rows.T
    d_decay = jnp.einsum(
        "ji,sjh->sih", lower, d_cum.reshape(sequences, SEQ, HEADS), precision=lax.Precision.HIGHEST
    ).reshape(count, HEADS)
    d_shifted = -d_decay * jnp.exp(decay_log) * jax.nn.sigmoid(shifted)
    d_rate = d_cols[:, :8] * rate * (1.0 - rate)
    d_logits = low(jnp.concatenate([d_shifted, d_rate], axis=1))
    grad_xn = grad_xn + lax.dot_general(d_logits, decay_full, (NT, ((), ())), preferred_element_type=F32)
    d_x, d_gain1 = rms_back(grad_xn, x, scale1, gain1)
    input_grad = d_x + grad_middle

    d_decay_in = lax.dot_general(normed_in, d_logits, (TN, ((), ())), preferred_element_type=F32)
    d_taps = from_head(d_taps, [DK, DK, DV])
    d_taps = jnp.moveaxis(d_taps.reshape(4, devices, conv_cols), 1, 0).reshape(width, -1)
    dw_small = jnp.concatenate([d_decay_in, d_gain1[:, None], d_gain2[:, None], d_taps], axis=1)
    dw_small = low(jnp.pad(dw_small, ((0, 0), (0, SMALL - dw_small.shape[1]))))
    shared = jnp.concatenate([jnp.sum(d_decay * log_decay, axis=0), jnp.sum(d_shifted, axis=0), d_gain[0]])

    own_ffn, own_out, own_mixer, own_small = [
        lax.psum_scatter(g.astype(F32), "dp", scatter_dimension=0, tiled=True)
        for g in (dw_ffn, dw_out, dw_mixer, dw_small)
    ]
    shared = lax.psum(shared, "dp")

    own_tiles = own_ffn.reshape(rows, tiles, 3, TILE)
    ffn_in_grad = jnp.concatenate([own_tiles[:, :, i].reshape(rows, hidden) for i in (0, 1)], axis=1)
    ffn_out_grad = own_tiles[:, :, 2].reshape(rows, hidden).T
    return (
        output,
        input_grad,
        own_small[:, 16],
        from_head(own_mixer, [DK, DK, DV, DV]),
        own_small[:, :16],
        own_small[:, 18 : 18 + 16].reshape(4, conv_cols),
        shared[:HEADS],
        shared[HEADS : 2 * HEADS],
        shared[2 * HEADS : 2 * HEADS + DV],
        own_out.T,
        own_small[:, 17],
        ffn_in_grad,
        ffn_out_grad,
    )


def direct_block(
    devices, tokens, segment_ids, cotangent, norm1_gain, mixer_in, decay_in, conv_weight, decay_log, decay_bias,
    head_gain, mixer_out, norm2_gain, ffn_in, ffn_out,
):
    rows = decay_in.shape[0]
    count = tokens.shape[0]
    hidden = ffn_out.shape[0]
    tiles = hidden // TILE
    planes = devices // 8
    low = lambda v: v.astype(BF16)
    pad = lambda v, lanes: jnp.pad(v, ((0, 0), (0, lanes - v.shape[1])))

    first = pad(jnp.concatenate([low(decay_in), low(norm1_gain)[:, None], low(norm2_gain)[:, None]], axis=1), SMALL)
    second = jnp.pad(low(conv_weight), ((0, rows - 4), (0, 0)))
    shard_small = jnp.concatenate([first, second], axis=1)
    shard_heads = by_head(split_heads(low(mixer_in)) + [low(mixer_out).T])
    ffn_low = low(ffn_in)
    pieces = [ffn_low[:, :hidden], ffn_low[:, hidden:], low(ffn_out).T]
    shard_tiles = jnp.concatenate([p.reshape(rows, tiles, TILE) for p in pieces], axis=2).reshape(rows, -1)

    position = jnp.arange(count) % SEQ
    keeps = [jnp.zeros((count, 16), F32)]
    for back in (1, 2, 3):
        earlier = jnp.pad(segment_ids[:-back], (back, 0), constant_values=-1)
        keeps.append(((earlier == segment_ids) & (position >= back)).astype(F32)[:, None])
    segment = segment_ids.astype(F32)
    aux = pad(jnp.concatenate(keeps + [segment[:, None]], axis=1), 128)
    seg_rows = jnp.broadcast_to(segment[None], (8, count))
    lines = jnp.stack([-jnp.exp(decay_log), decay_bias])
    consts = jnp.pad(lines, ((0, 6), (0, 128 - HEADS)))
    gain = head_gain[None]

    (
        _, full_heads, _, small, xnt, cols, seq_rows, logs, factor, proj, mixed, inverse, update, core, dwf,
        output, middle, nm_sum,
    ) = forward(planes, [shard_small, shard_heads, shard_tiles], tokens, cotangent, aux, seg_rows, consts, gain)
    input_grad, own_mixer, own_out, own_ffn, own_down, own_small, shared = backward(
        planes, dwf, middle, nm_sum, cotangent, xnt, full_heads, proj, mixed, inverse, update, core, small, cols,
        seq_rows, logs, factor, gain, tokens,
    )
    return (
        output,
        input_grad,
        own_small[:, 16],
        own_mixer,
        own_small[:, :16],
        own_small[:4, SMALL:],
        shared[0, :HEADS],
        shared[1, :HEADS],
        shared[2:4].reshape(-1),
        own_out.T,
        own_small[:, 17],
        own_ffn,
        own_down.T,
    )


def on_device(devices, *arguments):
    rows, conv_cols = arguments[4].shape[0], arguments[6].shape[1]
    direct = rows % 16 == 0 and devices == 32 and conv_cols == 128
    return (direct_block if direct else plain_block)(devices, *arguments)


def solution(mesh):
    in_specs = (
        P("dp", None), P("dp"), P("dp", None), P("dp"), P("dp", None), P("dp", None), P(None, "dp"), P(), P(), P(),
        P(None, "dp"), P("dp"), P("dp", None), P(None, "dp"),
    )
    out_specs = (
        P("dp", None), P("dp", None), P("dp"), P("dp", None), P("dp", None), P(None, "dp"), P(), P(), P(),
        P(None, "dp"), P("dp"), P("dp", None), P(None, "dp"),
    )
    return jax.shard_map(
        partial(on_device, mesh.shape["dp"]), mesh=mesh, in_specs=in_specs, out_specs=out_specs, check_vma=False
    )
```

```python
from functools import partial

import jax
import jax.numpy as jnp
from jax import lax
from jax.experimental import pallas as pl
from jax.experimental.pallas import tpu as pltpu
from jax.sharding import PartitionSpec as P

HEADS = 8
DK = 128
DV = 256
SEQ = 256
HEAD_COLS = 2 * DK + 2 * DV
CONV_COLS = 2 * DK + DV
TILE = 256
SMALL = 128
F32 = jnp.float32
BF16 = jnp.bfloat16
MESH = pl.DeviceIdType.MESH
MIB = 1 << 20
epsilon = 1e-06
head_epsilon = 0.001

NN = ((1,), (0,))
NT = ((1,), (1,))
TN = ((0,), (0,))


def dot1(left, right, dims):
    return lax.dot_general(
        left.astype(BF16), right.astype(BF16), (dims, ((), ())), preferred_element_type=F32
    )


def split(value):
    high = value.astype(BF16)
    return high, (value - high.astype(F32)).astype(BF16)


def dot3(left, right, dims):
    lh, ll = split(left)
    rh, rl = split(right)
    return dot1(lh, rh, dims) + (dot1(lh, rl, dims) + dot1(ll, rh, dims))


def sigmoid(value):
    return 1.0 / (1.0 + jnp.exp(-value))


def grid_of(size):
    rows = lax.broadcasted_iota(jnp.int32, (size, size), 0)
    cols = lax.broadcasted_iota(jnp.int32, (size, size), 1)
    return rows, cols


def unit_inverses(couplings):
    half = couplings[0].shape[0] // 2
    rows, cols = grid_of(half)
    apart = rows ^ cols
    eye = jnp.where(apart == 0, 1.0, 0.0)
    corners = [a[s : s + half, s : s + half] for a in couplings for s in (0, half)]
    lows = [a.astype(BF16) for a in corners]
    inverses = [eye - jnp.where(apart < 2, a, 0.0) for a in corners]
    rounded = [inv.astype(BF16) for inv in inverses]
    block = 2
    while block < half:
        here = jnp.where((apart >= block) & (apart < 2 * block), 1.0, 0.0).astype(BF16)
        firsts = [dot1(low * here, inv, NN) for low, inv in zip(lows, rounded)]
        added = [dot1(inv, first, NN) for inv, first in zip(rounded, firsts)]
        inverses = [inv - new for inv, new in zip(inverses, added)]
        rounded = [inv - new.astype(BF16) for inv, new in zip(rounded, added)]
        block *= 2
    results = []
    for i, a in enumerate(couplings):
        first, second = inverses[2 * i], inverses[2 * i + 1]
        below = -dot1(rounded[2 * i + 1], dot1(a[half:, :half], rounded[2 * i], NN), NN)
        top = jnp.concatenate([first, jnp.zeros_like(first)], axis=1)
        results.append(jnp.concatenate([top, jnp.concatenate([below, second], axis=1)], axis=0))
    return results


def pick_lane(columns, lane):
    at = lax.broadcasted_iota(jnp.int32, columns.shape, 1)
    return jnp.sum(jnp.where(at == lane, columns, 0.0), axis=1, keepdims=True)


def conv_of(values, taps, keep):
    total = values * taps[0:1]
    for back in (1, 2, 3):
        total = total + pltpu.roll(values, back, 0) * keep[back - 1] * taps[back : back + 1]
    return total


def decays(seg_col, seg_row, cum_col, cum_row):
    rows, cols = grid_of(SEQ)
    linked = (seg_col == seg_row) & (rows >= cols)
    return jnp.where(linked, jnp.exp(jnp.where(linked, cum_col - cum_row, 0.0)), 0.0)


def strict(value):
    rows, cols = grid_of(SEQ)
    return jnp.where(rows > cols, value, 0.0)


def head_inputs(projected, taps, cols, head):
    keep = [pick_lane(cols, 16 + i) for i in range(3)]
    conv = conv_of(projected[:, :CONV_COLS], taps, keep)
    gate = sigmoid(conv)
    act = conv * gate
    q_act, k_act, value = act[:, :DK], act[:, DK : 2 * DK], act[:, 2 * DK :]
    q_scale = lax.rsqrt(jnp.sum(q_act * q_act, axis=1, keepdims=True) + epsilon)
    k_scale = lax.rsqrt(jnp.sum(k_act * k_act, axis=1, keepdims=True) + epsilon)
    cum = pick_lane(cols, head)
    rate = pick_lane(cols, 8 + head)
    seg = pick_lane(cols, 19)
    return keep, conv, gate, act, q_act * q_scale, k_act * k_scale, value, q_scale, k_scale, cum, rate, seg


def flip(number, bit):
    return number + bit - 2 * bit * ((number // bit) % 2)


def enter(me, before=lambda: None):
    barrier = pltpu.get_barrier_semaphore()
    partners = [flip(me, bit) for bit in (1, 2, 4, 8, 16)]
    for other in partners:
        pl.semaphore_signal(barrier, inc=1, device_id=(other,), device_id_type=MESH)
    before()
    pl.semaphore_wait(barrier, len(partners))


def span(k, width, start, size):
    first = k * width + start
    return pl.ds(first if isinstance(first, int) else pl.multiple_of(first, 128), size)


def remote(source, target, send_sem, recv_sem, other):
    return pltpu.make_async_remote_copy(
        src_ref=source, dst_ref=target, send_sem=send_sem, recv_sem=recv_sem,
        device_id=(other,), device_id_type=MESH,
    )


(
    G_NEAR, G_FAR, G_RELAY, G_X, G_Y, G_CORNER_Y, G_CORNER_X, G_CORE_OWN,
    G_CORE_OTHER, G_TWO_X, G_TWO_Y, G_TWO_CORNER, G_TWO_NEAR, G_TWO_FAR, G_TWO_RELAY, G_TWO_CORE,
) = range(16)
(
    S_CORE, S_XY_X, S_XY_Y, S_X_EARLY, S_X_LATE, S_Y_EARLY, S_Y_LATE, S_RELAY,
    S_NEAR, S_FAR, S_TWO_RELAY, S_TWO_NEAR, S_TWO_FAR, S_TWO_XY, S_TWO_X, S_TWO_Y,
) = range(16)
B_CORE, B_KEEP, B_SUMS, B_XY, B_X, B_Y, B_Z, B_TWO_Z, B_TWO = range(9)
HEAD, FFN_TILE, SMALLS = range(3)


SHAPES = {
    HEAD: (HEAD_COLS + DV, HEAD_COLS, HEAD_COLS // 2),
    FFN_TILE: (3 * TILE, 5 * TILE // 2, 3 * TILE // 2),
    SMALLS: (2 * SMALL, 2 * SMALL, SMALL),
}


class Gather:
    copies = 16

    def __init__(self, me, kinds, local_sem, send_sem, recv_sem):
        self.me, self.kinds = me, kinds
        self.local_sem, self.send_sem, self.recv_sem = local_sem, send_sem, recv_sem
        self.z, self.y, self.x, self.core = me // 8, (me // 4) % 2, (me // 2) % 2, me % 2

    def local(self, kind, k):
        shard, full, base = self.kinds[kind]
        width = SHAPES[kind][0]
        cols = span(k, width, 0, width)
        return pltpu.make_async_copy(
            shard.at[:, cols], full.at[self.z, self.y, self.x, self.core, :, cols], self.local_sem.at[base + k]
        )

    def copy(self, kind, k, name):
        shard, full, base = self.kinds[kind]
        width, part, half = SHAPES[kind]
        one = span(k, width, 0, part)
        two = span(k, width, part, width - part)
        z, y, x, core = self.z, self.y, self.x, self.core
        near, far = flip(z, 1), flip(z, 2)
        here = lambda cols: (shard.at[:, cols], full.at[z, y, x, core, :, cols])
        same = lambda ref: (ref, ref)
        by_y = kind == FFN_TILE
        (source, target), bit = {
            G_NEAR: lambda: (here(one), 8),
            G_FAR: lambda: (here(one), 16),
            G_RELAY: lambda: (same(full.at[far, y, x, core, :, one]), 8),
            G_X: lambda: (same(full.at[:, y, x, core, :, one]), 2),
            G_Y: lambda: (same(full.at[:, y, x, core, :, one]), 4),
            G_CORNER_Y: lambda: (same(full.at[:, y, 1 - x, core, :, span(k, width, 0, half)]), 4),
            G_CORNER_X: lambda: (same(full.at[:, 1 - y, x, core, :, span(k, width, half, part - half)]), 2),
            G_CORE_OWN: lambda: (same(full.at[:, y, :, core, :, one]), 1),
            G_CORE_OTHER: lambda: (same(full.at[:, 1 - y, :, core, :, one]), 1),
            G_TWO_X: lambda: (here(two), 2),
            G_TWO_Y: lambda: (here(two), 4),
            G_TWO_CORNER: lambda: (
                (same(full.at[z, 1 - y, x, core, :, two]), 2)
                if by_y
                else (same(full.at[z, y, 1 - x, core, :, two]), 4)
            ),
            G_TWO_NEAR: lambda: (same(full.at[z, :, :, core, :, two]), 8),
            G_TWO_FAR: lambda: (same(full.at[z, :, :, core, :, two]), 16),
            G_TWO_RELAY: lambda: (same(full.at[far, :, :, core, :, two]), 8),
            G_TWO_CORE: lambda: (same(full.at[:, :, :, core, :, two]), 1),
        }[name]()
        sems = self.send_sem.at[base + k, name], self.recv_sem.at[base + k, name]
        return remote(source, target, *sems, flip(self.me, bit))

    def send(self, kind, k, *names):
        for name in names:
            self.copy(kind, k, name).start()

    def wait(self, kind, k, *names):
        for name in names:
            self.copy(kind, k, name).wait_recv()

    def two(self, kind):
        return SHAPES[kind][0] > SHAPES[kind][1]

    def start(self, kind, k):
        self.local(kind, k).start()
        self.send(kind, k, G_FAR, G_NEAR)
        if self.two(kind):
            self.send(kind, k, G_TWO_X, G_TWO_Y)

    def relay(self, kind, k):
        self.wait(kind, k, G_FAR)
        self.send(kind, k, G_RELAY)
        if self.two(kind):
            self.wait(kind, k, *((G_TWO_Y,) if kind == FFN_TILE else (G_TWO_X,)))
            self.send(kind, k, G_TWO_CORNER)

    def square(self, kind, k):
        self.local(kind, k).wait()
        self.wait(kind, k, G_NEAR, G_RELAY)
        self.send(kind, k, G_X, G_Y)
        if self.two(kind):
            self.wait(kind, k, *((G_TWO_X,) if kind == FFN_TILE else (G_TWO_Y,)), G_TWO_CORNER)
            self.send(kind, k, G_TWO_FAR, G_TWO_NEAR)

    def corner(self, kind, k):
        self.wait(kind, k, G_X)
        self.send(kind, k, G_CORNER_Y, G_CORE_OWN)
        self.wait(kind, k, G_Y)
        self.send(kind, k, G_CORNER_X)
        if self.two(kind):
            self.wait(kind, k, G_TWO_FAR)
            self.send(kind, k, G_TWO_RELAY)

    def across(self, kind, k):
        self.wait(kind, k, G_CORNER_Y, G_CORNER_X)
        self.send(kind, k, G_CORE_OTHER)
        if self.two(kind):
            self.wait(kind, k, G_TWO_NEAR, G_TWO_RELAY)
            self.send(kind, k, G_TWO_CORE)

    def complete(self, kind, k):
        self.wait(kind, k, G_CORE_OWN, G_CORE_OTHER)
        if self.two(kind):
            self.wait(kind, k, G_TWO_CORE)

    def finish(self, kind, k):
        names = [G_NEAR, G_FAR, G_RELAY, G_X, G_Y, G_CORNER_Y, G_CORNER_X, G_CORE_OWN, G_CORE_OTHER]
        if self.two(kind):
            names += [G_TWO_X, G_TWO_Y, G_TWO_CORNER, G_TWO_NEAR, G_TWO_FAR, G_TWO_RELAY, G_TWO_CORE]
        for name in names:
            self.copy(kind, k, name).wait_send()


class Scatter:
    copies = 16
    depths = {B_CORE: 4, B_KEEP: 2, B_SUMS: 6, B_XY: 4, B_X: 8, B_Y: 8, B_Z: 4, B_TWO_Z: 8, B_TWO: 4}

    def __init__(self, me, kinds, store, core, keep, sums, xy, x, y, z, two_z, two, local_sem, send_sem, recv_sem):
        self.me, self.kinds, self.store = me, kinds, store
        self.from_core, self.keep, self.sums = core, keep, sums
        self.from_xy, self.from_x, self.from_y, self.from_z = xy, x, y, z
        self.two_z, self.from_two = two_z, two
        self.local_sem, self.send_sem, self.recv_sem = local_sem, send_sem, recv_sem
        self.z, self.core = me // 8, me % 2
        self.here = (me // 2) % 4
        self.across_x, self.across_y = flip(self.here, 1), flip(self.here, 2)
        self.both = 3 - self.here
        self.near, self.far = flip(self.z, 1), flip(self.z, 2)
        self.opposite = 3 - self.z

    def slot(self, name, r):
        return r % self.depths[name]

    def copy(self, kind, r, k, name):
        source = self.kinds[kind][0]
        width, part, half = SHAPES[kind]
        whole, one, two = pl.ds(0, width), pl.ds(0, part), pl.ds(part, width - part)
        first, second = pl.ds(0, half), pl.ds(half, part - half)
        rest = pl.ds(0, width - part)
        sums = self.sums.at[self.slot(B_SUMS, r)]
        here, across_x, across_y, both, z = self.here, self.across_x, self.across_y, self.both, self.z
        by_y = kind == FFN_TILE
        place = lambda where, cols: sums.at[:, where, :, cols]
        origin, target, bit = {
            S_CORE: lambda: (
                source(k, 1 - self.core), self.from_core.at[self.slot(B_CORE, r), :, :, :, whole], 1
            ),
            S_XY_X: lambda: (place(both, first), self.from_xy.at[self.slot(B_XY, r), :, :, first], 2),
            S_XY_Y: lambda: (place(both, second), self.from_xy.at[self.slot(B_XY, r), :, :, second], 4),
            S_X_EARLY: lambda: (place(across_x, first), self.from_x.at[self.slot(B_X, r), :, :, first], 2),
            S_X_LATE: lambda: (place(across_x, second), self.from_x.at[self.slot(B_X, r), :, :, second], 2),
            S_Y_EARLY: lambda: (place(across_y, second), self.from_y.at[self.slot(B_Y, r), :, :, second], 4),
            S_Y_LATE: lambda: (place(across_y, first), self.from_y.at[self.slot(B_Y, r), :, :, first], 4),
            S_RELAY: lambda: (sums.at[self.opposite, here, :, one], self.from_z.at[self.slot(B_Z, r), 0, :, one], 8),
            S_NEAR: lambda: (sums.at[self.near, here, :, one], self.from_z.at[self.slot(B_Z, r), 1, :, one], 8),
            S_FAR: lambda: (sums.at[self.far, here, :, one], self.from_z.at[self.slot(B_Z, r), 2, :, one], 16),
            S_TWO_RELAY: lambda: (
                sums.at[self.opposite, :, :, two], self.two_z.at[self.slot(B_TWO_Z, r), 0, :, :, rest], 8
            ),
            S_TWO_NEAR: lambda: (
                sums.at[self.near, :, :, two], self.two_z.at[self.slot(B_TWO_Z, r), 1, :, :, rest], 8
            ),
            S_TWO_FAR: lambda: (
                sums.at[self.far, :, :, two], self.two_z.at[self.slot(B_TWO_Z, r), 2, :, :, rest], 16
            ),
            S_TWO_XY: lambda: (
                sums.at[z, both, :, two], self.from_two.at[self.slot(B_TWO, r), 0, :, rest], 4 if by_y else 2
            ),
            S_TWO_X: lambda: (sums.at[z, across_x, :, two], self.from_two.at[self.slot(B_TWO, r), 1, :, rest], 2),
            S_TWO_Y: lambda: (sums.at[z, across_y, :, two], self.from_two.at[self.slot(B_TWO, r), 2, :, rest], 4),
        }[name]()
        sems = self.send_sem.at[r, name], self.recv_sem.at[r, name]
        return remote(origin, target, *sems, flip(self.me, bit))

    def send(self, kind, r, k, *names):
        for name in names:
            self.copy(kind, r, k, name).start()

    def wait(self, kind, r, k, *names):
        for name in names:
            self.copy(kind, r, k, name).wait_recv()

    def two(self, kind):
        return SHAPES[kind][0] > SHAPES[kind][1]

    def load(self, kind, r, k):
        source = self.kinds[kind][0]
        return pltpu.make_async_copy(
            source(k, self.core), self.keep.at[r % 2, :, :, :, pl.ds(0, SHAPES[kind][0])], self.local_sem.at[r]
        )

    def core_step(self, kind, r, k):
        self.send(kind, r, k, S_CORE)

    def load_step(self, kind, r, k):
        if self.kinds[kind][1] is None:
            self.load(kind, r, k).start()

    def add_planes(self, r, place, cols, first, others):
        def one(plane, carry):
            total = first(plane).astype(F32)
            for read in others:
                total = total + read(plane).astype(F32)
            self.sums[self.slot(B_SUMS, r), plane, place, :, cols] = total.astype(BF16)
            return carry

        lax.fori_loop(0, 4, one, 0)

    def add_places(self, r, plane, cols, others):
        slot = self.slot(B_SUMS, r)
        for place in range(4):
            total = self.sums[slot, plane, place, :, cols].astype(F32)
            for read in others:
                total = total + read(place).astype(F32)
            self.sums[slot, plane, place, :, cols] = total.astype(BF16)

    def held(self, r, place, cols):
        return lambda plane: self.sums[self.slot(B_SUMS, r), plane, place, :, cols]

    def chip_step(self, kind, r, k):
        in_place = self.kinds[kind][1]
        width, part, half = SHAPES[kind]
        whole = pl.ds(0, width)
        self.wait(kind, r, k, S_CORE)
        if in_place is None:
            self.load(kind, r, k).wait()
            mine = lambda place: (lambda plane: self.keep[r % 2, plane, place, :, whole])
        else:
            mine = lambda place: (lambda plane: in_place(k, plane, place, self.core))
        got = lambda place: (lambda plane: self.from_core[self.slot(B_CORE, r), plane, place, :, whole])
        for place, names in (
            (self.both, (S_XY_X, S_XY_Y)),
            (self.across_x, (S_X_EARLY,)),
            (self.across_y, (S_Y_EARLY,)),
            (self.here, (S_TWO_RELAY, S_TWO_NEAR) if self.two(kind) else ()),
        ):
            self.add_planes(r, place, whole, got(place), [mine(place)])
            self.send(kind, r, k, *names)
        self.copy(kind, r, k, S_CORE).wait_send()

    def corner_step(self, kind, r, k):
        width, part, half = SHAPES[kind]
        first, second = pl.ds(0, half), pl.ds(half, part - half)
        passed = lambda cols: (lambda plane: self.from_xy[self.slot(B_XY, r), plane, :, cols])
        self.wait(kind, r, k, S_XY_X)
        self.add_planes(r, self.across_y, first, self.held(r, self.across_y, first), [passed(first)])
        self.send(kind, r, k, S_Y_LATE)
        self.wait(kind, r, k, S_XY_Y)
        self.add_planes(r, self.across_x, second, self.held(r, self.across_x, second), [passed(second)])
        self.send(kind, r, k, S_X_LATE)
        if self.two(kind):
            two, rest = pl.ds(part, width - part), pl.ds(0, width - part)
            self.wait(kind, r, k, S_TWO_RELAY)
            self.add_places(r, self.far, two, [lambda place: self.two_z[self.slot(B_TWO_Z, r), 0, place, :, rest]])
            self.send(kind, r, k, S_TWO_FAR)

    def square_step(self, kind, r, k):
        width, part, half = SHAPES[kind]
        one = pl.ds(0, part)
        self.wait(kind, r, k, S_X_EARLY, S_X_LATE, S_Y_EARLY, S_Y_LATE)
        from_x = lambda plane: self.from_x[self.slot(B_X, r), plane, :, one]
        from_y = lambda plane: self.from_y[self.slot(B_Y, r), plane, :, one]
        self.add_planes(r, self.here, one, self.held(r, self.here, one), [from_x, from_y])
        self.send(kind, r, k, S_RELAY, S_NEAR)
        if self.two(kind):
            two, rest = pl.ds(part, width - part), pl.ds(0, width - part)
            self.wait(kind, r, k, S_TWO_NEAR, S_TWO_FAR)
            self.add_places(
                r, self.z, two,
                [lambda place, i=i: self.two_z[self.slot(B_TWO_Z, r), i, place, :, rest] for i in (1, 2)],
            )
            self.send(kind, r, k, S_TWO_XY, S_TWO_X if kind != FFN_TILE else S_TWO_Y)

    def relay_step(self, kind, r, k):
        width, part, half = SHAPES[kind]
        slot, one = self.slot(B_SUMS, r), pl.ds(0, part)
        self.wait(kind, r, k, S_RELAY)
        total = self.sums[slot, self.far, self.here, :, one].astype(F32)
        total = total + self.from_z[self.slot(B_Z, r), 0, :, one].astype(F32)
        self.sums[slot, self.far, self.here, :, one] = total.astype(BF16)
        self.send(kind, r, k, S_FAR)
        if self.two(kind):
            two, rest = pl.ds(part, width - part), pl.ds(0, width - part)
            place = self.across_x if kind == FFN_TILE else self.across_y
            self.wait(kind, r, k, S_TWO_XY)
            total = self.sums[slot, self.z, place, :, two].astype(F32)
            total = total + self.from_two[self.slot(B_TWO, r), 0, :, rest].astype(F32)
            self.sums[slot, self.z, place, :, two] = total.astype(BF16)
            self.send(kind, r, k, S_TWO_X if kind == FFN_TILE else S_TWO_Y)

    def last_step(self, kind, r, k):
        width, part, half = SHAPES[kind]
        slot, one = self.slot(B_SUMS, r), pl.ds(0, part)
        self.wait(kind, r, k, S_NEAR, S_FAR)
        total = self.sums[slot, self.z, self.here, :, one].astype(F32)
        for i in (1, 2):
            total = total + self.from_z[self.slot(B_Z, r), i, :, one].astype(F32)
        names = [S_XY_X, S_XY_Y, S_X_EARLY, S_X_LATE, S_Y_EARLY, S_Y_LATE, S_RELAY, S_NEAR, S_FAR]
        if self.two(kind):
            two, rest = pl.ds(part, width - part), pl.ds(0, width - part)
            self.wait(kind, r, k, S_TWO_X, S_TWO_Y)
            more = self.sums[slot, self.z, self.here, :, two].astype(F32)
            for i in (1, 2):
                more = more + self.from_two[self.slot(B_TWO, r), i, :, rest].astype(F32)
            total = jnp.concatenate([total, more], axis=1)
            names += [S_TWO_RELAY, S_TWO_NEAR, S_TWO_FAR, S_TWO_XY, S_TWO_X, S_TWO_Y]
        self.store(kind, k, total)
        for name in names:
            self.copy(kind, r, k, name).wait_send()


class Total:
    bits = (1, 2, 4, 8, 16)

    def __init__(self, me, value_ref, store, got, stage, send_sem, recv_sem):
        self.me, self.value_ref, self.store = me, value_ref, store
        self.got, self.stage, self.send_sem, self.recv_sem = got, stage, send_sem, recv_sem

    def copy(self, number):
        sems = self.send_sem.at[number], self.recv_sem.at[number]
        return remote(self.stage.at[number], self.got.at[number], *sems, flip(self.me, self.bits[number]))

    def step(self, number):
        last = len(self.bits)
        value = self.value_ref[...]
        if number > 0:
            self.copy(number - 1).wait_recv()
            value = self.stage[number - 1] + self.got[number - 1]
        if number < last:
            self.stage[number] = value
            self.copy(number).start()
        else:
            self.store(value)
            for number in range(last):
                self.copy(number).wait_send()


def triangle_sum(values, dims):
    rows, cols = grid_of(SEQ)
    ones = jnp.where(rows >= cols, 1.0, 0.0).astype(BF16)
    first, rest = values.astype(BF16), values - values.astype(BF16).astype(F32)
    second, third = split(rest)
    return dot1(ones, first, dims) + (dot1(ones, second, dims) + dot1(ones, third, dims))


def log1p(value):
    series = value * (1.0 - value * (0.5 - value * (1.0 / 3.0 - value * (0.25 - value * 0.2))))
    return jnp.where(value < 0.01, series, jnp.log(1.0 + value))


def softplus(value):
    return jnp.maximum(value, 0.0) + log1p(jnp.exp(-jnp.abs(value)))


def merge(block):
    return block.reshape(-1, block.shape[-1])


def head_taps(small_ref, head):
    wide = 2 * head
    places = [(0, head), (1, head)] + [(2 + head // 4, wide % 8 + i) for i in (0, 1)]
    blocks = [
        small_ref[z, p // 4, (p // 2) % 2, p % 2, 0:16, SMALL : 2 * SMALL][0:4].astype(F32) for z, p in places
    ]
    return jnp.concatenate(blocks, axis=1)


def row_blocks(count, body, size=128):
    def one(i, carry):
        body(pl.ds(pl.multiple_of(i * size, size), size))
        return carry

    lax.fori_loop(0, count // size, one, 0)


def lane_index(shape):
    return lax.broadcasted_iota(jnp.int32, shape, 1)


def forward_body(
    planes, tiles,
    mixer_in_ref, mixer_out_ref, ffn_in_ref, ffn_out_ref, decay_in_ref, gain1_ref, gain2_ref, conv_ref,
    x_ref, cot_ref, seg_ref, log_ref, bias_ref, gain_ref,
    full_small, full_heads, full_tiles, small_ref, xnt_ref, cols_ref, rows_ref, logs_ref, factor_ref,
    proj_ref, mixed_ref, inv_ref, upd_ref, core_ref, dw_ref,
    output_ref, middle, nm_sum,
    shard_small, shard_heads, shard_tiles, turn, consts_ref,
    w_buf, xn, cott, nm, nmt, out_sum, gains, copy_sem, w_sem, local_sem, send_sem, recv_sem,
):
    step = pl.program_id(0)
    tokens = x_ref.shape[0]
    chunks = HEADS + tiles
    me = lax.axis_index("dp")
    kinds = {
        SMALLS: (shard_small, full_small, chunks),
        HEAD: (shard_heads, full_heads, 0),
        FFN_TILE: (shard_tiles, full_tiles, HEADS),
    }
    work = Gather(me, kinds, local_sem, send_sem, recv_sem)

    def at(chunk, act):
        pl.when((chunk >= 0) & (chunk < HEADS))(lambda: act(HEAD, chunk))
        pl.when((chunk >= HEADS) & (chunk < chunks))(lambda: act(FFN_TILE, chunk - HEADS))

    def weights(kind, k, slot, plane=None):
        full, width = kinds[kind][1], SHAPES[kind][0]
        source = full.at[:, :, :, :, :, span(k, width, 0, width)]
        place = w_buf.at[slot, :, :, :, :, :, pl.ds(0, width)]
        if plane is not None:
            source, place = source.at[plane], place.at[plane]
        return pltpu.make_async_copy(source, place, w_sem.at[slot])

    def load_weights(kind, k, slot):
        for plane in range(planes):
            weights(kind, k, slot, plane).start()

    ahead = ((6, work.start), (5, work.relay), (4, work.square), (2, work.corner), (1, work.across))

    def early(step):
        for lead, act in ahead:
            if step + lead >= 0:
                act(HEAD, step + lead)

    def midway():
        for lead, act in ahead[:3]:
            at(step + lead, act)
        at(step + 1, work.complete)
        at(step + 1, lambda kind, k: load_weights(kind, k, (step + 1) % 2))

    def pack_heads():
        turn[...] = jnp.zeros_like(turn)
        turn[0:16, 0 : conv_ref.shape[1] // 4] = decay_in_ref[...]
        turn[16:17, 0 : conv_ref.shape[1] // 4] = gain1_ref[...]
        turn[17:18, 0 : conv_ref.shape[1] // 4] = gain2_ref[...]
        rows = shard_small.shape[0]
        shard_small[:, 0:SMALL] = turn[...].T[0:rows].astype(BF16)
        taps = jnp.concatenate([conv_ref[...], jnp.zeros((rows - 4, SMALL), F32)], axis=0)
        shard_small[:, SMALL:] = taps.astype(BF16)
        for h in range(HEADS):
            at_col = h * (HEAD_COLS + DV)
            key, val = HEADS * DK, HEADS * DV
            for ref, start, size in (
                (mixer_in_ref, h * DK, DK),
                (mixer_in_ref, key + h * DK, DK),
                (mixer_in_ref, 2 * key + h * DV, DV),
                (mixer_in_ref, 2 * key + val + h * DV, DV),
                (mixer_out_ref, h * DV, DV),
            ):
                shard_heads[:, at_col : at_col + size] = ref[:, start : start + size].astype(BF16)
                at_col += size

    def pack_tiles():
        for t in range(tiles):
            at_col = t * 3 * TILE
            for ref, start in ((ffn_in_ref, t * TILE), (ffn_in_ref, (tiles + t) * TILE), (ffn_out_ref, t * TILE)):
                shard_tiles[:, at_col : at_col + TILE] = ref[:, start : start + TILE].astype(BF16)
                at_col += TILE

    @pl.when(step == 0)
    def _():
        enter(me, pack_heads)
        work.start(SMALLS, 0)
        early(-6)
        pack_tiles()
        consts_ref[...] = jnp.zeros_like(consts_ref)
        consts_ref[0:1, 0:HEADS] = -jnp.exp(log_ref[...])
        consts_ref[1:2, 0:HEADS] = bias_ref[...]

        def prepare(rows):
            middle[rows, :] = x_ref[rows, :].astype(F32)
            cott[:, rows] = cot_ref[rows, :].astype(F32).T.astype(BF16)

        row_blocks(tokens, prepare)
        work.relay(SMALLS, 0)
        early(-5)
        work.square(SMALLS, 0)
        early(-4)
        work.corner(SMALLS, 0)
        early(-3)
        work.across(SMALLS, 0)
        out_sum[...] = jnp.zeros_like(out_sum)
        nm_sum[...] = jnp.zeros_like(nm_sum)
        work.complete(SMALLS, 0)
        early(-2)
        copy = pltpu.make_async_copy(full_small, small_ref, copy_sem)
        copy.start()
        copy.wait()
        small = merge(small_ref[..., 0:SMALL])
        turned = small.astype(F32).T
        gains[0:1, :] = turned[16:17, :]
        gains[1:2, :] = turned[17:18, :]

        def norm(rows):
            x = middle[rows, :]
            scale = lax.rsqrt(jnp.mean(x * x, axis=1, keepdims=True) + epsilon)
            normed = x * scale * gains[0:1, :]
            xn[rows, :] = normed.astype(BF16)
            xnt_ref[:, rows] = normed.T.astype(BF16)

        row_blocks(tokens, norm)
        logits = jnp.dot(xn[...], small, preferred_element_type=F32)
        lanes = lane_index(logits.shape)
        decay_scale, bias = consts_ref[0:1, :], consts_ref[1:2, :]
        shifted = logits + bias
        rate = sigmoid(logits)
        log_decay = decay_scale * softplus(shifted)
        logs_ref[...] = log_decay
        factor_ref[...] = jnp.where(
            lanes < 8, decay_scale * sigmoid(shifted), jnp.where(lanes < 16, rate * (1.0 - rate), 0.0)
        )
        seg_row = jnp.broadcast_to(seg_ref[...].astype(F32), (128, tokens))
        segment = seg_row.T
        rows_ref[8:16, :] = seg_row[0:8]
        inside = lax.broadcasted_iota(jnp.int32, segment.shape, 0) % SEQ
        aux = segment
        for back in (1, 2, 3):
            linked = (pltpu.roll(segment, back, 0) == segment) & (inside >= back)
            aux = jnp.where(lanes == 15 + back, jnp.where(linked, 1.0, 0.0), aux)
        for start in range(0, tokens, SEQ):
            part = slice(start, start + SEQ)
            cum = triangle_sum(log_decay[part], NN)
            cols_ref[part, :] = jnp.where(lanes[part] < 8, cum, jnp.where(lanes[part] < 16, rate[part], aux[part]))
            rows_ref[0:8, part] = cum.T[0:8]
        early(-1)
        work.finish(SMALLS, 0)
        work.complete(HEAD, 0)
        load_weights(HEAD, 0, 0)

    for lead, act in ahead[3:]:
        at(step + lead, act)
    at(step, lambda kind, k: weights(kind, k, step % 2).wait())
    at(step - 1, work.finish)

    @pl.when(step < HEADS)
    def _():
        w = merge(w_buf[step % 2])
        projected = jnp.dot(xn[...], w[:, :HEAD_COLS], preferred_element_type=F32)
        proj_ref[...] = projected
        midway()
        _, _, _, _, q, k, value, _, _, cum, rate, seg = head_inputs(
            projected, head_taps(small_ref, step), cols_ref[...], step
        )
        q = q * DK**-0.5
        cum_row = rows_ref[pl.ds(step, 1), :]
        seg_row = rows_ref[8:9, :]
        parts = [slice(s, s + SEQ) for s in range(0, tokens, SEQ)]
        scores, couplings = [], []
        for part in parts:
            pair = decays(seg[part], seg_row[:, part], cum[part], cum_row[:, part])
            key_dots = dot3(k[part], k[part], NT)
            scores.append(pair * dot3(q[part], k[part], NT))
            couplings.append(strict(pair * key_dots) * rate[part])
        inverses = unit_inverses(couplings)
        for i, part in enumerate(parts):
            update = dot3(inverses[i], rate[part] * value[part], NN)
            core = dot3(scores[i], update, NN)
            inv_ref[0, part, :] = inverses[i].astype(BF16)
            upd_ref[0, part, :] = update
            core_ref[0, part, :] = core
            scale = lax.rsqrt(jnp.mean(core * core, axis=1, keepdims=True) + head_epsilon)
            out_gate = projected[part, CONV_COLS:]
            mixed_ref[part, :] = (core * scale * gain_ref[...] * (out_gate * sigmoid(out_gate))).astype(BF16)
        middle[...] += lax.dot_general(mixed_ref[...], w[:, HEAD_COLS:], (NT, ((), ())), preferred_element_type=F32)

    @pl.when(step == HEADS)
    def _():
        def norm(rows):
            mid = middle[rows, :]
            scale = lax.rsqrt(jnp.mean(mid * mid, axis=1, keepdims=True) + epsilon)
            normed = mid * scale * gains[1:2, :]
            nm[rows, :] = normed.astype(BF16)
            nmt[:, rows] = normed.T.astype(BF16)

        row_blocks(tokens, norm)

    @pl.when(step >= HEADS)
    def _():
        w = merge(w_buf[step % 2, :, :, :, :, :, 0 : 3 * TILE])
        gate_up = jnp.dot(nm[...], w[:, : 2 * TILE], preferred_element_type=F32)
        gate, up = gate_up[:, :TILE], gate_up[:, TILE:]
        sig = sigmoid(gate)
        swish = gate * sig
        hidden = (swish * up).astype(BF16)
        midway()
        grad_hidden = jnp.dot(cot_ref[...], w[:, 2 * TILE :], preferred_element_type=F32)
        grad_gate = grad_hidden * up * (sig + swish * (1.0 - sig))
        grad_up = grad_hidden * swish
        grad_low = jnp.concatenate([grad_gate, grad_up], axis=1).astype(BF16)
        out_sum[...] += lax.dot_general(hidden, w[:, 2 * TILE :], (NT, ((), ())), preferred_element_type=F32)
        nm_sum[...] += lax.dot_general(grad_low, w[:, : 2 * TILE], (NT, ((), ())), preferred_element_type=F32)
        dw_ref[:, : 2 * TILE] = jnp.dot(nmt[...], grad_low, preferred_element_type=F32).astype(BF16)
        dw_ref[:, 2 * TILE :] = jnp.dot(cott[...], hidden, preferred_element_type=F32).astype(BF16)

    @pl.when(step == chunks - 1)
    def _():
        def add(rows):
            output_ref[rows, :] = (middle[rows, :] + out_sum[rows, :]).astype(BF16)

        row_blocks(tokens, add)
        work.finish(FFN_TILE, tiles - 1)


def once(shape):
    return pl.BlockSpec(shape, lambda i: (0,) * len(shape), pipeline_mode=pl.Buffered(1))


def forward(planes, masters, x, cot, *others):
    rows, tokens, width = masters[0].shape[0], *x.shape
    tiles = masters[3].shape[1] // TILE
    chunks = HEADS + tiles
    widths = (2 * SMALL, HEADS * (HEAD_COLS + DV), tiles * 3 * TILE)
    hbm = pl.BlockSpec(memory_space=pl.ANY)
    head = lambda i: jnp.minimum(i, HEADS - 1)
    tile = lambda i: jnp.maximum(i - HEADS, 0)
    save = pl.BlockSpec((1, tokens, SEQ), lambda i: (head(i), 0, 0))
    shape = jax.ShapeDtypeStruct
    whole = [((planes, 2, 2, 2, rows, w), BF16) for w in widths]
    outs = [
        (hbm, *whole[0]),
        (hbm, *whole[1]),
        (hbm, *whole[2]),
        (once(whole[0][0]), *whole[0]),
        (once((width, tokens)), (width, tokens), BF16),
        (once((tokens, 128)), (tokens, 128), F32),
        (once((16, tokens)), (16, tokens), F32),
        (once((tokens, 128)), (tokens, 128), F32),
        (once((tokens, 128)), (tokens, 128), F32),
        (pl.BlockSpec((tokens, HEAD_COLS), lambda i: (0, head(i))), (tokens, HEADS * HEAD_COLS), F32),
        (pl.BlockSpec((tokens, DV), lambda i: (0, head(i))), (tokens, HEADS * DV), BF16),
        (save, (HEADS, tokens, SEQ), BF16),
        (save, (HEADS, tokens, DV), F32),
        (save, (HEADS, tokens, DV), F32),
        (pl.BlockSpec((width, 3 * TILE), lambda i: (0, tile(i))), (width, tiles * 3 * TILE), BF16),
        (once((tokens, width)), (tokens, width), BF16),
        (once((tokens, width)), (tokens, width), F32),
        (once((tokens, width)), (tokens, width), F32),
    ]
    return pl.pallas_call(
        partial(forward_body, planes, tiles),
        grid=(chunks,),
        in_specs=[once(a.shape) for a in (*masters, x, cot, *others)],
        out_specs=[o[0] for o in outs],
        out_shape=[shape(o[1], o[2]) for o in outs],
        scratch_shapes=[pltpu.VMEM((rows, w), BF16) for w in widths]
        + [
            pltpu.VMEM((128, 128), F32),
            pltpu.VMEM((8, 128), F32),
            pltpu.VMEM((2, planes, 2, 2, 2, rows, HEAD_COLS + DV), BF16),
            pltpu.VMEM((tokens, width), BF16),
            pltpu.VMEM((width, tokens), BF16),
            pltpu.VMEM((tokens, width), BF16),
            pltpu.VMEM((width, tokens), BF16),
            pltpu.VMEM((tokens, width), F32),
            pltpu.VMEM((8, width), F32),
            pltpu.SemaphoreType.DMA,
            pltpu.SemaphoreType.DMA((2,)),
            pltpu.SemaphoreType.DMA((chunks + 1,)),
            pltpu.SemaphoreType.DMA((chunks + 1, Gather.copies)),
            pltpu.SemaphoreType.DMA((chunks + 1, Gather.copies)),
        ],
        compiler_params=pltpu.CompilerParams(
            collective_id=0, has_side_effects=True, vmem_limit_bytes=60 * MIB
        ),
        name="forward",
    )(*masters, x, cot, *others)


FIRST = 4


def row_sums(count, body, width, size=128):
    def one(i, total):
        return body(pl.ds(pl.multiple_of(i * size, size), size), total)

    return lax.fori_loop(0, count // size, one, jnp.zeros((1, width), F32))


def head_step(j):
    return jnp.minimum(j // 2, HEADS - 1)


def backward_body(
    planes, tiles, total_chunks,
    dwf_ref, middle_ref, nm_sum_ref, cot_ref, xnt_ref, w_ref, proj_ref, mixed_ref, inv_ref, upd_ref, core_ref,
    small_ref, cols_ref, rows_ref, logs_ref, factor_ref, gain_ref, x_ref,
    input_grad_ref, own_gain1, own_mixer, own_decay, own_conv, own_log, own_bias, own_gain, own_out, own_gain2, own_ffn,
    own_down, gb_ref, gbt_ref, grad_mid_ref, gains, dw, d_small, gxn, dcols, drows, dgain, dproj, value_ref,
    *scratch,
):
    *buffers, got, stage, local_sem, send_sem, recv_sem, total_send, total_recv = scratch
    step = pl.program_id(0)
    tokens = middle_ref.shape[0]
    rows = own_mixer.shape[0]
    hidden = tiles * TILE
    me = lax.axis_index("dp")

    def tile_source(k, core):
        return dwf_ref.at[:, :, core, :, span(k, 3 * TILE, 0, 3 * TILE)]

    kinds = {
        FFN_TILE: (tile_source, None),
        HEAD: (
            lambda k, core: dw.at[k % 2, :, :, core],
            lambda k, plane, place, core: dw[k % 2, plane, place, core],
        ),
        SMALLS: (
            lambda k, core: d_small.at[:, :, core],
            lambda k, plane, place, core: d_small[plane, place, core],
        ),
    }

    def store(kind, k, total):
        def put(ref, start, source, width):
            ref[:, pl.ds(pl.multiple_of(start, 128), width)] = total[:, source : source + width]

        if kind == SMALLS:
            turned = jnp.concatenate([total[:, :SMALL], jnp.zeros((SMALL - rows, SMALL), F32)], axis=0).T
            own_decay[...] = turned[0:16, 0:rows]
            own_gain1[...] = turned[16:17, 0:rows]
            own_gain2[...] = turned[17:18, 0:rows]
            own_conv[...] = total[0:4, SMALL:]
        elif kind == HEAD:
            put(own_mixer, k * DK, 0, DK)
            put(own_mixer, HEADS * DK + k * DK, DK, DK)
            put(own_mixer, 2 * HEADS * DK + k * DV, 2 * DK, DV)
            put(own_mixer, 2 * HEADS * DK + HEADS * DV + k * DV, 2 * DK + DV, DV)
            put(own_out, k * DV, HEAD_COLS, DV)
        else:
            put(own_ffn, k * TILE, 0, TILE)
            put(own_ffn, hidden + k * TILE, TILE, TILE)
            put(own_down, k * TILE, 2 * TILE, TILE)

    work = Scatter(me, kinds, store, *buffers, local_sem, send_sem, recv_sem)
    def share(value):
        own_log[...] = value[0:1, 0:HEADS]
        own_bias[...] = value[1:2, 0:HEADS]
        own_gain[...] = jnp.concatenate([value[2:3], value[3:4]], axis=1)

    small_sum = Total(me, value_ref, share, got, stage, total_send, total_recv)

    last = total_chunks - 1

    def at(r, act):
        is_head = (r >= FIRST) & (r < last) & ((r - FIRST) % 2 == 0)
        is_early = (r >= 0) & (r < FIRST)
        is_tile = (r > FIRST) & (r < last) & ((r - FIRST) % 2 == 1)
        pl.when(is_early)(lambda: act(FFN_TILE, r, r))
        pl.when(is_tile)(lambda: act(FFN_TILE, r, (r + FIRST - 1) // 2))
        pl.when(is_head)(lambda: act(HEAD, r, (r - FIRST) // 2))
        pl.when(r == last)(lambda: act(SMALLS, r, 0))

    @pl.when(step == 0)
    def _():
        enter(me)
        work.core_step(FFN_TILE, 0, 0)
        work.core_step(FFN_TILE, 1, 1)
        work.load_step(FFN_TILE, 0, 0)
        gxn[...] = jnp.zeros_like(gxn)
        dcols[...] = jnp.zeros_like(dcols)
        drows[...] = jnp.zeros_like(drows)
        dgain[...] = jnp.zeros_like(dgain)
        d_small[...] = jnp.zeros_like(d_small)
        for r in (0, 1):
            work.chip_step(FFN_TILE, r, r)
            work.core_step(FFN_TILE, r + 2, r + 2)
            work.load_step(FFN_TILE, r + 1, r + 1)

    at(step - 4, work.last_step)
    at(step - 3, work.relay_step)
    at(step - 2, work.square_step)
    at(step, work.corner_step)
    at(step + 2, work.chip_step)
    at(step + 3, work.load_step)

    @pl.when(step == 0)
    def _():
        turned = merge(small_ref[..., 0:SMALL]).astype(F32).T
        gains[0:1, :] = turned[16:17, :]
        gains[1:2, :] = turned[17:18, :]

        def back(rows, total):
            mid = middle_ref[rows, :]
            scale = lax.rsqrt(jnp.mean(mid * mid, axis=1, keepdims=True) + epsilon)
            normed = mid * scale
            grad = nm_sum_ref[rows, :]
            d_normed = grad * gains[1:2, :]
            d_mid = scale * (d_normed - normed * jnp.mean(d_normed * normed, axis=1, keepdims=True))
            d_mid = d_mid + cot_ref[rows, :].astype(F32)
            grad_mid_ref[rows, :] = d_mid
            gb_ref[rows, :] = d_mid.astype(BF16)
            gbt_ref[:, rows] = d_mid.T.astype(BF16)
            return total + jnp.sum(grad * normed, axis=0, keepdims=True)

        gains[2:3, :] = row_sums(tokens, back, gains.shape[1])

    @pl.when((step < 2 * HEADS) & (step % 2 == 0))
    def _():
        head = step // 2
        w = merge(w_ref[...])
        grad_mixed = jnp.dot(gb_ref[...], w[:, HEAD_COLS:], preferred_element_type=F32)
        d_out = jnp.dot(gbt_ref[...], mixed_ref[...], preferred_element_type=F32).astype(BF16)
        dw[head % 2, :, :, :, :, pl.ds(HEAD_COLS, DV)] = d_out.reshape(dw.shape[1:5] + (DV,))

        projected = proj_ref[...]
        taps = head_taps(small_ref, head)
        keeps, conv, gate, act, qn, k, value, q_scale, k_scale, cum, rate, seg = head_inputs(
            projected, taps, cols_ref[...], head
        )
        q = qn * DK**-0.5
        cum_row = rows_ref[pl.ds(head, 1), :]
        seg_row = rows_ref[8:9, :]
        gain = gain_ref[...]
        lanes = lane_index((SEQ, 128))
        d_act, d_gain = [], jnp.zeros((1, DV), F32)
        for start in range(0, tokens, SEQ):
            part = slice(start, start + SEQ)
            core, update, inverse = core_ref[0, part, :], upd_ref[0, part, :], inv_ref[0, part, :]
            grad = grad_mixed[part]
            scale = lax.rsqrt(jnp.mean(core * core, axis=1, keepdims=True) + head_epsilon)
            normed = core * scale
            out_gate = projected[part, CONV_COLS:]
            out_sig = sigmoid(out_gate)
            swish = out_gate * out_sig
            dproj[part, CONV_COLS:] = (grad * normed * gain * (out_sig + swish * (1.0 - out_sig))).astype(BF16)
            d_normed = grad * swish
            d_gain = d_gain + jnp.sum(d_normed * normed, axis=0, keepdims=True)
            d_scaled = d_normed * gain
            d_core = scale * (d_scaled - normed * jnp.mean(d_scaled * normed, axis=1, keepdims=True))

            qs, ks, vs, rs = q[part], k[part], value[part], rate[part]
            pair = decays(seg[part], seg_row[:, part], cum[part], cum_row[:, part])
            key_dots = dot3(ks, ks, NT)
            query_dots = dot3(qs, ks, NT)
            d_scores = dot3(d_core, update, NT)
            d_update = dot1(pair * query_dots, d_core, TN)
            solved = dot1(inverse, d_update, TN)
            d_coupling = strict(-dot1(solved, update, NT)) * pair
            d_query_dots = pair * d_scores
            d_key_dots = d_coupling * rs
            weighed = d_coupling * key_dots
            d_spread = d_query_dots * query_dots + weighed * rs
            d_q = dot1(d_query_dots, ks, NN) * DK**-0.5
            d_k = dot1(d_query_dots, qs, TN) + dot1(d_key_dots, ks, NN) + dot1(d_key_dots, ks, TN)
            d_rate = jnp.sum(solved * vs, axis=1, keepdims=True) + jnp.sum(weighed, axis=1, keepdims=True)
            row_sum = jnp.sum(d_spread, axis=1, keepdims=True)
            dcols[part, :] += jnp.where(lanes == head, row_sum, 0.0) + jnp.where(lanes == 8 + head, d_rate, 0.0)
            drows[pl.ds(head, 1), part] = jnp.sum(d_spread, axis=0, keepdims=True)
            d_q_act = q_scale[part] * (d_q - qn[part] * jnp.sum(d_q * qn[part], axis=1, keepdims=True))
            d_k_act = k_scale[part] * (d_k - ks * jnp.sum(d_k * ks, axis=1, keepdims=True))
            d_act.append(jnp.concatenate([d_q_act, d_k_act, rs * solved], axis=1))
        dgain[0:1, :] += d_gain
        d_conv = jnp.concatenate(d_act, axis=0) * (gate + act * (1.0 - gate))
        source = projected[:, :CONV_COLS]
        d_source = d_conv * taps[0:1]
        d_taps = [jnp.sum(d_conv * source, axis=0, keepdims=True)]
        for back in (1, 2, 3):
            kept = d_conv * keeps[back - 1]
            d_source = d_source + pltpu.roll(kept, tokens - back, 0) * taps[back : back + 1]
            d_taps.append(jnp.sum(kept * pltpu.roll(source, back, 0), axis=0, keepdims=True))
        d_taps = jnp.concatenate(d_taps + [jnp.zeros((rows - 4, CONV_COLS), F32)], axis=0).astype(BF16)
        wide = 2 * head
        places = [(0, head), (1, head)] + [(2 + head // 4, wide % 8 + i) for i in (0, 1)]
        for i, (z, p) in enumerate(places):
            d_small[z, p // 2, p % 2, :, SMALL:] = d_taps[:, i * SMALL : (i + 1) * SMALL]
        dproj[:, :CONV_COLS] = d_source.astype(BF16)
        d_proj = dproj[...]
        d_in = jnp.dot(xnt_ref[...], d_proj, preferred_element_type=F32).astype(BF16)
        dw[head % 2, :, :, :, :, pl.ds(0, HEAD_COLS)] = d_in.reshape(dw.shape[1:5] + (HEAD_COLS,))
        gxn[...] += lax.dot_general(d_proj, w[:, :HEAD_COLS], (NT, ((), ())), preferred_element_type=F32)

    @pl.when(step == 2 * HEADS - 1)
    def _():
        small = merge(small_ref[..., 0:SMALL])
        lanes = lane_index((SEQ, 128))
        padded = jnp.concatenate([drows[...], jnp.zeros((120, tokens), F32)], axis=0).T
        d_logs = jnp.zeros((1, 128), F32)
        d_bias = jnp.zeros((1, 128), F32)
        d_logits = []
        for start in range(0, tokens, SEQ):
            part = slice(start, start + SEQ)
            d_cum = jnp.where(lanes < 8, dcols[part, :], 0.0) - padded[part]
            d_decay = triangle_sum(d_cum, TN)
            d_logit = jnp.where(lanes < 8, d_decay, dcols[part, :]) * factor_ref[part, :]
            d_logs = d_logs + jnp.sum(jnp.where(lanes < 8, d_decay * logs_ref[part, :], 0.0), axis=0, keepdims=True)
            d_bias = d_bias + jnp.sum(jnp.where(lanes < 8, d_logit, 0.0), axis=0, keepdims=True)
            d_logits.append(d_logit.astype(BF16))
        d_logits = jnp.concatenate(d_logits, axis=0)
        value_ref[...] = jnp.concatenate(
            [d_logs, d_bias, dgain[0:1, :128], dgain[0:1, 128:], jnp.zeros((4, 128), F32)], axis=0
        )
        gxn[...] += lax.dot_general(d_logits, small, (NT, ((), ())), preferred_element_type=F32)

        def back(at_rows, total):
            x = x_ref[at_rows, :].astype(F32)
            scale = lax.rsqrt(jnp.mean(x * x, axis=1, keepdims=True) + epsilon)
            normed = x * scale
            grad = gxn[at_rows, :]
            d_normed = grad * gains[0:1, :]
            d_x = scale * (d_normed - normed * jnp.mean(d_normed * normed, axis=1, keepdims=True))
            input_grad_ref[at_rows, :] = d_x + grad_mid_ref[at_rows, :]
            return total + jnp.sum(grad * normed, axis=0, keepdims=True)

        total = row_sums(tokens, back, gxn.shape[1])
        line = lax.broadcasted_iota(jnp.int32, (128, total.shape[1]), 0)
        lines = jnp.where(line == 16, total, jnp.where(line == 17, gains[2:3, :], 0.0))
        own = jnp.dot(xnt_ref[...], d_logits, preferred_element_type=F32) + lines.T
        d_small[:, :, :, :, 0:SMALL] = own.astype(BF16).reshape(d_small.shape[:4] + (SMALL,))

    at(step + 4, work.core_step)
    for number in range(len(Total.bits) + 1):
        pl.when(step == 2 * HEADS + number)(lambda number=number: small_sum.step(number))


def backward(planes, dwf, middle, nm_sum, cot, xnt, w, proj, mixed, inv, upd, core, small, cols, seq_rows, logs, factor,
             gain, x):
    tokens, width = middle.shape
    rows = small.shape[4]
    tiles = dwf.shape[1] // (3 * TILE)
    chunks = FIRST + 2 * HEADS
    assert tiles == FIRST + HEADS - 1
    hbm = pl.BlockSpec(memory_space=pl.ANY)
    head = head_step
    save = pl.BlockSpec((1, tokens, SEQ), lambda i: (head(i), 0, 0))
    shape = jax.ShapeDtypeStruct
    widest = HEAD_COLS + DV
    depth = Scatter.depths
    outs = [
        ((tokens, width), F32),
        ((1, rows), F32),
        ((rows, HEADS * HEAD_COLS), F32),
        ((16, rows), F32),
        ((4, SMALL), F32),
        ((1, HEADS), F32),
        ((1, HEADS), F32),
        ((1, DV), F32),
        ((rows, HEADS * DV), F32),
        ((1, rows), F32),
        ((rows, 2 * tiles * TILE), F32),
        ((rows, tiles * TILE), F32),
    ]
    return pl.pallas_call(
        partial(backward_body, planes, tiles, chunks),
        grid=(chunks + 4,),
        in_specs=[
            hbm,
            once((tokens, width)),
            once((tokens, width)),
            once((tokens, width)),
            once((width, tokens)),
            pl.BlockSpec((planes, 2, 2, 2, rows, widest), lambda i: (0, 0, 0, 0, 0, head(i))),
            pl.BlockSpec((tokens, HEAD_COLS), lambda i: (0, head(i))),
            pl.BlockSpec((tokens, DV), lambda i: (0, head(i))),
            save,
            save,
            save,
        ]
        + [once(a.shape) for a in (small, cols, seq_rows, logs, factor, gain, x)],
        out_specs=[once(o[0]) for o in outs],
        out_shape=[shape(*o) for o in outs],
        scratch_shapes=[
            pltpu.VMEM((tokens, width), BF16),
            pltpu.VMEM((width, tokens), BF16),
            pltpu.VMEM((tokens, width), F32),
            pltpu.VMEM((8, width), F32),
            pltpu.VMEM((2, planes, 4, 2, rows, widest), BF16),
            pltpu.VMEM((planes, 4, 2, rows, 2 * SMALL), BF16),
            pltpu.VMEM((tokens, width), F32),
            pltpu.VMEM((tokens, 128), F32),
            pltpu.VMEM((HEADS, tokens), F32),
            pltpu.VMEM((8, DV), F32),
            pltpu.VMEM((tokens, HEAD_COLS), BF16),
            pltpu.VMEM((8, 128), F32),
            pltpu.VMEM((depth[B_CORE], planes, 4, rows, widest), BF16),
            pltpu.VMEM((depth[B_KEEP], planes, 4, rows, 3 * TILE), BF16),
            pltpu.VMEM((depth[B_SUMS], planes, 4, rows, widest), BF16),
            pltpu.VMEM((depth[B_XY], planes, rows, HEAD_COLS), BF16),
            pltpu.VMEM((depth[B_X], planes, rows, HEAD_COLS), BF16),
            pltpu.VMEM((depth[B_Y], planes, rows, HEAD_COLS), BF16),
            pltpu.VMEM((depth[B_Z], 3, rows, HEAD_COLS), BF16),
            pltpu.VMEM((depth[B_TWO_Z], 3, 4, rows, DV), BF16),
            pltpu.VMEM((depth[B_TWO], 3, rows, DV), BF16),
            pltpu.VMEM((len(Total.bits), 8, 128), F32),
            pltpu.VMEM((len(Total.bits), 8, 128), F32),
            pltpu.SemaphoreType.DMA((chunks,)),
            pltpu.SemaphoreType.DMA((chunks, Scatter.copies)),
            pltpu.SemaphoreType.DMA((chunks, Scatter.copies)),
            pltpu.SemaphoreType.DMA((len(Total.bits),)),
            pltpu.SemaphoreType.DMA((len(Total.bits),)),
        ],
        compiler_params=pltpu.CompilerParams(
            collective_id=1, has_side_effects=True, vmem_limit_bytes=63 * MIB
        ),
        name="backward",
    )(
        dwf.reshape(planes, 4, 2, rows, dwf.shape[1]), middle, nm_sum, cot, xnt, w, proj, mixed, inv, upd, core, small,
        cols, seq_rows, logs, factor, gain, x,
    )


def hand_over_body(count, *refs):
    for source, target in zip(refs[:count], refs[count:]):
        target[...] = source[...]


def hand_over(arrays, steps=4):
    specs = []
    for a in arrays:
        rows, cols = a.shape
        if rows % (32 * steps) == 0:
            specs.append(pl.BlockSpec((rows // steps, cols), lambda i: (i, 0)))
        elif cols % (128 * steps) == 0:
            specs.append(pl.BlockSpec((rows, cols // steps), lambda i: (0, i)))
        else:
            specs.append(pl.BlockSpec((rows, cols), lambda i: (0, 0)))
    return pl.pallas_call(
        partial(hand_over_body, len(arrays)),
        grid=(steps,),
        in_specs=specs,
        out_specs=specs,
        out_shape=[jax.ShapeDtypeStruct(a.shape, a.dtype) for a in arrays],
        compiler_params=pltpu.CompilerParams(vmem_limit_bytes=60 * MIB),
        name="hand_over",
    )(*arrays)


def mixer_fwd_body(xn_ref, w_ref, taps_ref, cols_ref, rows_ref, gain_ref, proj_ref, mixed_ref, inv_ref, upd_ref, core_ref):
    head = pl.program_id(0)
    tokens = xn_ref.shape[0]
    projected = jnp.dot(xn_ref[...], w_ref[...], preferred_element_type=F32)
    proj_ref[...] = projected
    _, _, _, _, q, k, value, _, _, cum, rate, seg = head_inputs(
        projected, taps_ref[...], cols_ref[...], head
    )
    q = q * DK**-0.5
    cum_row = rows_ref[pl.ds(head, 1), :]
    seg_row = rows_ref[8:9, :]
    parts = [slice(s, s + SEQ) for s in range(0, tokens, SEQ)]
    scores, couplings = [], []
    for part in parts:
        pair = decays(seg[part], seg_row[:, part], cum[part], cum_row[:, part])
        key_dots = dot3(k[part], k[part], NT)
        scores.append(pair * dot3(q[part], k[part], NT))
        couplings.append(strict(pair * key_dots) * rate[part])
    inverses = unit_inverses(couplings)
    for i, part in enumerate(parts):
        update = dot3(inverses[i], rate[part] * value[part], NN)
        core = dot3(scores[i], update, NN)
        inv_ref[0, part, :] = inverses[i].astype(BF16)
        upd_ref[0, part, :] = update
        core_ref[0, part, :] = core
        scale = lax.rsqrt(jnp.mean(core * core, axis=1, keepdims=True) + head_epsilon)
        out_gate = projected[part, CONV_COLS:]
        mixed_ref[part, :] = (core * scale * gain_ref[...] * (out_gate * sigmoid(out_gate))).astype(BF16)


def mixer_fwd(xn, w, taps, cols, rows, gain):
    tokens, width = xn.shape
    const = lambda h: (0, 0)
    by_head = lambda h: (0, h)
    save = pl.BlockSpec((1, tokens, SEQ), lambda h: (h, 0, 0))
    return pl.pallas_call(
        mixer_fwd_body,
        grid=(HEADS,),
        in_specs=[
            pl.BlockSpec((tokens, width), const),
            pl.BlockSpec((width, HEAD_COLS), by_head),
            pl.BlockSpec((4, CONV_COLS), by_head),
            pl.BlockSpec(cols.shape, const),
            pl.BlockSpec(rows.shape, const),
            pl.BlockSpec((1, DV), const),
        ],
        out_specs=[
            pl.BlockSpec((tokens, HEAD_COLS), by_head),
            pl.BlockSpec((tokens, DV), by_head),
            save,
            save,
            save,
        ],
        out_shape=[
            jax.ShapeDtypeStruct((tokens, HEADS * HEAD_COLS), F32),
            jax.ShapeDtypeStruct((tokens, HEADS * DV), BF16),
            jax.ShapeDtypeStruct((HEADS, tokens, SEQ), BF16),
            jax.ShapeDtypeStruct((HEADS, tokens, DV), F32),
            jax.ShapeDtypeStruct((HEADS, tokens, DV), F32),
        ],
        compiler_params=pltpu.CompilerParams(vmem_limit_bytes=56 * MIB),
        name="mixer_fwd",
    )(xn, w, taps, cols, rows, gain)


def mixer_bwd_body(
    gb_ref, gbt_ref, xnt_ref, wo_ref, w_ref, proj_ref, mixed_ref, inv_ref, upd_ref, core_ref,
    taps_ref, cols_ref, rows_ref, gain_ref,
    dw_ref, dwo_ref, gxn_ref, dcols_ref, drows_ref, dtaps_ref, dgain_ref, dproj_ref,
):
    head = pl.program_id(0)
    tokens = gb_ref.shape[0]

    @pl.when(head == 0)
    def _():
        gxn_ref[...] = jnp.zeros_like(gxn_ref)
        dcols_ref[...] = jnp.zeros_like(dcols_ref)
        drows_ref[...] = jnp.zeros_like(drows_ref)
        dgain_ref[...] = jnp.zeros_like(dgain_ref)

    grad_mixed = jnp.dot(gb_ref[...], wo_ref[...], preferred_element_type=F32)
    dwo_ref[...] = jnp.dot(gbt_ref[...], mixed_ref[...], preferred_element_type=F32).astype(BF16)

    projected = proj_ref[...]
    taps = taps_ref[...]
    keep, conv, gate, act, qn, k, value, q_scale, k_scale, cum, rate, seg = head_inputs(
        projected, taps, cols_ref[...], head
    )
    q = qn * DK**-0.5
    cum_row = rows_ref[pl.ds(head, 1), :]
    seg_row = rows_ref[8:9, :]
    gain = gain_ref[...]
    lanes = lax.broadcasted_iota(jnp.int32, (SEQ, 128), 1)
    d_act, d_gain = [], jnp.zeros((1, DV), F32)
    for start in range(0, tokens, SEQ):
        part = slice(start, start + SEQ)
        core, update, inverse = core_ref[0, part, :], upd_ref[0, part, :], inv_ref[0, part, :]
        grad = grad_mixed[part]
        scale = lax.rsqrt(jnp.mean(core * core, axis=1, keepdims=True) + head_epsilon)
        normed = core * scale
        out_gate = projected[part, CONV_COLS:]
        out_sig = sigmoid(out_gate)
        swish = out_gate * out_sig
        dproj_ref[part, CONV_COLS:] = (grad * normed * gain * (out_sig + swish * (1.0 - out_sig))).astype(BF16)
        d_normed = grad * swish
        d_gain = d_gain + jnp.sum(d_normed * normed, axis=0, keepdims=True)
        d_scaled = d_normed * gain
        d_core = scale * (d_scaled - normed * jnp.mean(d_scaled * normed, axis=1, keepdims=True))

        qs, ks, vs, rs = q[part], k[part], value[part], rate[part]
        pair = decays(seg[part], seg_row[:, part], cum[part], cum_row[:, part])
        key_dots = dot3(ks, ks, NT)
        query_dots = dot3(qs, ks, NT)
        d_scores = dot3(d_core, update, NT)
        d_update = dot1(pair * query_dots, d_core, TN)
        solved = dot1(inverse, d_update, TN)
        d_coupling = strict(-dot1(solved, update, NT)) * pair
        d_query_dots = pair * d_scores
        d_key_dots = d_coupling * rs
        weighed = d_coupling * key_dots
        d_spread = d_query_dots * query_dots + weighed * rs
        d_q = dot1(d_query_dots, ks, NN) * DK**-0.5
        d_k = dot1(d_query_dots, qs, TN) + dot1(d_key_dots, ks, NN) + dot1(d_key_dots, ks, TN)
        d_rate = jnp.sum(solved * vs, axis=1, keepdims=True) + jnp.sum(weighed, axis=1, keepdims=True)
        row_sum = jnp.sum(d_spread, axis=1, keepdims=True)
        dcols_ref[part, :] += jnp.where(lanes == head, d_rate, 0.0) + jnp.where(lanes == 8 + head, row_sum, 0.0)
        drows_ref[pl.ds(head, 1), part] = jnp.sum(d_spread, axis=0, keepdims=True)
        d_q_act = q_scale[part] * (d_q - qn[part] * jnp.sum(d_q * qn[part], axis=1, keepdims=True))
        d_k_act = k_scale[part] * (d_k - ks * jnp.sum(d_k * ks, axis=1, keepdims=True))
        d_act.append(jnp.concatenate([d_q_act, d_k_act, rs * solved], axis=1))
    dgain_ref[...] += d_gain
    d_conv = jnp.concatenate(d_act, axis=0) * (gate + act * (1.0 - gate))
    source = projected[:, :CONV_COLS]
    d_source = d_conv * taps[0:1]
    d_taps = [jnp.sum(d_conv * source, axis=0, keepdims=True)]
    for back in (1, 2, 3):
        kept = d_conv * keep[back - 1]
        d_source = d_source + pltpu.roll(kept, tokens - back, 0) * taps[back : back + 1]
        d_taps.append(jnp.sum(kept * pltpu.roll(source, back, 0), axis=0, keepdims=True))
    dtaps_ref[...] = jnp.concatenate(d_taps, axis=0)
    dproj_ref[:, :CONV_COLS] = d_source.astype(BF16)
    d_proj = dproj_ref[...]
    dw_ref[...] = jnp.dot(xnt_ref[...], d_proj, preferred_element_type=F32).astype(BF16)
    gxn_ref[...] += lax.dot_general(d_proj, w_ref[...], (NT, ((), ())), preferred_element_type=F32)


def mixer_bwd(gb, gbt, xnt, wo, w, proj, mixed, inv, upd, core, taps, cols, rows, gain):
    tokens, width = gb.shape
    const = lambda h: (0, 0)
    by_head = lambda h: (0, h)
    save = pl.BlockSpec((1, tokens, SEQ), lambda h: (h, 0, 0))
    return pl.pallas_call(
        mixer_bwd_body,
        grid=(HEADS,),
        in_specs=[
            pl.BlockSpec((tokens, width), const),
            pl.BlockSpec((width, tokens), const),
            pl.BlockSpec((width, tokens), const),
            pl.BlockSpec((width, DV), by_head),
            pl.BlockSpec((width, HEAD_COLS), by_head),
            pl.BlockSpec((tokens, HEAD_COLS), by_head),
            pl.BlockSpec((tokens, DV), by_head),
            save,
            save,
            save,
            pl.BlockSpec((4, CONV_COLS), by_head),
            pl.BlockSpec(cols.shape, const),
            pl.BlockSpec(rows.shape, const),
            pl.BlockSpec((1, DV), const),
        ],
        out_specs=[
            pl.BlockSpec((width, HEAD_COLS), by_head),
            pl.BlockSpec((width, DV), by_head),
            pl.BlockSpec((tokens, width), const),
            pl.BlockSpec((tokens, 128), const),
            pl.BlockSpec((HEADS, tokens), const),
            pl.BlockSpec((4, CONV_COLS), by_head),
            pl.BlockSpec((1, DV), const),
        ],
        out_shape=[
            jax.ShapeDtypeStruct((width, HEADS * HEAD_COLS), BF16),
            jax.ShapeDtypeStruct((width, HEADS * DV), BF16),
            jax.ShapeDtypeStruct((tokens, width), F32),
            jax.ShapeDtypeStruct((tokens, 128), F32),
            jax.ShapeDtypeStruct((HEADS, tokens), F32),
            jax.ShapeDtypeStruct((4, HEADS * CONV_COLS), F32),
            jax.ShapeDtypeStruct((1, DV), F32),
        ],
        scratch_shapes=[pltpu.VMEM((tokens, HEAD_COLS), BF16)],
        compiler_params=pltpu.CompilerParams(vmem_limit_bytes=60 * MIB),
        name="mixer_bwd",
    )(gb, gbt, xnt, wo, w, proj, mixed, inv, upd, core, taps, cols, rows, gain)


def ffn_body(nm_ref, nmt_ref, cot_ref, cott_ref, w_ref, dw_ref, out_ref, gnm_ref):
    @pl.when(pl.program_id(0) == 0)
    def _():
        out_ref[...] = jnp.zeros_like(out_ref)
        gnm_ref[...] = jnp.zeros_like(gnm_ref)

    w = w_ref[...]
    gate_up = jnp.dot(nm_ref[...], w[:, : 2 * TILE], preferred_element_type=F32)
    gate, up = gate_up[:, :TILE], gate_up[:, TILE:]
    sig = sigmoid(gate)
    swish = gate * sig
    hidden = (swish * up).astype(BF16)
    grad_hidden = jnp.dot(cot_ref[...], w[:, 2 * TILE :], preferred_element_type=F32)
    grad_gate = grad_hidden * up * (sig + swish * (1.0 - sig))
    grad_up = grad_hidden * swish
    grad_low = jnp.concatenate([grad_gate, grad_up], axis=1).astype(BF16)
    out_ref[...] += lax.dot_general(hidden, w[:, 2 * TILE :], (NT, ((), ())), preferred_element_type=F32)
    gnm_ref[...] += lax.dot_general(grad_low, w[:, : 2 * TILE], (NT, ((), ())), preferred_element_type=F32)
    dw_ref[:, : 2 * TILE] = jnp.dot(nmt_ref[...], grad_low, preferred_element_type=F32).astype(BF16)
    dw_ref[:, 2 * TILE :] = jnp.dot(cott_ref[...], hidden, preferred_element_type=F32).astype(BF16)


def ffn(nm, nmt, cot, cott, w):
    tokens, width = nm.shape
    tiles = w.shape[1] // (3 * TILE)
    const = lambda t: (0, 0)
    by_tile = lambda t: (0, t)
    return pl.pallas_call(
        ffn_body,
        grid=(tiles,),
        in_specs=[
            pl.BlockSpec((tokens, width), const),
            pl.BlockSpec((width, tokens), const),
            pl.BlockSpec((tokens, width), const),
            pl.BlockSpec((width, tokens), const),
            pl.BlockSpec((width, 3 * TILE), by_tile),
        ],
        out_specs=[
            pl.BlockSpec((width, 3 * TILE), by_tile),
            pl.BlockSpec((tokens, width), const),
            pl.BlockSpec((tokens, width), const),
        ],
        out_shape=[
            jax.ShapeDtypeStruct((width, tiles * 3 * TILE), BF16),
            jax.ShapeDtypeStruct((tokens, width), F32),
            jax.ShapeDtypeStruct((tokens, width), F32),
        ],
        compiler_params=pltpu.CompilerParams(vmem_limit_bytes=48 * MIB),
        name="ffn",
    )(nm, nmt, cot, cott, w)


def rms_scale(values):
    return lax.rsqrt(jnp.mean(values * values, axis=-1, keepdims=True) + epsilon)


def rms_back(grad, values, scale, gain):
    normed = values * scale
    d_normed = grad * gain
    d_values = scale * (d_normed - normed * jnp.mean(d_normed * normed, axis=-1, keepdims=True))
    return d_values, jnp.sum(grad * normed, axis=0)


def by_head(parts):
    shaped = [p.reshape(p.shape[0], HEADS, -1) for p in parts]
    return jnp.concatenate(shaped, axis=2).reshape(parts[0].shape[0], -1)


def from_head(values, sizes):
    shaped = values.reshape(values.shape[0], HEADS, -1)
    ends = [sum(sizes[: i + 1]) for i in range(len(sizes))]
    cuts = [shaped[:, :, e - s : e].reshape(values.shape[0], -1) for s, e in zip(sizes, ends)]
    return jnp.concatenate(cuts, axis=1)


def split_heads(values):
    key = HEADS * DK
    val = HEADS * DV
    edges = [0, key, 2 * key, 2 * key + val, 2 * key + 2 * val]
    return [values[:, a:b] for a, b in zip(edges[:-1], edges[1:]) if b <= values.shape[1]]


def plain_block(
    devices, tokens, segment_ids, cotangent, norm1_gain, mixer_in, decay_in, conv_weight, decay_log, decay_bias,
    head_gain, mixer_out, norm2_gain, ffn_in, ffn_out,
):
    rows, width = decay_in.shape[0], tokens.shape[1]
    count = tokens.shape[0]
    hidden = ffn_out.shape[0]
    tiles = hidden // TILE

    low = lambda v: v.astype(BF16)
    shard_mixer = by_head(split_heads(low(mixer_in)))
    conv_cols = conv_weight.shape[1]
    shard_small = jnp.concatenate(
        [low(decay_in), low(norm1_gain)[:, None], low(norm2_gain)[:, None], low(conv_weight).reshape(rows, -1)], axis=1
    )
    shard_small = jnp.pad(shard_small, ((0, 0), (0, SMALL - shard_small.shape[1])))
    shard_out = low(mixer_out).T
    ffn_low = low(ffn_in)
    pieces = [ffn_low[:, :hidden], ffn_low[:, hidden:], low(ffn_out).T]
    shard_ffn = jnp.concatenate([p.reshape(rows, tiles, TILE) for p in pieces], axis=2).reshape(rows, -1)
    shards = [shard_small, shard_mixer, shard_out, shard_ffn]

    x = tokens.astype(F32)
    scale1 = rms_scale(x)
    full_small, full_mixer, full_out, full_ffn = [lax.all_gather(s, "dp", axis=0, tiled=True) for s in shards]

    decay_full = full_small[:, :16]
    gain1 = full_small[:, 16].astype(F32)
    gain2 = full_small[:, 17].astype(F32)
    taps = full_small[:, 18 : 18 + 16].reshape(devices, 4, conv_cols)
    taps = jnp.moveaxis(taps, 0, 1).reshape(4, -1).astype(F32)
    taps = by_head(split_heads(taps))

    normed_in = low(x * scale1 * gain1)
    logits = jnp.dot(normed_in, decay_full, preferred_element_type=F32)
    shifted = logits[:, :HEADS] + decay_bias
    log_decay = -jnp.exp(decay_log) * jax.nn.softplus(shifted)
    rate = jax.nn.sigmoid(logits[:, HEADS:])
    sequences = count // SEQ
    lower = jnp.tril(jnp.ones((SEQ, SEQ), F32))
    cumulative = jnp.einsum(
        "ij,sjh->sih", lower, log_decay.reshape(sequences, SEQ, HEADS), precision=lax.Precision.HIGHEST
    ).reshape(count, HEADS)
    position = jnp.arange(count) % SEQ
    keeps = []
    for back in (1, 2, 3):
        earlier = jnp.pad(segment_ids[:-back], (back, 0), constant_values=-1)
        keeps.append(((earlier == segment_ids) & (position >= back)).astype(F32)[:, None])
    segment = segment_ids.astype(F32)
    cols = jnp.concatenate([cumulative, rate] + keeps + [segment[:, None]], axis=1)
    cols = jnp.pad(cols, ((0, 0), (0, 128 - cols.shape[1])))
    seq_rows = jnp.concatenate([cumulative.T, segment[None], jnp.zeros((7, count), F32)], axis=0)
    gain_row = head_gain[None]

    proj, mixed, inverse, update, core = mixer_fwd(normed_in, full_mixer, taps, cols, seq_rows, gain_row)

    middle = x + lax.dot_general(mixed, full_out, (NT, ((), ())), preferred_element_type=F32)
    scale2 = rms_scale(middle)
    normed_mid = low(middle * scale2 * gain2)
    dw_ffn, ffn_sum, grad_nm = ffn(normed_mid, normed_mid.T, cotangent, cotangent.T, full_ffn)
    output = low(middle + ffn_sum)

    d_middle, d_gain2 = rms_back(grad_nm, middle, scale2, gain2)
    grad_middle = d_middle + cotangent.astype(F32)
    branch = low(grad_middle)
    dw_mixer, dw_out, grad_xn, d_cols, d_rows, d_taps, d_gain = mixer_bwd(
        branch, branch.T, normed_in.T, full_out, full_mixer, proj, mixed, inverse, update, core,
        taps, cols, seq_rows, gain_row,
    )

    d_cum = d_cols[:, 8:16] - d_rows.T
    d_decay = jnp.einsum(
        "ji,sjh->sih", lower, d_cum.reshape(sequences, SEQ, HEADS), precision=lax.Precision.HIGHEST
    ).reshape(count, HEADS)
    d_shifted = -d_decay * jnp.exp(decay_log) * jax.nn.sigmoid(shifted)
    d_rate = d_cols[:, :8] * rate * (1.0 - rate)
    d_logits = low(jnp.concatenate([d_shifted, d_rate], axis=1))
    grad_xn = grad_xn + lax.dot_general(d_logits, decay_full, (NT, ((), ())), preferred_element_type=F32)
    d_x, d_gain1 = rms_back(grad_xn, x, scale1, gain1)
    input_grad = d_x + grad_middle

    d_decay_in = lax.dot_general(normed_in, d_logits, (TN, ((), ())), preferred_element_type=F32)
    d_taps = from_head(d_taps, [DK, DK, DV])
    d_taps = jnp.moveaxis(d_taps.reshape(4, devices, conv_cols), 1, 0).reshape(width, -1)
    dw_small = jnp.concatenate([d_decay_in, d_gain1[:, None], d_gain2[:, None], d_taps], axis=1)
    dw_small = low(jnp.pad(dw_small, ((0, 0), (0, SMALL - dw_small.shape[1]))))
    shared = jnp.concatenate([jnp.sum(d_decay * log_decay, axis=0), jnp.sum(d_shifted, axis=0), d_gain[0]])

    own_ffn, own_out, own_mixer, own_small = [
        lax.psum_scatter(g.astype(F32), "dp", scatter_dimension=0, tiled=True)
        for g in (dw_ffn, dw_out, dw_mixer, dw_small)
    ]
    shared = lax.psum(shared, "dp")

    own_tiles = own_ffn.reshape(rows, tiles, 3, TILE)
    ffn_in_grad = jnp.concatenate([own_tiles[:, :, i].reshape(rows, hidden) for i in (0, 1)], axis=1)
    ffn_out_grad = own_tiles[:, :, 2].reshape(rows, hidden).T
    return (
        output,
        input_grad,
        own_small[:, 16],
        from_head(own_mixer, [DK, DK, DV, DV]),
        own_small[:, :16],
        own_small[:, 18 : 18 + 16].reshape(4, conv_cols),
        shared[:HEADS],
        shared[HEADS : 2 * HEADS],
        shared[2 * HEADS : 2 * HEADS + DV],
        own_out.T,
        own_small[:, 17],
        ffn_in_grad,
        ffn_out_grad,
    )


def direct_block(
    devices, tokens, segment_ids, cotangent, norm1_gain, mixer_in, decay_in, conv_weight, decay_log, decay_bias,
    head_gain, mixer_out, norm2_gain, ffn_in, ffn_out,
):
    planes = devices // 8
    gain = head_gain[None]
    masters = [
        mixer_in, mixer_out.T, ffn_in, ffn_out.T, decay_in.T, norm1_gain[None], norm2_gain[None], conv_weight,
    ]
    (
        _, full_heads, _, small, xnt, cols, seq_rows, logs, factor, proj, mixed, inverse, update, core, dwf,
        output, middle, nm_sum,
    ) = forward(
        planes, masters, tokens, cotangent, segment_ids[None], decay_log[None], decay_bias[None], gain
    )
    results = backward(
        planes, dwf, middle, nm_sum, cotangent, xnt, full_heads, proj, mixed, inverse, update, core, small, cols,
        seq_rows, logs, factor, gain, tokens,
    )
    (
        output, input_grad, d_gain1, d_mixer_in, d_decay_in, d_conv, d_log, d_bias, d_gain, d_mixer_out, d_gain2, d_ffn_in,
        d_ffn_out,
    ) = hand_over([output, *results])
    return (
        output, input_grad, d_gain1[0], d_mixer_in, d_decay_in.T, d_conv, d_log[0], d_bias[0], d_gain[0], d_mixer_out.T,
        d_gain2[0], d_ffn_in, d_ffn_out.T,
    )


def on_device(devices, *arguments):
    rows, conv_cols = arguments[4].shape[0], arguments[6].shape[1]
    direct = rows % 16 == 0 and devices == 32 and conv_cols == 128
    return (direct_block if direct else plain_block)(devices, *arguments)


def solution(mesh):
    in_specs = (
        P("dp", None), P("dp"), P("dp", None), P("dp"), P("dp", None), P("dp", None), P(None, "dp"), P(), P(), P(),
        P(None, "dp"), P("dp"), P("dp", None), P(None, "dp"),
    )
    out_specs = (
        P("dp", None), P("dp", None), P("dp"), P("dp", None), P("dp", None), P(None, "dp"), P(), P(), P(),
        P(None, "dp"), P("dp"), P("dp", None), P(None, "dp"),
    )
    return jax.shard_map(
        partial(on_device, mesh.shape["dp"]), mesh=mesh, in_specs=in_specs, out_specs=out_specs, check_vma=False
    )
```

```python
from functools import partial

import jax
import jax.numpy as jnp
from jax import lax
from jax.experimental import pallas as pl
from jax.experimental.pallas import tpu as pltpu
from jax.sharding import PartitionSpec as P

HEADS = 8
DK = 128
DV = 256
SEQ = 256
HEAD_COLS = 2 * DK + 2 * DV
CONV_COLS = 2 * DK + DV
TILE = 256
SMALL = 128
F32 = jnp.float32
BF16 = jnp.bfloat16
MESH = pl.DeviceIdType.MESH
MIB = 1 << 20
epsilon = 1e-06
head_epsilon = 0.001

NN = ((1,), (0,))
NT = ((1,), (1,))
TN = ((0,), (0,))


def dot1(left, right, dims):
    return lax.dot_general(
        left.astype(BF16), right.astype(BF16), (dims, ((), ())), preferred_element_type=F32
    )


def split(value):
    high = value.astype(BF16)
    return high, (value - high.astype(F32)).astype(BF16)


def dot3(left, right, dims):
    lh, ll = split(left)
    rh, rl = split(right)
    return dot1(lh, rh, dims) + (dot1(lh, rl, dims) + dot1(ll, rh, dims))


def sigmoid(value):
    return 1.0 / (1.0 + jnp.exp(-value))


def grid_of(size):
    rows = lax.broadcasted_iota(jnp.int32, (size, size), 0)
    cols = lax.broadcasted_iota(jnp.int32, (size, size), 1)
    return rows, cols


def unit_inverses(couplings):
    half = couplings[0].shape[0] // 2
    rows, cols = grid_of(half)
    apart = rows ^ cols
    eye = jnp.where(apart == 0, 1.0, 0.0)
    corners = [a[s : s + half, s : s + half] for a in couplings for s in (0, half)]
    lows = [a.astype(BF16) for a in corners]
    inverses = [eye - jnp.where(apart < 2, a, 0.0) for a in corners]
    rounded = [inv.astype(BF16) for inv in inverses]
    block = 2
    while block < half:
        here = jnp.where((apart >= block) & (apart < 2 * block), 1.0, 0.0).astype(BF16)
        firsts = [dot1(low * here, inv, NN) for low, inv in zip(lows, rounded)]
        added = [dot1(inv, first, NN) for inv, first in zip(rounded, firsts)]
        inverses = [inv - new for inv, new in zip(inverses, added)]
        rounded = [inv - new.astype(BF16) for inv, new in zip(rounded, added)]
        block *= 2
    results = []
    for i, a in enumerate(couplings):
        first, second = inverses[2 * i], inverses[2 * i + 1]
        below = -dot1(rounded[2 * i + 1], dot1(a[half:, :half], rounded[2 * i], NN), NN)
        top = jnp.concatenate([first, jnp.zeros_like(first)], axis=1)
        results.append(jnp.concatenate([top, jnp.concatenate([below, second], axis=1)], axis=0))
    return results


def pick_lane(columns, lane):
    at = lax.broadcasted_iota(jnp.int32, columns.shape, 1)
    return jnp.sum(jnp.where(at == lane, columns, 0.0), axis=1, keepdims=True)


def conv_of(values, taps, keep):
    total = values * taps[0:1]
    for back in (1, 2, 3):
        total = total + pltpu.roll(values, back, 0) * keep[back - 1] * taps[back : back + 1]
    return total


def decays(seg_col, seg_row, cum_col, cum_row):
    rows, cols = grid_of(SEQ)
    linked = (seg_col == seg_row) & (rows >= cols)
    return jnp.where(linked, jnp.exp(jnp.where(linked, cum_col - cum_row, 0.0)), 0.0)


def strict(value):
    rows, cols = grid_of(SEQ)
    return jnp.where(rows > cols, value, 0.0)


def head_inputs(projected, taps, cols, head):
    keep = [pick_lane(cols, 16 + i) for i in range(3)]
    conv = conv_of(projected[:, :CONV_COLS], taps, keep)
    gate = sigmoid(conv)
    act = conv * gate
    q_act, k_act, value = act[:, :DK], act[:, DK : 2 * DK], act[:, 2 * DK :]
    q_scale = lax.rsqrt(jnp.sum(q_act * q_act, axis=1, keepdims=True) + epsilon)
    k_scale = lax.rsqrt(jnp.sum(k_act * k_act, axis=1, keepdims=True) + epsilon)
    cum = pick_lane(cols, head)
    rate = pick_lane(cols, 8 + head)
    seg = pick_lane(cols, 19)
    return keep, conv, gate, act, q_act * q_scale, k_act * k_scale, value, q_scale, k_scale, cum, rate, seg


def flip(number, bit):
    return number + bit - 2 * bit * ((number // bit) % 2)


def enter(me, before=lambda: None):
    barrier = pltpu.get_barrier_semaphore()
    partners = [flip(me, bit) for bit in (1, 2, 4, 8, 16)]
    for other in partners:
        pl.semaphore_signal(barrier, inc=1, device_id=(other,), device_id_type=MESH)
    before()
    pl.semaphore_wait(barrier, len(partners))


def span(k, width, start, size):
    first = k * width + start
    return pl.ds(first if isinstance(first, int) else pl.multiple_of(first, 128), size)


def remote(source, target, send_sem, recv_sem, other):
    return pltpu.make_async_remote_copy(
        src_ref=source, dst_ref=target, send_sem=send_sem, recv_sem=recv_sem,
        device_id=(other,), device_id_type=MESH,
    )


(
    G_NEAR, G_FAR, G_RELAY, G_X, G_Y, G_CORNER_Y, G_CORNER_X, G_CORE_OWN,
    G_CORE_OTHER, G_TWO_X, G_TWO_Y, G_TWO_CORNER, G_TWO_NEAR, G_TWO_FAR, G_TWO_RELAY, G_TWO_CORE,
) = range(16)
(
    S_CORE, S_XY_X, S_XY_Y, S_X_EARLY, S_X_LATE, S_Y_EARLY, S_Y_LATE, S_RELAY,
    S_NEAR, S_FAR, S_TWO_RELAY, S_TWO_NEAR, S_TWO_FAR, S_TWO_XY, S_TWO_X, S_TWO_Y,
) = range(16)
B_CORE, B_KEEP, B_SUMS, B_XY, B_X, B_Y, B_Z, B_TWO_Z, B_TWO = range(9)
HEAD, FFN_TILE, SMALLS = range(3)


SHAPES = {
    HEAD: (HEAD_COLS + DV, HEAD_COLS, HEAD_COLS // 2),
    FFN_TILE: (3 * TILE, 5 * TILE // 2, 3 * TILE // 2),
    SMALLS: (2 * SMALL, 2 * SMALL, SMALL),
}


class Gather:
    copies = 16

    def __init__(self, me, kinds, local_sem, send_sem, recv_sem):
        self.me, self.kinds = me, kinds
        self.local_sem, self.send_sem, self.recv_sem = local_sem, send_sem, recv_sem
        self.z, self.y, self.x, self.core = me // 8, (me // 4) % 2, (me // 2) % 2, me % 2

    def local(self, kind, k):
        shard, full, base = self.kinds[kind]
        width = SHAPES[kind][0]
        cols = span(k, width, 0, width)
        return pltpu.make_async_copy(
            shard.at[:, cols], full.at[self.z, self.y, self.x, self.core, :, cols], self.local_sem.at[base + k]
        )

    def copy(self, kind, k, name):
        shard, full, base = self.kinds[kind]
        width, part, half = SHAPES[kind]
        one = span(k, width, 0, part)
        two = span(k, width, part, width - part)
        z, y, x, core = self.z, self.y, self.x, self.core
        near, far = flip(z, 1), flip(z, 2)
        here = lambda cols: (shard.at[:, cols], full.at[z, y, x, core, :, cols])
        same = lambda ref: (ref, ref)
        by_y = kind == FFN_TILE
        (source, target), bit = {
            G_NEAR: lambda: (here(one), 8),
            G_FAR: lambda: (here(one), 16),
            G_RELAY: lambda: (same(full.at[far, y, x, core, :, one]), 8),
            G_X: lambda: (same(full.at[:, y, x, core, :, one]), 2),
            G_Y: lambda: (same(full.at[:, y, x, core, :, one]), 4),
            G_CORNER_Y: lambda: (same(full.at[:, y, 1 - x, core, :, span(k, width, 0, half)]), 4),
            G_CORNER_X: lambda: (same(full.at[:, 1 - y, x, core, :, span(k, width, half, part - half)]), 2),
            G_CORE_OWN: lambda: (same(full.at[:, y, :, core, :, one]), 1),
            G_CORE_OTHER: lambda: (same(full.at[:, 1 - y, :, core, :, one]), 1),
            G_TWO_X: lambda: (here(two), 2),
            G_TWO_Y: lambda: (here(two), 4),
            G_TWO_CORNER: lambda: (
                (same(full.at[z, 1 - y, x, core, :, two]), 2)
                if by_y
                else (same(full.at[z, y, 1 - x, core, :, two]), 4)
            ),
            G_TWO_NEAR: lambda: (same(full.at[z, :, :, core, :, two]), 8),
            G_TWO_FAR: lambda: (same(full.at[z, :, :, core, :, two]), 16),
            G_TWO_RELAY: lambda: (same(full.at[far, :, :, core, :, two]), 8),
            G_TWO_CORE: lambda: (same(full.at[:, :, :, core, :, two]), 1),
        }[name]()
        sems = self.send_sem.at[base + k, name], self.recv_sem.at[base + k, name]
        return remote(source, target, *sems, flip(self.me, bit))

    def send(self, kind, k, *names):
        for name in names:
            self.copy(kind, k, name).start()

    def wait(self, kind, k, *names):
        for name in names:
            self.copy(kind, k, name).wait_recv()

    def two(self, kind):
        return SHAPES[kind][0] > SHAPES[kind][1]

    def start(self, kind, k):
        self.local(kind, k).start()
        self.send(kind, k, G_FAR, G_NEAR)
        if self.two(kind):
            self.send(kind, k, G_TWO_X, G_TWO_Y)

    def relay(self, kind, k):
        self.wait(kind, k, G_FAR)
        self.send(kind, k, G_RELAY)
        if self.two(kind):
            self.wait(kind, k, *((G_TWO_Y,) if kind == FFN_TILE else (G_TWO_X,)))
            self.send(kind, k, G_TWO_CORNER)

    def square(self, kind, k):
        self.local(kind, k).wait()
        self.wait(kind, k, G_NEAR, G_RELAY)
        self.send(kind, k, G_X, G_Y)
        if self.two(kind):
            self.wait(kind, k, *((G_TWO_X,) if kind == FFN_TILE else (G_TWO_Y,)), G_TWO_CORNER)
            self.send(kind, k, G_TWO_FAR, G_TWO_NEAR)

    def corner(self, kind, k):
        self.wait(kind, k, G_X)
        self.send(kind, k, G_CORNER_Y, G_CORE_OWN)
        self.wait(kind, k, G_Y)
        self.send(kind, k, G_CORNER_X)
        if self.two(kind):
            self.wait(kind, k, G_TWO_FAR)
            self.send(kind, k, G_TWO_RELAY)

    def across(self, kind, k):
        self.wait(kind, k, G_CORNER_Y, G_CORNER_X)
        self.send(kind, k, G_CORE_OTHER)
        if self.two(kind):
            self.wait(kind, k, G_TWO_NEAR, G_TWO_RELAY)
            self.send(kind, k, G_TWO_CORE)

    def complete(self, kind, k):
        self.wait(kind, k, G_CORE_OWN, G_CORE_OTHER)
        if self.two(kind):
            self.wait(kind, k, G_TWO_CORE)

    def finish(self, kind, k):
        names = [G_NEAR, G_FAR, G_RELAY, G_X, G_Y, G_CORNER_Y, G_CORNER_X, G_CORE_OWN, G_CORE_OTHER]
        if self.two(kind):
            names += [G_TWO_X, G_TWO_Y, G_TWO_CORNER, G_TWO_NEAR, G_TWO_FAR, G_TWO_RELAY, G_TWO_CORE]
        for name in names:
            self.copy(kind, k, name).wait_send()


class Scatter:
    copies = 16
    depths = {B_CORE: 4, B_KEEP: 2, B_SUMS: 8, B_XY: 4, B_X: 8, B_Y: 8, B_Z: 8, B_TWO_Z: 8, B_TWO: 8}

    def __init__(self, me, kinds, store, core, keep, sums, xy, x, y, z, two_z, two, local_sem, send_sem, recv_sem):
        self.me, self.kinds, self.store = me, kinds, store
        self.from_core, self.keep, self.sums = core, keep, sums
        self.from_xy, self.from_x, self.from_y, self.from_z = xy, x, y, z
        self.two_z, self.from_two = two_z, two
        self.local_sem, self.send_sem, self.recv_sem = local_sem, send_sem, recv_sem
        self.z, self.core = me // 8, me % 2
        self.here = (me // 2) % 4
        self.across_x, self.across_y = flip(self.here, 1), flip(self.here, 2)
        self.both = 3 - self.here
        self.near, self.far = flip(self.z, 1), flip(self.z, 2)
        self.opposite = 3 - self.z

    def slot(self, name, r):
        return r % self.depths[name]

    def copy(self, kind, r, k, name):
        source = self.kinds[kind][0]
        width, part, half = SHAPES[kind]
        whole, one, two = pl.ds(0, width), pl.ds(0, part), pl.ds(part, width - part)
        first, second = pl.ds(0, half), pl.ds(half, part - half)
        rest = pl.ds(0, width - part)
        sums = self.sums.at[self.slot(B_SUMS, r)]
        here, across_x, across_y, both, z = self.here, self.across_x, self.across_y, self.both, self.z
        by_y = kind == FFN_TILE
        place = lambda where, cols: sums.at[:, where, :, cols]
        origin, target, bit = {
            S_CORE: lambda: (
                source(k, 1 - self.core), self.from_core.at[self.slot(B_CORE, r), :, :, :, whole], 1
            ),
            S_XY_X: lambda: (place(both, first), self.from_xy.at[self.slot(B_XY, r), :, :, first], 2),
            S_XY_Y: lambda: (place(both, second), self.from_xy.at[self.slot(B_XY, r), :, :, second], 4),
            S_X_EARLY: lambda: (place(across_x, first), self.from_x.at[self.slot(B_X, r), :, :, first], 2),
            S_X_LATE: lambda: (place(across_x, second), self.from_x.at[self.slot(B_X, r), :, :, second], 2),
            S_Y_EARLY: lambda: (place(across_y, second), self.from_y.at[self.slot(B_Y, r), :, :, second], 4),
            S_Y_LATE: lambda: (place(across_y, first), self.from_y.at[self.slot(B_Y, r), :, :, first], 4),
            S_RELAY: lambda: (sums.at[self.opposite, here, :, one], self.from_z.at[self.slot(B_Z, r), 0, :, one], 8),
            S_NEAR: lambda: (sums.at[self.near, here, :, one], self.from_z.at[self.slot(B_Z, r), 1, :, one], 8),
            S_FAR: lambda: (sums.at[self.far, here, :, one], self.from_z.at[self.slot(B_Z, r), 2, :, one], 16),
            S_TWO_RELAY: lambda: (
                sums.at[self.opposite, :, :, two], self.two_z.at[self.slot(B_TWO_Z, r), 0, :, :, rest], 8
            ),
            S_TWO_NEAR: lambda: (
                sums.at[self.near, :, :, two], self.two_z.at[self.slot(B_TWO_Z, r), 1, :, :, rest], 8
            ),
            S_TWO_FAR: lambda: (
                sums.at[self.far, :, :, two], self.two_z.at[self.slot(B_TWO_Z, r), 2, :, :, rest], 16
            ),
            S_TWO_XY: lambda: (
                sums.at[z, both, :, two], self.from_two.at[self.slot(B_TWO, r), 0, :, rest], 4 if by_y else 2
            ),
            S_TWO_X: lambda: (sums.at[z, across_x, :, two], self.from_two.at[self.slot(B_TWO, r), 1, :, rest], 2),
            S_TWO_Y: lambda: (sums.at[z, across_y, :, two], self.from_two.at[self.slot(B_TWO, r), 2, :, rest], 4),
        }[name]()
        sems = self.send_sem.at[r, name], self.recv_sem.at[r, name]
        return remote(origin, target, *sems, flip(self.me, bit))

    def send(self, kind, r, k, *names):
        for name in names:
            self.copy(kind, r, k, name).start()

    def wait(self, kind, r, k, *names):
        for name in names:
            self.copy(kind, r, k, name).wait_recv()

    def two(self, kind):
        return SHAPES[kind][0] > SHAPES[kind][1]

    def load(self, kind, r, k):
        source = self.kinds[kind][0]
        return pltpu.make_async_copy(
            source(k, self.core), self.keep.at[r % 2, :, :, :, pl.ds(0, SHAPES[kind][0])], self.local_sem.at[r]
        )

    def core_step(self, kind, r, k):
        self.send(kind, r, k, S_CORE)

    def load_step(self, kind, r, k):
        if self.kinds[kind][1] is None:
            self.load(kind, r, k).start()

    def add_planes(self, r, place, cols, first, others):
        def one(plane, carry):
            total = first(plane).astype(F32)
            for read in others:
                total = total + read(plane).astype(F32)
            self.sums[self.slot(B_SUMS, r), plane, place, :, cols] = total.astype(BF16)
            return carry

        lax.fori_loop(0, 4, one, 0)

    def add_places(self, r, plane, cols, others):
        slot = self.slot(B_SUMS, r)
        for place in range(4):
            total = self.sums[slot, plane, place, :, cols].astype(F32)
            for read in others:
                total = total + read(place).astype(F32)
            self.sums[slot, plane, place, :, cols] = total.astype(BF16)

    def held(self, r, place, cols):
        return lambda plane: self.sums[self.slot(B_SUMS, r), plane, place, :, cols]

    def chip_step(self, kind, r, k):
        in_place = self.kinds[kind][1]
        width, part, half = SHAPES[kind]
        whole = pl.ds(0, width)
        self.wait(kind, r, k, S_CORE)
        if in_place is None:
            self.load(kind, r, k).wait()
            mine = lambda place: (lambda plane: self.keep[r % 2, plane, place, :, whole])
        else:
            mine = lambda place: (lambda plane: in_place(k, plane, place, self.core))
        got = lambda place: (lambda plane: self.from_core[self.slot(B_CORE, r), plane, place, :, whole])
        for place, names in (
            (self.both, (S_XY_X, S_XY_Y)),
            (self.across_x, (S_X_EARLY,)),
            (self.across_y, (S_Y_EARLY,)),
            (self.here, (S_TWO_RELAY, S_TWO_NEAR) if self.two(kind) else ()),
        ):
            self.add_planes(r, place, whole, got(place), [mine(place)])
            self.send(kind, r, k, *names)
        self.copy(kind, r, k, S_CORE).wait_send()

    def corner_step(self, kind, r, k):
        width, part, half = SHAPES[kind]
        first, second = pl.ds(0, half), pl.ds(half, part - half)
        passed = lambda cols: (lambda plane: self.from_xy[self.slot(B_XY, r), plane, :, cols])
        self.wait(kind, r, k, S_XY_X)
        self.add_planes(r, self.across_y, first, self.held(r, self.across_y, first), [passed(first)])
        self.send(kind, r, k, S_Y_LATE)
        self.wait(kind, r, k, S_XY_Y)
        self.add_planes(r, self.across_x, second, self.held(r, self.across_x, second), [passed(second)])
        self.send(kind, r, k, S_X_LATE)
        if self.two(kind):
            two, rest = pl.ds(part, width - part), pl.ds(0, width - part)
            self.wait(kind, r, k, S_TWO_RELAY)
            self.add_places(r, self.far, two, [lambda place: self.two_z[self.slot(B_TWO_Z, r), 0, place, :, rest]])
            self.send(kind, r, k, S_TWO_FAR)

    def square_step(self, kind, r, k):
        width, part, half = SHAPES[kind]
        one = pl.ds(0, part)
        self.wait(kind, r, k, S_X_EARLY, S_X_LATE, S_Y_EARLY, S_Y_LATE)
        from_x = lambda plane: self.from_x[self.slot(B_X, r), plane, :, one]
        from_y = lambda plane: self.from_y[self.slot(B_Y, r), plane, :, one]
        self.add_planes(r, self.here, one, self.held(r, self.here, one), [from_x, from_y])
        self.send(kind, r, k, S_RELAY, S_NEAR)
        if self.two(kind):
            two, rest = pl.ds(part, width - part), pl.ds(0, width - part)
            self.wait(kind, r, k, S_TWO_NEAR, S_TWO_FAR)
            self.add_places(
                r, self.z, two,
                [lambda place, i=i: self.two_z[self.slot(B_TWO_Z, r), i, place, :, rest] for i in (1, 2)],
            )
            self.send(kind, r, k, S_TWO_XY, S_TWO_X if kind != FFN_TILE else S_TWO_Y)

    def relay_step(self, kind, r, k):
        width, part, half = SHAPES[kind]
        slot, one = self.slot(B_SUMS, r), pl.ds(0, part)
        self.wait(kind, r, k, S_RELAY)
        total = self.sums[slot, self.far, self.here, :, one].astype(F32)
        total = total + self.from_z[self.slot(B_Z, r), 0, :, one].astype(F32)
        self.sums[slot, self.far, self.here, :, one] = total.astype(BF16)
        self.send(kind, r, k, S_FAR)
        if self.two(kind):
            two, rest = pl.ds(part, width - part), pl.ds(0, width - part)
            place = self.across_x if kind == FFN_TILE else self.across_y
            self.wait(kind, r, k, S_TWO_XY)
            total = self.sums[slot, self.z, place, :, two].astype(F32)
            total = total + self.from_two[self.slot(B_TWO, r), 0, :, rest].astype(F32)
            self.sums[slot, self.z, place, :, two] = total.astype(BF16)
            self.send(kind, r, k, S_TWO_X if kind == FFN_TILE else S_TWO_Y)

    def last_step(self, kind, r, k):
        width, part, half = SHAPES[kind]
        slot, one = self.slot(B_SUMS, r), pl.ds(0, part)
        self.wait(kind, r, k, S_NEAR, S_FAR)
        total = self.sums[slot, self.z, self.here, :, one].astype(F32)
        for i in (1, 2):
            total = total + self.from_z[self.slot(B_Z, r), i, :, one].astype(F32)
        names = [S_XY_X, S_XY_Y, S_X_EARLY, S_X_LATE, S_Y_EARLY, S_Y_LATE, S_RELAY, S_NEAR, S_FAR]
        if self.two(kind):
            two, rest = pl.ds(part, width - part), pl.ds(0, width - part)
            self.wait(kind, r, k, S_TWO_X, S_TWO_Y)
            more = self.sums[slot, self.z, self.here, :, two].astype(F32)
            for i in (1, 2):
                more = more + self.from_two[self.slot(B_TWO, r), i, :, rest].astype(F32)
            total = jnp.concatenate([total, more], axis=1)
            names += [S_TWO_RELAY, S_TWO_NEAR, S_TWO_FAR, S_TWO_XY, S_TWO_X, S_TWO_Y]
        self.store(kind, k, total)
        for name in names:
            self.copy(kind, r, k, name).wait_send()


class Total:
    bits = (1, 2, 4, 8, 16)

    def __init__(self, me, value_ref, store, got, stage, send_sem, recv_sem):
        self.me, self.value_ref, self.store = me, value_ref, store
        self.got, self.stage, self.send_sem, self.recv_sem = got, stage, send_sem, recv_sem

    def copy(self, number):
        sems = self.send_sem.at[number], self.recv_sem.at[number]
        return remote(self.stage.at[number], self.got.at[number], *sems, flip(self.me, self.bits[number]))

    def step(self, number):
        last = len(self.bits)
        value = self.value_ref[...]
        if number > 0:
            self.copy(number - 1).wait_recv()
            value = self.stage[number - 1] + self.got[number - 1]
        if number < last:
            self.stage[number] = value
            self.copy(number).start()
        else:
            self.store(value)
            for number in range(last):
                self.copy(number).wait_send()


def triangle_sum(values, dims):
    rows, cols = grid_of(SEQ)
    ones = jnp.where(rows >= cols, 1.0, 0.0).astype(BF16)
    first, rest = values.astype(BF16), values - values.astype(BF16).astype(F32)
    second, third = split(rest)
    return dot1(ones, first, dims) + (dot1(ones, second, dims) + dot1(ones, third, dims))


def log1p(value):
    series = value * (1.0 - value * (0.5 - value * (1.0 / 3.0 - value * (0.25 - value * 0.2))))
    return jnp.where(value < 0.01, series, jnp.log(1.0 + value))


def softplus(value):
    return jnp.maximum(value, 0.0) + log1p(jnp.exp(-jnp.abs(value)))


def merge(block):
    return block.reshape(-1, block.shape[-1])


def head_taps(small_ref, head):
    wide = 2 * head
    places = [(0, head), (1, head)] + [(2 + head // 4, wide % 8 + i) for i in (0, 1)]
    blocks = [
        small_ref[z, p // 4, (p // 2) % 2, p % 2, 0:16, SMALL : 2 * SMALL][0:4].astype(F32) for z, p in places
    ]
    return jnp.concatenate(blocks, axis=1)


def row_blocks(count, body, size=128):
    def one(i, carry):
        body(pl.ds(pl.multiple_of(i * size, size), size))
        return carry

    lax.fori_loop(0, count // size, one, 0)


def lane_index(shape):
    return lax.broadcasted_iota(jnp.int32, shape, 1)


def forward_body(
    planes, tiles,
    mixer_in_ref, mixer_out_ref, ffn_in_ref, ffn_out_ref, decay_in_ref, gain1_ref, gain2_ref, conv_ref,
    x_in, cot_in, seg_ref, log_ref, bias_ref, gain_ref,
    full_small, full_heads, full_tiles, small_out, xnt_out, cols_out, rows_out, logs_out, factor_out, middle_out,
    proj_ref, mixed_ref, inv_ref, upd_ref, core_ref, dw_ref, output_ref, nm_sum,
    small_ref, xnt_ref, cols_ref, rows_ref, logs_ref, factor_ref, middle, x_ref, cot_ref, load_sem, flush_sem,
    shard_small, shard_heads, shard_tiles, turn, consts_ref,
    w_buf, xn, cott, nm, nmt, out_sum, gains, copy_sem, w_sem, local_sem, send_sem, recv_sem,
):
    step = pl.program_id(0)
    tokens = x_ref.shape[0]
    chunks = HEADS + tiles
    me = lax.axis_index("dp")
    kinds = {
        SMALLS: (shard_small, full_small, chunks),
        HEAD: (shard_heads, full_heads, 0),
        FFN_TILE: (shard_tiles, full_tiles, HEADS),
    }
    work = Gather(me, kinds, local_sem, send_sem, recv_sem)

    def at(chunk, act):
        pl.when((chunk >= 0) & (chunk < HEADS))(lambda: act(HEAD, chunk))
        pl.when((chunk >= HEADS) & (chunk < chunks))(lambda: act(FFN_TILE, chunk - HEADS))

    def weights(kind, k, slot, plane=None):
        full, width = kinds[kind][1], SHAPES[kind][0]
        source = full.at[:, :, :, :, :, span(k, width, 0, width)]
        place = w_buf.at[slot, :, :, :, :, :, pl.ds(0, width)]
        if plane is not None:
            source, place = source.at[plane], place.at[plane]
        return pltpu.make_async_copy(source, place, w_sem.at[slot])

    def load_weights(kind, k, slot):
        for plane in range(planes):
            weights(kind, k, slot, plane).start()

    def arrive(kind, k):
        work.complete(kind, k)
        load_weights(kind, k, k % 2 if isinstance(k, int) else (step + 1) % 2)

    def arrive_early(kind, k):
        pl.when(step + 1 != chunks - 1)(lambda: arrive(kind, k))

    def arrive_late(kind, k):
        pl.when(step + 1 == chunks - 1)(lambda: arrive(kind, k))

    at_start = ((3, work.corner), (1, arrive_early))
    at_middle = ((7, work.start), (6, work.relay), (5, work.square), (2, work.across))

    def early(step):
        for lead, act in sorted(at_start[:1] + at_middle + ((1, arrive),), key=lambda item: -item[0]):
            if step + lead >= 0:
                act(HEAD, step + lead)

    def midway():
        for lead, act in at_middle:
            at(step + lead, act)
        at(step + 1, arrive_late)

    loads = [
        pltpu.make_async_copy(source, target, load_sem.at[i])
        for i, (source, target) in enumerate(((x_in, x_ref), (cot_in, cot_ref)))
    ]
    flushes = [
        pltpu.make_async_copy(source, target, flush_sem.at[i])
        for i, (source, target) in enumerate(
            (
                (small_ref, small_out), (xnt_ref, xnt_out), (cols_ref, cols_out), (rows_ref, rows_out),
                (logs_ref, logs_out), (factor_ref, factor_out), (middle, middle_out),
            )
        )
    ]

    def pack_heads():
        for copy in loads:
            copy.start()
        turn[...] = jnp.zeros_like(turn)
        turn[0:16, 0 : conv_ref.shape[1] // 4] = decay_in_ref[...]
        turn[16:17, 0 : conv_ref.shape[1] // 4] = gain1_ref[...]
        turn[17:18, 0 : conv_ref.shape[1] // 4] = gain2_ref[...]
        rows = shard_small.shape[0]
        shard_small[:, 0:SMALL] = turn[...].T[0:rows].astype(BF16)
        taps = jnp.concatenate([conv_ref[...], jnp.zeros((rows - 4, SMALL), F32)], axis=0)
        shard_small[:, SMALL:] = taps.astype(BF16)
        for h in range(HEADS):
            at_col = h * (HEAD_COLS + DV)
            key, val = HEADS * DK, HEADS * DV
            for ref, start, size in (
                (mixer_in_ref, h * DK, DK),
                (mixer_in_ref, key + h * DK, DK),
                (mixer_in_ref, 2 * key + h * DV, DV),
                (mixer_in_ref, 2 * key + val + h * DV, DV),
                (mixer_out_ref, h * DV, DV),
            ):
                shard_heads[:, at_col : at_col + size] = ref[:, start : start + size].astype(BF16)
                at_col += size

    def pack_tiles():
        for t in range(tiles):
            at_col = t * 3 * TILE
            for ref, start in ((ffn_in_ref, t * TILE), (ffn_in_ref, (tiles + t) * TILE), (ffn_out_ref, t * TILE)):
                shard_tiles[:, at_col : at_col + TILE] = ref[:, start : start + TILE].astype(BF16)
                at_col += TILE

    @pl.when(step == 0)
    def _():
        enter(me, pack_heads)
        work.start(SMALLS, 0)
        early(-7)
        pack_tiles()
        consts_ref[...] = jnp.zeros_like(consts_ref)
        consts_ref[0:1, 0:HEADS] = -jnp.exp(log_ref[...])
        consts_ref[1:2, 0:HEADS] = bias_ref[...]

        def prepare(rows):
            middle[rows, :] = x_ref[rows, :].astype(F32)
            cott[:, rows] = cot_ref[rows, :].astype(F32).T.astype(BF16)

        for copy in loads:
            copy.wait()
        row_blocks(tokens, prepare)
        work.relay(SMALLS, 0)
        early(-6)
        work.square(SMALLS, 0)
        early(-5)
        work.corner(SMALLS, 0)
        early(-4)
        work.across(SMALLS, 0)
        out_sum[...] = jnp.zeros_like(out_sum)
        nm_sum[...] = jnp.zeros_like(nm_sum)
        early(-3)
        work.complete(SMALLS, 0)
        early(-2)
        copy = pltpu.make_async_copy(full_small, small_ref, copy_sem)
        copy.start()
        copy.wait()
        small = merge(small_ref[..., 0:SMALL])
        turned = small.astype(F32).T
        gains[0:1, :] = turned[16:17, :]
        gains[1:2, :] = turned[17:18, :]

        def norm(rows):
            x = middle[rows, :]
            scale = lax.rsqrt(jnp.mean(x * x, axis=1, keepdims=True) + epsilon)
            normed = x * scale * gains[0:1, :]
            xn[rows, :] = normed.astype(BF16)
            xnt_ref[:, rows] = normed.T.astype(BF16)

        row_blocks(tokens, norm)
        logits = jnp.dot(xn[...], small, preferred_element_type=F32)
        lanes = lane_index(logits.shape)
        decay_scale, bias = consts_ref[0:1, :], consts_ref[1:2, :]
        shifted = logits + bias
        rate = sigmoid(logits)
        log_decay = decay_scale * softplus(shifted)
        logs_ref[...] = log_decay
        factor_ref[...] = jnp.where(
            lanes < 8, decay_scale * sigmoid(shifted), jnp.where(lanes < 16, rate * (1.0 - rate), 0.0)
        )
        seg_row = jnp.broadcast_to(seg_ref[...].astype(F32), (128, tokens))
        segment = seg_row.T
        rows_ref[8:16, :] = seg_row[0:8]
        inside = lax.broadcasted_iota(jnp.int32, segment.shape, 0) % SEQ
        aux = segment
        for back in (1, 2, 3):
            linked = (pltpu.roll(segment, back, 0) == segment) & (inside >= back)
            aux = jnp.where(lanes == 15 + back, jnp.where(linked, 1.0, 0.0), aux)
        for start in range(0, tokens, SEQ):
            part = slice(start, start + SEQ)
            cum = triangle_sum(log_decay[part], NN)
            cols_ref[part, :] = jnp.where(lanes[part] < 8, cum, jnp.where(lanes[part] < 16, rate[part], aux[part]))
            rows_ref[0:8, part] = cum.T[0:8]
        early(-1)
        work.finish(SMALLS, 0)

    for lead, act in at_start:
        at(step + lead, act)
    at(step, lambda kind, k: weights(kind, k, step % 2).wait())
    at(step - 1, work.finish)

    @pl.when(step == 1)
    def _():
        for copy in flushes[:-1]:
            copy.start()

    @pl.when(step < HEADS)
    def _():
        w = merge(w_buf[step % 2])
        projected = jnp.dot(xn[...], w[:, :HEAD_COLS], preferred_element_type=F32)
        proj_ref[...] = projected
        midway()
        _, _, _, _, q, k, value, _, _, cum, rate, seg = head_inputs(
            projected, head_taps(small_ref, step), cols_ref[...], step
        )
        q = q * DK**-0.5
        cum_row = rows_ref[pl.ds(step, 1), :]
        seg_row = rows_ref[8:9, :]
        parts = [slice(s, s + SEQ) for s in range(0, tokens, SEQ)]
        scores, couplings = [], []
        for part in parts:
            pair = decays(seg[part], seg_row[:, part], cum[part], cum_row[:, part])
            key_dots = dot3(k[part], k[part], NT)
            scores.append(pair * dot3(q[part], k[part], NT))
            couplings.append(strict(pair * key_dots) * rate[part])
        inverses = unit_inverses(couplings)
        for i, part in enumerate(parts):
            update = dot3(inverses[i], rate[part] * value[part], NN)
            core = dot3(scores[i], update, NN)
            inv_ref[0, part, :] = inverses[i].astype(BF16)
            upd_ref[0, part, :] = update
            core_ref[0, part, :] = core
            scale = lax.rsqrt(jnp.mean(core * core, axis=1, keepdims=True) + head_epsilon)
            out_gate = projected[part, CONV_COLS:]
            mixed_ref[part, :] = (core * scale * gain_ref[...] * (out_gate * sigmoid(out_gate))).astype(BF16)
        middle[...] += lax.dot_general(mixed_ref[...], w[:, HEAD_COLS:], (NT, ((), ())), preferred_element_type=F32)

    @pl.when(step == HEADS)
    def _():
        def norm(rows):
            mid = middle[rows, :]
            scale = lax.rsqrt(jnp.mean(mid * mid, axis=1, keepdims=True) + epsilon)
            normed = mid * scale * gains[1:2, :]
            nm[rows, :] = normed.astype(BF16)
            nmt[:, rows] = normed.T.astype(BF16)

        flushes[-1].start()
        row_blocks(tokens, norm)

    @pl.when(step >= HEADS)
    def _():
        w = merge(w_buf[step % 2, :, :, :, :, :, 0 : 3 * TILE])
        gate_up = jnp.dot(nm[...], w[:, : 2 * TILE], preferred_element_type=F32)
        gate, up = gate_up[:, :TILE], gate_up[:, TILE:]
        sig = sigmoid(gate)
        swish = gate * sig
        hidden = (swish * up).astype(BF16)
        midway()
        grad_hidden = jnp.dot(cot_ref[...], w[:, 2 * TILE :], preferred_element_type=F32)
        grad_gate = grad_hidden * up * (sig + swish * (1.0 - sig))
        grad_up = grad_hidden * swish
        grad_low = jnp.concatenate([grad_gate, grad_up], axis=1).astype(BF16)
        out_sum[...] += lax.dot_general(hidden, w[:, 2 * TILE :], (NT, ((), ())), preferred_element_type=F32)
        nm_sum[...] += lax.dot_general(grad_low, w[:, : 2 * TILE], (NT, ((), ())), preferred_element_type=F32)
        dw_ref[:, : 2 * TILE] = jnp.dot(nmt[...], grad_low, preferred_element_type=F32).astype(BF16)
        dw_ref[:, 2 * TILE :] = jnp.dot(cott[...], hidden, preferred_element_type=F32).astype(BF16)

    @pl.when(step == chunks - 1)
    def _():
        def add(rows):
            output_ref[rows, :] = (middle[rows, :] + out_sum[rows, :]).astype(BF16)

        row_blocks(tokens, add)
        work.finish(FFN_TILE, tiles - 1)
        for copy in flushes:
            copy.wait()


def once(shape):
    return pl.BlockSpec(shape, lambda i: (0,) * len(shape), pipeline_mode=pl.Buffered(1))


def forward(planes, masters, x, cot, *others):
    rows, tokens, width = masters[0].shape[0], *x.shape
    tiles = masters[3].shape[1] // TILE
    chunks = HEADS + tiles
    widths = (2 * SMALL, HEADS * (HEAD_COLS + DV), tiles * 3 * TILE)
    hbm = pl.BlockSpec(memory_space=pl.ANY)
    head = lambda i: jnp.minimum(i, HEADS - 1)
    tile = lambda i: jnp.maximum(i - HEADS, 0)
    save = pl.BlockSpec((1, tokens, SEQ), lambda i: (head(i), 0, 0))
    shape = jax.ShapeDtypeStruct
    whole = [((planes, 2, 2, 2, rows, w), BF16) for w in widths]
    outs = [
        (hbm, *whole[0]),
        (hbm, *whole[1]),
        (hbm, *whole[2]),
        (hbm, *whole[0]),
        (hbm, (width, tokens), BF16),
        (hbm, (tokens, 128), F32),
        (hbm, (16, tokens), F32),
        (hbm, (tokens, 128), F32),
        (hbm, (tokens, 128), F32),
        (hbm, (tokens, width), F32),
        (pl.BlockSpec((tokens, HEAD_COLS), lambda i: (0, head(i))), (tokens, HEADS * HEAD_COLS), F32),
        (pl.BlockSpec((tokens, DV), lambda i: (0, head(i))), (tokens, HEADS * DV), BF16),
        (save, (HEADS, tokens, SEQ), BF16),
        (save, (HEADS, tokens, DV), F32),
        (save, (HEADS, tokens, DV), F32),
        (pl.BlockSpec((width, 3 * TILE), lambda i: (0, tile(i))), (width, tiles * 3 * TILE), BF16),
        (once((tokens, width)), (tokens, width), BF16),
        (once((tokens, width)), (tokens, width), F32),
    ]
    return pl.pallas_call(
        partial(forward_body, planes, tiles),
        grid=(chunks,),
        in_specs=[once(a.shape) for a in masters] + [hbm, hbm] + [once(a.shape) for a in others],
        out_specs=[o[0] for o in outs],
        out_shape=[shape(o[1], o[2]) for o in outs],
        scratch_shapes=[pltpu.VMEM(o[1], o[2]) for o in outs[3:10]]
        + [
            pltpu.VMEM((tokens, width), BF16),
            pltpu.VMEM((tokens, width), BF16),
            pltpu.SemaphoreType.DMA((2,)),
            pltpu.SemaphoreType.DMA((7,)),
        ]
        + [pltpu.VMEM((rows, w), BF16) for w in widths]
        + [
            pltpu.VMEM((128, 128), F32),
            pltpu.VMEM((8, 128), F32),
            pltpu.VMEM((2, planes, 2, 2, 2, rows, HEAD_COLS + DV), BF16),
            pltpu.VMEM((tokens, width), BF16),
            pltpu.VMEM((width, tokens), BF16),
            pltpu.VMEM((tokens, width), BF16),
            pltpu.VMEM((width, tokens), BF16),
            pltpu.VMEM((tokens, width), F32),
            pltpu.VMEM((8, width), F32),
            pltpu.SemaphoreType.DMA,
            pltpu.SemaphoreType.DMA((2,)),
            pltpu.SemaphoreType.DMA((chunks + 1,)),
            pltpu.SemaphoreType.DMA((chunks + 1, Gather.copies)),
            pltpu.SemaphoreType.DMA((chunks + 1, Gather.copies)),
        ],
        compiler_params=pltpu.CompilerParams(
            collective_id=0, has_side_effects=True, vmem_limit_bytes=60 * MIB
        ),
        name="forward",
    )(*masters, x, cot, *others)


FIRST = 4


def row_sums(count, body, width, size=128):
    def one(i, total):
        return body(pl.ds(pl.multiple_of(i * size, size), size), total)

    return lax.fori_loop(0, count // size, one, jnp.zeros((1, width), F32))


def head_step(j):
    return jnp.minimum(j // 2, HEADS - 1)


def backward_body(
    planes, tiles, total_chunks,
    dwf_ref, middle_in, nm_sum_in, cot_in, xnt_in, x_in, w_ref, proj_ref, mixed_ref, inv_ref, upd_ref, core_ref,
    small_ref, cols_ref, rows_ref, logs_ref, factor_ref, gain_ref,
    input_grad_out, own_gain1, own_mixer, own_decay, own_conv, own_log, own_bias, own_gain, own_out, own_gain2, own_ffn,
    own_down,
    middle_ref, nm_sum_ref, cot_ref, xnt_ref, x_ref, load_sem, flush_sem, gbt_ref, gains, dw, d_small, dcols, drows, dgain, dproj,
    value_ref, *scratch,
):
    gxn, grad_mid_ref, gb_ref = middle_ref, nm_sum_ref, cot_ref
    *buffers, got, stage, local_sem, send_sem, recv_sem, total_send, total_recv = scratch
    step = pl.program_id(0)
    tokens = middle_ref.shape[0]
    rows = own_mixer.shape[0]
    hidden = tiles * TILE
    me = lax.axis_index("dp")

    def tile_source(k, core):
        return dwf_ref.at[:, :, core, :, span(k, 3 * TILE, 0, 3 * TILE)]

    kinds = {
        FFN_TILE: (tile_source, None),
        HEAD: (
            lambda k, core: dw.at[k % 2, :, :, core],
            lambda k, plane, place, core: dw[k % 2, plane, place, core],
        ),
        SMALLS: (
            lambda k, core: d_small.at[:, :, core],
            lambda k, plane, place, core: d_small[plane, place, core],
        ),
    }

    def store(kind, k, total):
        def put(ref, start, source, width):
            ref[:, pl.ds(pl.multiple_of(start, 128), width)] = total[:, source : source + width]

        if kind == SMALLS:
            turned = jnp.concatenate([total[:, :SMALL], jnp.zeros((SMALL - rows, SMALL), F32)], axis=0).T
            own_decay[...] = turned[0:16, 0:rows]
            own_gain1[...] = turned[16:17, 0:rows]
            own_gain2[...] = turned[17:18, 0:rows]
            own_conv[...] = total[0:4, SMALL:]
        elif kind == HEAD:
            put(own_mixer, k * DK, 0, DK)
            put(own_mixer, HEADS * DK + k * DK, DK, DK)
            put(own_mixer, 2 * HEADS * DK + k * DV, 2 * DK, DV)
            put(own_mixer, 2 * HEADS * DK + HEADS * DV + k * DV, 2 * DK + DV, DV)
            put(own_out, k * DV, HEAD_COLS, DV)
        else:
            put(own_ffn, k * TILE, 0, TILE)
            put(own_ffn, hidden + k * TILE, TILE, TILE)
            put(own_down, k * TILE, 2 * TILE, TILE)

    work = Scatter(me, kinds, store, *buffers, local_sem, send_sem, recv_sem)
    def share(value):
        own_log[...] = value[0:1, 0:HEADS]
        own_bias[...] = value[1:2, 0:HEADS]
        own_gain[...] = jnp.concatenate([value[2:3], value[3:4]], axis=1)

    small_sum = Total(me, value_ref, share, got, stage, total_send, total_recv)

    last = total_chunks - 1

    def at(r, act):
        is_head = (r >= FIRST) & (r < last) & ((r - FIRST) % 2 == 0)
        is_early = (r >= 0) & (r < FIRST)
        is_tile = (r > FIRST) & (r < last) & ((r - FIRST) % 2 == 1)
        pl.when(is_early)(lambda: act(FFN_TILE, r, r))
        pl.when(is_tile)(lambda: act(FFN_TILE, r, (r + FIRST - 1) // 2))
        pl.when(is_head)(lambda: act(HEAD, r, (r - FIRST) // 2))
        pl.when(r == last)(lambda: act(SMALLS, r, 0))

    loads = [
        pltpu.make_async_copy(source, target, load_sem.at[i])
        for i, (source, target) in enumerate(
            (
                (middle_in, middle_ref), (nm_sum_in, nm_sum_ref), (cot_in, cot_ref), (xnt_in, xnt_ref), (x_in, x_ref),
            )
        )
    ]

    @pl.when(step == 0)
    def _():
        enter(me)
        work.core_step(FFN_TILE, 0, 0)
        work.core_step(FFN_TILE, 1, 1)
        work.load_step(FFN_TILE, 0, 0)
        dcols[...] = jnp.zeros_like(dcols)
        drows[...] = jnp.zeros_like(drows)
        dgain[...] = jnp.zeros_like(dgain)
        d_small[...] = jnp.zeros_like(d_small)
        for copy in loads:
            copy.start()
        for r in (0, 1):
            work.chip_step(FFN_TILE, r, r)
            work.core_step(FFN_TILE, r + 2, r + 2)
            work.load_step(FFN_TILE, r + 1, r + 1)

    at(step - 6, work.last_step)
    at(step - 4, work.relay_step)
    at(step - 2, work.square_step)
    at(step, work.corner_step)
    at(step + 2, work.chip_step)
    at(step + 3, work.load_step)

    @pl.when(step == 0)
    def _():
        for copy in loads:
            copy.wait()
        turned = merge(small_ref[..., 0:SMALL]).astype(F32).T
        gains[0:1, :] = turned[16:17, :]
        gains[1:2, :] = turned[17:18, :]

        def back(rows, total):
            mid = middle_ref[rows, :]
            scale = lax.rsqrt(jnp.mean(mid * mid, axis=1, keepdims=True) + epsilon)
            normed = mid * scale
            grad = nm_sum_ref[rows, :]
            d_normed = grad * gains[1:2, :]
            d_mid = scale * (d_normed - normed * jnp.mean(d_normed * normed, axis=1, keepdims=True))
            d_mid = d_mid + cot_ref[rows, :].astype(F32)
            gxn[rows, :] = jnp.zeros_like(mid)
            grad_mid_ref[rows, :] = d_mid
            gb_ref[rows, :] = d_mid.astype(BF16)
            gbt_ref[:, rows] = d_mid.T.astype(BF16)
            return total + jnp.sum(grad * normed, axis=0, keepdims=True)

        gains[2:3, :] = row_sums(tokens, back, gains.shape[1])

    @pl.when((step < 2 * HEADS) & (step % 2 == 0))
    def _():
        head = step // 2
        w = merge(w_ref[...])
        grad_mixed = jnp.dot(gb_ref[...], w[:, HEAD_COLS:], preferred_element_type=F32)
        d_out = jnp.dot(gbt_ref[...], mixed_ref[...], preferred_element_type=F32).astype(BF16)
        dw[head % 2, :, :, :, :, pl.ds(HEAD_COLS, DV)] = d_out.reshape(dw.shape[1:5] + (DV,))

        projected = proj_ref[...]
        taps = head_taps(small_ref, head)
        keeps, conv, gate, act, qn, k, value, q_scale, k_scale, cum, rate, seg = head_inputs(
            projected, taps, cols_ref[...], head
        )
        q = qn * DK**-0.5
        cum_row = rows_ref[pl.ds(head, 1), :]
        seg_row = rows_ref[8:9, :]
        gain = gain_ref[...]
        lanes = lane_index((SEQ, 128))
        d_act, d_gain = [], jnp.zeros((1, DV), F32)
        for start in range(0, tokens, SEQ):
            part = slice(start, start + SEQ)
            core, update, inverse = core_ref[0, part, :], upd_ref[0, part, :], inv_ref[0, part, :]
            grad = grad_mixed[part]
            scale = lax.rsqrt(jnp.mean(core * core, axis=1, keepdims=True) + head_epsilon)
            normed = core * scale
            out_gate = projected[part, CONV_COLS:]
            out_sig = sigmoid(out_gate)
            swish = out_gate * out_sig
            dproj[part, CONV_COLS:] = (grad * normed * gain * (out_sig + swish * (1.0 - out_sig))).astype(BF16)
            d_normed = grad * swish
            d_gain = d_gain + jnp.sum(d_normed * normed, axis=0, keepdims=True)
            d_scaled = d_normed * gain
            d_core = scale * (d_scaled - normed * jnp.mean(d_scaled * normed, axis=1, keepdims=True))

            qs, ks, vs, rs = q[part], k[part], value[part], rate[part]
            pair = decays(seg[part], seg_row[:, part], cum[part], cum_row[:, part])
            key_dots = dot3(ks, ks, NT)
            query_dots = dot3(qs, ks, NT)
            d_scores = dot3(d_core, update, NT)
            d_update = dot1(pair * query_dots, d_core, TN)
            solved = dot1(inverse, d_update, TN)
            d_coupling = strict(-dot1(solved, update, NT)) * pair
            d_query_dots = pair * d_scores
            d_key_dots = d_coupling * rs
            weighed = d_coupling * key_dots
            d_spread = d_query_dots * query_dots + weighed * rs
            d_q = dot1(d_query_dots, ks, NN) * DK**-0.5
            d_k = dot1(d_query_dots, qs, TN) + dot1(d_key_dots, ks, NN) + dot1(d_key_dots, ks, TN)
            d_rate = jnp.sum(solved * vs, axis=1, keepdims=True) + jnp.sum(weighed, axis=1, keepdims=True)
            row_sum = jnp.sum(d_spread, axis=1, keepdims=True)
            dcols[part, :] += jnp.where(lanes == head, row_sum, 0.0) + jnp.where(lanes == 8 + head, d_rate, 0.0)
            drows[pl.ds(head, 1), part] = jnp.sum(d_spread, axis=0, keepdims=True)
            d_q_act = q_scale[part] * (d_q - qn[part] * jnp.sum(d_q * qn[part], axis=1, keepdims=True))
            d_k_act = k_scale[part] * (d_k - ks * jnp.sum(d_k * ks, axis=1, keepdims=True))
            d_act.append(jnp.concatenate([d_q_act, d_k_act, rs * solved], axis=1))
        dgain[0:1, :] += d_gain
        d_conv = jnp.concatenate(d_act, axis=0) * (gate + act * (1.0 - gate))
        source = projected[:, :CONV_COLS]
        d_source = d_conv * taps[0:1]
        d_taps = [jnp.sum(d_conv * source, axis=0, keepdims=True)]
        for back in (1, 2, 3):
            kept = d_conv * keeps[back - 1]
            d_source = d_source + pltpu.roll(kept, tokens - back, 0) * taps[back : back + 1]
            d_taps.append(jnp.sum(kept * pltpu.roll(source, back, 0), axis=0, keepdims=True))
        d_taps = jnp.concatenate(d_taps + [jnp.zeros((rows - 4, CONV_COLS), F32)], axis=0).astype(BF16)
        wide = 2 * head
        places = [(0, head), (1, head)] + [(2 + head // 4, wide % 8 + i) for i in (0, 1)]
        for i, (z, p) in enumerate(places):
            d_small[z, p // 2, p % 2, :, SMALL:] = d_taps[:, i * SMALL : (i + 1) * SMALL]
        dproj[:, :CONV_COLS] = d_source.astype(BF16)
        d_proj = dproj[...]
        d_in = jnp.dot(xnt_ref[...], d_proj, preferred_element_type=F32).astype(BF16)
        dw[head % 2, :, :, :, :, pl.ds(0, HEAD_COLS)] = d_in.reshape(dw.shape[1:5] + (HEAD_COLS,))
        gxn[...] += lax.dot_general(d_proj, w[:, :HEAD_COLS], (NT, ((), ())), preferred_element_type=F32)

    @pl.when(step == 2 * HEADS - 1)
    def _():
        small = merge(small_ref[..., 0:SMALL])
        lanes = lane_index((SEQ, 128))
        padded = jnp.concatenate([drows[...], jnp.zeros((120, tokens), F32)], axis=0).T
        d_logs = jnp.zeros((1, 128), F32)
        d_bias = jnp.zeros((1, 128), F32)
        d_logits = []
        for start in range(0, tokens, SEQ):
            part = slice(start, start + SEQ)
            d_cum = jnp.where(lanes < 8, dcols[part, :], 0.0) - padded[part]
            d_decay = triangle_sum(d_cum, TN)
            d_logit = jnp.where(lanes < 8, d_decay, dcols[part, :]) * factor_ref[part, :]
            d_logs = d_logs + jnp.sum(jnp.where(lanes < 8, d_decay * logs_ref[part, :], 0.0), axis=0, keepdims=True)
            d_bias = d_bias + jnp.sum(jnp.where(lanes < 8, d_logit, 0.0), axis=0, keepdims=True)
            d_logits.append(d_logit.astype(BF16))
        d_logits = jnp.concatenate(d_logits, axis=0)
        value_ref[...] = jnp.concatenate(
            [d_logs, d_bias, dgain[0:1, :128], dgain[0:1, 128:], jnp.zeros((4, 128), F32)], axis=0
        )
        gxn[...] += lax.dot_general(d_logits, small, (NT, ((), ())), preferred_element_type=F32)

        def back(at_rows, total):
            x = x_ref[at_rows, :].astype(F32)
            scale = lax.rsqrt(jnp.mean(x * x, axis=1, keepdims=True) + epsilon)
            normed = x * scale
            grad = gxn[at_rows, :]
            d_normed = grad * gains[0:1, :]
            d_x = scale * (d_normed - normed * jnp.mean(d_normed * normed, axis=1, keepdims=True))
            grad_mid_ref[at_rows, :] = d_x + grad_mid_ref[at_rows, :]
            return total + jnp.sum(grad * normed, axis=0, keepdims=True)

        total = row_sums(tokens, back, gxn.shape[1])
        line = lax.broadcasted_iota(jnp.int32, (128, total.shape[1]), 0)
        lines = jnp.where(line == 16, total, jnp.where(line == 17, gains[2:3, :], 0.0))
        own = jnp.dot(xnt_ref[...], d_logits, preferred_element_type=F32) + lines.T
        d_small[:, :, :, :, 0:SMALL] = own.astype(BF16).reshape(d_small.shape[:4] + (SMALL,))

    flush = pltpu.make_async_copy(grad_mid_ref, input_grad_out, flush_sem)
    pl.when(step == 2 * HEADS)(flush.start)
    pl.when(step == pl.num_programs(0) - 1)(flush.wait)

    at(step + 4, work.core_step)
    for number in range(len(Total.bits) + 1):
        pl.when(step == 2 * HEADS + number)(lambda number=number: small_sum.step(number))


def backward(planes, dwf, middle, nm_sum, cot, xnt, w, proj, mixed, inv, upd, core, small, cols, seq_rows, logs, factor,
             gain, x):
    tokens, width = middle.shape
    rows = small.shape[4]
    tiles = dwf.shape[1] // (3 * TILE)
    chunks = FIRST + 2 * HEADS
    assert tiles == FIRST + HEADS - 1
    hbm = pl.BlockSpec(memory_space=pl.ANY)
    head = head_step
    save = pl.BlockSpec((1, tokens, SEQ), lambda i: (head(i), 0, 0))
    shape = jax.ShapeDtypeStruct
    widest = HEAD_COLS + DV
    depth = Scatter.depths
    outs = [
        ((tokens, width), F32),
        ((1, rows), F32),
        ((rows, HEADS * HEAD_COLS), F32),
        ((16, rows), F32),
        ((4, SMALL), F32),
        ((1, HEADS), F32),
        ((1, HEADS), F32),
        ((1, DV), F32),
        ((rows, HEADS * DV), F32),
        ((1, rows), F32),
        ((rows, 2 * tiles * TILE), F32),
        ((rows, tiles * TILE), F32),
    ]
    return pl.pallas_call(
        partial(backward_body, planes, tiles, chunks),
        grid=(chunks + 6,),
        in_specs=[
            hbm,
            hbm,
            hbm,
            hbm,
            hbm,
            hbm,
            pl.BlockSpec((planes, 2, 2, 2, rows, widest), lambda i: (0, 0, 0, 0, 0, head(i))),
            pl.BlockSpec((tokens, HEAD_COLS), lambda i: (0, head(i))),
            pl.BlockSpec((tokens, DV), lambda i: (0, head(i))),
            save,
            save,
            save,
        ]
        + [once(a.shape) for a in (small, cols, seq_rows, logs, factor, gain)],
        out_specs=[hbm] + [once(o[0]) for o in outs[1:]],
        out_shape=[shape(*o) for o in outs],
        scratch_shapes=[
            pltpu.VMEM((tokens, width), F32),
            pltpu.VMEM((tokens, width), F32),
            pltpu.VMEM((tokens, width), BF16),
            pltpu.VMEM((width, tokens), BF16),
            pltpu.VMEM((tokens, width), BF16),
            pltpu.SemaphoreType.DMA((5,)),
            pltpu.SemaphoreType.DMA,
            pltpu.VMEM((width, tokens), BF16),
            pltpu.VMEM((8, width), F32),
            pltpu.VMEM((2, planes, 4, 2, rows, widest), BF16),
            pltpu.VMEM((planes, 4, 2, rows, 2 * SMALL), BF16),
            pltpu.VMEM((tokens, 128), F32),
            pltpu.VMEM((HEADS, tokens), F32),
            pltpu.VMEM((8, DV), F32),
            pltpu.VMEM((tokens, HEAD_COLS), BF16),
            pltpu.VMEM((8, 128), F32),
            pltpu.VMEM((depth[B_CORE], planes, 4, rows, widest), BF16),
            pltpu.VMEM((depth[B_KEEP], planes, 4, rows, 3 * TILE), BF16),
            pltpu.VMEM((depth[B_SUMS], planes, 4, rows, widest), BF16),
            pltpu.VMEM((depth[B_XY], planes, rows, HEAD_COLS), BF16),
            pltpu.VMEM((depth[B_X], planes, rows, HEAD_COLS), BF16),
            pltpu.VMEM((depth[B_Y], planes, rows, HEAD_COLS), BF16),
            pltpu.VMEM((depth[B_Z], 3, rows, HEAD_COLS), BF16),
            pltpu.VMEM((depth[B_TWO_Z], 3, 4, rows, DV), BF16),
            pltpu.VMEM((depth[B_TWO], 3, rows, DV), BF16),
            pltpu.VMEM((len(Total.bits), 8, 128), F32),
            pltpu.VMEM((len(Total.bits), 8, 128), F32),
            pltpu.SemaphoreType.DMA((chunks,)),
            pltpu.SemaphoreType.DMA((chunks, Scatter.copies)),
            pltpu.SemaphoreType.DMA((chunks, Scatter.copies)),
            pltpu.SemaphoreType.DMA((len(Total.bits),)),
            pltpu.SemaphoreType.DMA((len(Total.bits),)),
        ],
        compiler_params=pltpu.CompilerParams(
            collective_id=1, has_side_effects=True, vmem_limit_bytes=63 * MIB
        ),
        name="backward",
    )(
        dwf.reshape(planes, 4, 2, rows, dwf.shape[1]), middle, nm_sum, cot, xnt, x, w, proj, mixed, inv, upd, core, small,
        cols, seq_rows, logs, factor, gain,
    )


def hand_over_body(count, *refs):
    for source, target in zip(refs[:count], refs[count:]):
        target[...] = source[...]


def hand_over(arrays, steps=4):
    specs = []
    for a in arrays:
        rows, cols = a.shape
        if rows % (32 * steps) == 0:
            specs.append(pl.BlockSpec((rows // steps, cols), lambda i: (i, 0)))
        elif cols % (128 * steps) == 0:
            specs.append(pl.BlockSpec((rows, cols // steps), lambda i: (0, i)))
        else:
            specs.append(pl.BlockSpec((rows, cols), lambda i: (0, 0)))
    return pl.pallas_call(
        partial(hand_over_body, len(arrays)),
        grid=(steps,),
        in_specs=specs,
        out_specs=specs,
        out_shape=[jax.ShapeDtypeStruct(a.shape, a.dtype) for a in arrays],
        compiler_params=pltpu.CompilerParams(vmem_limit_bytes=60 * MIB),
        name="hand_over",
    )(*arrays)


def mixer_fwd_body(xn_ref, w_ref, taps_ref, cols_ref, rows_ref, gain_ref, proj_ref, mixed_ref, inv_ref, upd_ref, core_ref):
    head = pl.program_id(0)
    tokens = xn_ref.shape[0]
    projected = jnp.dot(xn_ref[...], w_ref[...], preferred_element_type=F32)
    proj_ref[...] = projected
    _, _, _, _, q, k, value, _, _, cum, rate, seg = head_inputs(
        projected, taps_ref[...], cols_ref[...], head
    )
    q = q * DK**-0.5
    cum_row = rows_ref[pl.ds(head, 1), :]
    seg_row = rows_ref[8:9, :]
    parts = [slice(s, s + SEQ) for s in range(0, tokens, SEQ)]
    scores, couplings = [], []
    for part in parts:
        pair = decays(seg[part], seg_row[:, part], cum[part], cum_row[:, part])
        key_dots = dot3(k[part], k[part], NT)
        scores.append(pair * dot3(q[part], k[part], NT))
        couplings.append(strict(pair * key_dots) * rate[part])
    inverses = unit_inverses(couplings)
    for i, part in enumerate(parts):
        update = dot3(inverses[i], rate[part] * value[part], NN)
        core = dot3(scores[i], update, NN)
        inv_ref[0, part, :] = inverses[i].astype(BF16)
        upd_ref[0, part, :] = update
        core_ref[0, part, :] = core
        scale = lax.rsqrt(jnp.mean(core * core, axis=1, keepdims=True) + head_epsilon)
        out_gate = projected[part, CONV_COLS:]
        mixed_ref[part, :] = (core * scale * gain_ref[...] * (out_gate * sigmoid(out_gate))).astype(BF16)


def mixer_fwd(xn, w, taps, cols, rows, gain):
    tokens, width = xn.shape
    const = lambda h: (0, 0)
    by_head = lambda h: (0, h)
    save = pl.BlockSpec((1, tokens, SEQ), lambda h: (h, 0, 0))
    return pl.pallas_call(
        mixer_fwd_body,
        grid=(HEADS,),
        in_specs=[
            pl.BlockSpec((tokens, width), const),
            pl.BlockSpec((width, HEAD_COLS), by_head),
            pl.BlockSpec((4, CONV_COLS), by_head),
            pl.BlockSpec(cols.shape, const),
            pl.BlockSpec(rows.shape, const),
            pl.BlockSpec((1, DV), const),
        ],
        out_specs=[
            pl.BlockSpec((tokens, HEAD_COLS), by_head),
            pl.BlockSpec((tokens, DV), by_head),
            save,
            save,
            save,
        ],
        out_shape=[
            jax.ShapeDtypeStruct((tokens, HEADS * HEAD_COLS), F32),
            jax.ShapeDtypeStruct((tokens, HEADS * DV), BF16),
            jax.ShapeDtypeStruct((HEADS, tokens, SEQ), BF16),
            jax.ShapeDtypeStruct((HEADS, tokens, DV), F32),
            jax.ShapeDtypeStruct((HEADS, tokens, DV), F32),
        ],
        compiler_params=pltpu.CompilerParams(vmem_limit_bytes=56 * MIB),
        name="mixer_fwd",
    )(xn, w, taps, cols, rows, gain)


def mixer_bwd_body(
    gb_ref, gbt_ref, xnt_ref, wo_ref, w_ref, proj_ref, mixed_ref, inv_ref, upd_ref, core_ref,
    taps_ref, cols_ref, rows_ref, gain_ref,
    dw_ref, dwo_ref, gxn_ref, dcols_ref, drows_ref, dtaps_ref, dgain_ref, dproj_ref,
):
    head = pl.program_id(0)
    tokens = gb_ref.shape[0]

    @pl.when(head == 0)
    def _():
        gxn_ref[...] = jnp.zeros_like(gxn_ref)
        dcols_ref[...] = jnp.zeros_like(dcols_ref)
        drows_ref[...] = jnp.zeros_like(drows_ref)
        dgain_ref[...] = jnp.zeros_like(dgain_ref)

    grad_mixed = jnp.dot(gb_ref[...], wo_ref[...], preferred_element_type=F32)
    dwo_ref[...] = jnp.dot(gbt_ref[...], mixed_ref[...], preferred_element_type=F32).astype(BF16)

    projected = proj_ref[...]
    taps = taps_ref[...]
    keep, conv, gate, act, qn, k, value, q_scale, k_scale, cum, rate, seg = head_inputs(
        projected, taps, cols_ref[...], head
    )
    q = qn * DK**-0.5
    cum_row = rows_ref[pl.ds(head, 1), :]
    seg_row = rows_ref[8:9, :]
    gain = gain_ref[...]
    lanes = lax.broadcasted_iota(jnp.int32, (SEQ, 128), 1)
    d_act, d_gain = [], jnp.zeros((1, DV), F32)
    for start in range(0, tokens, SEQ):
        part = slice(start, start + SEQ)
        core, update, inverse = core_ref[0, part, :], upd_ref[0, part, :], inv_ref[0, part, :]
        grad = grad_mixed[part]
        scale = lax.rsqrt(jnp.mean(core * core, axis=1, keepdims=True) + head_epsilon)
        normed = core * scale
        out_gate = projected[part, CONV_COLS:]
        out_sig = sigmoid(out_gate)
        swish = out_gate * out_sig
        dproj_ref[part, CONV_COLS:] = (grad * normed * gain * (out_sig + swish * (1.0 - out_sig))).astype(BF16)
        d_normed = grad * swish
        d_gain = d_gain + jnp.sum(d_normed * normed, axis=0, keepdims=True)
        d_scaled = d_normed * gain
        d_core = scale * (d_scaled - normed * jnp.mean(d_scaled * normed, axis=1, keepdims=True))

        qs, ks, vs, rs = q[part], k[part], value[part], rate[part]
        pair = decays(seg[part], seg_row[:, part], cum[part], cum_row[:, part])
        key_dots = dot3(ks, ks, NT)
        query_dots = dot3(qs, ks, NT)
        d_scores = dot3(d_core, update, NT)
        d_update = dot1(pair * query_dots, d_core, TN)
        solved = dot1(inverse, d_update, TN)
        d_coupling = strict(-dot1(solved, update, NT)) * pair
        d_query_dots = pair * d_scores
        d_key_dots = d_coupling * rs
        weighed = d_coupling * key_dots
        d_spread = d_query_dots * query_dots + weighed * rs
        d_q = dot1(d_query_dots, ks, NN) * DK**-0.5
        d_k = dot1(d_query_dots, qs, TN) + dot1(d_key_dots, ks, NN) + dot1(d_key_dots, ks, TN)
        d_rate = jnp.sum(solved * vs, axis=1, keepdims=True) + jnp.sum(weighed, axis=1, keepdims=True)
        row_sum = jnp.sum(d_spread, axis=1, keepdims=True)
        dcols_ref[part, :] += jnp.where(lanes == head, d_rate, 0.0) + jnp.where(lanes == 8 + head, row_sum, 0.0)
        drows_ref[pl.ds(head, 1), part] = jnp.sum(d_spread, axis=0, keepdims=True)
        d_q_act = q_scale[part] * (d_q - qn[part] * jnp.sum(d_q * qn[part], axis=1, keepdims=True))
        d_k_act = k_scale[part] * (d_k - ks * jnp.sum(d_k * ks, axis=1, keepdims=True))
        d_act.append(jnp.concatenate([d_q_act, d_k_act, rs * solved], axis=1))
    dgain_ref[...] += d_gain
    d_conv = jnp.concatenate(d_act, axis=0) * (gate + act * (1.0 - gate))
    source = projected[:, :CONV_COLS]
    d_source = d_conv * taps[0:1]
    d_taps = [jnp.sum(d_conv * source, axis=0, keepdims=True)]
    for back in (1, 2, 3):
        kept = d_conv * keep[back - 1]
        d_source = d_source + pltpu.roll(kept, tokens - back, 0) * taps[back : back + 1]
        d_taps.append(jnp.sum(kept * pltpu.roll(source, back, 0), axis=0, keepdims=True))
    dtaps_ref[...] = jnp.concatenate(d_taps, axis=0)
    dproj_ref[:, :CONV_COLS] = d_source.astype(BF16)
    d_proj = dproj_ref[...]
    dw_ref[...] = jnp.dot(xnt_ref[...], d_proj, preferred_element_type=F32).astype(BF16)
    gxn_ref[...] += lax.dot_general(d_proj, w_ref[...], (NT, ((), ())), preferred_element_type=F32)


def mixer_bwd(gb, gbt, xnt, wo, w, proj, mixed, inv, upd, core, taps, cols, rows, gain):
    tokens, width = gb.shape
    const = lambda h: (0, 0)
    by_head = lambda h: (0, h)
    save = pl.BlockSpec((1, tokens, SEQ), lambda h: (h, 0, 0))
    return pl.pallas_call(
        mixer_bwd_body,
        grid=(HEADS,),
        in_specs=[
            pl.BlockSpec((tokens, width), const),
            pl.BlockSpec((width, tokens), const),
            pl.BlockSpec((width, tokens), const),
            pl.BlockSpec((width, DV), by_head),
            pl.BlockSpec((width, HEAD_COLS), by_head),
            pl.BlockSpec((tokens, HEAD_COLS), by_head),
            pl.BlockSpec((tokens, DV), by_head),
            save,
            save,
            save,
            pl.BlockSpec((4, CONV_COLS), by_head),
            pl.BlockSpec(cols.shape, const),
            pl.BlockSpec(rows.shape, const),
            pl.BlockSpec((1, DV), const),
        ],
        out_specs=[
            pl.BlockSpec((width, HEAD_COLS), by_head),
            pl.BlockSpec((width, DV), by_head),
            pl.BlockSpec((tokens, width), const),
            pl.BlockSpec((tokens, 128), const),
            pl.BlockSpec((HEADS, tokens), const),
            pl.BlockSpec((4, CONV_COLS), by_head),
            pl.BlockSpec((1, DV), const),
        ],
        out_shape=[
            jax.ShapeDtypeStruct((width, HEADS * HEAD_COLS), BF16),
            jax.ShapeDtypeStruct((width, HEADS * DV), BF16),
            jax.ShapeDtypeStruct((tokens, width), F32),
            jax.ShapeDtypeStruct((tokens, 128), F32),
            jax.ShapeDtypeStruct((HEADS, tokens), F32),
            jax.ShapeDtypeStruct((4, HEADS * CONV_COLS), F32),
            jax.ShapeDtypeStruct((1, DV), F32),
        ],
        scratch_shapes=[pltpu.VMEM((tokens, HEAD_COLS), BF16)],
        compiler_params=pltpu.CompilerParams(vmem_limit_bytes=60 * MIB),
        name="mixer_bwd",
    )(gb, gbt, xnt, wo, w, proj, mixed, inv, upd, core, taps, cols, rows, gain)


def ffn_body(nm_ref, nmt_ref, cot_ref, cott_ref, w_ref, dw_ref, out_ref, gnm_ref):
    @pl.when(pl.program_id(0) == 0)
    def _():
        out_ref[...] = jnp.zeros_like(out_ref)
        gnm_ref[...] = jnp.zeros_like(gnm_ref)

    w = w_ref[...]
    gate_up = jnp.dot(nm_ref[...], w[:, : 2 * TILE], preferred_element_type=F32)
    gate, up = gate_up[:, :TILE], gate_up[:, TILE:]
    sig = sigmoid(gate)
    swish = gate * sig
    hidden = (swish * up).astype(BF16)
    grad_hidden = jnp.dot(cot_ref[...], w[:, 2 * TILE :], preferred_element_type=F32)
    grad_gate = grad_hidden * up * (sig + swish * (1.0 - sig))
    grad_up = grad_hidden * swish
    grad_low = jnp.concatenate([grad_gate, grad_up], axis=1).astype(BF16)
    out_ref[...] += lax.dot_general(hidden, w[:, 2 * TILE :], (NT, ((), ())), preferred_element_type=F32)
    gnm_ref[...] += lax.dot_general(grad_low, w[:, : 2 * TILE], (NT, ((), ())), preferred_element_type=F32)
    dw_ref[:, : 2 * TILE] = jnp.dot(nmt_ref[...], grad_low, preferred_element_type=F32).astype(BF16)
    dw_ref[:, 2 * TILE :] = jnp.dot(cott_ref[...], hidden, preferred_element_type=F32).astype(BF16)


def ffn(nm, nmt, cot, cott, w):
    tokens, width = nm.shape
    tiles = w.shape[1] // (3 * TILE)
    const = lambda t: (0, 0)
    by_tile = lambda t: (0, t)
    return pl.pallas_call(
        ffn_body,
        grid=(tiles,),
        in_specs=[
            pl.BlockSpec((tokens, width), const),
            pl.BlockSpec((width, tokens), const),
            pl.BlockSpec((tokens, width), const),
            pl.BlockSpec((width, tokens), const),
            pl.BlockSpec((width, 3 * TILE), by_tile),
        ],
        out_specs=[
            pl.BlockSpec((width, 3 * TILE), by_tile),
            pl.BlockSpec((tokens, width), const),
            pl.BlockSpec((tokens, width), const),
        ],
        out_shape=[
            jax.ShapeDtypeStruct((width, tiles * 3 * TILE), BF16),
            jax.ShapeDtypeStruct((tokens, width), F32),
            jax.ShapeDtypeStruct((tokens, width), F32),
        ],
        compiler_params=pltpu.CompilerParams(vmem_limit_bytes=48 * MIB),
        name="ffn",
    )(nm, nmt, cot, cott, w)


def rms_scale(values):
    return lax.rsqrt(jnp.mean(values * values, axis=-1, keepdims=True) + epsilon)


def rms_back(grad, values, scale, gain):
    normed = values * scale
    d_normed = grad * gain
    d_values = scale * (d_normed - normed * jnp.mean(d_normed * normed, axis=-1, keepdims=True))
    return d_values, jnp.sum(grad * normed, axis=0)


def by_head(parts):
    shaped = [p.reshape(p.shape[0], HEADS, -1) for p in parts]
    return jnp.concatenate(shaped, axis=2).reshape(parts[0].shape[0], -1)


def from_head(values, sizes):
    shaped = values.reshape(values.shape[0], HEADS, -1)
    ends = [sum(sizes[: i + 1]) for i in range(len(sizes))]
    cuts = [shaped[:, :, e - s : e].reshape(values.shape[0], -1) for s, e in zip(sizes, ends)]
    return jnp.concatenate(cuts, axis=1)


def split_heads(values):
    key = HEADS * DK
    val = HEADS * DV
    edges = [0, key, 2 * key, 2 * key + val, 2 * key + 2 * val]
    return [values[:, a:b] for a, b in zip(edges[:-1], edges[1:]) if b <= values.shape[1]]


def plain_block(
    devices, tokens, segment_ids, cotangent, norm1_gain, mixer_in, decay_in, conv_weight, decay_log, decay_bias,
    head_gain, mixer_out, norm2_gain, ffn_in, ffn_out,
):
    rows, width = decay_in.shape[0], tokens.shape[1]
    count = tokens.shape[0]
    hidden = ffn_out.shape[0]
    tiles = hidden // TILE

    low = lambda v: v.astype(BF16)
    shard_mixer = by_head(split_heads(low(mixer_in)))
    conv_cols = conv_weight.shape[1]
    shard_small = jnp.concatenate(
        [low(decay_in), low(norm1_gain)[:, None], low(norm2_gain)[:, None], low(conv_weight).reshape(rows, -1)], axis=1
    )
    shard_small = jnp.pad(shard_small, ((0, 0), (0, SMALL - shard_small.shape[1])))
    shard_out = low(mixer_out).T
    ffn_low = low(ffn_in)
    pieces = [ffn_low[:, :hidden], ffn_low[:, hidden:], low(ffn_out).T]
    shard_ffn = jnp.concatenate([p.reshape(rows, tiles, TILE) for p in pieces], axis=2).reshape(rows, -1)
    shards = [shard_small, shard_mixer, shard_out, shard_ffn]

    x = tokens.astype(F32)
    scale1 = rms_scale(x)
    full_small, full_mixer, full_out, full_ffn = [lax.all_gather(s, "dp", axis=0, tiled=True) for s in shards]

    decay_full = full_small[:, :16]
    gain1 = full_small[:, 16].astype(F32)
    gain2 = full_small[:, 17].astype(F32)
    taps = full_small[:, 18 : 18 + 16].reshape(devices, 4, conv_cols)
    taps = jnp.moveaxis(taps, 0, 1).reshape(4, -1).astype(F32)
    taps = by_head(split_heads(taps))

    normed_in = low(x * scale1 * gain1)
    logits = jnp.dot(normed_in, decay_full, preferred_element_type=F32)
    shifted = logits[:, :HEADS] + decay_bias
    log_decay = -jnp.exp(decay_log) * jax.nn.softplus(shifted)
    rate = jax.nn.sigmoid(logits[:, HEADS:])
    sequences = count // SEQ
    lower = jnp.tril(jnp.ones((SEQ, SEQ), F32))
    cumulative = jnp.einsum(
        "ij,sjh->sih", lower, log_decay.reshape(sequences, SEQ, HEADS), precision=lax.Precision.HIGHEST
    ).reshape(count, HEADS)
    position = jnp.arange(count) % SEQ
    keeps = []
    for back in (1, 2, 3):
        earlier = jnp.pad(segment_ids[:-back], (back, 0), constant_values=-1)
        keeps.append(((earlier == segment_ids) & (position >= back)).astype(F32)[:, None])
    segment = segment_ids.astype(F32)
    cols = jnp.concatenate([cumulative, rate] + keeps + [segment[:, None]], axis=1)
    cols = jnp.pad(cols, ((0, 0), (0, 128 - cols.shape[1])))
    seq_rows = jnp.concatenate([cumulative.T, segment[None], jnp.zeros((7, count), F32)], axis=0)
    gain_row = head_gain[None]

    proj, mixed, inverse, update, core = mixer_fwd(normed_in, full_mixer, taps, cols, seq_rows, gain_row)

    middle = x + lax.dot_general(mixed, full_out, (NT, ((), ())), preferred_element_type=F32)
    scale2 = rms_scale(middle)
    normed_mid = low(middle * scale2 * gain2)
    dw_ffn, ffn_sum, grad_nm = ffn(normed_mid, normed_mid.T, cotangent, cotangent.T, full_ffn)
    output = low(middle + ffn_sum)

    d_middle, d_gain2 = rms_back(grad_nm, middle, scale2, gain2)
    grad_middle = d_middle + cotangent.astype(F32)
    branch = low(grad_middle)
    dw_mixer, dw_out, grad_xn, d_cols, d_rows, d_taps, d_gain = mixer_bwd(
        branch, branch.T, normed_in.T, full_out, full_mixer, proj, mixed, inverse, update, core,
        taps, cols, seq_rows, gain_row,
    )

    d_cum = d_cols[:, 8:16] - d_rows.T
    d_decay = jnp.einsum(
        "ji,sjh->sih", lower, d_cum.reshape(sequences, SEQ, HEADS), precision=lax.Precision.HIGHEST
    ).reshape(count, HEADS)
    d_shifted = -d_decay * jnp.exp(decay_log) * jax.nn.sigmoid(shifted)
    d_rate = d_cols[:, :8] * rate * (1.0 - rate)
    d_logits = low(jnp.concatenate([d_shifted, d_rate], axis=1))
    grad_xn = grad_xn + lax.dot_general(d_logits, decay_full, (NT, ((), ())), preferred_element_type=F32)
    d_x, d_gain1 = rms_back(grad_xn, x, scale1, gain1)
    input_grad = d_x + grad_middle

    d_decay_in = lax.dot_general(normed_in, d_logits, (TN, ((), ())), preferred_element_type=F32)
    d_taps = from_head(d_taps, [DK, DK, DV])
    d_taps = jnp.moveaxis(d_taps.reshape(4, devices, conv_cols), 1, 0).reshape(width, -1)
    dw_small = jnp.concatenate([d_decay_in, d_gain1[:, None], d_gain2[:, None], d_taps], axis=1)
    dw_small = low(jnp.pad(dw_small, ((0, 0), (0, SMALL - dw_small.shape[1]))))
    shared = jnp.concatenate([jnp.sum(d_decay * log_decay, axis=0), jnp.sum(d_shifted, axis=0), d_gain[0]])

    own_ffn, own_out, own_mixer, own_small = [
        lax.psum_scatter(g.astype(F32), "dp", scatter_dimension=0, tiled=True)
        for g in (dw_ffn, dw_out, dw_mixer, dw_small)
    ]
    shared = lax.psum(shared, "dp")

    own_tiles = own_ffn.reshape(rows, tiles, 3, TILE)
    ffn_in_grad = jnp.concatenate([own_tiles[:, :, i].reshape(rows, hidden) for i in (0, 1)], axis=1)
    ffn_out_grad = own_tiles[:, :, 2].reshape(rows, hidden).T
    return (
        output,
        input_grad,
        own_small[:, 16],
        from_head(own_mixer, [DK, DK, DV, DV]),
        own_small[:, :16],
        own_small[:, 18 : 18 + 16].reshape(4, conv_cols),
        shared[:HEADS],
        shared[HEADS : 2 * HEADS],
        shared[2 * HEADS : 2 * HEADS + DV],
        own_out.T,
        own_small[:, 17],
        ffn_in_grad,
        ffn_out_grad,
    )


def direct_block(
    devices, tokens, segment_ids, cotangent, norm1_gain, mixer_in, decay_in, conv_weight, decay_log, decay_bias,
    head_gain, mixer_out, norm2_gain, ffn_in, ffn_out,
):
    planes = devices // 8
    gain = head_gain[None]
    masters = [
        mixer_in, mixer_out.T, ffn_in, ffn_out.T, decay_in.T, norm1_gain[None], norm2_gain[None], conv_weight,
    ]
    (
        _, full_heads, _, small, xnt, cols, seq_rows, logs, factor, middle, proj, mixed, inverse, update, core, dwf,
        output, nm_sum,
    ) = forward(
        planes, masters, tokens, cotangent, segment_ids[None], decay_log[None], decay_bias[None], gain
    )
    results = backward(
        planes, dwf, middle, nm_sum, cotangent, xnt, full_heads, proj, mixed, inverse, update, core, small, cols,
        seq_rows, logs, factor, gain, tokens,
    )
    (
        output, input_grad, d_gain1, d_mixer_in, d_decay_in, d_conv, d_log, d_bias, d_gain, d_mixer_out, d_gain2, d_ffn_in,
        d_ffn_out,
    ) = hand_over([output, *results])
    return (
        output, input_grad, d_gain1[0], d_mixer_in, d_decay_in.T, d_conv, d_log[0], d_bias[0], d_gain[0], d_mixer_out.T,
        d_gain2[0], d_ffn_in, d_ffn_out.T,
    )


def on_device(devices, *arguments):
    rows, conv_cols = arguments[4].shape[0], arguments[6].shape[1]
    direct = rows % 16 == 0 and devices == 32 and conv_cols == 128
    return (direct_block if direct else plain_block)(devices, *arguments)


def solution(mesh):
    in_specs = (
        P("dp", None), P("dp"), P("dp", None), P("dp"), P("dp", None), P("dp", None), P(None, "dp"), P(), P(), P(),
        P(None, "dp"), P("dp"), P("dp", None), P(None, "dp"),
    )
    out_specs = (
        P("dp", None), P("dp", None), P("dp"), P("dp", None), P("dp", None), P(None, "dp"), P(), P(), P(),
        P(None, "dp"), P("dp"), P("dp", None), P(None, "dp"),
    )
    return jax.shard_map(
        partial(on_device, mesh.shape["dp"]), mesh=mesh, in_specs=in_specs, out_specs=out_specs, check_vma=False
    )
```

```python
from functools import partial

import jax
import jax.numpy as jnp
from jax import lax
from jax.experimental import pallas as pl
from jax.experimental.pallas import tpu as pltpu
from jax.sharding import PartitionSpec as P

HEADS = 8
DK = 128
DV = 256
SEQ = 256
HEAD_COLS = 2 * DK + 2 * DV
CONV_COLS = 2 * DK + DV
TILE = 256
SMALL = 128
F32 = jnp.float32
BF16 = jnp.bfloat16
MESH = pl.DeviceIdType.MESH
MIB = 1 << 20
epsilon = 1e-06
head_epsilon = 0.001

NN = ((1,), (0,))
NT = ((1,), (1,))
TN = ((0,), (0,))


def dot1(left, right, dims):
    return lax.dot_general(
        left.astype(BF16), right.astype(BF16), (dims, ((), ())), preferred_element_type=F32
    )


def split(value):
    high = value.astype(BF16)
    return high, (value - high.astype(F32)).astype(BF16)


def dot3(left, right, dims):
    lh, ll = split(left)
    rh, rl = split(right)
    return dot1(lh, rh, dims) + (dot1(lh, rl, dims) + dot1(ll, rh, dims))


def dot_high(left, right, dims):
    rh, rl = split(right)
    return dot1(left, rh, dims) + dot1(left, rl, dims)


def sigmoid(value):
    return 1.0 / (1.0 + jnp.exp(-value))


def grid_of(size):
    rows = lax.broadcasted_iota(jnp.int32, (size, size), 0)
    cols = lax.broadcasted_iota(jnp.int32, (size, size), 1)
    return rows, cols


def unit_inverses(couplings):
    half = couplings[0].shape[0] // 2
    rows, cols = grid_of(half)
    apart = rows ^ cols
    eye = jnp.where(apart == 0, 1.0, 0.0)
    corners = [a[s : s + half, s : s + half] for a in couplings for s in (0, half)]
    lows = [a.astype(BF16) for a in corners]
    inverses = [eye - jnp.where(apart < 2, a, 0.0) for a in corners]
    rounded = [inv.astype(BF16) for inv in inverses]
    block = 2
    while block < half:
        here = jnp.where((apart >= block) & (apart < 2 * block), 1.0, 0.0).astype(BF16)
        firsts = [dot1(low * here, inv, NN) for low, inv in zip(lows, rounded)]
        added = [dot1(inv, first, NN) for inv, first in zip(rounded, firsts)]
        inverses = [inv - new for inv, new in zip(inverses, added)]
        rounded = [inv - new.astype(BF16) for inv, new in zip(rounded, added)]
        block *= 2
    results = []
    for i, a in enumerate(couplings):
        first, second = inverses[2 * i], inverses[2 * i + 1]
        below = -dot1(rounded[2 * i + 1], dot1(a[half:, :half], rounded[2 * i], NN), NN)
        top = jnp.concatenate([first, jnp.zeros_like(first)], axis=1)
        results.append(jnp.concatenate([top, jnp.concatenate([below, second], axis=1)], axis=0))
    return results


def pick_lane(columns, lane):
    at = lax.broadcasted_iota(jnp.int32, columns.shape, 1)
    return jnp.sum(jnp.where(at == lane, columns, 0.0), axis=1, keepdims=True)


def conv_of(values, taps, keep):
    total = values * taps[0:1]
    for back in (1, 2, 3):
        total = total + pltpu.roll(values, back, 0) * keep[back - 1] * taps[back : back + 1]
    return total


def decays(seg_col, seg_row, cum_col, cum_row):
    rows, cols = grid_of(SEQ)
    linked = (seg_col == seg_row) & (rows >= cols)
    return jnp.where(linked, jnp.exp(jnp.where(linked, cum_col - cum_row, 0.0)), 0.0)


def strict(value):
    rows, cols = grid_of(SEQ)
    return jnp.where(rows > cols, value, 0.0)


def head_inputs(projected, taps, cols, head):
    keep = [pick_lane(cols, 16 + i) for i in range(3)]
    conv = conv_of(projected[:, :CONV_COLS], taps, keep)
    gate = sigmoid(conv)
    act = conv * gate
    q_act, k_act, value = act[:, :DK], act[:, DK : 2 * DK], act[:, 2 * DK :]
    q_scale = lax.rsqrt(jnp.sum(q_act * q_act, axis=1, keepdims=True) + epsilon)
    k_scale = lax.rsqrt(jnp.sum(k_act * k_act, axis=1, keepdims=True) + epsilon)
    cum = pick_lane(cols, head)
    rate = pick_lane(cols, 8 + head)
    seg = pick_lane(cols, 19)
    return keep, conv, gate, act, q_act * q_scale, k_act * k_scale, value, q_scale, k_scale, cum, rate, seg


def flip(number, bit):
    return number + bit - 2 * bit * ((number // bit) % 2)


def enter(me, before=lambda: None):
    barrier = pltpu.get_barrier_semaphore()
    partners = [flip(me, bit) for bit in (1, 2, 4, 8, 16)]
    for other in partners:
        pl.semaphore_signal(barrier, inc=1, device_id=(other,), device_id_type=MESH)
    before()
    pl.semaphore_wait(barrier, len(partners))


def span(k, width, start, size):
    first = k * width + start
    return pl.ds(first if isinstance(first, int) else pl.multiple_of(first, 128), size)


def remote(source, target, send_sem, recv_sem, other):
    return pltpu.make_async_remote_copy(
        src_ref=source, dst_ref=target, send_sem=send_sem, recv_sem=recv_sem,
        device_id=(other,), device_id_type=MESH,
    )


(
    G_NEAR, G_FAR, G_RELAY, G_X, G_Y, G_CORNER_Y, G_CORNER_X, G_CORE_OWN,
    G_CORE_OTHER, G_TWO_X, G_TWO_Y, G_TWO_CORNER, G_TWO_NEAR, G_TWO_FAR, G_TWO_RELAY, G_TWO_CORE,
) = range(16)
(
    S_CORE, S_XY_X, S_XY_Y, S_X_EARLY, S_X_LATE, S_Y_EARLY, S_Y_LATE, S_RELAY,
    S_NEAR, S_FAR, S_TWO_RELAY, S_TWO_NEAR, S_TWO_FAR, S_TWO_XY, S_TWO_X, S_TWO_Y,
) = range(16)
B_CORE, B_KEEP, B_SUMS, B_XY, B_X, B_Y, B_Z, B_TWO_Z, B_TWO = range(9)
HEAD, FFN_TILE, SMALLS = range(3)


SHAPES = {
    HEAD: (HEAD_COLS + DV, HEAD_COLS, HEAD_COLS // 2),
    FFN_TILE: (3 * TILE, 5 * TILE // 2, 3 * TILE // 2),
    SMALLS: (2 * SMALL, 2 * SMALL, SMALL),
}


class Gather:
    copies = 16

    def __init__(self, me, kinds, local_sem, send_sem, recv_sem):
        self.me, self.kinds = me, kinds
        self.local_sem, self.send_sem, self.recv_sem = local_sem, send_sem, recv_sem
        self.z, self.y, self.x, self.core = me // 8, (me // 4) % 2, (me // 2) % 2, me % 2

    def local(self, kind, k):
        shard, full, base = self.kinds[kind]
        width = SHAPES[kind][0]
        cols = span(k, width, 0, width)
        return pltpu.make_async_copy(
            shard.at[:, cols], full.at[self.z, self.y, self.x, self.core, :, cols], self.local_sem.at[base + k]
        )

    def copy(self, kind, k, name):
        shard, full, base = self.kinds[kind]
        width, part, half = SHAPES[kind]
        one = span(k, width, 0, part)
        two = span(k, width, part, width - part)
        z, y, x, core = self.z, self.y, self.x, self.core
        near, far = flip(z, 1), flip(z, 2)
        here = lambda cols: (shard.at[:, cols], full.at[z, y, x, core, :, cols])
        same = lambda ref: (ref, ref)
        by_y = kind == FFN_TILE
        (source, target), bit = {
            G_NEAR: lambda: (here(one), 8),
            G_FAR: lambda: (here(one), 16),
            G_RELAY: lambda: (same(full.at[far, y, x, core, :, one]), 8),
            G_X: lambda: (same(full.at[:, y, x, core, :, one]), 2),
            G_Y: lambda: (same(full.at[:, y, x, core, :, one]), 4),
            G_CORNER_Y: lambda: (same(full.at[:, y, 1 - x, core, :, span(k, width, 0, half)]), 4),
            G_CORNER_X: lambda: (same(full.at[:, 1 - y, x, core, :, span(k, width, half, part - half)]), 2),
            G_CORE_OWN: lambda: (same(full.at[:, y, :, core, :, one]), 1),
            G_CORE_OTHER: lambda: (same(full.at[:, 1 - y, :, core, :, one]), 1),
            G_TWO_X: lambda: (here(two), 2),
            G_TWO_Y: lambda: (here(two), 4),
            G_TWO_CORNER: lambda: (
                (same(full.at[z, 1 - y, x, core, :, two]), 2)
                if by_y
                else (same(full.at[z, y, 1 - x, core, :, two]), 4)
            ),
            G_TWO_NEAR: lambda: (same(full.at[z, :, :, core, :, two]), 8),
            G_TWO_FAR: lambda: (same(full.at[z, :, :, core, :, two]), 16),
            G_TWO_RELAY: lambda: (same(full.at[far, :, :, core, :, two]), 8),
            G_TWO_CORE: lambda: (same(full.at[:, :, :, core, :, two]), 1),
        }[name]()
        sems = self.send_sem.at[base + k, name], self.recv_sem.at[base + k, name]
        return remote(source, target, *sems, flip(self.me, bit))

    def send(self, kind, k, *names):
        for name in names:
            self.copy(kind, k, name).start()

    def wait(self, kind, k, *names):
        for name in names:
            self.copy(kind, k, name).wait_recv()

    def two(self, kind):
        return SHAPES[kind][0] > SHAPES[kind][1]

    def start(self, kind, k):
        self.local(kind, k).start()
        self.send(kind, k, G_FAR, G_NEAR)
        if self.two(kind):
            self.send(kind, k, G_TWO_X, G_TWO_Y)

    def relay(self, kind, k):
        self.wait(kind, k, G_FAR)
        self.send(kind, k, G_RELAY)
        if self.two(kind):
            self.wait(kind, k, *((G_TWO_Y,) if kind == FFN_TILE else (G_TWO_X,)))
            self.send(kind, k, G_TWO_CORNER)

    def square(self, kind, k):
        self.local(kind, k).wait()
        self.wait(kind, k, G_NEAR, G_RELAY)
        self.send(kind, k, G_X, G_Y)
        if self.two(kind):
            self.wait(kind, k, *((G_TWO_X,) if kind == FFN_TILE else (G_TWO_Y,)), G_TWO_CORNER)
            self.send(kind, k, G_TWO_FAR, G_TWO_NEAR)

    def corner(self, kind, k):
        self.wait(kind, k, G_X)
        self.send(kind, k, G_CORNER_Y, G_CORE_OWN)
        self.wait(kind, k, G_Y)
        self.send(kind, k, G_CORNER_X)
        if self.two(kind):
            self.wait(kind, k, G_TWO_FAR)
            self.send(kind, k, G_TWO_RELAY)

    def across(self, kind, k):
        self.wait(kind, k, G_CORNER_Y, G_CORNER_X)
        self.send(kind, k, G_CORE_OTHER)
        if self.two(kind):
            self.wait(kind, k, G_TWO_NEAR, G_TWO_RELAY)
            self.send(kind, k, G_TWO_CORE)

    def complete(self, kind, k):
        self.wait(kind, k, G_CORE_OWN, G_CORE_OTHER)
        if self.two(kind):
            self.wait(kind, k, G_TWO_CORE)

    def finish(self, kind, k):
        names = [G_NEAR, G_FAR, G_RELAY, G_X, G_Y, G_CORNER_Y, G_CORNER_X, G_CORE_OWN, G_CORE_OTHER]
        if self.two(kind):
            names += [G_TWO_X, G_TWO_Y, G_TWO_CORNER, G_TWO_NEAR, G_TWO_FAR, G_TWO_RELAY, G_TWO_CORE]
        for name in names:
            self.copy(kind, k, name).wait_send()


class Scatter:
    copies = 16
    depths = {B_CORE: 4, B_KEEP: 2, B_SUMS: 8, B_XY: 4, B_X: 8, B_Y: 8, B_Z: 8, B_TWO_Z: 8, B_TWO: 8}

    def __init__(self, me, kinds, store, core, keep, sums, xy, x, y, z, two_z, two, local_sem, send_sem, recv_sem):
        self.me, self.kinds, self.store = me, kinds, store
        self.from_core, self.keep, self.sums = core, keep, sums
        self.from_xy, self.from_x, self.from_y, self.from_z = xy, x, y, z
        self.two_z, self.from_two = two_z, two
        self.local_sem, self.send_sem, self.recv_sem = local_sem, send_sem, recv_sem
        self.z, self.core = me // 8, me % 2
        self.here = (me // 2) % 4
        self.across_x, self.across_y = flip(self.here, 1), flip(self.here, 2)
        self.both = 3 - self.here
        self.near, self.far = flip(self.z, 1), flip(self.z, 2)
        self.opposite = 3 - self.z

    def slot(self, name, r):
        return r % self.depths[name]

    def copy(self, kind, r, k, name):
        source = self.kinds[kind][0]
        width, part, half = SHAPES[kind]
        whole, one, two = pl.ds(0, width), pl.ds(0, part), pl.ds(part, width - part)
        first, second = pl.ds(0, half), pl.ds(half, part - half)
        rest = pl.ds(0, width - part)
        sums = self.sums.at[self.slot(B_SUMS, r)]
        here, across_x, across_y, both, z = self.here, self.across_x, self.across_y, self.both, self.z
        by_y = kind == FFN_TILE
        place = lambda where, cols: sums.at[:, where, :, cols]
        origin, target, bit = {
            S_CORE: lambda: (
                source(k, 1 - self.core), self.from_core.at[self.slot(B_CORE, r), :, :, :, whole], 1
            ),
            S_XY_X: lambda: (place(both, first), self.from_xy.at[self.slot(B_XY, r), :, :, first], 2),
            S_XY_Y: lambda: (place(both, second), self.from_xy.at[self.slot(B_XY, r), :, :, second], 4),
            S_X_EARLY: lambda: (place(across_x, first), self.from_x.at[self.slot(B_X, r), :, :, first], 2),
            S_X_LATE: lambda: (place(across_x, second), self.from_x.at[self.slot(B_X, r), :, :, second], 2),
            S_Y_EARLY: lambda: (place(across_y, second), self.from_y.at[self.slot(B_Y, r), :, :, second], 4),
            S_Y_LATE: lambda: (place(across_y, first), self.from_y.at[self.slot(B_Y, r), :, :, first], 4),
            S_RELAY: lambda: (sums.at[self.opposite, here, :, one], self.from_z.at[self.slot(B_Z, r), 0, :, one], 8),
            S_NEAR: lambda: (sums.at[self.near, here, :, one], self.from_z.at[self.slot(B_Z, r), 1, :, one], 8),
            S_FAR: lambda: (sums.at[self.far, here, :, one], self.from_z.at[self.slot(B_Z, r), 2, :, one], 16),
            S_TWO_RELAY: lambda: (
                sums.at[self.opposite, :, :, two], self.two_z.at[self.slot(B_TWO_Z, r), 0, :, :, rest], 8
            ),
            S_TWO_NEAR: lambda: (
                sums.at[self.near, :, :, two], self.two_z.at[self.slot(B_TWO_Z, r), 1, :, :, rest], 8
            ),
            S_TWO_FAR: lambda: (
                sums.at[self.far, :, :, two], self.two_z.at[self.slot(B_TWO_Z, r), 2, :, :, rest], 16
            ),
            S_TWO_XY: lambda: (
                sums.at[z, both, :, two], self.from_two.at[self.slot(B_TWO, r), 0, :, rest], 4 if by_y else 2
            ),
            S_TWO_X: lambda: (sums.at[z, across_x, :, two], self.from_two.at[self.slot(B_TWO, r), 1, :, rest], 2),
            S_TWO_Y: lambda: (sums.at[z, across_y, :, two], self.from_two.at[self.slot(B_TWO, r), 2, :, rest], 4),
        }[name]()
        sems = self.send_sem.at[r, name], self.recv_sem.at[r, name]
        return remote(origin, target, *sems, flip(self.me, bit))

    def send(self, kind, r, k, *names):
        for name in names:
            self.copy(kind, r, k, name).start()

    def wait(self, kind, r, k, *names):
        for name in names:
            self.copy(kind, r, k, name).wait_recv()

    def two(self, kind):
        return SHAPES[kind][0] > SHAPES[kind][1]

    def load(self, kind, r, k):
        source = self.kinds[kind][0]
        return pltpu.make_async_copy(
            source(k, self.core), self.keep.at[r % 2, :, :, :, pl.ds(0, SHAPES[kind][0])], self.local_sem.at[r]
        )

    def core_step(self, kind, r, k):
        self.send(kind, r, k, S_CORE)

    def load_step(self, kind, r, k):
        if self.kinds[kind][1] is None:
            self.load(kind, r, k).start()

    def add_planes(self, r, place, cols, first, others):
        def one(plane, carry):
            total = first(plane).astype(F32)
            for read in others:
                total = total + read(plane).astype(F32)
            self.sums[self.slot(B_SUMS, r), plane, place, :, cols] = total.astype(BF16)
            return carry

        lax.fori_loop(0, 4, one, 0)

    def add_places(self, r, plane, cols, others):
        slot = self.slot(B_SUMS, r)
        for place in range(4):
            total = self.sums[slot, plane, place, :, cols].astype(F32)
            for read in others:
                total = total + read(place).astype(F32)
            self.sums[slot, plane, place, :, cols] = total.astype(BF16)

    def held(self, r, place, cols):
        return lambda plane: self.sums[self.slot(B_SUMS, r), plane, place, :, cols]

    def chip_step(self, kind, r, k):
        in_place = self.kinds[kind][1]
        width, part, half = SHAPES[kind]
        whole = pl.ds(0, width)
        self.wait(kind, r, k, S_CORE)
        if in_place is None:
            self.load(kind, r, k).wait()
            mine = lambda place: (lambda plane: self.keep[r % 2, plane, place, :, whole])
        else:
            mine = lambda place: (lambda plane: in_place(k, plane, place, self.core))
        got = lambda place: (lambda plane: self.from_core[self.slot(B_CORE, r), plane, place, :, whole])
        for place, names in (
            (self.both, (S_XY_X, S_XY_Y)),
            (self.across_x, (S_X_EARLY,)),
            (self.across_y, (S_Y_EARLY,)),
            (self.here, (S_TWO_RELAY, S_TWO_NEAR) if self.two(kind) else ()),
        ):
            self.add_planes(r, place, whole, got(place), [mine(place)])
            self.send(kind, r, k, *names)
        self.copy(kind, r, k, S_CORE).wait_send()

    def corner_step(self, kind, r, k):
        width, part, half = SHAPES[kind]
        first, second = pl.ds(0, half), pl.ds(half, part - half)
        passed = lambda cols: (lambda plane: self.from_xy[self.slot(B_XY, r), plane, :, cols])
        self.wait(kind, r, k, S_XY_X)
        self.add_planes(r, self.across_y, first, self.held(r, self.across_y, first), [passed(first)])
        self.send(kind, r, k, S_Y_LATE)
        self.wait(kind, r, k, S_XY_Y)
        self.add_planes(r, self.across_x, second, self.held(r, self.across_x, second), [passed(second)])
        self.send(kind, r, k, S_X_LATE)
        if self.two(kind):
            two, rest = pl.ds(part, width - part), pl.ds(0, width - part)
            self.wait(kind, r, k, S_TWO_RELAY)
            self.add_places(r, self.far, two, [lambda place: self.two_z[self.slot(B_TWO_Z, r), 0, place, :, rest]])
            self.send(kind, r, k, S_TWO_FAR)

    def square_step(self, kind, r, k):
        width, part, half = SHAPES[kind]
        one = pl.ds(0, part)
        self.wait(kind, r, k, S_X_EARLY, S_X_LATE, S_Y_EARLY, S_Y_LATE)
        from_x = lambda plane: self.from_x[self.slot(B_X, r), plane, :, one]
        from_y = lambda plane: self.from_y[self.slot(B_Y, r), plane, :, one]
        self.add_planes(r, self.here, one, self.held(r, self.here, one), [from_x, from_y])
        self.send(kind, r, k, S_RELAY, S_NEAR)
        if self.two(kind):
            two, rest = pl.ds(part, width - part), pl.ds(0, width - part)
            self.wait(kind, r, k, S_TWO_NEAR, S_TWO_FAR)
            self.add_places(
                r, self.z, two,
                [lambda place, i=i: self.two_z[self.slot(B_TWO_Z, r), i, place, :, rest] for i in (1, 2)],
            )
            self.send(kind, r, k, S_TWO_XY, S_TWO_X if kind != FFN_TILE else S_TWO_Y)

    def relay_step(self, kind, r, k):
        width, part, half = SHAPES[kind]
        slot, one = self.slot(B_SUMS, r), pl.ds(0, part)
        self.wait(kind, r, k, S_RELAY)
        total = self.sums[slot, self.far, self.here, :, one].astype(F32)
        total = total + self.from_z[self.slot(B_Z, r), 0, :, one].astype(F32)
        self.sums[slot, self.far, self.here, :, one] = total.astype(BF16)
        self.send(kind, r, k, S_FAR)
        if self.two(kind):
            two, rest = pl.ds(part, width - part), pl.ds(0, width - part)
            place = self.across_x if kind == FFN_TILE else self.across_y
            self.wait(kind, r, k, S_TWO_XY)
            total = self.sums[slot, self.z, place, :, two].astype(F32)
            total = total + self.from_two[self.slot(B_TWO, r), 0, :, rest].astype(F32)
            self.sums[slot, self.z, place, :, two] = total.astype(BF16)
            self.send(kind, r, k, S_TWO_X if kind == FFN_TILE else S_TWO_Y)

    def last_step(self, kind, r, k):
        width, part, half = SHAPES[kind]
        slot, one = self.slot(B_SUMS, r), pl.ds(0, part)
        self.wait(kind, r, k, S_NEAR, S_FAR)
        total = self.sums[slot, self.z, self.here, :, one].astype(F32)
        for i in (1, 2):
            total = total + self.from_z[self.slot(B_Z, r), i, :, one].astype(F32)
        names = [S_XY_X, S_XY_Y, S_X_EARLY, S_X_LATE, S_Y_EARLY, S_Y_LATE, S_RELAY, S_NEAR, S_FAR]
        if self.two(kind):
            two, rest = pl.ds(part, width - part), pl.ds(0, width - part)
            self.wait(kind, r, k, S_TWO_X, S_TWO_Y)
            more = self.sums[slot, self.z, self.here, :, two].astype(F32)
            for i in (1, 2):
                more = more + self.from_two[self.slot(B_TWO, r), i, :, rest].astype(F32)
            total = jnp.concatenate([total, more], axis=1)
            names += [S_TWO_RELAY, S_TWO_NEAR, S_TWO_FAR, S_TWO_XY, S_TWO_X, S_TWO_Y]
        self.store(kind, k, total)
        for name in names:
            self.copy(kind, r, k, name).wait_send()


class Total:
    bits = (1, 2, 4, 8, 16)

    def __init__(self, me, value_ref, store, got, stage, send_sem, recv_sem):
        self.me, self.value_ref, self.store = me, value_ref, store
        self.got, self.stage, self.send_sem, self.recv_sem = got, stage, send_sem, recv_sem

    def copy(self, number):
        sems = self.send_sem.at[number], self.recv_sem.at[number]
        return remote(self.stage.at[number], self.got.at[number], *sems, flip(self.me, self.bits[number]))

    def step(self, number):
        last = len(self.bits)
        value = self.value_ref[...]
        if number > 0:
            self.copy(number - 1).wait_recv()
            value = self.stage[number - 1] + self.got[number - 1]
        if number < last:
            self.stage[number] = value
            self.copy(number).start()
        else:
            self.store(value)
            for number in range(last):
                self.copy(number).wait_send()


def triangle_sum(values, dims):
    rows, cols = grid_of(SEQ)
    ones = jnp.where(rows >= cols, 1.0, 0.0).astype(BF16)
    first, rest = values.astype(BF16), values - values.astype(BF16).astype(F32)
    second, third = split(rest)
    return dot1(ones, first, dims) + (dot1(ones, second, dims) + dot1(ones, third, dims))


def log1p(value):
    series = value * (1.0 - value * (0.5 - value * (1.0 / 3.0 - value * (0.25 - value * 0.2))))
    return jnp.where(value < 0.01, series, jnp.log(1.0 + value))


def softplus(value):
    return jnp.maximum(value, 0.0) + log1p(jnp.exp(-jnp.abs(value)))


def merge(block):
    return block.reshape(-1, block.shape[-1])


def head_taps(small_ref, head):
    wide = 2 * head
    places = [(0, head), (1, head)] + [(2 + head // 4, wide % 8 + i) for i in (0, 1)]
    blocks = [
        small_ref[z, p // 4, (p // 2) % 2, p % 2, 0:16, SMALL : 2 * SMALL][0:4].astype(F32) for z, p in places
    ]
    return jnp.concatenate(blocks, axis=1)


def row_blocks(count, body, size=128):
    def one(i, carry):
        body(pl.ds(pl.multiple_of(i * size, size), size))
        return carry

    lax.fori_loop(0, count // size, one, 0)


def lane_index(shape):
    return lax.broadcasted_iota(jnp.int32, shape, 1)


def forward_body(
    planes, tiles,
    mixer_in_ref, mixer_out_ref, ffn_in_ref, ffn_out_ref, decay_in_ref, gain1_ref, gain2_ref, conv_ref,
    x_in, cot_in, seg_ref, log_ref, bias_ref, gain_ref,
    full_small, full_heads, full_tiles, small_out, xnt_out, cols_out, rows_out, logs_out, factor_out, middle_out,
    proj_ref, mixed_ref, inv_ref, upd_ref, core_ref, dw_ref, output_ref, nm_sum,
    small_ref, xnt_ref, cols_ref, rows_ref, logs_ref, factor_ref, middle, x_ref, cot_ref, load_sem, flush_sem,
    shard_small, shard_heads, shard_tiles, turn, consts_ref,
    w_buf, xn, cott, nm, nmt, out_sum, gains, copy_sem, w_sem, local_sem, send_sem, recv_sem,
):
    step = pl.program_id(0)
    tokens = x_ref.shape[0]
    chunks = HEADS + tiles
    me = lax.axis_index("dp")
    kinds = {
        SMALLS: (shard_small, full_small, chunks),
        HEAD: (shard_heads, full_heads, 0),
        FFN_TILE: (shard_tiles, full_tiles, HEADS),
    }
    work = Gather(me, kinds, local_sem, send_sem, recv_sem)

    def at(chunk, act):
        pl.when((chunk >= 0) & (chunk < HEADS))(lambda: act(HEAD, chunk))
        pl.when((chunk >= HEADS) & (chunk < chunks))(lambda: act(FFN_TILE, chunk - HEADS))

    def weights(kind, k, slot, plane=None):
        full, width = kinds[kind][1], SHAPES[kind][0]
        source = full.at[:, :, :, :, :, span(k, width, 0, width)]
        place = w_buf.at[slot, :, :, :, :, :, pl.ds(0, width)]
        if plane is not None:
            source, place = source.at[plane], place.at[plane]
        return pltpu.make_async_copy(source, place, w_sem.at[slot])

    def load_weights(kind, k, slot):
        for plane in range(planes):
            weights(kind, k, slot, plane).start()

    def arrive(kind, k):
        work.complete(kind, k)
        load_weights(kind, k, k % 2 if isinstance(k, int) else (step + 1) % 2)

    def arrive_early(kind, k):
        pl.when(step + 1 != chunks - 1)(lambda: arrive(kind, k))

    def arrive_late(kind, k):
        pl.when(step + 1 == chunks - 1)(lambda: arrive(kind, k))

    at_start = ((3, work.corner), (1, arrive_early))
    at_middle = ((7, work.start), (6, work.relay), (5, work.square), (2, work.across))

    def early(step):
        for lead, act in sorted(at_start[:1] + at_middle + ((1, arrive),), key=lambda item: -item[0]):
            if step + lead >= 0:
                act(HEAD, step + lead)

    def midway():
        for lead, act in at_middle:
            at(step + lead, act)
        at(step + 1, arrive_late)

    loads = [
        pltpu.make_async_copy(source, target, load_sem.at[i])
        for i, (source, target) in enumerate(((x_in, x_ref), (cot_in, cot_ref)))
    ]
    flushes = [
        pltpu.make_async_copy(source, target, flush_sem.at[i])
        for i, (source, target) in enumerate(
            (
                (small_ref, small_out), (xnt_ref, xnt_out), (cols_ref, cols_out), (rows_ref, rows_out),
                (logs_ref, logs_out), (factor_ref, factor_out), (middle, middle_out),
            )
        )
    ]

    def pack_heads():
        for copy in loads:
            copy.start()
        turn[...] = jnp.zeros_like(turn)
        turn[0:16, 0 : conv_ref.shape[1] // 4] = decay_in_ref[...]
        turn[16:17, 0 : conv_ref.shape[1] // 4] = gain1_ref[...]
        turn[17:18, 0 : conv_ref.shape[1] // 4] = gain2_ref[...]
        rows = shard_small.shape[0]
        shard_small[:, 0:SMALL] = turn[...].T[0:rows].astype(BF16)
        taps = jnp.concatenate([conv_ref[...], jnp.zeros((rows - 4, SMALL), F32)], axis=0)
        shard_small[:, SMALL:] = taps.astype(BF16)
        for h in range(HEADS):
            at_col = h * (HEAD_COLS + DV)
            key, val = HEADS * DK, HEADS * DV
            for ref, start, size in (
                (mixer_in_ref, h * DK, DK),
                (mixer_in_ref, key + h * DK, DK),
                (mixer_in_ref, 2 * key + h * DV, DV),
                (mixer_in_ref, 2 * key + val + h * DV, DV),
                (mixer_out_ref, h * DV, DV),
            ):
                shard_heads[:, at_col : at_col + size] = ref[:, start : start + size].astype(BF16)
                at_col += size

    def pack_tiles():
        for t in range(tiles):
            at_col = t * 3 * TILE
            for ref, start in ((ffn_in_ref, t * TILE), (ffn_in_ref, (tiles + t) * TILE), (ffn_out_ref, t * TILE)):
                shard_tiles[:, at_col : at_col + TILE] = ref[:, start : start + TILE].astype(BF16)
                at_col += TILE

    @pl.when(step == 0)
    def _():
        enter(me, pack_heads)
        work.start(SMALLS, 0)
        early(-7)
        pack_tiles()
        consts_ref[...] = jnp.zeros_like(consts_ref)
        consts_ref[0:1, 0:HEADS] = -jnp.exp(log_ref[...])
        consts_ref[1:2, 0:HEADS] = bias_ref[...]

        def prepare(rows):
            middle[rows, :] = x_ref[rows, :].astype(F32)
            cott[:, rows] = cot_ref[rows, :].astype(F32).T.astype(BF16)

        for copy in loads:
            copy.wait()
        row_blocks(tokens, prepare)
        work.relay(SMALLS, 0)
        early(-6)
        work.square(SMALLS, 0)
        early(-5)
        work.corner(SMALLS, 0)
        early(-4)
        work.across(SMALLS, 0)
        out_sum[...] = jnp.zeros_like(out_sum)
        nm_sum[...] = jnp.zeros_like(nm_sum)
        early(-3)
        work.complete(SMALLS, 0)
        early(-2)
        copy = pltpu.make_async_copy(full_small, small_ref, copy_sem)
        copy.start()
        copy.wait()
        small = merge(small_ref[..., 0:SMALL])
        turned = small.astype(F32).T
        gains[0:1, :] = turned[16:17, :]
        gains[1:2, :] = turned[17:18, :]

        def norm(rows):
            x = middle[rows, :]
            scale = lax.rsqrt(jnp.mean(x * x, axis=1, keepdims=True) + epsilon)
            normed = x * scale * gains[0:1, :]
            xn[rows, :] = normed.astype(BF16)
            xnt_ref[:, rows] = normed.T.astype(BF16)

        row_blocks(tokens, norm)
        logits = jnp.dot(xn[...], small, preferred_element_type=F32)
        lanes = lane_index(logits.shape)
        decay_scale, bias = consts_ref[0:1, :], consts_ref[1:2, :]
        shifted = logits + bias
        rate = sigmoid(logits)
        log_decay = decay_scale * softplus(shifted)
        logs_ref[...] = log_decay
        factor_ref[...] = jnp.where(
            lanes < 8, decay_scale * sigmoid(shifted), jnp.where(lanes < 16, rate * (1.0 - rate), 0.0)
        )
        seg_row = jnp.broadcast_to(seg_ref[...].astype(F32), (128, tokens))
        segment = seg_row.T
        rows_ref[8:16, :] = seg_row[0:8]
        inside = lax.broadcasted_iota(jnp.int32, segment.shape, 0) % SEQ
        aux = segment
        for back in (1, 2, 3):
            linked = (pltpu.roll(segment, back, 0) == segment) & (inside >= back)
            aux = jnp.where(lanes == 15 + back, jnp.where(linked, 1.0, 0.0), aux)
        for start in range(0, tokens, SEQ):
            part = slice(start, start + SEQ)
            cum = triangle_sum(log_decay[part], NN)
            cols_ref[part, :] = jnp.where(lanes[part] < 8, cum, jnp.where(lanes[part] < 16, rate[part], aux[part]))
            rows_ref[0:8, part] = cum.T[0:8]
        early(-1)
        work.finish(SMALLS, 0)

    for lead, act in at_start:
        at(step + lead, act)
    at(step, lambda kind, k: weights(kind, k, step % 2).wait())
    at(step - 1, work.finish)

    @pl.when(step == 1)
    def _():
        for copy in flushes[:-1]:
            copy.start()

    @pl.when(step < HEADS)
    def _():
        w = merge(w_buf[step % 2])
        projected = jnp.dot(xn[...], w[:, :HEAD_COLS], preferred_element_type=F32)
        proj_ref[...] = projected
        midway()
        _, _, _, _, q, k, value, _, _, cum, rate, seg = head_inputs(
            projected, head_taps(small_ref, step), cols_ref[...], step
        )
        q = q * DK**-0.5
        cum_row = rows_ref[pl.ds(step, 1), :]
        seg_row = rows_ref[8:9, :]
        parts = [slice(s, s + SEQ) for s in range(0, tokens, SEQ)]
        scores, couplings = [], []
        for part in parts:
            pair = decays(seg[part], seg_row[:, part], cum[part], cum_row[:, part])
            key_dots = dot3(k[part], k[part], NT)
            scores.append(pair * dot3(q[part], k[part], NT))
            couplings.append(strict(pair * key_dots) * rate[part])
        inverses = unit_inverses(couplings)
        for i, part in enumerate(parts):
            update = dot3(inverses[i], rate[part] * value[part], NN)
            core = dot3(scores[i], update, NN)
            inv_ref[0, part, :] = inverses[i].astype(BF16)
            upd_ref[0, part, :] = update
            core_ref[0, part, :] = core
            scale = lax.rsqrt(jnp.mean(core * core, axis=1, keepdims=True) + head_epsilon)
            out_gate = projected[part, CONV_COLS:]
            mixed_ref[part, :] = (core * scale * gain_ref[...] * (out_gate * sigmoid(out_gate))).astype(BF16)
        middle[...] += lax.dot_general(mixed_ref[...], w[:, HEAD_COLS:], (NT, ((), ())), preferred_element_type=F32)

    @pl.when(step == HEADS)
    def _():
        def norm(rows):
            mid = middle[rows, :]
            scale = lax.rsqrt(jnp.mean(mid * mid, axis=1, keepdims=True) + epsilon)
            normed = mid * scale * gains[1:2, :]
            nm[rows, :] = normed.astype(BF16)
            nmt[:, rows] = normed.T.astype(BF16)

        flushes[-1].start()
        row_blocks(tokens, norm)

    @pl.when(step >= HEADS)
    def _():
        w = merge(w_buf[step % 2, :, :, :, :, :, 0 : 3 * TILE])
        gate_up = jnp.dot(nm[...], w[:, : 2 * TILE], preferred_element_type=F32)
        gate, up = gate_up[:, :TILE], gate_up[:, TILE:]
        sig = sigmoid(gate)
        swish = gate * sig
        hidden = (swish * up).astype(BF16)
        midway()
        grad_hidden = jnp.dot(cot_ref[...], w[:, 2 * TILE :], preferred_element_type=F32)
        grad_gate = grad_hidden * up * (sig + swish * (1.0 - sig))
        grad_up = grad_hidden * swish
        grad_low = jnp.concatenate([grad_gate, grad_up], axis=1).astype(BF16)
        out_sum[...] += lax.dot_general(hidden, w[:, 2 * TILE :], (NT, ((), ())), preferred_element_type=F32)
        nm_sum[...] += lax.dot_general(grad_low, w[:, : 2 * TILE], (NT, ((), ())), preferred_element_type=F32)
        dw_ref[:, : 2 * TILE] = jnp.dot(nmt[...], grad_low, preferred_element_type=F32).astype(BF16)
        dw_ref[:, 2 * TILE :] = jnp.dot(cott[...], hidden, preferred_element_type=F32).astype(BF16)

    @pl.when(step == chunks - 1)
    def _():
        def add(rows):
            output_ref[rows, :] = (middle[rows, :] + out_sum[rows, :]).astype(BF16)

        row_blocks(tokens, add)
        work.finish(FFN_TILE, tiles - 1)
        for copy in flushes:
            copy.wait()


def once(shape):
    return pl.BlockSpec(shape, lambda i: (0,) * len(shape), pipeline_mode=pl.Buffered(1))


def forward(planes, masters, x, cot, *others):
    rows, tokens, width = masters[0].shape[0], *x.shape
    tiles = masters[3].shape[1] // TILE
    chunks = HEADS + tiles
    widths = (2 * SMALL, HEADS * (HEAD_COLS + DV), tiles * 3 * TILE)
    hbm = pl.BlockSpec(memory_space=pl.ANY)
    head = lambda i: jnp.minimum(i, HEADS - 1)
    tile = lambda i: jnp.maximum(i - HEADS, 0)
    save = pl.BlockSpec((1, tokens, SEQ), lambda i: (head(i), 0, 0))
    shape = jax.ShapeDtypeStruct
    whole = [((planes, 2, 2, 2, rows, w), BF16) for w in widths]
    outs = [
        (hbm, *whole[0]),
        (hbm, *whole[1]),
        (hbm, *whole[2]),
        (hbm, *whole[0]),
        (hbm, (width, tokens), BF16),
        (hbm, (tokens, 128), F32),
        (hbm, (16, tokens), F32),
        (hbm, (tokens, 128), F32),
        (hbm, (tokens, 128), F32),
        (hbm, (tokens, width), F32),
        (pl.BlockSpec((tokens, HEAD_COLS), lambda i: (0, head(i))), (tokens, HEADS * HEAD_COLS), F32),
        (pl.BlockSpec((tokens, DV), lambda i: (0, head(i))), (tokens, HEADS * DV), BF16),
        (save, (HEADS, tokens, SEQ), BF16),
        (save, (HEADS, tokens, DV), F32),
        (save, (HEADS, tokens, DV), F32),
        (pl.BlockSpec((width, 3 * TILE), lambda i: (0, tile(i))), (width, tiles * 3 * TILE), BF16),
        (once((tokens, width)), (tokens, width), BF16),
        (once((tokens, width)), (tokens, width), F32),
    ]
    return pl.pallas_call(
        partial(forward_body, planes, tiles),
        grid=(chunks,),
        in_specs=[once(a.shape) for a in masters] + [hbm, hbm] + [once(a.shape) for a in others],
        out_specs=[o[0] for o in outs],
        out_shape=[shape(o[1], o[2]) for o in outs],
        scratch_shapes=[pltpu.VMEM(o[1], o[2]) for o in outs[3:10]]
        + [
            pltpu.VMEM((tokens, width), BF16),
            pltpu.VMEM((tokens, width), BF16),
            pltpu.SemaphoreType.DMA((2,)),
            pltpu.SemaphoreType.DMA((7,)),
        ]
        + [pltpu.VMEM((rows, w), BF16) for w in widths]
        + [
            pltpu.VMEM((128, 128), F32),
            pltpu.VMEM((8, 128), F32),
            pltpu.VMEM((2, planes, 2, 2, 2, rows, HEAD_COLS + DV), BF16),
            pltpu.VMEM((tokens, width), BF16),
            pltpu.VMEM((width, tokens), BF16),
            pltpu.VMEM((tokens, width), BF16),
            pltpu.VMEM((width, tokens), BF16),
            pltpu.VMEM((tokens, width), F32),
            pltpu.VMEM((8, width), F32),
            pltpu.SemaphoreType.DMA,
            pltpu.SemaphoreType.DMA((2,)),
            pltpu.SemaphoreType.DMA((chunks + 1,)),
            pltpu.SemaphoreType.DMA((chunks + 1, Gather.copies)),
            pltpu.SemaphoreType.DMA((chunks + 1, Gather.copies)),
        ],
        compiler_params=pltpu.CompilerParams(
            collective_id=0, has_side_effects=True, vmem_limit_bytes=60 * MIB
        ),
        name="forward",
    )(*masters, x, cot, *others)


FIRST = 4


def row_sums(count, body, width, size=128):
    def one(i, total):
        return body(pl.ds(pl.multiple_of(i * size, size), size), total)

    return lax.fori_loop(0, count // size, one, jnp.zeros((1, width), F32))


def head_step(j):
    return jnp.minimum(j // 2, HEADS - 1)


def backward_body(
    planes, tiles, total_chunks,
    dwf_ref, middle_in, nm_sum_in, cot_in, xnt_in, x_in, w_ref, proj_ref, mixed_ref, inv_ref, upd_ref, core_ref,
    small_ref, cols_ref, rows_ref, logs_ref, factor_ref, gain_ref,
    input_grad_out, own_gain1, own_mixer, own_decay, own_conv, own_log, own_bias, own_gain, own_out, own_gain2, own_ffn,
    own_down,
    middle_ref, nm_sum_ref, cot_ref, xnt_ref, x_ref, load_sem, flush_sem, gbt_ref, gains, dw, d_small, dcols, drows, dgain, dproj,
    value_ref, *scratch,
):
    gxn, grad_mid_ref, gb_ref = middle_ref, nm_sum_ref, cot_ref
    *buffers, got, stage, local_sem, send_sem, recv_sem, total_send, total_recv = scratch
    step = pl.program_id(0)
    tokens = middle_ref.shape[0]
    rows = own_mixer.shape[0]
    hidden = tiles * TILE
    me = lax.axis_index("dp")

    def tile_source(k, core):
        return dwf_ref.at[:, :, core, :, span(k, 3 * TILE, 0, 3 * TILE)]

    kinds = {
        FFN_TILE: (tile_source, None),
        HEAD: (
            lambda k, core: dw.at[k % 2, :, :, core],
            lambda k, plane, place, core: dw[k % 2, plane, place, core],
        ),
        SMALLS: (
            lambda k, core: d_small.at[:, :, core],
            lambda k, plane, place, core: d_small[plane, place, core],
        ),
    }

    def store(kind, k, total):
        def put(ref, start, source, width):
            ref[:, pl.ds(pl.multiple_of(start, 128), width)] = total[:, source : source + width]

        if kind == SMALLS:
            turned = jnp.concatenate([total[:, :SMALL], jnp.zeros((SMALL - rows, SMALL), F32)], axis=0).T
            own_decay[...] = turned[0:16, 0:rows]
            own_gain1[...] = turned[16:17, 0:rows]
            own_gain2[...] = turned[17:18, 0:rows]
            own_conv[...] = total[0:4, SMALL:]
        elif kind == HEAD:
            put(own_mixer, k * DK, 0, DK)
            put(own_mixer, HEADS * DK + k * DK, DK, DK)
            put(own_mixer, 2 * HEADS * DK + k * DV, 2 * DK, DV)
            put(own_mixer, 2 * HEADS * DK + HEADS * DV + k * DV, 2 * DK + DV, DV)
            put(own_out, k * DV, HEAD_COLS, DV)
        else:
            put(own_ffn, k * TILE, 0, TILE)
            put(own_ffn, hidden + k * TILE, TILE, TILE)
            put(own_down, k * TILE, 2 * TILE, TILE)

    work = Scatter(me, kinds, store, *buffers, local_sem, send_sem, recv_sem)
    def share(value):
        own_log[...] = value[0:1, 0:HEADS]
        own_bias[...] = value[1:2, 0:HEADS]
        own_gain[...] = jnp.concatenate([value[2:3], value[3:4]], axis=1)

    small_sum = Total(me, value_ref, share, got, stage, total_send, total_recv)

    last = total_chunks - 1

    def at(r, act):
        is_head = (r >= FIRST) & (r < last) & ((r - FIRST) % 2 == 0)
        is_early = (r >= 0) & (r < FIRST)
        is_tile = (r > FIRST) & (r < last) & ((r - FIRST) % 2 == 1)
        pl.when(is_early)(lambda: act(FFN_TILE, r, r))
        pl.when(is_tile)(lambda: act(FFN_TILE, r, (r + FIRST - 1) // 2))
        pl.when(is_head)(lambda: act(HEAD, r, (r - FIRST) // 2))
        pl.when(r == last)(lambda: act(SMALLS, r, 0))

    loads = [
        pltpu.make_async_copy(source, target, load_sem.at[i])
        for i, (source, target) in enumerate(
            (
                (middle_in, middle_ref), (nm_sum_in, nm_sum_ref), (cot_in, cot_ref), (xnt_in, xnt_ref), (x_in, x_ref),
            )
        )
    ]

    @pl.when(step == 0)
    def _():
        enter(me)
        work.core_step(FFN_TILE, 0, 0)
        work.core_step(FFN_TILE, 1, 1)
        work.load_step(FFN_TILE, 0, 0)
        dcols[...] = jnp.zeros_like(dcols)
        drows[...] = jnp.zeros_like(drows)
        dgain[...] = jnp.zeros_like(dgain)
        d_small[...] = jnp.zeros_like(d_small)
        for copy in loads:
            copy.start()
        for r in (0, 1):
            work.chip_step(FFN_TILE, r, r)
            work.core_step(FFN_TILE, r + 2, r + 2)
            work.load_step(FFN_TILE, r + 1, r + 1)

    at(step - 6, work.last_step)
    at(step - 4, work.relay_step)
    at(step - 2, work.square_step)
    at(step, work.corner_step)
    at(step + 2, work.chip_step)
    at(step + 3, work.load_step)

    @pl.when(step == 0)
    def _():
        for copy in loads:
            copy.wait()
        turned = merge(small_ref[..., 0:SMALL]).astype(F32).T
        gains[0:1, :] = turned[16:17, :]
        gains[1:2, :] = turned[17:18, :]

        def back(rows, total):
            mid = middle_ref[rows, :]
            scale = lax.rsqrt(jnp.mean(mid * mid, axis=1, keepdims=True) + epsilon)
            normed = mid * scale
            grad = nm_sum_ref[rows, :]
            d_normed = grad * gains[1:2, :]
            d_mid = scale * (d_normed - normed * jnp.mean(d_normed * normed, axis=1, keepdims=True))
            d_mid = d_mid + cot_ref[rows, :].astype(F32)
            gxn[rows, :] = jnp.zeros_like(mid)
            grad_mid_ref[rows, :] = d_mid
            gb_ref[rows, :] = d_mid.astype(BF16)
            gbt_ref[:, rows] = d_mid.T.astype(BF16)
            return total + jnp.sum(grad * normed, axis=0, keepdims=True)

        gains[2:3, :] = row_sums(tokens, back, gains.shape[1])

    @pl.when((step < 2 * HEADS) & (step % 2 == 0))
    def _():
        head = step // 2
        w = merge(w_ref[...])
        grad_mixed = jnp.dot(gb_ref[...], w[:, HEAD_COLS:], preferred_element_type=F32)
        d_out = jnp.dot(gbt_ref[...], mixed_ref[...], preferred_element_type=F32).astype(BF16)
        dw[head % 2, :, :, :, :, pl.ds(HEAD_COLS, DV)] = d_out.reshape(dw.shape[1:5] + (DV,))

        projected = proj_ref[...]
        taps = head_taps(small_ref, head)
        keeps, conv, gate, act, qn, k, value, q_scale, k_scale, cum, rate, seg = head_inputs(
            projected, taps, cols_ref[...], head
        )
        q = qn * DK**-0.5
        cum_row = rows_ref[pl.ds(head, 1), :]
        seg_row = rows_ref[8:9, :]
        gain = gain_ref[...]
        lanes = lane_index((SEQ, 128))
        d_act, d_gain = [], jnp.zeros((1, DV), F32)
        for start in range(0, tokens, SEQ):
            part = slice(start, start + SEQ)
            core, update, inverse = core_ref[0, part, :], upd_ref[0, part, :], inv_ref[0, part, :]
            grad = grad_mixed[part]
            scale = lax.rsqrt(jnp.mean(core * core, axis=1, keepdims=True) + head_epsilon)
            normed = core * scale
            out_gate = projected[part, CONV_COLS:]
            out_sig = sigmoid(out_gate)
            swish = out_gate * out_sig
            dproj[part, CONV_COLS:] = (grad * normed * gain * (out_sig + swish * (1.0 - out_sig))).astype(BF16)
            d_normed = grad * swish
            d_gain = d_gain + jnp.sum(d_normed * normed, axis=0, keepdims=True)
            d_scaled = d_normed * gain
            d_core = scale * (d_scaled - normed * jnp.mean(d_scaled * normed, axis=1, keepdims=True))

            qs, ks, vs, rs = q[part], k[part], value[part], rate[part]
            pair = decays(seg[part], seg_row[:, part], cum[part], cum_row[:, part])
            key_dots = dot3(ks, ks, NT)
            query_dots = dot3(qs, ks, NT)
            d_scores = dot3(d_core, update, NT)
            d_update = dot3(pair * query_dots, d_core, TN)
            solved = dot_high(inverse, d_update, TN)
            d_coupling = strict(-dot3(solved, update, NT)) * pair
            d_query_dots = pair * d_scores
            d_key_dots = d_coupling * rs
            weighed = d_coupling * key_dots
            d_spread = d_query_dots * query_dots + weighed * rs
            d_q = dot1(d_query_dots, ks, NN) * DK**-0.5
            d_k = dot1(d_query_dots, qs, TN) + dot1(d_key_dots, ks, NN) + dot1(d_key_dots, ks, TN)
            d_rate = jnp.sum(solved * vs, axis=1, keepdims=True) + jnp.sum(weighed, axis=1, keepdims=True)
            row_sum = jnp.sum(d_spread, axis=1, keepdims=True)
            dcols[part, :] += jnp.where(lanes == head, row_sum, 0.0) + jnp.where(lanes == 8 + head, d_rate, 0.0)
            drows[pl.ds(head, 1), part] = jnp.sum(d_spread, axis=0, keepdims=True)
            d_q_act = q_scale[part] * (d_q - qn[part] * jnp.sum(d_q * qn[part], axis=1, keepdims=True))
            d_k_act = k_scale[part] * (d_k - ks * jnp.sum(d_k * ks, axis=1, keepdims=True))
            d_act.append(jnp.concatenate([d_q_act, d_k_act, rs * solved], axis=1))
        dgain[0:1, :] += d_gain
        d_conv = jnp.concatenate(d_act, axis=0) * (gate + act * (1.0 - gate))
        source = projected[:, :CONV_COLS]
        d_source = d_conv * taps[0:1]
        d_taps = [jnp.sum(d_conv * source, axis=0, keepdims=True)]
        for back in (1, 2, 3):
            kept = d_conv * keeps[back - 1]
            d_source = d_source + pltpu.roll(kept, tokens - back, 0) * taps[back : back + 1]
            d_taps.append(jnp.sum(kept * pltpu.roll(source, back, 0), axis=0, keepdims=True))
        d_taps = jnp.concatenate(d_taps + [jnp.zeros((rows - 4, CONV_COLS), F32)], axis=0).astype(BF16)
        wide = 2 * head
        places = [(0, head), (1, head)] + [(2 + head // 4, wide % 8 + i) for i in (0, 1)]
        for i, (z, p) in enumerate(places):
            d_small[z, p // 2, p % 2, :, SMALL:] = d_taps[:, i * SMALL : (i + 1) * SMALL]
        dproj[:, :CONV_COLS] = d_source.astype(BF16)
        d_proj = dproj[...]
        d_in = jnp.dot(xnt_ref[...], d_proj, preferred_element_type=F32).astype(BF16)
        dw[head % 2, :, :, :, :, pl.ds(0, HEAD_COLS)] = d_in.reshape(dw.shape[1:5] + (HEAD_COLS,))
        gxn[...] += lax.dot_general(d_proj, w[:, :HEAD_COLS], (NT, ((), ())), preferred_element_type=F32)

    @pl.when(step == 2 * HEADS - 1)
    def _():
        small = merge(small_ref[..., 0:SMALL])
        lanes = lane_index((SEQ, 128))
        padded = jnp.concatenate([drows[...], jnp.zeros((120, tokens), F32)], axis=0).T
        d_logs = jnp.zeros((1, 128), F32)
        d_bias = jnp.zeros((1, 128), F32)
        d_logits = []
        for start in range(0, tokens, SEQ):
            part = slice(start, start + SEQ)
            d_cum = jnp.where(lanes < 8, dcols[part, :], 0.0) - padded[part]
            d_decay = triangle_sum(d_cum, TN)
            d_logit = jnp.where(lanes < 8, d_decay, dcols[part, :]) * factor_ref[part, :]
            d_logs = d_logs + jnp.sum(jnp.where(lanes < 8, d_decay * logs_ref[part, :], 0.0), axis=0, keepdims=True)
            d_bias = d_bias + jnp.sum(jnp.where(lanes < 8, d_logit, 0.0), axis=0, keepdims=True)
            d_logits.append(d_logit.astype(BF16))
        d_logits = jnp.concatenate(d_logits, axis=0)
        value_ref[...] = jnp.concatenate(
            [d_logs, d_bias, dgain[0:1, :128], dgain[0:1, 128:], jnp.zeros((4, 128), F32)], axis=0
        )
        gxn[...] += lax.dot_general(d_logits, small, (NT, ((), ())), preferred_element_type=F32)

        def back(at_rows, total):
            x = x_ref[at_rows, :].astype(F32)
            scale = lax.rsqrt(jnp.mean(x * x, axis=1, keepdims=True) + epsilon)
            normed = x * scale
            grad = gxn[at_rows, :]
            d_normed = grad * gains[0:1, :]
            d_x = scale * (d_normed - normed * jnp.mean(d_normed * normed, axis=1, keepdims=True))
            grad_mid_ref[at_rows, :] = d_x + grad_mid_ref[at_rows, :]
            return total + jnp.sum(grad * normed, axis=0, keepdims=True)

        total = row_sums(tokens, back, gxn.shape[1])
        line = lax.broadcasted_iota(jnp.int32, (128, total.shape[1]), 0)
        lines = jnp.where(line == 16, total, jnp.where(line == 17, gains[2:3, :], 0.0))
        own = jnp.dot(xnt_ref[...], d_logits, preferred_element_type=F32) + lines.T
        d_small[:, :, :, :, 0:SMALL] = own.astype(BF16).reshape(d_small.shape[:4] + (SMALL,))

    flush = pltpu.make_async_copy(grad_mid_ref, input_grad_out, flush_sem)
    pl.when(step == 2 * HEADS)(flush.start)
    pl.when(step == pl.num_programs(0) - 1)(flush.wait)

    at(step + 4, work.core_step)
    for number in range(len(Total.bits) + 1):
        pl.when(step == 2 * HEADS + number)(lambda number=number: small_sum.step(number))


def backward(planes, dwf, middle, nm_sum, cot, xnt, w, proj, mixed, inv, upd, core, small, cols, seq_rows, logs, factor,
             gain, x):
    tokens, width = middle.shape
    rows = small.shape[4]
    tiles = dwf.shape[1] // (3 * TILE)
    chunks = FIRST + 2 * HEADS
    assert tiles == FIRST + HEADS - 1
    hbm = pl.BlockSpec(memory_space=pl.ANY)
    head = head_step
    save = pl.BlockSpec((1, tokens, SEQ), lambda i: (head(i), 0, 0))
    shape = jax.ShapeDtypeStruct
    widest = HEAD_COLS + DV
    depth = Scatter.depths
    outs = [
        ((tokens, width), F32),
        ((1, rows), F32),
        ((rows, HEADS * HEAD_COLS), F32),
        ((16, rows), F32),
        ((4, SMALL), F32),
        ((1, HEADS), F32),
        ((1, HEADS), F32),
        ((1, DV), F32),
        ((rows, HEADS * DV), F32),
        ((1, rows), F32),
        ((rows, 2 * tiles * TILE), F32),
        ((rows, tiles * TILE), F32),
    ]
    return pl.pallas_call(
        partial(backward_body, planes, tiles, chunks),
        grid=(chunks + 6,),
        in_specs=[
            hbm,
            hbm,
            hbm,
            hbm,
            hbm,
            hbm,
            pl.BlockSpec((planes, 2, 2, 2, rows, widest), lambda i: (0, 0, 0, 0, 0, head(i))),
            pl.BlockSpec((tokens, HEAD_COLS), lambda i: (0, head(i))),
            pl.BlockSpec((tokens, DV), lambda i: (0, head(i))),
            save,
            save,
            save,
        ]
        + [once(a.shape) for a in (small, cols, seq_rows, logs, factor, gain)],
        out_specs=[hbm] + [once(o[0]) for o in outs[1:]],
        out_shape=[shape(*o) for o in outs],
        scratch_shapes=[
            pltpu.VMEM((tokens, width), F32),
            pltpu.VMEM((tokens, width), F32),
            pltpu.VMEM((tokens, width), BF16),
            pltpu.VMEM((width, tokens), BF16),
            pltpu.VMEM((tokens, width), BF16),
            pltpu.SemaphoreType.DMA((5,)),
            pltpu.SemaphoreType.DMA,
            pltpu.VMEM((width, tokens), BF16),
            pltpu.VMEM((8, width), F32),
            pltpu.VMEM((2, planes, 4, 2, rows, widest), BF16),
            pltpu.VMEM((planes, 4, 2, rows, 2 * SMALL), BF16),
            pltpu.VMEM((tokens, 128), F32),
            pltpu.VMEM((HEADS, tokens), F32),
            pltpu.VMEM((8, DV), F32),
            pltpu.VMEM((tokens, HEAD_COLS), BF16),
            pltpu.VMEM((8, 128), F32),
            pltpu.VMEM((depth[B_CORE], planes, 4, rows, widest), BF16),
            pltpu.VMEM((depth[B_KEEP], planes, 4, rows, 3 * TILE), BF16),
            pltpu.VMEM((depth[B_SUMS], planes, 4, rows, widest), BF16),
            pltpu.VMEM((depth[B_XY], planes, rows, HEAD_COLS), BF16),
            pltpu.VMEM((depth[B_X], planes, rows, HEAD_COLS), BF16),
            pltpu.VMEM((depth[B_Y], planes, rows, HEAD_COLS), BF16),
            pltpu.VMEM((depth[B_Z], 3, rows, HEAD_COLS), BF16),
            pltpu.VMEM((depth[B_TWO_Z], 3, 4, rows, DV), BF16),
            pltpu.VMEM((depth[B_TWO], 3, rows, DV), BF16),
            pltpu.VMEM((len(Total.bits), 8, 128), F32),
            pltpu.VMEM((len(Total.bits), 8, 128), F32),
            pltpu.SemaphoreType.DMA((chunks,)),
            pltpu.SemaphoreType.DMA((chunks, Scatter.copies)),
            pltpu.SemaphoreType.DMA((chunks, Scatter.copies)),
            pltpu.SemaphoreType.DMA((len(Total.bits),)),
            pltpu.SemaphoreType.DMA((len(Total.bits),)),
        ],
        compiler_params=pltpu.CompilerParams(
            collective_id=1, has_side_effects=True, vmem_limit_bytes=63 * MIB
        ),
        name="backward",
    )(
        dwf.reshape(planes, 4, 2, rows, dwf.shape[1]), middle, nm_sum, cot, xnt, x, w, proj, mixed, inv, upd, core, small,
        cols, seq_rows, logs, factor, gain,
    )


def hand_over_body(count, *refs):
    for source, target in zip(refs[:count], refs[count:]):
        target[...] = source[...]


def hand_over(arrays, steps=2):
    specs = []
    for a in arrays:
        rows, cols = a.shape
        if rows % (32 * steps) == 0:
            specs.append(pl.BlockSpec((rows // steps, cols), lambda i: (i, 0)))
        elif cols % (128 * steps) == 0:
            specs.append(pl.BlockSpec((rows, cols // steps), lambda i: (0, i)))
        else:
            specs.append(pl.BlockSpec((rows, cols), lambda i: (0, 0)))
    return pl.pallas_call(
        partial(hand_over_body, len(arrays)),
        grid=(steps,),
        in_specs=specs,
        out_specs=specs,
        out_shape=[jax.ShapeDtypeStruct(a.shape, a.dtype) for a in arrays],
        compiler_params=pltpu.CompilerParams(vmem_limit_bytes=60 * MIB),
        name="hand_over",
    )(*arrays)


def mixer_fwd_body(xn_ref, w_ref, taps_ref, cols_ref, rows_ref, gain_ref, proj_ref, mixed_ref, inv_ref, upd_ref, core_ref):
    head = pl.program_id(0)
    tokens = xn_ref.shape[0]
    projected = jnp.dot(xn_ref[...], w_ref[...], preferred_element_type=F32)
    proj_ref[...] = projected
    _, _, _, _, q, k, value, _, _, cum, rate, seg = head_inputs(
        projected, taps_ref[...], cols_ref[...], head
    )
    q = q * DK**-0.5
    cum_row = rows_ref[pl.ds(head, 1), :]
    seg_row = rows_ref[8:9, :]
    parts = [slice(s, s + SEQ) for s in range(0, tokens, SEQ)]
    scores, couplings = [], []
    for part in parts:
        pair = decays(seg[part], seg_row[:, part], cum[part], cum_row[:, part])
        key_dots = dot3(k[part], k[part], NT)
        scores.append(pair * dot3(q[part], k[part], NT))
        couplings.append(strict(pair * key_dots) * rate[part])
    inverses = unit_inverses(couplings)
    for i, part in enumerate(parts):
        update = dot3(inverses[i], rate[part] * value[part], NN)
        core = dot3(scores[i], update, NN)
        inv_ref[0, part, :] = inverses[i].astype(BF16)
        upd_ref[0, part, :] = update
        core_ref[0, part, :] = core
        scale = lax.rsqrt(jnp.mean(core * core, axis=1, keepdims=True) + head_epsilon)
        out_gate = projected[part, CONV_COLS:]
        mixed_ref[part, :] = (core * scale * gain_ref[...] * (out_gate * sigmoid(out_gate))).astype(BF16)


def mixer_fwd(xn, w, taps, cols, rows, gain):
    tokens, width = xn.shape
    const = lambda h: (0, 0)
    by_head = lambda h: (0, h)
    save = pl.BlockSpec((1, tokens, SEQ), lambda h: (h, 0, 0))
    return pl.pallas_call(
        mixer_fwd_body,
        grid=(HEADS,),
        in_specs=[
            pl.BlockSpec((tokens, width), const),
            pl.BlockSpec((width, HEAD_COLS), by_head),
            pl.BlockSpec((4, CONV_COLS), by_head),
            pl.BlockSpec(cols.shape, const),
            pl.BlockSpec(rows.shape, const),
            pl.BlockSpec((1, DV), const),
        ],
        out_specs=[
            pl.BlockSpec((tokens, HEAD_COLS), by_head),
            pl.BlockSpec((tokens, DV), by_head),
            save,
            save,
            save,
        ],
        out_shape=[
            jax.ShapeDtypeStruct((tokens, HEADS * HEAD_COLS), F32),
            jax.ShapeDtypeStruct((tokens, HEADS * DV), BF16),
            jax.ShapeDtypeStruct((HEADS, tokens, SEQ), BF16),
            jax.ShapeDtypeStruct((HEADS, tokens, DV), F32),
            jax.ShapeDtypeStruct((HEADS, tokens, DV), F32),
        ],
        compiler_params=pltpu.CompilerParams(vmem_limit_bytes=56 * MIB),
        name="mixer_fwd",
    )(xn, w, taps, cols, rows, gain)


def mixer_bwd_body(
    gb_ref, gbt_ref, xnt_ref, wo_ref, w_ref, proj_ref, mixed_ref, inv_ref, upd_ref, core_ref,
    taps_ref, cols_ref, rows_ref, gain_ref,
    dw_ref, dwo_ref, gxn_ref, dcols_ref, drows_ref, dtaps_ref, dgain_ref, dproj_ref,
):
    head = pl.program_id(0)
    tokens = gb_ref.shape[0]

    @pl.when(head == 0)
    def _():
        gxn_ref[...] = jnp.zeros_like(gxn_ref)
        dcols_ref[...] = jnp.zeros_like(dcols_ref)
        drows_ref[...] = jnp.zeros_like(drows_ref)
        dgain_ref[...] = jnp.zeros_like(dgain_ref)

    grad_mixed = jnp.dot(gb_ref[...], wo_ref[...], preferred_element_type=F32)
    dwo_ref[...] = jnp.dot(gbt_ref[...], mixed_ref[...], preferred_element_type=F32).astype(BF16)

    projected = proj_ref[...]
    taps = taps_ref[...]
    keep, conv, gate, act, qn, k, value, q_scale, k_scale, cum, rate, seg = head_inputs(
        projected, taps, cols_ref[...], head
    )
    q = qn * DK**-0.5
    cum_row = rows_ref[pl.ds(head, 1), :]
    seg_row = rows_ref[8:9, :]
    gain = gain_ref[...]
    lanes = lax.broadcasted_iota(jnp.int32, (SEQ, 128), 1)
    d_act, d_gain = [], jnp.zeros((1, DV), F32)
    for start in range(0, tokens, SEQ):
        part = slice(start, start + SEQ)
        core, update, inverse = core_ref[0, part, :], upd_ref[0, part, :], inv_ref[0, part, :]
        grad = grad_mixed[part]
        scale = lax.rsqrt(jnp.mean(core * core, axis=1, keepdims=True) + head_epsilon)
        normed = core * scale
        out_gate = projected[part, CONV_COLS:]
        out_sig = sigmoid(out_gate)
        swish = out_gate * out_sig
        dproj_ref[part, CONV_COLS:] = (grad * normed * gain * (out_sig + swish * (1.0 - out_sig))).astype(BF16)
        d_normed = grad * swish
        d_gain = d_gain + jnp.sum(d_normed * normed, axis=0, keepdims=True)
        d_scaled = d_normed * gain
        d_core = scale * (d_scaled - normed * jnp.mean(d_scaled * normed, axis=1, keepdims=True))

        qs, ks, vs, rs = q[part], k[part], value[part], rate[part]
        pair = decays(seg[part], seg_row[:, part], cum[part], cum_row[:, part])
        key_dots = dot3(ks, ks, NT)
        query_dots = dot3(qs, ks, NT)
        d_scores = dot3(d_core, update, NT)
        d_update = dot1(pair * query_dots, d_core, TN)
        solved = dot1(inverse, d_update, TN)
        d_coupling = strict(-dot1(solved, update, NT)) * pair
        d_query_dots = pair * d_scores
        d_key_dots = d_coupling * rs
        weighed = d_coupling * key_dots
        d_spread = d_query_dots * query_dots + weighed * rs
        d_q = dot1(d_query_dots, ks, NN) * DK**-0.5
        d_k = dot1(d_query_dots, qs, TN) + dot1(d_key_dots, ks, NN) + dot1(d_key_dots, ks, TN)
        d_rate = jnp.sum(solved * vs, axis=1, keepdims=True) + jnp.sum(weighed, axis=1, keepdims=True)
        row_sum = jnp.sum(d_spread, axis=1, keepdims=True)
        dcols_ref[part, :] += jnp.where(lanes == head, d_rate, 0.0) + jnp.where(lanes == 8 + head, row_sum, 0.0)
        drows_ref[pl.ds(head, 1), part] = jnp.sum(d_spread, axis=0, keepdims=True)
        d_q_act = q_scale[part] * (d_q - qn[part] * jnp.sum(d_q * qn[part], axis=1, keepdims=True))
        d_k_act = k_scale[part] * (d_k - ks * jnp.sum(d_k * ks, axis=1, keepdims=True))
        d_act.append(jnp.concatenate([d_q_act, d_k_act, rs * solved], axis=1))
    dgain_ref[...] += d_gain
    d_conv = jnp.concatenate(d_act, axis=0) * (gate + act * (1.0 - gate))
    source = projected[:, :CONV_COLS]
    d_source = d_conv * taps[0:1]
    d_taps = [jnp.sum(d_conv * source, axis=0, keepdims=True)]
    for back in (1, 2, 3):
        kept = d_conv * keep[back - 1]
        d_source = d_source + pltpu.roll(kept, tokens - back, 0) * taps[back : back + 1]
        d_taps.append(jnp.sum(kept * pltpu.roll(source, back, 0), axis=0, keepdims=True))
    dtaps_ref[...] = jnp.concatenate(d_taps, axis=0)
    dproj_ref[:, :CONV_COLS] = d_source.astype(BF16)
    d_proj = dproj_ref[...]
    dw_ref[...] = jnp.dot(xnt_ref[...], d_proj, preferred_element_type=F32).astype(BF16)
    gxn_ref[...] += lax.dot_general(d_proj, w_ref[...], (NT, ((), ())), preferred_element_type=F32)


def mixer_bwd(gb, gbt, xnt, wo, w, proj, mixed, inv, upd, core, taps, cols, rows, gain):
    tokens, width = gb.shape
    const = lambda h: (0, 0)
    by_head = lambda h: (0, h)
    save = pl.BlockSpec((1, tokens, SEQ), lambda h: (h, 0, 0))
    return pl.pallas_call(
        mixer_bwd_body,
        grid=(HEADS,),
        in_specs=[
            pl.BlockSpec((tokens, width), const),
            pl.BlockSpec((width, tokens), const),
            pl.BlockSpec((width, tokens), const),
            pl.BlockSpec((width, DV), by_head),
            pl.BlockSpec((width, HEAD_COLS), by_head),
            pl.BlockSpec((tokens, HEAD_COLS), by_head),
            pl.BlockSpec((tokens, DV), by_head),
            save,
            save,
            save,
            pl.BlockSpec((4, CONV_COLS), by_head),
            pl.BlockSpec(cols.shape, const),
            pl.BlockSpec(rows.shape, const),
            pl.BlockSpec((1, DV), const),
        ],
        out_specs=[
            pl.BlockSpec((width, HEAD_COLS), by_head),
            pl.BlockSpec((width, DV), by_head),
            pl.BlockSpec((tokens, width), const),
            pl.BlockSpec((tokens, 128), const),
            pl.BlockSpec((HEADS, tokens), const),
            pl.BlockSpec((4, CONV_COLS), by_head),
            pl.BlockSpec((1, DV), const),
        ],
        out_shape=[
            jax.ShapeDtypeStruct((width, HEADS * HEAD_COLS), BF16),
            jax.ShapeDtypeStruct((width, HEADS * DV), BF16),
            jax.ShapeDtypeStruct((tokens, width), F32),
            jax.ShapeDtypeStruct((tokens, 128), F32),
            jax.ShapeDtypeStruct((HEADS, tokens), F32),
            jax.ShapeDtypeStruct((4, HEADS * CONV_COLS), F32),
            jax.ShapeDtypeStruct((1, DV), F32),
        ],
        scratch_shapes=[pltpu.VMEM((tokens, HEAD_COLS), BF16)],
        compiler_params=pltpu.CompilerParams(vmem_limit_bytes=60 * MIB),
        name="mixer_bwd",
    )(gb, gbt, xnt, wo, w, proj, mixed, inv, upd, core, taps, cols, rows, gain)


def ffn_body(nm_ref, nmt_ref, cot_ref, cott_ref, w_ref, dw_ref, out_ref, gnm_ref):
    @pl.when(pl.program_id(0) == 0)
    def _():
        out_ref[...] = jnp.zeros_like(out_ref)
        gnm_ref[...] = jnp.zeros_like(gnm_ref)

    w = w_ref[...]
    gate_up = jnp.dot(nm_ref[...], w[:, : 2 * TILE], preferred_element_type=F32)
    gate, up = gate_up[:, :TILE], gate_up[:, TILE:]
    sig = sigmoid(gate)
    swish = gate * sig
    hidden = (swish * up).astype(BF16)
    grad_hidden = jnp.dot(cot_ref[...], w[:, 2 * TILE :], preferred_element_type=F32)
    grad_gate = grad_hidden * up * (sig + swish * (1.0 - sig))
    grad_up = grad_hidden * swish
    grad_low = jnp.concatenate([grad_gate, grad_up], axis=1).astype(BF16)
    out_ref[...] += lax.dot_general(hidden, w[:, 2 * TILE :], (NT, ((), ())), preferred_element_type=F32)
    gnm_ref[...] += lax.dot_general(grad_low, w[:, : 2 * TILE], (NT, ((), ())), preferred_element_type=F32)
    dw_ref[:, : 2 * TILE] = jnp.dot(nmt_ref[...], grad_low, preferred_element_type=F32).astype(BF16)
    dw_ref[:, 2 * TILE :] = jnp.dot(cott_ref[...], hidden, preferred_element_type=F32).astype(BF16)


def ffn(nm, nmt, cot, cott, w):
    tokens, width = nm.shape
    tiles = w.shape[1] // (3 * TILE)
    const = lambda t: (0, 0)
    by_tile = lambda t: (0, t)
    return pl.pallas_call(
        ffn_body,
        grid=(tiles,),
        in_specs=[
            pl.BlockSpec((tokens, width), const),
            pl.BlockSpec((width, tokens), const),
            pl.BlockSpec((tokens, width), const),
            pl.BlockSpec((width, tokens), const),
            pl.BlockSpec((width, 3 * TILE), by_tile),
        ],
        out_specs=[
            pl.BlockSpec((width, 3 * TILE), by_tile),
            pl.BlockSpec((tokens, width), const),
            pl.BlockSpec((tokens, width), const),
        ],
        out_shape=[
            jax.ShapeDtypeStruct((width, tiles * 3 * TILE), BF16),
            jax.ShapeDtypeStruct((tokens, width), F32),
            jax.ShapeDtypeStruct((tokens, width), F32),
        ],
        compiler_params=pltpu.CompilerParams(vmem_limit_bytes=48 * MIB),
        name="ffn",
    )(nm, nmt, cot, cott, w)


def rms_scale(values):
    return lax.rsqrt(jnp.mean(values * values, axis=-1, keepdims=True) + epsilon)


def rms_back(grad, values, scale, gain):
    normed = values * scale
    d_normed = grad * gain
    d_values = scale * (d_normed - normed * jnp.mean(d_normed * normed, axis=-1, keepdims=True))
    return d_values, jnp.sum(grad * normed, axis=0)


def by_head(parts):
    shaped = [p.reshape(p.shape[0], HEADS, -1) for p in parts]
    return jnp.concatenate(shaped, axis=2).reshape(parts[0].shape[0], -1)


def from_head(values, sizes):
    shaped = values.reshape(values.shape[0], HEADS, -1)
    ends = [sum(sizes[: i + 1]) for i in range(len(sizes))]
    cuts = [shaped[:, :, e - s : e].reshape(values.shape[0], -1) for s, e in zip(sizes, ends)]
    return jnp.concatenate(cuts, axis=1)


def split_heads(values):
    key = HEADS * DK
    val = HEADS * DV
    edges = [0, key, 2 * key, 2 * key + val, 2 * key + 2 * val]
    return [values[:, a:b] for a, b in zip(edges[:-1], edges[1:]) if b <= values.shape[1]]


def plain_block(
    devices, tokens, segment_ids, cotangent, norm1_gain, mixer_in, decay_in, conv_weight, decay_log, decay_bias,
    head_gain, mixer_out, norm2_gain, ffn_in, ffn_out,
):
    rows, width = decay_in.shape[0], tokens.shape[1]
    count = tokens.shape[0]
    hidden = ffn_out.shape[0]
    tiles = hidden // TILE

    low = lambda v: v.astype(BF16)
    shard_mixer = by_head(split_heads(low(mixer_in)))
    conv_cols = conv_weight.shape[1]
    shard_small = jnp.concatenate(
        [low(decay_in), low(norm1_gain)[:, None], low(norm2_gain)[:, None], low(conv_weight).reshape(rows, -1)], axis=1
    )
    shard_small = jnp.pad(shard_small, ((0, 0), (0, SMALL - shard_small.shape[1])))
    shard_out = low(mixer_out).T
    ffn_low = low(ffn_in)
    pieces = [ffn_low[:, :hidden], ffn_low[:, hidden:], low(ffn_out).T]
    shard_ffn = jnp.concatenate([p.reshape(rows, tiles, TILE) for p in pieces], axis=2).reshape(rows, -1)
    shards = [shard_small, shard_mixer, shard_out, shard_ffn]

    x = tokens.astype(F32)
    scale1 = rms_scale(x)
    full_small, full_mixer, full_out, full_ffn = [lax.all_gather(s, "dp", axis=0, tiled=True) for s in shards]

    decay_full = full_small[:, :16]
    gain1 = full_small[:, 16].astype(F32)
    gain2 = full_small[:, 17].astype(F32)
    taps = full_small[:, 18 : 18 + 16].reshape(devices, 4, conv_cols)
    taps = jnp.moveaxis(taps, 0, 1).reshape(4, -1).astype(F32)
    taps = by_head(split_heads(taps))

    normed_in = low(x * scale1 * gain1)
    logits = jnp.dot(normed_in, decay_full, preferred_element_type=F32)
    shifted = logits[:, :HEADS] + decay_bias
    log_decay = -jnp.exp(decay_log) * jax.nn.softplus(shifted)
    rate = jax.nn.sigmoid(logits[:, HEADS:])
    sequences = count // SEQ
    lower = jnp.tril(jnp.ones((SEQ, SEQ), F32))
    cumulative = jnp.einsum(
        "ij,sjh->sih", lower, log_decay.reshape(sequences, SEQ, HEADS), precision=lax.Precision.HIGHEST
    ).reshape(count, HEADS)
    position = jnp.arange(count) % SEQ
    keeps = []
    for back in (1, 2, 3):
        earlier = jnp.pad(segment_ids[:-back], (back, 0), constant_values=-1)
        keeps.append(((earlier == segment_ids) & (position >= back)).astype(F32)[:, None])
    segment = segment_ids.astype(F32)
    cols = jnp.concatenate([cumulative, rate] + keeps + [segment[:, None]], axis=1)
    cols = jnp.pad(cols, ((0, 0), (0, 128 - cols.shape[1])))
    seq_rows = jnp.concatenate([cumulative.T, segment[None], jnp.zeros((7, count), F32)], axis=0)
    gain_row = head_gain[None]

    proj, mixed, inverse, update, core = mixer_fwd(normed_in, full_mixer, taps, cols, seq_rows, gain_row)

    middle = x + lax.dot_general(mixed, full_out, (NT, ((), ())), preferred_element_type=F32)
    scale2 = rms_scale(middle)
    normed_mid = low(middle * scale2 * gain2)
    dw_ffn, ffn_sum, grad_nm = ffn(normed_mid, normed_mid.T, cotangent, cotangent.T, full_ffn)
    output = low(middle + ffn_sum)

    d_middle, d_gain2 = rms_back(grad_nm, middle, scale2, gain2)
    grad_middle = d_middle + cotangent.astype(F32)
    branch = low(grad_middle)
    dw_mixer, dw_out, grad_xn, d_cols, d_rows, d_taps, d_gain = mixer_bwd(
        branch, branch.T, normed_in.T, full_out, full_mixer, proj, mixed, inverse, update, core,
        taps, cols, seq_rows, gain_row,
    )

    d_cum = d_cols[:, 8:16] - d_rows.T
    d_decay = jnp.einsum(
        "ji,sjh->sih", lower, d_cum.reshape(sequences, SEQ, HEADS), precision=lax.Precision.HIGHEST
    ).reshape(count, HEADS)
    d_shifted = -d_decay * jnp.exp(decay_log) * jax.nn.sigmoid(shifted)
    d_rate = d_cols[:, :8] * rate * (1.0 - rate)
    d_logits = low(jnp.concatenate([d_shifted, d_rate], axis=1))
    grad_xn = grad_xn + lax.dot_general(d_logits, decay_full, (NT, ((), ())), preferred_element_type=F32)
    d_x, d_gain1 = rms_back(grad_xn, x, scale1, gain1)
    input_grad = d_x + grad_middle

    d_decay_in = lax.dot_general(normed_in, d_logits, (TN, ((), ())), preferred_element_type=F32)
    d_taps = from_head(d_taps, [DK, DK, DV])
    d_taps = jnp.moveaxis(d_taps.reshape(4, devices, conv_cols), 1, 0).reshape(width, -1)
    dw_small = jnp.concatenate([d_decay_in, d_gain1[:, None], d_gain2[:, None], d_taps], axis=1)
    dw_small = low(jnp.pad(dw_small, ((0, 0), (0, SMALL - dw_small.shape[1]))))
    shared = jnp.concatenate([jnp.sum(d_decay * log_decay, axis=0), jnp.sum(d_shifted, axis=0), d_gain[0]])

    own_ffn, own_out, own_mixer, own_small = [
        lax.psum_scatter(g.astype(F32), "dp", scatter_dimension=0, tiled=True)
        for g in (dw_ffn, dw_out, dw_mixer, dw_small)
    ]
    shared = lax.psum(shared, "dp")

    own_tiles = own_ffn.reshape(rows, tiles, 3, TILE)
    ffn_in_grad = jnp.concatenate([own_tiles[:, :, i].reshape(rows, hidden) for i in (0, 1)], axis=1)
    ffn_out_grad = own_tiles[:, :, 2].reshape(rows, hidden).T
    return (
        output,
        input_grad,
        own_small[:, 16],
        from_head(own_mixer, [DK, DK, DV, DV]),
        own_small[:, :16],
        own_small[:, 18 : 18 + 16].reshape(4, conv_cols),
        shared[:HEADS],
        shared[HEADS : 2 * HEADS],
        shared[2 * HEADS : 2 * HEADS + DV],
        own_out.T,
        own_small[:, 17],
        ffn_in_grad,
        ffn_out_grad,
    )


def direct_block(
    devices, tokens, segment_ids, cotangent, norm1_gain, mixer_in, decay_in, conv_weight, decay_log, decay_bias,
    head_gain, mixer_out, norm2_gain, ffn_in, ffn_out,
):
    planes = devices // 8
    gain = head_gain[None]
    masters = [
        mixer_in, mixer_out.T, ffn_in, ffn_out.T, decay_in.T, norm1_gain[None], norm2_gain[None], conv_weight,
    ]
    (
        _, full_heads, _, small, xnt, cols, seq_rows, logs, factor, middle, proj, mixed, inverse, update, core, dwf,
        output, nm_sum,
    ) = forward(
        planes, masters, tokens, cotangent, segment_ids[None], decay_log[None], decay_bias[None], gain
    )
    results = backward(
        planes, dwf, middle, nm_sum, cotangent, xnt, full_heads, proj, mixed, inverse, update, core, small, cols,
        seq_rows, logs, factor, gain, tokens,
    )
    (
        output, input_grad, d_gain1, d_mixer_in, d_decay_in, d_conv, d_log, d_bias, d_gain, d_mixer_out, d_gain2, d_ffn_in,
        d_ffn_out,
    ) = hand_over([output, *results])
    return (
        output, input_grad, d_gain1[0], d_mixer_in, d_decay_in.T, d_conv, d_log[0], d_bias[0], d_gain[0], d_mixer_out.T,
        d_gain2[0], d_ffn_in, d_ffn_out.T,
    )


def on_device(devices, *arguments):
    rows, conv_cols = arguments[4].shape[0], arguments[6].shape[1]
    direct = rows % 16 == 0 and devices == 32 and conv_cols == 128
    return (direct_block if direct else plain_block)(devices, *arguments)


def solution(mesh):
    in_specs = (
        P("dp", None), P("dp"), P("dp", None), P("dp"), P("dp", None), P("dp", None), P(None, "dp"), P(), P(), P(),
        P(None, "dp"), P("dp"), P("dp", None), P(None, "dp"),
    )
    out_specs = (
        P("dp", None), P("dp", None), P("dp"), P("dp", None), P("dp", None), P(None, "dp"), P(), P(), P(),
        P(None, "dp"), P("dp"), P("dp", None), P(None, "dp"),
    )
    return jax.shard_map(
        partial(on_device, mesh.shape["dp"]), mesh=mesh, in_specs=in_specs, out_specs=out_specs, check_vma=False
    )
```

```python
from functools import partial

import jax
import jax.numpy as jnp
from jax import lax
from jax.experimental import pallas as pl
from jax.experimental.pallas import tpu as pltpu
from jax.sharding import PartitionSpec as P

HEADS = 8
DK = 128
DV = 256
SEQ = 256
HEAD_COLS = 2 * DK + 2 * DV
CONV_COLS = 2 * DK + DV
TILE = 256
SMALL = 128
F32 = jnp.float32
BF16 = jnp.bfloat16
MESH = pl.DeviceIdType.MESH
MIB = 1 << 20
epsilon = 1e-06
head_epsilon = 0.001

NN = ((1,), (0,))
NT = ((1,), (1,))
TN = ((0,), (0,))


def dot1(left, right, dims):
    return lax.dot_general(
        left.astype(BF16), right.astype(BF16), (dims, ((), ())), preferred_element_type=F32
    )


def split(value):
    high = value.astype(BF16)
    return high, (value - high.astype(F32)).astype(BF16)


def dot3(left, right, dims):
    lh, ll = split(left)
    rh, rl = split(right)
    return dot1(lh, rh, dims) + (dot1(lh, rl, dims) + dot1(ll, rh, dims))


def dot_high(left, right, dims):
    rh, rl = split(right)
    return dot1(left, rh, dims) + dot1(left, rl, dims)


def sigmoid(value):
    return 1.0 / (1.0 + jnp.exp(-value))


def grid_of(size):
    rows = lax.broadcasted_iota(jnp.int32, (size, size), 0)
    cols = lax.broadcasted_iota(jnp.int32, (size, size), 1)
    return rows, cols


def unit_inverses(couplings):
    half = couplings[0].shape[0] // 2
    rows, cols = grid_of(half)
    apart = rows ^ cols
    eye = jnp.where(apart == 0, 1.0, 0.0)
    corners = [a[s : s + half, s : s + half] for a in couplings for s in (0, half)]
    lows = [a.astype(BF16) for a in corners]
    inverses = [eye - jnp.where(apart < 2, a, 0.0) for a in corners]
    rounded = [inv.astype(BF16) for inv in inverses]
    block = 2
    while block < half:
        here = jnp.where((apart >= block) & (apart < 2 * block), 1.0, 0.0).astype(BF16)
        firsts = [dot1(low * here, inv, NN) for low, inv in zip(lows, rounded)]
        added = [dot1(inv, first, NN) for inv, first in zip(rounded, firsts)]
        inverses = [inv - new for inv, new in zip(inverses, added)]
        rounded = [inv - new.astype(BF16) for inv, new in zip(rounded, added)]
        block *= 2
    results = []
    for i, a in enumerate(couplings):
        first, second = inverses[2 * i], inverses[2 * i + 1]
        below = -dot1(rounded[2 * i + 1], dot1(a[half:, :half], rounded[2 * i], NN), NN)
        top = jnp.concatenate([first, jnp.zeros_like(first)], axis=1)
        results.append(jnp.concatenate([top, jnp.concatenate([below, second], axis=1)], axis=0))
    return results


def pick_lane(columns, lane):
    at = lax.broadcasted_iota(jnp.int32, columns.shape, 1)
    return jnp.sum(jnp.where(at == lane, columns, 0.0), axis=1, keepdims=True)


def conv_of(values, taps, keep):
    total = values * taps[0:1]
    for back in (1, 2, 3):
        total = total + pltpu.roll(values, back, 0) * keep[back - 1] * taps[back : back + 1]
    return total


def decays(seg_col, seg_row, cum_col, cum_row):
    rows, cols = grid_of(SEQ)
    linked = (seg_col == seg_row) & (rows >= cols)
    return jnp.where(linked, jnp.exp(jnp.where(linked, cum_col - cum_row, 0.0)), 0.0)


def strict(value):
    rows, cols = grid_of(SEQ)
    return jnp.where(rows > cols, value, 0.0)


def head_inputs(projected, taps, cols, head):
    keep = [pick_lane(cols, 16 + i) for i in range(3)]
    conv = conv_of(projected[:, :CONV_COLS], taps, keep)
    gate = sigmoid(conv)
    act = conv * gate
    q_act, k_act, value = act[:, :DK], act[:, DK : 2 * DK], act[:, 2 * DK :]
    q_scale = lax.rsqrt(jnp.sum(q_act * q_act, axis=1, keepdims=True) + epsilon)
    k_scale = lax.rsqrt(jnp.sum(k_act * k_act, axis=1, keepdims=True) + epsilon)
    cum = pick_lane(cols, head)
    rate = pick_lane(cols, 8 + head)
    seg = pick_lane(cols, 19)
    return keep, conv, gate, act, q_act * q_scale, k_act * k_scale, value, q_scale, k_scale, cum, rate, seg


def flip(number, bit):
    return number + bit - 2 * bit * ((number // bit) % 2)


def enter(me, before=lambda: None):
    barrier = pltpu.get_barrier_semaphore()
    partners = [flip(me, bit) for bit in (1, 2, 4, 8, 16)]
    for other in partners:
        pl.semaphore_signal(barrier, inc=1, device_id=(other,), device_id_type=MESH)
    before()
    pl.semaphore_wait(barrier, len(partners))


def span(k, width, start, size):
    first = k * width + start
    return pl.ds(first if isinstance(first, int) else pl.multiple_of(first, 128), size)


def remote(source, target, send_sem, recv_sem, other):
    return pltpu.make_async_remote_copy(
        src_ref=source, dst_ref=target, send_sem=send_sem, recv_sem=recv_sem,
        device_id=(other,), device_id_type=MESH,
    )


(
    G_NEAR, G_FAR, G_RELAY, G_X, G_Y, G_CORNER_Y, G_CORNER_X, G_CORE_OWN,
    G_CORE_OTHER, G_TWO_X, G_TWO_Y, G_TWO_CORNER, G_TWO_NEAR, G_TWO_FAR, G_TWO_RELAY, G_TWO_CORE,
) = range(16)
(
    S_CORE, S_XY_X, S_XY_Y, S_X_EARLY, S_X_LATE, S_Y_EARLY, S_Y_LATE, S_RELAY,
    S_NEAR, S_FAR, S_TWO_RELAY, S_TWO_NEAR, S_TWO_FAR, S_TWO_XY, S_TWO_X, S_TWO_Y,
) = range(16)
B_CORE, B_KEEP, B_SUMS, B_XY, B_X, B_Y, B_Z, B_TWO_Z, B_TWO = range(9)
HEAD, FFN_TILE, SMALLS = range(3)


SHAPES = {
    HEAD: (HEAD_COLS + DV, HEAD_COLS, HEAD_COLS // 2),
    FFN_TILE: (3 * TILE, 5 * TILE // 2, 3 * TILE // 2),
    SMALLS: (2 * SMALL, 2 * SMALL, SMALL),
}


class Gather:
    copies = 16

    def __init__(self, me, kinds, local_sem, send_sem, recv_sem):
        self.me, self.kinds = me, kinds
        self.local_sem, self.send_sem, self.recv_sem = local_sem, send_sem, recv_sem
        self.z, self.y, self.x, self.core = me // 8, (me // 4) % 2, (me // 2) % 2, me % 2

    def local(self, kind, k):
        shard, full, base = self.kinds[kind]
        width = SHAPES[kind][0]
        cols = span(k, width, 0, width)
        return pltpu.make_async_copy(
            shard.at[:, cols], full.at[self.z, self.y, self.x, self.core, :, cols], self.local_sem.at[base + k]
        )

    def copy(self, kind, k, name):
        shard, full, base = self.kinds[kind]
        width, part, half = SHAPES[kind]
        one = span(k, width, 0, part)
        two = span(k, width, part, width - part)
        z, y, x, core = self.z, self.y, self.x, self.core
        near, far = flip(z, 1), flip(z, 2)
        here = lambda cols: (shard.at[:, cols], full.at[z, y, x, core, :, cols])
        same = lambda ref: (ref, ref)
        (source, target), bit = {
            G_NEAR: lambda: (here(one), 8),
            G_FAR: lambda: (here(one), 16),
            G_RELAY: lambda: (same(full.at[far, y, x, core, :, one]), 8),
            G_X: lambda: (same(full.at[:, y, x, core, :, one]), 2),
            G_Y: lambda: (same(full.at[:, y, x, core, :, one]), 4),
            G_CORNER_Y: lambda: (same(full.at[:, y, 1 - x, core, :, span(k, width, 0, half)]), 4),
            G_CORNER_X: lambda: (same(full.at[:, 1 - y, x, core, :, span(k, width, half, part - half)]), 2),
            G_CORE_OWN: lambda: (same(full.at[:, y, :, core, :, one]), 1),
            G_CORE_OTHER: lambda: (same(full.at[:, 1 - y, :, core, :, one]), 1),
            G_TWO_X: lambda: (here(two), 2),
            G_TWO_Y: lambda: (here(two), 4),
            G_TWO_CORNER: lambda: (same(full.at[z, 1 - y, x, core, :, two]), 2),
            G_TWO_NEAR: lambda: (same(full.at[z, :, :, core, :, two]), 8),
            G_TWO_FAR: lambda: (same(full.at[z, :, :, core, :, two]), 16),
            G_TWO_RELAY: lambda: (same(full.at[far, :, :, core, :, two]), 8),
            G_TWO_CORE: lambda: (same(full.at[:, :, :, core, :, two]), 1),
        }[name]()
        sems = self.send_sem.at[base + k, name], self.recv_sem.at[base + k, name]
        return remote(source, target, *sems, flip(self.me, bit))

    def send(self, kind, k, *names):
        for name in names:
            self.copy(kind, k, name).start()

    def wait(self, kind, k, *names):
        for name in names:
            self.copy(kind, k, name).wait_recv()

    def two(self, kind):
        return SHAPES[kind][0] > SHAPES[kind][1]

    def start(self, kind, k):
        self.local(kind, k).start()
        self.send(kind, k, G_FAR, G_NEAR)
        if self.two(kind):
            self.send(kind, k, G_TWO_X, G_TWO_Y)

    def relay(self, kind, k):
        self.wait(kind, k, G_FAR)
        self.send(kind, k, G_RELAY)
        if self.two(kind):
            self.wait(kind, k, G_TWO_Y)
            self.send(kind, k, G_TWO_CORNER)

    def square(self, kind, k):
        self.local(kind, k).wait()
        self.wait(kind, k, G_NEAR, G_RELAY)
        self.send(kind, k, G_X, G_Y)
        if self.two(kind):
            self.wait(kind, k, G_TWO_X, G_TWO_CORNER)
            self.send(kind, k, G_TWO_FAR, G_TWO_NEAR)

    def corner(self, kind, k):
        self.wait(kind, k, G_X)
        self.send(kind, k, G_CORNER_Y, G_CORE_OWN)
        self.wait(kind, k, G_Y)
        self.send(kind, k, G_CORNER_X)
        if self.two(kind):
            self.wait(kind, k, G_TWO_FAR)
            self.send(kind, k, G_TWO_RELAY)

    def across(self, kind, k):
        self.wait(kind, k, G_CORNER_Y, G_CORNER_X)
        self.send(kind, k, G_CORE_OTHER)
        if self.two(kind):
            self.wait(kind, k, G_TWO_NEAR, G_TWO_RELAY)
            self.send(kind, k, G_TWO_CORE)

    def complete(self, kind, k):
        self.wait(kind, k, G_CORE_OWN, G_CORE_OTHER)
        if self.two(kind):
            self.wait(kind, k, G_TWO_CORE)

    def finish(self, kind, k):
        names = [G_NEAR, G_FAR, G_RELAY, G_X, G_Y, G_CORNER_Y, G_CORNER_X, G_CORE_OWN, G_CORE_OTHER]
        if self.two(kind):
            names += [G_TWO_X, G_TWO_Y, G_TWO_CORNER, G_TWO_NEAR, G_TWO_FAR, G_TWO_RELAY, G_TWO_CORE]
        for name in names:
            self.copy(kind, k, name).wait_send()


class Scatter:
    copies = 16
    depths = {B_CORE: 4, B_KEEP: 2, B_SUMS: 8, B_XY: 4, B_X: 8, B_Y: 8, B_Z: 8, B_TWO_Z: 8, B_TWO: 8}

    def __init__(self, me, kinds, store, core, keep, sums, xy, x, y, z, two_z, two, local_sem, send_sem, recv_sem):
        self.me, self.kinds, self.store = me, kinds, store
        self.from_core, self.keep, self.sums = core, keep, sums
        self.from_xy, self.from_x, self.from_y, self.from_z = xy, x, y, z
        self.two_z, self.from_two = two_z, two
        self.local_sem, self.send_sem, self.recv_sem = local_sem, send_sem, recv_sem
        self.z, self.core = me // 8, me % 2
        self.here = (me // 2) % 4
        self.across_x, self.across_y = flip(self.here, 1), flip(self.here, 2)
        self.both = 3 - self.here
        self.near, self.far = flip(self.z, 1), flip(self.z, 2)
        self.opposite = 3 - self.z

    def slot(self, name, r):
        return r % self.depths[name]

    def copy(self, kind, r, k, name):
        source = self.kinds[kind][0]
        width, part, half = SHAPES[kind]
        whole, one, two = pl.ds(0, width), pl.ds(0, part), pl.ds(part, width - part)
        first, second = pl.ds(0, half), pl.ds(half, part - half)
        rest = pl.ds(0, width - part)
        sums = self.sums.at[self.slot(B_SUMS, r)]
        here, across_x, across_y, both, z = self.here, self.across_x, self.across_y, self.both, self.z
        place = lambda where, cols: sums.at[:, where, :, cols]
        origin, target, bit = {
            S_CORE: lambda: (
                source(k, 1 - self.core), self.from_core.at[self.slot(B_CORE, r), :, :, :, whole], 1
            ),
            S_XY_X: lambda: (place(both, first), self.from_xy.at[self.slot(B_XY, r), :, :, first], 2),
            S_XY_Y: lambda: (place(both, second), self.from_xy.at[self.slot(B_XY, r), :, :, second], 4),
            S_X_EARLY: lambda: (place(across_x, first), self.from_x.at[self.slot(B_X, r), :, :, first], 2),
            S_X_LATE: lambda: (place(across_x, second), self.from_x.at[self.slot(B_X, r), :, :, second], 2),
            S_Y_EARLY: lambda: (place(across_y, second), self.from_y.at[self.slot(B_Y, r), :, :, second], 4),
            S_Y_LATE: lambda: (place(across_y, first), self.from_y.at[self.slot(B_Y, r), :, :, first], 4),
            S_RELAY: lambda: (sums.at[self.opposite, here, :, one], self.from_z.at[self.slot(B_Z, r), 0, :, one], 8),
            S_NEAR: lambda: (sums.at[self.near, here, :, one], self.from_z.at[self.slot(B_Z, r), 1, :, one], 8),
            S_FAR: lambda: (sums.at[self.far, here, :, one], self.from_z.at[self.slot(B_Z, r), 2, :, one], 16),
            S_TWO_RELAY: lambda: (
                sums.at[self.opposite, :, :, two], self.two_z.at[self.slot(B_TWO_Z, r), 0, :, :, rest], 8
            ),
            S_TWO_NEAR: lambda: (
                sums.at[self.near, :, :, two], self.two_z.at[self.slot(B_TWO_Z, r), 1, :, :, rest], 8
            ),
            S_TWO_FAR: lambda: (
                sums.at[self.far, :, :, two], self.two_z.at[self.slot(B_TWO_Z, r), 2, :, :, rest], 16
            ),
            S_TWO_XY: lambda: (
                sums.at[z, both, :, two], self.from_two.at[self.slot(B_TWO, r), 0, :, rest], 4
            ),
            S_TWO_X: lambda: (sums.at[z, across_x, :, two], self.from_two.at[self.slot(B_TWO, r), 1, :, rest], 2),
            S_TWO_Y: lambda: (sums.at[z, across_y, :, two], self.from_two.at[self.slot(B_TWO, r), 2, :, rest], 4),
        }[name]()
        sems = self.send_sem.at[r, name], self.recv_sem.at[r, name]
        return remote(origin, target, *sems, flip(self.me, bit))

    def send(self, kind, r, k, *names):
        for name in names:
            self.copy(kind, r, k, name).start()

    def wait(self, kind, r, k, *names):
        for name in names:
            self.copy(kind, r, k, name).wait_recv()

    def two(self, kind):
        return SHAPES[kind][0] > SHAPES[kind][1]

    def load(self, kind, r, k):
        source = self.kinds[kind][0]
        return pltpu.make_async_copy(
            source(k, self.core), self.keep.at[r % 2, :, :, :, pl.ds(0, SHAPES[kind][0])], self.local_sem.at[r]
        )

    def core_step(self, kind, r, k):
        self.send(kind, r, k, S_CORE)

    def load_step(self, kind, r, k):
        if self.kinds[kind][1] is None:
            self.load(kind, r, k).start()

    def add_planes(self, r, place, cols, first, others):
        def one(plane, carry):
            total = first(plane).astype(F32)
            for read in others:
                total = total + read(plane).astype(F32)
            self.sums[self.slot(B_SUMS, r), plane, place, :, cols] = total.astype(BF16)
            return carry

        lax.fori_loop(0, 4, one, 0)

    def add_places(self, r, plane, cols, others):
        slot = self.slot(B_SUMS, r)
        for place in range(4):
            total = self.sums[slot, plane, place, :, cols].astype(F32)
            for read in others:
                total = total + read(place).astype(F32)
            self.sums[slot, plane, place, :, cols] = total.astype(BF16)

    def held(self, r, place, cols):
        return lambda plane: self.sums[self.slot(B_SUMS, r), plane, place, :, cols]

    def chip_step(self, kind, r, k):
        in_place = self.kinds[kind][1]
        width, part, half = SHAPES[kind]
        whole = pl.ds(0, width)
        self.wait(kind, r, k, S_CORE)
        if in_place is None:
            self.load(kind, r, k).wait()
            mine = lambda place: (lambda plane: self.keep[r % 2, plane, place, :, whole])
        else:
            mine = lambda place: (lambda plane: in_place(k, plane, place, self.core))
        got = lambda place: (lambda plane: self.from_core[self.slot(B_CORE, r), plane, place, :, whole])
        for place, names in (
            (self.both, (S_XY_X, S_XY_Y)),
            (self.across_x, (S_X_EARLY,)),
            (self.across_y, (S_Y_EARLY,)),
            (self.here, (S_TWO_RELAY, S_TWO_NEAR) if self.two(kind) else ()),
        ):
            self.add_planes(r, place, whole, got(place), [mine(place)])
            self.send(kind, r, k, *names)
        self.copy(kind, r, k, S_CORE).wait_send()

    def corner_step(self, kind, r, k):
        width, part, half = SHAPES[kind]
        first, second = pl.ds(0, half), pl.ds(half, part - half)
        passed = lambda cols: (lambda plane: self.from_xy[self.slot(B_XY, r), plane, :, cols])
        self.wait(kind, r, k, S_XY_X)
        self.add_planes(r, self.across_y, first, self.held(r, self.across_y, first), [passed(first)])
        self.send(kind, r, k, S_Y_LATE)
        self.wait(kind, r, k, S_XY_Y)
        self.add_planes(r, self.across_x, second, self.held(r, self.across_x, second), [passed(second)])
        self.send(kind, r, k, S_X_LATE)
        if self.two(kind):
            two, rest = pl.ds(part, width - part), pl.ds(0, width - part)
            self.wait(kind, r, k, S_TWO_RELAY)
            self.add_places(r, self.far, two, [lambda place: self.two_z[self.slot(B_TWO_Z, r), 0, place, :, rest]])
            self.send(kind, r, k, S_TWO_FAR)

    def square_step(self, kind, r, k):
        width, part, half = SHAPES[kind]
        one = pl.ds(0, part)
        self.wait(kind, r, k, S_X_EARLY, S_X_LATE, S_Y_EARLY, S_Y_LATE)
        from_x = lambda plane: self.from_x[self.slot(B_X, r), plane, :, one]
        from_y = lambda plane: self.from_y[self.slot(B_Y, r), plane, :, one]
        self.add_planes(r, self.here, one, self.held(r, self.here, one), [from_x, from_y])
        self.send(kind, r, k, S_RELAY, S_NEAR)
        if self.two(kind):
            two, rest = pl.ds(part, width - part), pl.ds(0, width - part)
            self.wait(kind, r, k, S_TWO_NEAR, S_TWO_FAR)
            self.add_places(
                r, self.z, two,
                [lambda place, i=i: self.two_z[self.slot(B_TWO_Z, r), i, place, :, rest] for i in (1, 2)],
            )
            self.send(kind, r, k, S_TWO_XY, S_TWO_Y)

    def relay_step(self, kind, r, k):
        width, part, half = SHAPES[kind]
        slot, one = self.slot(B_SUMS, r), pl.ds(0, part)
        self.wait(kind, r, k, S_RELAY)
        total = self.sums[slot, self.far, self.here, :, one].astype(F32)
        total = total + self.from_z[self.slot(B_Z, r), 0, :, one].astype(F32)
        self.sums[slot, self.far, self.here, :, one] = total.astype(BF16)
        self.send(kind, r, k, S_FAR)
        if self.two(kind):
            two, rest = pl.ds(part, width - part), pl.ds(0, width - part)
            place = self.across_x
            self.wait(kind, r, k, S_TWO_XY)
            total = self.sums[slot, self.z, place, :, two].astype(F32)
            total = total + self.from_two[self.slot(B_TWO, r), 0, :, rest].astype(F32)
            self.sums[slot, self.z, place, :, two] = total.astype(BF16)
            self.send(kind, r, k, S_TWO_X)

    def last_step(self, kind, r, k):
        width, part, half = SHAPES[kind]
        slot, one = self.slot(B_SUMS, r), pl.ds(0, part)
        self.wait(kind, r, k, S_NEAR, S_FAR)
        total = self.sums[slot, self.z, self.here, :, one].astype(F32)
        for i in (1, 2):
            total = total + self.from_z[self.slot(B_Z, r), i, :, one].astype(F32)
        names = [S_XY_X, S_XY_Y, S_X_EARLY, S_X_LATE, S_Y_EARLY, S_Y_LATE, S_RELAY, S_NEAR, S_FAR]
        if self.two(kind):
            two, rest = pl.ds(part, width - part), pl.ds(0, width - part)
            self.wait(kind, r, k, S_TWO_X, S_TWO_Y)
            more = self.sums[slot, self.z, self.here, :, two].astype(F32)
            for i in (1, 2):
                more = more + self.from_two[self.slot(B_TWO, r), i, :, rest].astype(F32)
            total = jnp.concatenate([total, more], axis=1)
            names += [S_TWO_RELAY, S_TWO_NEAR, S_TWO_FAR, S_TWO_XY, S_TWO_X, S_TWO_Y]
        self.store(kind, k, total)
        for name in names:
            self.copy(kind, r, k, name).wait_send()


class Total:
    bits = (1, 2, 4, 8, 16)

    def __init__(self, me, value_ref, store, got, stage, send_sem, recv_sem):
        self.me, self.value_ref, self.store = me, value_ref, store
        self.got, self.stage, self.send_sem, self.recv_sem = got, stage, send_sem, recv_sem

    def copy(self, number):
        sems = self.send_sem.at[number], self.recv_sem.at[number]
        return remote(self.stage.at[number], self.got.at[number], *sems, flip(self.me, self.bits[number]))

    def step(self, number):
        last = len(self.bits)
        value = self.value_ref[...]
        if number > 0:
            self.copy(number - 1).wait_recv()
            value = self.stage[number - 1] + self.got[number - 1]
        if number < last:
            self.stage[number] = value
            self.copy(number).start()
        else:
            self.store(value)
            for number in range(last):
                self.copy(number).wait_send()


def triangle_sum(values, dims):
    rows, cols = grid_of(SEQ)
    ones = jnp.where(rows >= cols, 1.0, 0.0).astype(BF16)
    first, rest = values.astype(BF16), values - values.astype(BF16).astype(F32)
    second, third = split(rest)
    return dot1(ones, first, dims) + (dot1(ones, second, dims) + dot1(ones, third, dims))


def log1p(value):
    series = value * (1.0 - value * (0.5 - value * (1.0 / 3.0 - value * (0.25 - value * 0.2))))
    return jnp.where(value < 0.01, series, jnp.log(1.0 + value))


def softplus(value):
    return jnp.maximum(value, 0.0) + log1p(jnp.exp(-jnp.abs(value)))


def merge(block):
    return block.reshape(-1, block.shape[-1])


def head_taps(small_ref, head):
    wide = 2 * head
    places = [(0, head), (1, head)] + [(2 + head // 4, wide % 8 + i) for i in (0, 1)]
    blocks = [
        small_ref[z, p // 4, (p // 2) % 2, p % 2, 0:16, SMALL : 2 * SMALL][0:4].astype(F32) for z, p in places
    ]
    return jnp.concatenate(blocks, axis=1)


def row_blocks(count, body, size=128):
    def one(i, carry):
        body(pl.ds(pl.multiple_of(i * size, size), size))
        return carry

    lax.fori_loop(0, count // size, one, 0)


def lane_index(shape):
    return lax.broadcasted_iota(jnp.int32, shape, 1)


def forward_body(
    planes, tiles,
    mixer_in_ref, mixer_out_ref, ffn_in_ref, ffn_out_ref, decay_in_ref, gain1_ref, gain2_ref, conv_ref,
    x_in, cot_in, seg_ref, log_ref, bias_ref, gain_ref,
    full_small, full_heads, full_tiles, small_out, xnt_out, cols_out, rows_out, logs_out, factor_out, middle_out,
    proj_ref, mixed_ref, inv_ref, upd_ref, core_ref, dw_ref, output_ref, nm_sum,
    small_ref, xnt_ref, cols_ref, rows_ref, logs_ref, factor_ref, middle, x_ref, cot_ref, load_sem, flush_sem,
    shard_small, shard_heads, shard_tiles, turn, consts_ref,
    w_buf, xn, cott, nm, nmt, out_sum, gains, copy_sem, w_sem, local_sem, send_sem, recv_sem,
):
    step = pl.program_id(0)
    tokens = x_ref.shape[0]
    chunks = HEADS + tiles
    me = lax.axis_index("dp")
    kinds = {
        SMALLS: (shard_small, full_small, chunks),
        HEAD: (shard_heads, full_heads, 0),
        FFN_TILE: (shard_tiles, full_tiles, HEADS),
    }
    work = Gather(me, kinds, local_sem, send_sem, recv_sem)

    def at(chunk, act):
        pl.when((chunk >= 0) & (chunk < HEADS))(lambda: act(HEAD, chunk))
        pl.when((chunk >= HEADS) & (chunk < chunks))(lambda: act(FFN_TILE, chunk - HEADS))

    def weights(kind, k, slot, plane=None):
        full, width = kinds[kind][1], SHAPES[kind][0]
        source = full.at[:, :, :, :, :, span(k, width, 0, width)]
        place = w_buf.at[slot, :, :, :, :, :, pl.ds(0, width)]
        if plane is not None:
            source, place = source.at[plane], place.at[plane]
        return pltpu.make_async_copy(source, place, w_sem.at[slot])

    def load_weights(kind, k, slot):
        for plane in range(planes):
            weights(kind, k, slot, plane).start()

    def arrive(kind, k):
        work.complete(kind, k)
        load_weights(kind, k, k % 2 if isinstance(k, int) else (step + 1) % 2)

    def arrive_early(kind, k):
        pl.when(step + 1 != chunks - 1)(lambda: arrive(kind, k))

    def arrive_late(kind, k):
        pl.when(step + 1 == chunks - 1)(lambda: arrive(kind, k))

    at_start = ((3, work.corner), (1, arrive_early))
    at_middle = ((7, work.start), (6, work.relay), (5, work.square), (2, work.across))

    def early(step):
        for lead, act in sorted(at_start[:1] + at_middle + ((1, arrive),), key=lambda item: -item[0]):
            if step + lead >= 0:
                act(HEAD, step + lead)

    def midway():
        for lead, act in at_middle:
            at(step + lead, act)
        at(step + 1, arrive_late)

    loads = [
        pltpu.make_async_copy(source, target, load_sem.at[i])
        for i, (source, target) in enumerate(((x_in, x_ref), (cot_in, cot_ref)))
    ]
    flushes = [
        pltpu.make_async_copy(source, target, flush_sem.at[i])
        for i, (source, target) in enumerate(
            (
                (small_ref, small_out), (xnt_ref, xnt_out), (cols_ref, cols_out), (rows_ref, rows_out),
                (logs_ref, logs_out), (factor_ref, factor_out), (middle, middle_out),
            )
        )
    ]

    def pack_heads():
        for copy in loads:
            copy.start()
        turn[...] = jnp.zeros_like(turn)
        turn[0:16, 0 : conv_ref.shape[1] // 4] = decay_in_ref[...]
        turn[16:17, 0 : conv_ref.shape[1] // 4] = gain1_ref[...]
        turn[17:18, 0 : conv_ref.shape[1] // 4] = gain2_ref[...]
        rows = shard_small.shape[0]
        shard_small[:, 0:SMALL] = turn[...].T[0:rows].astype(BF16)
        taps = jnp.concatenate([conv_ref[...], jnp.zeros((rows - 4, SMALL), F32)], axis=0)
        shard_small[:, SMALL:] = taps.astype(BF16)
        for h in range(HEADS):
            at_col = h * (HEAD_COLS + DV)
            key, val = HEADS * DK, HEADS * DV
            for ref, start, size in (
                (mixer_in_ref, h * DK, DK),
                (mixer_in_ref, key + h * DK, DK),
                (mixer_in_ref, 2 * key + h * DV, DV),
                (mixer_in_ref, 2 * key + val + h * DV, DV),
                (mixer_out_ref, h * DV, DV),
            ):
                shard_heads[:, at_col : at_col + size] = ref[:, start : start + size].astype(BF16)
                at_col += size

    def pack_tiles():
        for t in range(tiles):
            at_col = t * 3 * TILE
            for ref, start in ((ffn_in_ref, t * TILE), (ffn_in_ref, (tiles + t) * TILE), (ffn_out_ref, t * TILE)):
                shard_tiles[:, at_col : at_col + TILE] = ref[:, start : start + TILE].astype(BF16)
                at_col += TILE

    @pl.when(step == 0)
    def _():
        enter(me, pack_heads)
        work.start(SMALLS, 0)
        early(-7)
        pack_tiles()
        consts_ref[...] = jnp.zeros_like(consts_ref)
        consts_ref[0:1, 0:HEADS] = -jnp.exp(log_ref[...])
        consts_ref[1:2, 0:HEADS] = bias_ref[...]

        def prepare(rows):
            middle[rows, :] = x_ref[rows, :].astype(F32)
            cott[:, rows] = cot_ref[rows, :].astype(F32).T.astype(BF16)

        for copy in loads:
            copy.wait()
        row_blocks(tokens, prepare)
        work.relay(SMALLS, 0)
        early(-6)
        work.square(SMALLS, 0)
        early(-5)
        work.corner(SMALLS, 0)
        early(-4)
        work.across(SMALLS, 0)
        out_sum[...] = jnp.zeros_like(out_sum)
        nm_sum[...] = jnp.zeros_like(nm_sum)
        early(-3)
        work.complete(SMALLS, 0)
        early(-2)
        copy = pltpu.make_async_copy(full_small, small_ref, copy_sem)
        copy.start()
        copy.wait()
        small = merge(small_ref[..., 0:SMALL])
        turned = small.astype(F32).T
        gains[0:1, :] = turned[16:17, :]
        gains[1:2, :] = turned[17:18, :]

        def norm(rows):
            x = middle[rows, :]
            scale = lax.rsqrt(jnp.mean(x * x, axis=1, keepdims=True) + epsilon)
            normed = x * scale * gains[0:1, :]
            xn[rows, :] = normed.astype(BF16)
            xnt_ref[:, rows] = normed.T.astype(BF16)

        row_blocks(tokens, norm)
        logits = jnp.dot(xn[...], small, preferred_element_type=F32)
        lanes = lane_index(logits.shape)
        decay_scale, bias = consts_ref[0:1, :], consts_ref[1:2, :]
        shifted = logits + bias
        rate = sigmoid(logits)
        log_decay = decay_scale * softplus(shifted)
        logs_ref[...] = log_decay
        factor_ref[...] = jnp.where(
            lanes < 8, decay_scale * sigmoid(shifted), jnp.where(lanes < 16, rate * (1.0 - rate), 0.0)
        )
        seg_row = jnp.broadcast_to(seg_ref[...].astype(F32), (128, tokens))
        segment = seg_row.T
        rows_ref[8:16, :] = seg_row[0:8]
        inside = lax.broadcasted_iota(jnp.int32, segment.shape, 0) % SEQ
        aux = segment
        for back in (1, 2, 3):
            linked = (pltpu.roll(segment, back, 0) == segment) & (inside >= back)
            aux = jnp.where(lanes == 15 + back, jnp.where(linked, 1.0, 0.0), aux)
        for start in range(0, tokens, SEQ):
            part = slice(start, start + SEQ)
            cum = triangle_sum(log_decay[part], NN)
            cols_ref[part, :] = jnp.where(lanes[part] < 8, cum, jnp.where(lanes[part] < 16, rate[part], aux[part]))
            rows_ref[0:8, part] = cum.T[0:8]
        early(-1)
        work.finish(SMALLS, 0)

    for lead, act in at_start:
        at(step + lead, act)
    at(step, lambda kind, k: weights(kind, k, step % 2).wait())
    at(step - 1, work.finish)

    @pl.when(step == 1)
    def _():
        for copy in flushes[:-1]:
            copy.start()

    @pl.when(step < HEADS)
    def _():
        w = merge(w_buf[step % 2])
        projected = jnp.dot(xn[...], w[:, :HEAD_COLS], preferred_element_type=F32)
        proj_ref[...] = projected
        midway()
        _, _, _, _, q, k, value, _, _, cum, rate, seg = head_inputs(
            projected, head_taps(small_ref, step), cols_ref[...], step
        )
        q = q * DK**-0.5
        cum_row = rows_ref[pl.ds(step, 1), :]
        seg_row = rows_ref[8:9, :]
        parts = [slice(s, s + SEQ) for s in range(0, tokens, SEQ)]
        scores, couplings = [], []
        for part in parts:
            pair = decays(seg[part], seg_row[:, part], cum[part], cum_row[:, part])
            key_dots = dot3(k[part], k[part], NT)
            scores.append(pair * dot3(q[part], k[part], NT))
            couplings.append(strict(pair * key_dots) * rate[part])
        inverses = unit_inverses(couplings)
        for i, part in enumerate(parts):
            update = dot3(inverses[i], rate[part] * value[part], NN)
            core = dot3(scores[i], update, NN)
            inv_ref[0, part, :] = inverses[i].astype(BF16)
            upd_ref[0, part, :] = update
            core_ref[0, part, :] = core
            scale = lax.rsqrt(jnp.mean(core * core, axis=1, keepdims=True) + head_epsilon)
            out_gate = projected[part, CONV_COLS:]
            mixed_ref[part, :] = (core * scale * gain_ref[...] * (out_gate * sigmoid(out_gate))).astype(BF16)
        middle[...] += lax.dot_general(mixed_ref[...], w[:, HEAD_COLS:], (NT, ((), ())), preferred_element_type=F32)

    @pl.when(step == HEADS)
    def _():
        def norm(rows):
            mid = middle[rows, :]
            scale = lax.rsqrt(jnp.mean(mid * mid, axis=1, keepdims=True) + epsilon)
            normed = mid * scale * gains[1:2, :]
            nm[rows, :] = normed.astype(BF16)
            nmt[:, rows] = normed.T.astype(BF16)

        flushes[-1].start()
        row_blocks(tokens, norm)

    @pl.when(step >= HEADS)
    def _():
        w = merge(w_buf[step % 2, :, :, :, :, :, 0 : 3 * TILE])
        gate_up = jnp.dot(nm[...], w[:, : 2 * TILE], preferred_element_type=F32)
        gate, up = gate_up[:, :TILE], gate_up[:, TILE:]
        sig = sigmoid(gate)
        swish = gate * sig
        hidden = (swish * up).astype(BF16)
        midway()
        grad_hidden = jnp.dot(cot_ref[...], w[:, 2 * TILE :], preferred_element_type=F32)
        grad_gate = grad_hidden * up * (sig + swish * (1.0 - sig))
        grad_up = grad_hidden * swish
        grad_low = jnp.concatenate([grad_gate, grad_up], axis=1).astype(BF16)
        out_sum[...] += lax.dot_general(hidden, w[:, 2 * TILE :], (NT, ((), ())), preferred_element_type=F32)
        nm_sum[...] += lax.dot_general(grad_low, w[:, : 2 * TILE], (NT, ((), ())), preferred_element_type=F32)
        dw_ref[:, : 2 * TILE] = jnp.dot(nmt[...], grad_low, preferred_element_type=F32).astype(BF16)
        dw_ref[:, 2 * TILE :] = jnp.dot(cott[...], hidden, preferred_element_type=F32).astype(BF16)

    @pl.when(step == chunks - 1)
    def _():
        def add(rows):
            output_ref[rows, :] = (middle[rows, :] + out_sum[rows, :]).astype(BF16)

        row_blocks(tokens, add)
        work.finish(FFN_TILE, tiles - 1)
        for copy in flushes:
            copy.wait()


def once(shape):
    return pl.BlockSpec(shape, lambda i: (0,) * len(shape), pipeline_mode=pl.Buffered(1))


def forward(planes, masters, x, cot, *others):
    rows, tokens, width = masters[0].shape[0], *x.shape
    tiles = masters[3].shape[1] // TILE
    chunks = HEADS + tiles
    widths = (2 * SMALL, HEADS * (HEAD_COLS + DV), tiles * 3 * TILE)
    hbm = pl.BlockSpec(memory_space=pl.ANY)
    head = lambda i: jnp.minimum(i, HEADS - 1)
    tile = lambda i: jnp.maximum(i - HEADS, 0)
    save = pl.BlockSpec((1, tokens, SEQ), lambda i: (head(i), 0, 0))
    shape = jax.ShapeDtypeStruct
    whole = [((planes, 2, 2, 2, rows, w), BF16) for w in widths]
    outs = [
        (hbm, *whole[0]),
        (hbm, *whole[1]),
        (hbm, *whole[2]),
        (hbm, *whole[0]),
        (hbm, (width, tokens), BF16),
        (hbm, (tokens, 128), F32),
        (hbm, (16, tokens), F32),
        (hbm, (tokens, 128), F32),
        (hbm, (tokens, 128), F32),
        (hbm, (tokens, width), F32),
        (pl.BlockSpec((tokens, HEAD_COLS), lambda i: (0, head(i))), (tokens, HEADS * HEAD_COLS), F32),
        (pl.BlockSpec((tokens, DV), lambda i: (0, head(i))), (tokens, HEADS * DV), BF16),
        (save, (HEADS, tokens, SEQ), BF16),
        (save, (HEADS, tokens, DV), F32),
        (save, (HEADS, tokens, DV), F32),
        (pl.BlockSpec((width, 3 * TILE), lambda i: (0, tile(i))), (width, tiles * 3 * TILE), BF16),
        (once((tokens, width)), (tokens, width), BF16),
        (once((tokens, width)), (tokens, width), F32),
    ]
    return pl.pallas_call(
        partial(forward_body, planes, tiles),
        grid=(chunks,),
        in_specs=[once(a.shape) for a in masters] + [hbm, hbm] + [once(a.shape) for a in others],
        out_specs=[o[0] for o in outs],
        out_shape=[shape(o[1], o[2]) for o in outs],
        scratch_shapes=[pltpu.VMEM(o[1], o[2]) for o in outs[3:10]]
        + [
            pltpu.VMEM((tokens, width), BF16),
            pltpu.VMEM((tokens, width), BF16),
            pltpu.SemaphoreType.DMA((2,)),
            pltpu.SemaphoreType.DMA((7,)),
        ]
        + [pltpu.VMEM((rows, w), BF16) for w in widths]
        + [
            pltpu.VMEM((128, 128), F32),
            pltpu.VMEM((8, 128), F32),
            pltpu.VMEM((2, planes, 2, 2, 2, rows, HEAD_COLS + DV), BF16),
            pltpu.VMEM((tokens, width), BF16),
            pltpu.VMEM((width, tokens), BF16),
            pltpu.VMEM((tokens, width), BF16),
            pltpu.VMEM((width, tokens), BF16),
            pltpu.VMEM((tokens, width), F32),
            pltpu.VMEM((8, width), F32),
            pltpu.SemaphoreType.DMA,
            pltpu.SemaphoreType.DMA((2,)),
            pltpu.SemaphoreType.DMA((chunks + 1,)),
            pltpu.SemaphoreType.DMA((chunks + 1, Gather.copies)),
            pltpu.SemaphoreType.DMA((chunks + 1, Gather.copies)),
        ],
        compiler_params=pltpu.CompilerParams(
            collective_id=0, has_side_effects=True, vmem_limit_bytes=60 * MIB
        ),
        name="forward",
    )(*masters, x, cot, *others)


FIRST = 4


def row_sums(count, body, width, size=128):
    def one(i, total):
        return body(pl.ds(pl.multiple_of(i * size, size), size), total)

    return lax.fori_loop(0, count // size, one, jnp.zeros((1, width), F32))


def head_step(j):
    return jnp.minimum(j // 2, HEADS - 1)


def backward_body(
    planes, tiles, total_chunks,
    dwf_ref, middle_in, nm_sum_in, cot_in, xnt_in, x_in, w_ref, proj_ref, mixed_ref, inv_ref, upd_ref, core_ref,
    small_ref, cols_ref, rows_ref, logs_ref, factor_ref, gain_ref,
    input_grad_out, own_gain1, own_mixer, own_decay, own_conv, own_log, own_bias, own_gain, own_out, own_gain2, own_ffn,
    own_down,
    middle_ref, nm_sum_ref, cot_ref, xnt_ref, x_ref, load_sem, flush_sem, gbt_ref, gains, dw, d_small, dcols, drows, dgain, dproj,
    value_ref, *scratch,
):
    gxn, grad_mid_ref, gb_ref = middle_ref, nm_sum_ref, cot_ref
    *buffers, got, stage, local_sem, send_sem, recv_sem, total_send, total_recv = scratch
    step = pl.program_id(0)
    tokens = middle_ref.shape[0]
    rows = own_mixer.shape[0]
    hidden = tiles * TILE
    me = lax.axis_index("dp")

    def tile_source(k, core):
        return dwf_ref.at[:, :, core, :, span(k, 3 * TILE, 0, 3 * TILE)]

    kinds = {
        FFN_TILE: (tile_source, None),
        HEAD: (
            lambda k, core: dw.at[k % 2, :, :, core],
            lambda k, plane, place, core: dw[k % 2, plane, place, core],
        ),
        SMALLS: (
            lambda k, core: d_small.at[:, :, core],
            lambda k, plane, place, core: d_small[plane, place, core],
        ),
    }

    def store(kind, k, total):
        def put(ref, start, source, width):
            ref[:, pl.ds(pl.multiple_of(start, 128), width)] = total[:, source : source + width]

        if kind == SMALLS:
            turned = jnp.concatenate([total[:, :SMALL], jnp.zeros((SMALL - rows, SMALL), F32)], axis=0).T
            own_decay[...] = turned[0:16, 0:rows]
            own_gain1[...] = turned[16:17, 0:rows]
            own_gain2[...] = turned[17:18, 0:rows]
            own_conv[...] = total[0:4, SMALL:]
        elif kind == HEAD:
            put(own_mixer, k * DK, 0, DK)
            put(own_mixer, HEADS * DK + k * DK, DK, DK)
            put(own_mixer, 2 * HEADS * DK + k * DV, 2 * DK, DV)
            put(own_mixer, 2 * HEADS * DK + HEADS * DV + k * DV, 2 * DK + DV, DV)
            put(own_out, k * DV, HEAD_COLS, DV)
        else:
            put(own_ffn, k * TILE, 0, TILE)
            put(own_ffn, hidden + k * TILE, TILE, TILE)
            put(own_down, k * TILE, 2 * TILE, TILE)

    work = Scatter(me, kinds, store, *buffers, local_sem, send_sem, recv_sem)
    def share(value):
        own_log[...] = value[0:1, 0:HEADS]
        own_bias[...] = value[1:2, 0:HEADS]
        own_gain[...] = jnp.concatenate([value[2:3], value[3:4]], axis=1)

    small_sum = Total(me, value_ref, share, got, stage, total_send, total_recv)

    last = total_chunks - 1

    def at(r, act):
        is_head = (r >= FIRST) & (r < last) & ((r - FIRST) % 2 == 0)
        is_early = (r >= 0) & (r < FIRST)
        is_tile = (r > FIRST) & (r < last) & ((r - FIRST) % 2 == 1)
        pl.when(is_early)(lambda: act(FFN_TILE, r, r))
        pl.when(is_tile)(lambda: act(FFN_TILE, r, (r + FIRST - 1) // 2))
        pl.when(is_head)(lambda: act(HEAD, r, (r - FIRST) // 2))
        pl.when(r == last)(lambda: act(SMALLS, r, 0))

    loads = [
        pltpu.make_async_copy(source, target, load_sem.at[i])
        for i, (source, target) in enumerate(
            (
                (middle_in, middle_ref), (nm_sum_in, nm_sum_ref), (cot_in, cot_ref), (xnt_in, xnt_ref), (x_in, x_ref),
            )
        )
    ]

    @pl.when(step == 0)
    def _():
        enter(me)
        work.core_step(FFN_TILE, 0, 0)
        work.core_step(FFN_TILE, 1, 1)
        work.load_step(FFN_TILE, 0, 0)
        dcols[...] = jnp.zeros_like(dcols)
        drows[...] = jnp.zeros_like(drows)
        dgain[...] = jnp.zeros_like(dgain)
        d_small[...] = jnp.zeros_like(d_small)
        for copy in loads:
            copy.start()
        for r in (0, 1):
            work.chip_step(FFN_TILE, r, r)
            work.core_step(FFN_TILE, r + 2, r + 2)
            work.load_step(FFN_TILE, r + 1, r + 1)

    at(step - 6, work.last_step)
    at(step - 4, work.relay_step)
    at(step - 2, work.square_step)
    at(step, work.corner_step)
    at(step + 2, work.chip_step)
    at(step + 3, work.load_step)

    @pl.when(step == 0)
    def _():
        for copy in loads:
            copy.wait()
        turned = merge(small_ref[..., 0:SMALL]).astype(F32).T
        gains[0:1, :] = turned[16:17, :]
        gains[1:2, :] = turned[17:18, :]

        def back(rows, total):
            mid = middle_ref[rows, :]
            scale = lax.rsqrt(jnp.mean(mid * mid, axis=1, keepdims=True) + epsilon)
            normed = mid * scale
            grad = nm_sum_ref[rows, :]
            d_normed = grad * gains[1:2, :]
            d_mid = scale * (d_normed - normed * jnp.mean(d_normed * normed, axis=1, keepdims=True))
            d_mid = d_mid + cot_ref[rows, :].astype(F32)
            gxn[rows, :] = jnp.zeros_like(mid)
            grad_mid_ref[rows, :] = d_mid
            gb_ref[rows, :] = d_mid.astype(BF16)
            gbt_ref[:, rows] = d_mid.T.astype(BF16)
            return total + jnp.sum(grad * normed, axis=0, keepdims=True)

        gains[2:3, :] = row_sums(tokens, back, gains.shape[1])

    @pl.when((step < 2 * HEADS) & (step % 2 == 0))
    def _():
        head = step // 2
        w = merge(w_ref[...])
        grad_mixed = jnp.dot(gb_ref[...], w[:, HEAD_COLS:], preferred_element_type=F32)
        d_out = jnp.dot(gbt_ref[...], mixed_ref[...], preferred_element_type=F32).astype(BF16)
        dw[head % 2, :, :, :, :, pl.ds(HEAD_COLS, DV)] = d_out.reshape(dw.shape[1:5] + (DV,))

        projected = proj_ref[...]
        taps = head_taps(small_ref, head)
        keeps, conv, gate, act, qn, k, value, q_scale, k_scale, cum, rate, seg = head_inputs(
            projected, taps, cols_ref[...], head
        )
        q = qn * DK**-0.5
        cum_row = rows_ref[pl.ds(head, 1), :]
        seg_row = rows_ref[8:9, :]
        gain = gain_ref[...]
        lanes = lane_index((SEQ, 128))
        d_act, d_gain = [], jnp.zeros((1, DV), F32)
        for start in range(0, tokens, SEQ):
            part = slice(start, start + SEQ)
            core, update, inverse = core_ref[0, part, :], upd_ref[0, part, :], inv_ref[0, part, :]
            grad = grad_mixed[part]
            scale = lax.rsqrt(jnp.mean(core * core, axis=1, keepdims=True) + head_epsilon)
            normed = core * scale
            out_gate = projected[part, CONV_COLS:]
            out_sig = sigmoid(out_gate)
            swish = out_gate * out_sig
            dproj[part, CONV_COLS:] = (grad * normed * gain * (out_sig + swish * (1.0 - out_sig))).astype(BF16)
            d_normed = grad * swish
            d_gain = d_gain + jnp.sum(d_normed * normed, axis=0, keepdims=True)
            d_scaled = d_normed * gain
            d_core = scale * (d_scaled - normed * jnp.mean(d_scaled * normed, axis=1, keepdims=True))

            qs, ks, vs, rs = q[part], k[part], value[part], rate[part]
            pair = decays(seg[part], seg_row[:, part], cum[part], cum_row[:, part])
            key_dots = dot3(ks, ks, NT)
            query_dots = dot3(qs, ks, NT)
            d_scores = dot3(d_core, update, NT)
            d_update = dot3(pair * query_dots, d_core, TN)
            solved = dot_high(inverse, d_update, TN)
            d_coupling = strict(-dot3(solved, update, NT)) * pair
            d_query_dots = pair * d_scores
            d_key_dots = d_coupling * rs
            weighed = d_coupling * key_dots
            d_spread = d_query_dots * query_dots + weighed * rs
            d_q = dot1(d_query_dots, ks, NN) * DK**-0.5
            d_k = dot1(d_query_dots, qs, TN) + dot1(d_key_dots, ks, NN) + dot1(d_key_dots, ks, TN)
            d_rate = jnp.sum(solved * vs, axis=1, keepdims=True) + jnp.sum(weighed, axis=1, keepdims=True)
            row_sum = jnp.sum(d_spread, axis=1, keepdims=True)
            dcols[part, :] += jnp.where(lanes == head, row_sum, 0.0) + jnp.where(lanes == 8 + head, d_rate, 0.0)
            drows[pl.ds(head, 1), part] = jnp.sum(d_spread, axis=0, keepdims=True)
            d_q_act = q_scale[part] * (d_q - qn[part] * jnp.sum(d_q * qn[part], axis=1, keepdims=True))
            d_k_act = k_scale[part] * (d_k - ks * jnp.sum(d_k * ks, axis=1, keepdims=True))
            d_act.append(jnp.concatenate([d_q_act, d_k_act, rs * solved], axis=1))
        dgain[0:1, :] += d_gain
        d_conv = jnp.concatenate(d_act, axis=0) * (gate + act * (1.0 - gate))
        source = projected[:, :CONV_COLS]
        d_source = d_conv * taps[0:1]
        d_taps = [jnp.sum(d_conv * source, axis=0, keepdims=True)]
        for back in (1, 2, 3):
            kept = d_conv * keeps[back - 1]
            d_source = d_source + pltpu.roll(kept, tokens - back, 0) * taps[back : back + 1]
            d_taps.append(jnp.sum(kept * pltpu.roll(source, back, 0), axis=0, keepdims=True))
        d_taps = jnp.concatenate(d_taps + [jnp.zeros((rows - 4, CONV_COLS), F32)], axis=0).astype(BF16)
        wide = 2 * head
        places = [(0, head), (1, head)] + [(2 + head // 4, wide % 8 + i) for i in (0, 1)]
        for i, (z, p) in enumerate(places):
            d_small[z, p // 2, p % 2, :, SMALL:] = d_taps[:, i * SMALL : (i + 1) * SMALL]
        dproj[:, :CONV_COLS] = d_source.astype(BF16)
        d_proj = dproj[...]
        d_in = jnp.dot(xnt_ref[...], d_proj, preferred_element_type=F32).astype(BF16)
        dw[head % 2, :, :, :, :, pl.ds(0, HEAD_COLS)] = d_in.reshape(dw.shape[1:5] + (HEAD_COLS,))
        gxn[...] += lax.dot_general(d_proj, w[:, :HEAD_COLS], (NT, ((), ())), preferred_element_type=F32)

    @pl.when(step == 2 * HEADS - 1)
    def _():
        small = merge(small_ref[..., 0:SMALL])
        lanes = lane_index((SEQ, 128))
        padded = jnp.concatenate([drows[...], jnp.zeros((120, tokens), F32)], axis=0).T
        d_logs = jnp.zeros((1, 128), F32)
        d_bias = jnp.zeros((1, 128), F32)
        d_logits = []
        for start in range(0, tokens, SEQ):
            part = slice(start, start + SEQ)
            d_cum = jnp.where(lanes < 8, dcols[part, :], 0.0) - padded[part]
            d_decay = triangle_sum(d_cum, TN)
            d_logit = jnp.where(lanes < 8, d_decay, dcols[part, :]) * factor_ref[part, :]
            d_logs = d_logs + jnp.sum(jnp.where(lanes < 8, d_decay * logs_ref[part, :], 0.0), axis=0, keepdims=True)
            d_bias = d_bias + jnp.sum(jnp.where(lanes < 8, d_logit, 0.0), axis=0, keepdims=True)
            d_logits.append(d_logit.astype(BF16))
        d_logits = jnp.concatenate(d_logits, axis=0)
        value_ref[...] = jnp.concatenate(
            [d_logs, d_bias, dgain[0:1, :128], dgain[0:1, 128:], jnp.zeros((4, 128), F32)], axis=0
        )
        gxn[...] += lax.dot_general(d_logits, small, (NT, ((), ())), preferred_element_type=F32)

        def back(at_rows, total):
            x = x_ref[at_rows, :].astype(F32)
            scale = lax.rsqrt(jnp.mean(x * x, axis=1, keepdims=True) + epsilon)
            normed = x * scale
            grad = gxn[at_rows, :]
            d_normed = grad * gains[0:1, :]
            d_x = scale * (d_normed - normed * jnp.mean(d_normed * normed, axis=1, keepdims=True))
            grad_mid_ref[at_rows, :] = d_x + grad_mid_ref[at_rows, :]
            return total + jnp.sum(grad * normed, axis=0, keepdims=True)

        total = row_sums(tokens, back, gxn.shape[1])
        line = lax.broadcasted_iota(jnp.int32, (128, total.shape[1]), 0)
        lines = jnp.where(line == 16, total, jnp.where(line == 17, gains[2:3, :], 0.0))
        own = jnp.dot(xnt_ref[...], d_logits, preferred_element_type=F32) + lines.T
        d_small[:, :, :, :, 0:SMALL] = own.astype(BF16).reshape(d_small.shape[:4] + (SMALL,))

    flush = pltpu.make_async_copy(grad_mid_ref, input_grad_out, flush_sem)
    pl.when(step == 2 * HEADS)(flush.start)
    pl.when(step == pl.num_programs(0) - 1)(flush.wait)

    at(step + 4, work.core_step)
    for number in range(len(Total.bits) + 1):
        pl.when(step == 2 * HEADS + number)(lambda number=number: small_sum.step(number))


def backward(planes, dwf, middle, nm_sum, cot, xnt, w, proj, mixed, inv, upd, core, small, cols, seq_rows, logs, factor,
             gain, x):
    tokens, width = middle.shape
    rows = small.shape[4]
    tiles = dwf.shape[1] // (3 * TILE)
    chunks = FIRST + 2 * HEADS
    assert tiles == FIRST + HEADS - 1
    hbm = pl.BlockSpec(memory_space=pl.ANY)
    head = head_step
    save = pl.BlockSpec((1, tokens, SEQ), lambda i: (head(i), 0, 0))
    shape = jax.ShapeDtypeStruct
    widest = HEAD_COLS + DV
    depth = Scatter.depths
    outs = [
        ((tokens, width), F32),
        ((1, rows), F32),
        ((rows, HEADS * HEAD_COLS), F32),
        ((16, rows), F32),
        ((4, SMALL), F32),
        ((1, HEADS), F32),
        ((1, HEADS), F32),
        ((1, DV), F32),
        ((rows, HEADS * DV), F32),
        ((1, rows), F32),
        ((rows, 2 * tiles * TILE), F32),
        ((rows, tiles * TILE), F32),
    ]
    return pl.pallas_call(
        partial(backward_body, planes, tiles, chunks),
        grid=(chunks + 6,),
        in_specs=[
            hbm,
            hbm,
            hbm,
            hbm,
            hbm,
            hbm,
            pl.BlockSpec((planes, 2, 2, 2, rows, widest), lambda i: (0, 0, 0, 0, 0, head(i))),
            pl.BlockSpec((tokens, HEAD_COLS), lambda i: (0, head(i))),
            pl.BlockSpec((tokens, DV), lambda i: (0, head(i))),
            save,
            save,
            save,
        ]
        + [once(a.shape) for a in (small, cols, seq_rows, logs, factor, gain)],
        out_specs=[hbm] + [once(o[0]) for o in outs[1:]],
        out_shape=[shape(*o) for o in outs],
        scratch_shapes=[
            pltpu.VMEM((tokens, width), F32),
            pltpu.VMEM((tokens, width), F32),
            pltpu.VMEM((tokens, width), BF16),
            pltpu.VMEM((width, tokens), BF16),
            pltpu.VMEM((tokens, width), BF16),
            pltpu.SemaphoreType.DMA((5,)),
            pltpu.SemaphoreType.DMA,
            pltpu.VMEM((width, tokens), BF16),
            pltpu.VMEM((8, width), F32),
            pltpu.VMEM((2, planes, 4, 2, rows, widest), BF16),
            pltpu.VMEM((planes, 4, 2, rows, 2 * SMALL), BF16),
            pltpu.VMEM((tokens, 128), F32),
            pltpu.VMEM((HEADS, tokens), F32),
            pltpu.VMEM((8, DV), F32),
            pltpu.VMEM((tokens, HEAD_COLS), BF16),
            pltpu.VMEM((8, 128), F32),
            pltpu.VMEM((depth[B_CORE], planes, 4, rows, widest), BF16),
            pltpu.VMEM((depth[B_KEEP], planes, 4, rows, 3 * TILE), BF16),
            pltpu.VMEM((depth[B_SUMS], planes, 4, rows, widest), BF16),
            pltpu.VMEM((depth[B_XY], planes, rows, HEAD_COLS), BF16),
            pltpu.VMEM((depth[B_X], planes, rows, HEAD_COLS), BF16),
            pltpu.VMEM((depth[B_Y], planes, rows, HEAD_COLS), BF16),
            pltpu.VMEM((depth[B_Z], 3, rows, HEAD_COLS), BF16),
            pltpu.VMEM((depth[B_TWO_Z], 3, 4, rows, DV), BF16),
            pltpu.VMEM((depth[B_TWO], 3, rows, DV), BF16),
            pltpu.VMEM((len(Total.bits), 8, 128), F32),
            pltpu.VMEM((len(Total.bits), 8, 128), F32),
            pltpu.SemaphoreType.DMA((chunks,)),
            pltpu.SemaphoreType.DMA((chunks, Scatter.copies)),
            pltpu.SemaphoreType.DMA((chunks, Scatter.copies)),
            pltpu.SemaphoreType.DMA((len(Total.bits),)),
            pltpu.SemaphoreType.DMA((len(Total.bits),)),
        ],
        compiler_params=pltpu.CompilerParams(
            collective_id=1, has_side_effects=True, vmem_limit_bytes=63 * MIB
        ),
        name="backward",
    )(
        dwf.reshape(planes, 4, 2, rows, dwf.shape[1]), middle, nm_sum, cot, xnt, x, w, proj, mixed, inv, upd, core, small,
        cols, seq_rows, logs, factor, gain,
    )


def hand_over_body(count, *refs):
    for source, target in zip(refs[:count], refs[count:]):
        target[...] = source[...]


def hand_over(arrays, steps=2):
    specs = []
    for a in arrays:
        rows, cols = a.shape
        if rows % (32 * steps) == 0:
            specs.append(pl.BlockSpec((rows // steps, cols), lambda i: (i, 0)))
        elif cols % (128 * steps) == 0:
            specs.append(pl.BlockSpec((rows, cols // steps), lambda i: (0, i)))
        else:
            specs.append(pl.BlockSpec((rows, cols), lambda i: (0, 0)))
    return pl.pallas_call(
        partial(hand_over_body, len(arrays)),
        grid=(steps,),
        in_specs=specs,
        out_specs=specs,
        out_shape=[jax.ShapeDtypeStruct(a.shape, a.dtype) for a in arrays],
        compiler_params=pltpu.CompilerParams(vmem_limit_bytes=60 * MIB),
        name="hand_over",
    )(*arrays)


def mixer_fwd_body(xn_ref, w_ref, taps_ref, cols_ref, rows_ref, gain_ref, proj_ref, mixed_ref, inv_ref, upd_ref, core_ref):
    head = pl.program_id(0)
    tokens = xn_ref.shape[0]
    projected = jnp.dot(xn_ref[...], w_ref[...], preferred_element_type=F32)
    proj_ref[...] = projected
    _, _, _, _, q, k, value, _, _, cum, rate, seg = head_inputs(
        projected, taps_ref[...], cols_ref[...], head
    )
    q = q * DK**-0.5
    cum_row = rows_ref[pl.ds(head, 1), :]
    seg_row = rows_ref[8:9, :]
    parts = [slice(s, s + SEQ) for s in range(0, tokens, SEQ)]
    scores, couplings = [], []
    for part in parts:
        pair = decays(seg[part], seg_row[:, part], cum[part], cum_row[:, part])
        key_dots = dot3(k[part], k[part], NT)
        scores.append(pair * dot3(q[part], k[part], NT))
        couplings.append(strict(pair * key_dots) * rate[part])
    inverses = unit_inverses(couplings)
    for i, part in enumerate(parts):
        update = dot3(inverses[i], rate[part] * value[part], NN)
        core = dot3(scores[i], update, NN)
        inv_ref[0, part, :] = inverses[i].astype(BF16)
        upd_ref[0, part, :] = update
        core_ref[0, part, :] = core
        scale = lax.rsqrt(jnp.mean(core * core, axis=1, keepdims=True) + head_epsilon)
        out_gate = projected[part, CONV_COLS:]
        mixed_ref[part, :] = (core * scale * gain_ref[...] * (out_gate * sigmoid(out_gate))).astype(BF16)


def mixer_fwd(xn, w, taps, cols, rows, gain):
    tokens, width = xn.shape
    const = lambda h: (0, 0)
    by_head = lambda h: (0, h)
    save = pl.BlockSpec((1, tokens, SEQ), lambda h: (h, 0, 0))
    return pl.pallas_call(
        mixer_fwd_body,
        grid=(HEADS,),
        in_specs=[
            pl.BlockSpec((tokens, width), const),
            pl.BlockSpec((width, HEAD_COLS), by_head),
            pl.BlockSpec((4, CONV_COLS), by_head),
            pl.BlockSpec(cols.shape, const),
            pl.BlockSpec(rows.shape, const),
            pl.BlockSpec((1, DV), const),
        ],
        out_specs=[
            pl.BlockSpec((tokens, HEAD_COLS), by_head),
            pl.BlockSpec((tokens, DV), by_head),
            save,
            save,
            save,
        ],
        out_shape=[
            jax.ShapeDtypeStruct((tokens, HEADS * HEAD_COLS), F32),
            jax.ShapeDtypeStruct((tokens, HEADS * DV), BF16),
            jax.ShapeDtypeStruct((HEADS, tokens, SEQ), BF16),
            jax.ShapeDtypeStruct((HEADS, tokens, DV), F32),
            jax.ShapeDtypeStruct((HEADS, tokens, DV), F32),
        ],
        compiler_params=pltpu.CompilerParams(vmem_limit_bytes=56 * MIB),
        name="mixer_fwd",
    )(xn, w, taps, cols, rows, gain)


def mixer_bwd_body(
    gb_ref, gbt_ref, xnt_ref, wo_ref, w_ref, proj_ref, mixed_ref, inv_ref, upd_ref, core_ref,
    taps_ref, cols_ref, rows_ref, gain_ref,
    dw_ref, dwo_ref, gxn_ref, dcols_ref, drows_ref, dtaps_ref, dgain_ref, dproj_ref,
):
    head = pl.program_id(0)
    tokens = gb_ref.shape[0]

    @pl.when(head == 0)
    def _():
        gxn_ref[...] = jnp.zeros_like(gxn_ref)
        dcols_ref[...] = jnp.zeros_like(dcols_ref)
        drows_ref[...] = jnp.zeros_like(drows_ref)
        dgain_ref[...] = jnp.zeros_like(dgain_ref)

    grad_mixed = jnp.dot(gb_ref[...], wo_ref[...], preferred_element_type=F32)
    dwo_ref[...] = jnp.dot(gbt_ref[...], mixed_ref[...], preferred_element_type=F32).astype(BF16)

    projected = proj_ref[...]
    taps = taps_ref[...]
    keep, conv, gate, act, qn, k, value, q_scale, k_scale, cum, rate, seg = head_inputs(
        projected, taps, cols_ref[...], head
    )
    q = qn * DK**-0.5
    cum_row = rows_ref[pl.ds(head, 1), :]
    seg_row = rows_ref[8:9, :]
    gain = gain_ref[...]
    lanes = lax.broadcasted_iota(jnp.int32, (SEQ, 128), 1)
    d_act, d_gain = [], jnp.zeros((1, DV), F32)
    for start in range(0, tokens, SEQ):
        part = slice(start, start + SEQ)
        core, update, inverse = core_ref[0, part, :], upd_ref[0, part, :], inv_ref[0, part, :]
        grad = grad_mixed[part]
        scale = lax.rsqrt(jnp.mean(core * core, axis=1, keepdims=True) + head_epsilon)
        normed = core * scale
        out_gate = projected[part, CONV_COLS:]
        out_sig = sigmoid(out_gate)
        swish = out_gate * out_sig
        dproj_ref[part, CONV_COLS:] = (grad * normed * gain * (out_sig + swish * (1.0 - out_sig))).astype(BF16)
        d_normed = grad * swish
        d_gain = d_gain + jnp.sum(d_normed * normed, axis=0, keepdims=True)
        d_scaled = d_normed * gain
        d_core = scale * (d_scaled - normed * jnp.mean(d_scaled * normed, axis=1, keepdims=True))

        qs, ks, vs, rs = q[part], k[part], value[part], rate[part]
        pair = decays(seg[part], seg_row[:, part], cum[part], cum_row[:, part])
        key_dots = dot3(ks, ks, NT)
        query_dots = dot3(qs, ks, NT)
        d_scores = dot3(d_core, update, NT)
        d_update = dot1(pair * query_dots, d_core, TN)
        solved = dot1(inverse, d_update, TN)
        d_coupling = strict(-dot1(solved, update, NT)) * pair
        d_query_dots = pair * d_scores
        d_key_dots = d_coupling * rs
        weighed = d_coupling * key_dots
        d_spread = d_query_dots * query_dots + weighed * rs
        d_q = dot1(d_query_dots, ks, NN) * DK**-0.5
        d_k = dot1(d_query_dots, qs, TN) + dot1(d_key_dots, ks, NN) + dot1(d_key_dots, ks, TN)
        d_rate = jnp.sum(solved * vs, axis=1, keepdims=True) + jnp.sum(weighed, axis=1, keepdims=True)
        row_sum = jnp.sum(d_spread, axis=1, keepdims=True)
        dcols_ref[part, :] += jnp.where(lanes == head, d_rate, 0.0) + jnp.where(lanes == 8 + head, row_sum, 0.0)
        drows_ref[pl.ds(head, 1), part] = jnp.sum(d_spread, axis=0, keepdims=True)
        d_q_act = q_scale[part] * (d_q - qn[part] * jnp.sum(d_q * qn[part], axis=1, keepdims=True))
        d_k_act = k_scale[part] * (d_k - ks * jnp.sum(d_k * ks, axis=1, keepdims=True))
        d_act.append(jnp.concatenate([d_q_act, d_k_act, rs * solved], axis=1))
    dgain_ref[...] += d_gain
    d_conv = jnp.concatenate(d_act, axis=0) * (gate + act * (1.0 - gate))
    source = projected[:, :CONV_COLS]
    d_source = d_conv * taps[0:1]
    d_taps = [jnp.sum(d_conv * source, axis=0, keepdims=True)]
    for back in (1, 2, 3):
        kept = d_conv * keep[back - 1]
        d_source = d_source + pltpu.roll(kept, tokens - back, 0) * taps[back : back + 1]
        d_taps.append(jnp.sum(kept * pltpu.roll(source, back, 0), axis=0, keepdims=True))
    dtaps_ref[...] = jnp.concatenate(d_taps, axis=0)
    dproj_ref[:, :CONV_COLS] = d_source.astype(BF16)
    d_proj = dproj_ref[...]
    dw_ref[...] = jnp.dot(xnt_ref[...], d_proj, preferred_element_type=F32).astype(BF16)
    gxn_ref[...] += lax.dot_general(d_proj, w_ref[...], (NT, ((), ())), preferred_element_type=F32)


def mixer_bwd(gb, gbt, xnt, wo, w, proj, mixed, inv, upd, core, taps, cols, rows, gain):
    tokens, width = gb.shape
    const = lambda h: (0, 0)
    by_head = lambda h: (0, h)
    save = pl.BlockSpec((1, tokens, SEQ), lambda h: (h, 0, 0))
    return pl.pallas_call(
        mixer_bwd_body,
        grid=(HEADS,),
        in_specs=[
            pl.BlockSpec((tokens, width), const),
            pl.BlockSpec((width, tokens), const),
            pl.BlockSpec((width, tokens), const),
            pl.BlockSpec((width, DV), by_head),
            pl.BlockSpec((width, HEAD_COLS), by_head),
            pl.BlockSpec((tokens, HEAD_COLS), by_head),
            pl.BlockSpec((tokens, DV), by_head),
            save,
            save,
            save,
            pl.BlockSpec((4, CONV_COLS), by_head),
            pl.BlockSpec(cols.shape, const),
            pl.BlockSpec(rows.shape, const),
            pl.BlockSpec((1, DV), const),
        ],
        out_specs=[
            pl.BlockSpec((width, HEAD_COLS), by_head),
            pl.BlockSpec((width, DV), by_head),
            pl.BlockSpec((tokens, width), const),
            pl.BlockSpec((tokens, 128), const),
            pl.BlockSpec((HEADS, tokens), const),
            pl.BlockSpec((4, CONV_COLS), by_head),
            pl.BlockSpec((1, DV), const),
        ],
        out_shape=[
            jax.ShapeDtypeStruct((width, HEADS * HEAD_COLS), BF16),
            jax.ShapeDtypeStruct((width, HEADS * DV), BF16),
            jax.ShapeDtypeStruct((tokens, width), F32),
            jax.ShapeDtypeStruct((tokens, 128), F32),
            jax.ShapeDtypeStruct((HEADS, tokens), F32),
            jax.ShapeDtypeStruct((4, HEADS * CONV_COLS), F32),
            jax.ShapeDtypeStruct((1, DV), F32),
        ],
        scratch_shapes=[pltpu.VMEM((tokens, HEAD_COLS), BF16)],
        compiler_params=pltpu.CompilerParams(vmem_limit_bytes=60 * MIB),
        name="mixer_bwd",
    )(gb, gbt, xnt, wo, w, proj, mixed, inv, upd, core, taps, cols, rows, gain)


def ffn_body(nm_ref, nmt_ref, cot_ref, cott_ref, w_ref, dw_ref, out_ref, gnm_ref):
    @pl.when(pl.program_id(0) == 0)
    def _():
        out_ref[...] = jnp.zeros_like(out_ref)
        gnm_ref[...] = jnp.zeros_like(gnm_ref)

    w = w_ref[...]
    gate_up = jnp.dot(nm_ref[...], w[:, : 2 * TILE], preferred_element_type=F32)
    gate, up = gate_up[:, :TILE], gate_up[:, TILE:]
    sig = sigmoid(gate)
    swish = gate * sig
    hidden = (swish * up).astype(BF16)
    grad_hidden = jnp.dot(cot_ref[...], w[:, 2 * TILE :], preferred_element_type=F32)
    grad_gate = grad_hidden * up * (sig + swish * (1.0 - sig))
    grad_up = grad_hidden * swish
    grad_low = jnp.concatenate([grad_gate, grad_up], axis=1).astype(BF16)
    out_ref[...] += lax.dot_general(hidden, w[:, 2 * TILE :], (NT, ((), ())), preferred_element_type=F32)
    gnm_ref[...] += lax.dot_general(grad_low, w[:, : 2 * TILE], (NT, ((), ())), preferred_element_type=F32)
    dw_ref[:, : 2 * TILE] = jnp.dot(nmt_ref[...], grad_low, preferred_element_type=F32).astype(BF16)
    dw_ref[:, 2 * TILE :] = jnp.dot(cott_ref[...], hidden, preferred_element_type=F32).astype(BF16)


def ffn(nm, nmt, cot, cott, w):
    tokens, width = nm.shape
    tiles = w.shape[1] // (3 * TILE)
    const = lambda t: (0, 0)
    by_tile = lambda t: (0, t)
    return pl.pallas_call(
        ffn_body,
        grid=(tiles,),
        in_specs=[
            pl.BlockSpec((tokens, width), const),
            pl.BlockSpec((width, tokens), const),
            pl.BlockSpec((tokens, width), const),
            pl.BlockSpec((width, tokens), const),
            pl.BlockSpec((width, 3 * TILE), by_tile),
        ],
        out_specs=[
            pl.BlockSpec((width, 3 * TILE), by_tile),
            pl.BlockSpec((tokens, width), const),
            pl.BlockSpec((tokens, width), const),
        ],
        out_shape=[
            jax.ShapeDtypeStruct((width, tiles * 3 * TILE), BF16),
            jax.ShapeDtypeStruct((tokens, width), F32),
            jax.ShapeDtypeStruct((tokens, width), F32),
        ],
        compiler_params=pltpu.CompilerParams(vmem_limit_bytes=48 * MIB),
        name="ffn",
    )(nm, nmt, cot, cott, w)


def rms_scale(values):
    return lax.rsqrt(jnp.mean(values * values, axis=-1, keepdims=True) + epsilon)


def rms_back(grad, values, scale, gain):
    normed = values * scale
    d_normed = grad * gain
    d_values = scale * (d_normed - normed * jnp.mean(d_normed * normed, axis=-1, keepdims=True))
    return d_values, jnp.sum(grad * normed, axis=0)


def by_head(parts):
    shaped = [p.reshape(p.shape[0], HEADS, -1) for p in parts]
    return jnp.concatenate(shaped, axis=2).reshape(parts[0].shape[0], -1)


def from_head(values, sizes):
    shaped = values.reshape(values.shape[0], HEADS, -1)
    ends = [sum(sizes[: i + 1]) for i in range(len(sizes))]
    cuts = [shaped[:, :, e - s : e].reshape(values.shape[0], -1) for s, e in zip(sizes, ends)]
    return jnp.concatenate(cuts, axis=1)


def split_heads(values):
    key = HEADS * DK
    val = HEADS * DV
    edges = [0, key, 2 * key, 2 * key + val, 2 * key + 2 * val]
    return [values[:, a:b] for a, b in zip(edges[:-1], edges[1:]) if b <= values.shape[1]]


def plain_block(
    devices, tokens, segment_ids, cotangent, norm1_gain, mixer_in, decay_in, conv_weight, decay_log, decay_bias,
    head_gain, mixer_out, norm2_gain, ffn_in, ffn_out,
):
    rows, width = decay_in.shape[0], tokens.shape[1]
    count = tokens.shape[0]
    hidden = ffn_out.shape[0]
    tiles = hidden // TILE

    low = lambda v: v.astype(BF16)
    shard_mixer = by_head(split_heads(low(mixer_in)))
    conv_cols = conv_weight.shape[1]
    shard_small = jnp.concatenate(
        [low(decay_in), low(norm1_gain)[:, None], low(norm2_gain)[:, None], low(conv_weight).reshape(rows, -1)], axis=1
    )
    shard_small = jnp.pad(shard_small, ((0, 0), (0, SMALL - shard_small.shape[1])))
    shard_out = low(mixer_out).T
    ffn_low = low(ffn_in)
    pieces = [ffn_low[:, :hidden], ffn_low[:, hidden:], low(ffn_out).T]
    shard_ffn = jnp.concatenate([p.reshape(rows, tiles, TILE) for p in pieces], axis=2).reshape(rows, -1)
    shards = [shard_small, shard_mixer, shard_out, shard_ffn]

    x = tokens.astype(F32)
    scale1 = rms_scale(x)
    full_small, full_mixer, full_out, full_ffn = [lax.all_gather(s, "dp", axis=0, tiled=True) for s in shards]

    decay_full = full_small[:, :16]
    gain1 = full_small[:, 16].astype(F32)
    gain2 = full_small[:, 17].astype(F32)
    taps = full_small[:, 18 : 18 + 16].reshape(devices, 4, conv_cols)
    taps = jnp.moveaxis(taps, 0, 1).reshape(4, -1).astype(F32)
    taps = by_head(split_heads(taps))

    normed_in = low(x * scale1 * gain1)
    logits = jnp.dot(normed_in, decay_full, preferred_element_type=F32)
    shifted = logits[:, :HEADS] + decay_bias
    log_decay = -jnp.exp(decay_log) * jax.nn.softplus(shifted)
    rate = jax.nn.sigmoid(logits[:, HEADS:])
    sequences = count // SEQ
    lower = jnp.tril(jnp.ones((SEQ, SEQ), F32))
    cumulative = jnp.einsum(
        "ij,sjh->sih", lower, log_decay.reshape(sequences, SEQ, HEADS), precision=lax.Precision.HIGHEST
    ).reshape(count, HEADS)
    position = jnp.arange(count) % SEQ
    keeps = []
    for back in (1, 2, 3):
        earlier = jnp.pad(segment_ids[:-back], (back, 0), constant_values=-1)
        keeps.append(((earlier == segment_ids) & (position >= back)).astype(F32)[:, None])
    segment = segment_ids.astype(F32)
    cols = jnp.concatenate([cumulative, rate] + keeps + [segment[:, None]], axis=1)
    cols = jnp.pad(cols, ((0, 0), (0, 128 - cols.shape[1])))
    seq_rows = jnp.concatenate([cumulative.T, segment[None], jnp.zeros((7, count), F32)], axis=0)
    gain_row = head_gain[None]

    proj, mixed, inverse, update, core = mixer_fwd(normed_in, full_mixer, taps, cols, seq_rows, gain_row)

    middle = x + lax.dot_general(mixed, full_out, (NT, ((), ())), preferred_element_type=F32)
    scale2 = rms_scale(middle)
    normed_mid = low(middle * scale2 * gain2)
    dw_ffn, ffn_sum, grad_nm = ffn(normed_mid, normed_mid.T, cotangent, cotangent.T, full_ffn)
    output = low(middle + ffn_sum)

    d_middle, d_gain2 = rms_back(grad_nm, middle, scale2, gain2)
    grad_middle = d_middle + cotangent.astype(F32)
    branch = low(grad_middle)
    dw_mixer, dw_out, grad_xn, d_cols, d_rows, d_taps, d_gain = mixer_bwd(
        branch, branch.T, normed_in.T, full_out, full_mixer, proj, mixed, inverse, update, core,
        taps, cols, seq_rows, gain_row,
    )

    d_cum = d_cols[:, 8:16] - d_rows.T
    d_decay = jnp.einsum(
        "ji,sjh->sih", lower, d_cum.reshape(sequences, SEQ, HEADS), precision=lax.Precision.HIGHEST
    ).reshape(count, HEADS)
    d_shifted = -d_decay * jnp.exp(decay_log) * jax.nn.sigmoid(shifted)
    d_rate = d_cols[:, :8] * rate * (1.0 - rate)
    d_logits = low(jnp.concatenate([d_shifted, d_rate], axis=1))
    grad_xn = grad_xn + lax.dot_general(d_logits, decay_full, (NT, ((), ())), preferred_element_type=F32)
    d_x, d_gain1 = rms_back(grad_xn, x, scale1, gain1)
    input_grad = d_x + grad_middle

    d_decay_in = lax.dot_general(normed_in, d_logits, (TN, ((), ())), preferred_element_type=F32)
    d_taps = from_head(d_taps, [DK, DK, DV])
    d_taps = jnp.moveaxis(d_taps.reshape(4, devices, conv_cols), 1, 0).reshape(width, -1)
    dw_small = jnp.concatenate([d_decay_in, d_gain1[:, None], d_gain2[:, None], d_taps], axis=1)
    dw_small = low(jnp.pad(dw_small, ((0, 0), (0, SMALL - dw_small.shape[1]))))
    shared = jnp.concatenate([jnp.sum(d_decay * log_decay, axis=0), jnp.sum(d_shifted, axis=0), d_gain[0]])

    own_ffn, own_out, own_mixer, own_small = [
        lax.psum_scatter(g.astype(F32), "dp", scatter_dimension=0, tiled=True)
        for g in (dw_ffn, dw_out, dw_mixer, dw_small)
    ]
    shared = lax.psum(shared, "dp")

    own_tiles = own_ffn.reshape(rows, tiles, 3, TILE)
    ffn_in_grad = jnp.concatenate([own_tiles[:, :, i].reshape(rows, hidden) for i in (0, 1)], axis=1)
    ffn_out_grad = own_tiles[:, :, 2].reshape(rows, hidden).T
    return (
        output,
        input_grad,
        own_small[:, 16],
        from_head(own_mixer, [DK, DK, DV, DV]),
        own_small[:, :16],
        own_small[:, 18 : 18 + 16].reshape(4, conv_cols),
        shared[:HEADS],
        shared[HEADS : 2 * HEADS],
        shared[2 * HEADS : 2 * HEADS + DV],
        own_out.T,
        own_small[:, 17],
        ffn_in_grad,
        ffn_out_grad,
    )


def direct_block(
    devices, tokens, segment_ids, cotangent, norm1_gain, mixer_in, decay_in, conv_weight, decay_log, decay_bias,
    head_gain, mixer_out, norm2_gain, ffn_in, ffn_out,
):
    planes = devices // 8
    gain = head_gain[None]
    masters = [
        mixer_in, mixer_out.T, ffn_in, ffn_out.T, decay_in.T, norm1_gain[None], norm2_gain[None], conv_weight,
    ]
    (
        _, full_heads, _, small, xnt, cols, seq_rows, logs, factor, middle, proj, mixed, inverse, update, core, dwf,
        output, nm_sum,
    ) = forward(
        planes, masters, tokens, cotangent, segment_ids[None], decay_log[None], decay_bias[None], gain
    )
    results = backward(
        planes, dwf, middle, nm_sum, cotangent, xnt, full_heads, proj, mixed, inverse, update, core, small, cols,
        seq_rows, logs, factor, gain, tokens,
    )
    (
        output, input_grad, d_gain1, d_mixer_in, d_decay_in, d_conv, d_log, d_bias, d_gain, d_mixer_out, d_gain2, d_ffn_in,
        d_ffn_out,
    ) = hand_over([output, *results])
    return (
        output, input_grad, d_gain1[0], d_mixer_in, d_decay_in.T, d_conv, d_log[0], d_bias[0], d_gain[0], d_mixer_out.T,
        d_gain2[0], d_ffn_in, d_ffn_out.T,
    )


def on_device(devices, *arguments):
    rows, conv_cols = arguments[4].shape[0], arguments[6].shape[1]
    direct = rows % 16 == 0 and devices == 32 and conv_cols == 128
    return (direct_block if direct else plain_block)(devices, *arguments)


def solution(mesh):
    in_specs = (
        P("dp", None), P("dp"), P("dp", None), P("dp"), P("dp", None), P("dp", None), P(None, "dp"), P(), P(), P(),
        P(None, "dp"), P("dp"), P("dp", None), P(None, "dp"),
    )
    out_specs = (
        P("dp", None), P("dp", None), P("dp"), P("dp", None), P("dp", None), P(None, "dp"), P(), P(), P(),
        P(None, "dp"), P("dp"), P("dp", None), P(None, "dp"),
    )
    return jax.shard_map(
        partial(on_device, mesh.shape["dp"]), mesh=mesh, in_specs=in_specs, out_specs=out_specs, check_vma=False
    )
```
